32 devices in a mesh: batch: 4 (over y, x), expert: 8 (over z, core).
Axes of the slice: x: 2, y: 2, z: 4, core: 2. Of those that a mesh axis runs over, the one named last changes fastest.
Arguments:
- tokens: bfloat16 [4, 4096, 768], P('batch', 'expert'), may hold values from -6 to 6
- routes: int32 [4, 4096, 1], P('batch', 'expert'), may hold values from 0 to 7
- gain_one: float32 [768], replicated, may hold values from 0.5 to 1.5
- in_proj: bfloat16 [768, 3072], replicated, may hold values from -0.21875 to 0.21875
- conv_weight: float32 [4, 1536], replicated, may hold values from -3 to 3
- conv_bias: float32 [1536], replicated, may hold values from -1.5 to 1.5
- x_proj: bfloat16 [80, 1536], replicated, may hold values from -0.15625 to 0.15625
- dt_proj: bfloat16 [48, 1536], replicated, may hold values from -1.75 to 1.75
- dt_bias: float32 [1536], replicated, may hold values from -8 to -2
- rate_log: float32 [16, 1536], replicated, may hold values from -8 to 3
- skip: float32 [1536], replicated, may hold values from 0.5 to 1.5
- out_proj: bfloat16 [1536, 768], replicated, may hold values from -0.15625 to 0.15625
- gain_two: float32 [768], replicated, may hold values from 0.5 to 1.5
- router: bfloat16 [8, 768], replicated, may hold values from -0.109375 to 0.109375
- expert_in: bfloat16 [8, 768, 3072], P('expert'), may hold values from -0.21875 to 0.21875
- expert_out: bfloat16 [8, 3072, 768], P('expert'), may hold values from -2.5 to 2.5
- cotangent: bfloat16 [4, 4096, 768], P('batch', 'expert'), may hold values from -6 to 6
Outputs:
- output: bfloat16 [4, 4096, 768], P('batch', 'expert')
- tokens_grad: float32 [4, 4096, 768], P('batch', 'expert')
- gain_one_grad: float32 [768], replicated
- in_proj_grad: float32 [768, 3072], P('expert')
- conv_weight_grad: float32 [4, 1536], replicated
- conv_bias_grad: float32 [1536], replicated
- x_proj_grad: float32 [80, 1536], replicated
- dt_proj_grad: float32 [48, 1536], replicated
- dt_bias_grad: float32 [1536], replicated
- rate_log_grad: float32 [16, 1536], replicated
- skip_grad: float32 [1536], replicated
- out_proj_grad: float32 [1536, 768], P('expert')
- gain_two_grad: float32 [768], replicated
- router_grad: float32 [8, 768], replicated
- expert_in_grad: float32 [8, 768, 3072], P('expert', 'batch')
- expert_out_grad: float32 [8, 3072, 768], P('expert', 'batch')
The draws below stay inside these ranges and needn't reach their ends.
All inputs are finite; a program needn't handle non-finite values.
Results may differ from the reference program's by a relative error of at most 0.02.
Values may be sent and summed in bfloat16 or wider, within the bound.
A program may use at most 256 MiB of HBM per device.

```python
import math
import jax
import jax.numpy as jnp
from jax import lax

D = 768
INNER = 1536
STATE = 16
RANK = 48
WIDTH = 4
FF = 3072
TOK_DEV = 512
EXPERTS = 8
CAP = 80
SEQ = 4096
SEQS = 4


def draw_dt_bias(key, part):
    key = jax.random.fold_in(key, 23)
    lowest = 0.3
    factor = jax.random.uniform(key, (INNER,), jnp.float32, lowest, 1.5)
    return jnp.log(factor / math.sqrt(SEQ))


def draw_rate_log(key, part):
    key = jax.random.fold_in(key, 11)
    pick_key, slow_key, fast_key = jax.random.split(key, 3)
    root = math.sqrt(SEQ)
    slow = jax.random.uniform(slow_key, (STATE, INNER), jnp.float32, math.log(0.2 / root), math.log(3.0 / root))
    fast = jax.random.uniform(fast_key, (STATE, INNER), jnp.float32, math.log(2.0), math.log(16.0))
    share = 0.5
    chosen = jax.random.uniform(pick_key, (STATE, INNER), jnp.float32) < share
    return jnp.where(chosen, slow, fast)


def level_of(rng, shape, cuts, least, largest):
    level, own = 1.0, jax.random.fold_in(rng, 6)
    for axis_at, parts in cuts:
        draws = jnp.exp(jax.random.uniform(jax.random.fold_in(own, axis_at), (parts,), jnp.float32, least / len(cuts), largest / len(cuts)))
        level = level * jnp.repeat(draws, shape[axis_at] // parts).reshape([-1 if axis == axis_at else 1 for axis in range(len(shape))])
    return level


def different_ones(own_key, rows, number_of, top, lift):
    sequence = jax.random.permutation(jax.random.fold_in(own_key, 1), number_of)
    boost = sequence
    for power in range(3):
        boost = boost * boost // number_of
    boost = boost * lift // number_of
    chance = jax.random.randint(jax.random.fold_in(own_key, 2), (rows, number_of), 0, 4096) + boost
    fixed_rows = jax.random.permutation(jax.random.fold_in(own_key, 3), rows)[jnp.arange(number_of) % rows]
    chance = jnp.where(jnp.arange(rows)[:, None] == fixed_rows[None, :], 1 << 14, chance)
    priority = chance * number_of + jnp.arange(number_of)
    return lax.top_k(priority.astype(jnp.int32), top)[1].astype(jnp.int32)


def normal_values(own_key, extent, scale, limit, cuts=(), kind=jnp.bfloat16):
    values = jax.random.normal(own_key, extent, jnp.float32) * scale
    if len(cuts) > 0:
        values = level_of(own_key, extent, cuts, -0.22, 0.18) * values
    return jnp.clip(values, min=-limit, max=limit).astype(kind)


def setup_inputs(seed: int = 0) -> dict:
    splits = jax.random.split(jax.random.key(seed), 18)
    return {
        "tokens": normal_values(splits[0], (SEQS, SEQ, D), 1.0, 6.0, ((0, 4), (1, 8))),
        "routes": different_ones(splits[1], SEQS * SEQ, EXPERTS, 1, 2048).reshape((SEQS, SEQ, 1)),
        "gain_one": jnp.clip(1.0 + 0.1 * jax.random.normal(splits[2], (D,), jnp.float32), 0.5, 1.5),
        "in_proj": normal_values(splits[3], (D, 2 * INNER), D ** -0.5, 0.21875),
        "conv_weight": normal_values(splits[4], (WIDTH, INNER), WIDTH ** -0.5, 3.0, (), jnp.float32),
        "conv_bias": normal_values(splits[5], (INNER,), 0.3, 1.5, (), jnp.float32),
        "x_proj": normal_values(splits[6], (RANK + 2 * STATE, INNER), INNER ** -0.5, 0.15625),
        "dt_proj": normal_values(splits[7], (RANK, INNER), (max(1, RANK // 4)) ** -0.5, 1.75),
        "dt_bias": draw_dt_bias(jax.random.fold_in(splits[17], 71), 0),
        "rate_log": draw_rate_log(jax.random.fold_in(splits[17], 71), 0),
        "skip": jnp.clip(1.0 + 0.1 * jax.random.normal(splits[10], (INNER,), jnp.float32), 0.5, 1.5),
        "out_proj": normal_values(splits[11], (INNER, D), INNER ** -0.5, 0.15625),
        "gain_two": jnp.clip(1.0 + 0.1 * jax.random.normal(splits[12], (D,), jnp.float32), 0.5, 1.5),
        "router": normal_values(splits[13], (EXPERTS, D), (4 * D) ** -0.5, 0.109375),
        "expert_in": normal_values(splits[14], (EXPERTS, D, FF), D ** -0.5, 0.21875, ((0, 8),)),
        "expert_out": normal_values(splits[15], (EXPERTS, FF, D), (max(1, (FF * 16) // (EXPERTS * 1024))) ** -0.5, 2.5, ((0, 8),)),
        "cotangent": normal_values(splits[16], (SEQS, SEQ, D), 1.0, 6.0, ((0, 4), (1, 8))),
    }


@jax.custom_vjp
def low(v):
    return lax.optimization_barrier(v.astype(jnp.bfloat16)).astype(jnp.float32)

@jax.custom_vjp
def low_back(v):
    return v

def low_keep(v):
    return (low(v), None)

def low_pass(kept, grad):
    return (grad,)

def back_keep(v):
    return (v, None)

def back_low(kept, grad):
    return (low(grad),)
low.defvjp(low_keep, low_pass)
low_back.defvjp(back_keep, back_low)
highest_mode = lax.Precision.HIGHEST

def rms_scale(value, gain):
    return value * lax.rsqrt(lax.optimization_barrier(jnp.mean(value * value, axis=-1, keepdims=True)) + 1e-05) * gain

def block_step(carry, pieces):
    state, decay_rate = carry
    step_delta, step_input, step_b, step_c = pieces
    results = []
    for offset in range(64):
        state = jnp.exp(step_delta[offset][None, :] * decay_rate) * state + (step_delta[offset] * step_input[offset])[None, :] * step_b[:, offset:offset + 1]
        results.append(lax.optimization_barrier(jnp.sum(step_c[:, offset:offset + 1] * state, axis=0)))
    return ((state, decay_rate), jnp.stack(results))

def selective(start, delta, inputs, b_rows, c_rows, rate_log, skip):
    decay_rate = -jnp.exp(rate_log)
    count = delta.shape[0] // 64
    channels = delta.shape[1]
    states = b_rows.shape[0]
    blocks = (delta.reshape(count, 64, channels), inputs.reshape(count, 64, channels), b_rows.reshape(states, count, 64).transpose(1, 0, 2), c_rows.reshape(states, count, 64).transpose(1, 0, 2))
    (final_state, unused_rate), results = lax.scan(jax.checkpoint(block_step), (start, decay_rate), blocks)
    return (results.reshape(delta.shape) + skip * inputs, final_state)

def conv_silu(extended, weight, bias):
    count = extended.shape[0] - weight.shape[0] + 1
    total = bias + weight[0] * extended[0:count]
    for offset in range(1, weight.shape[0]):
        total = total + weight[offset] * extended[offset:offset + count]
    return jax.nn.silu(total)

def router_gate(logits, picked):
    peak = lax.optimization_barrier(jnp.max(logits, axis=0, keepdims=True))
    scores = jnp.exp(logits - peak)
    return lax.optimization_barrier(jnp.sum(scores * picked, axis=0)) / lax.optimization_barrier(jnp.sum(scores, axis=0))

def expert_apply(pieces):
    rows_in, first_weight, second_weight = pieces
    pre_hidden = low_back(jnp.dot(rows_in, first_weight, precision=highest_mode, preferred_element_type=jnp.float32))
    active = low(jax.nn.gelu(pre_hidden, approximate=False))
    return low(low_back(jnp.dot(active, second_weight, precision=highest_mode, preferred_element_type=jnp.float32)))

def layer(value, route, weights):
    gain_one, in_proj, conv_weight, conv_bias, x_proj, dt_proj, dt_bias, rate_log, skip, out_proj, gain_two, router, expert_in, expert_out = weights
    normed_one = low(rms_scale(value, gain_one))
    both = low_back(jnp.dot(normed_one, in_proj, precision=highest_mode, preferred_element_type=jnp.float32))
    inner = low(both[:, :INNER])
    gate_z = both[:, INNER:]
    extended = jnp.concatenate([jnp.zeros((WIDTH - 1, INNER), jnp.float32), inner], 0)
    mixed_in = low(conv_silu(extended, conv_weight, conv_bias))
    proj = low_back(jnp.dot(x_proj, mixed_in.T, precision=highest_mode, preferred_element_type=jnp.float32))
    low_rank = low(proj[:RANK])
    b_rows = proj[RANK:RANK + STATE]
    c_rows = proj[RANK + STATE:]
    pre_delta = low_back(jnp.dot(low_rank.T, dt_proj, precision=highest_mode, preferred_element_type=jnp.float32))
    delta = jax.nn.softplus(pre_delta + dt_bias)
    ssm, final_state = selective(jnp.zeros((STATE, INNER), jnp.float32), delta, mixed_in, b_rows, c_rows, rate_log, skip)
    gated = low(ssm * jax.nn.silu(gate_z))
    branch = low_back(jnp.dot(gated, out_proj, precision=highest_mode, preferred_element_type=jnp.float32))
    hidden = value + branch
    normed_two = low(rms_scale(hidden, gain_two))
    logits = low_back(jnp.dot(router, normed_two.T, precision=highest_mode, preferred_element_type=jnp.float32))
    expert_ids = jnp.arange(EXPERTS, dtype=jnp.int32)
    onehot = (expert_ids[:, None] == route[None, :]).astype(jnp.int32)
    gate = router_gate(logits, onehot.astype(jnp.float32))
    blocks = SEQ // TOK_DEV
    running = jnp.cumsum(onehot.reshape(EXPERTS, blocks, TOK_DEV), axis=2).reshape(EXPERTS, SEQ).astype(jnp.int32)
    place = (lax.optimization_barrier(jnp.sum(running * onehot, axis=0)) - 1).astype(jnp.int32)
    block_ids = (jnp.arange(SEQ, dtype=jnp.int32) // TOK_DEV).astype(jnp.int32)
    target = jnp.where(place < CAP, (block_ids * EXPERTS + route) * CAP + place, blocks * EXPERTS * CAP).astype(jnp.int32)
    buffer = jnp.zeros((blocks * EXPERTS * CAP + 1, D), jnp.float32).at[target].add(normed_two)
    per_expert = buffer[:-1].reshape(blocks, EXPERTS, CAP, D).transpose(1, 0, 2, 3).reshape(EXPERTS, blocks * CAP, D)
    per_expert = low_back(per_expert)
    results = lax.map(jax.checkpoint(expert_apply), (per_expert, expert_in, expert_out))
    returned = results.reshape(EXPERTS, blocks, CAP, D).transpose(1, 0, 2, 3).reshape(blocks * EXPERTS * CAP, D)
    returned = jnp.concatenate([returned, jnp.zeros((1, D), jnp.float32)], 0)
    return hidden + gate[:, None] * returned[target]

def reference(tokens, routes, gain_one, in_proj, conv_weight, conv_bias, x_proj, dt_proj, dt_bias, rate_log, skip, out_proj, gain_two, router, expert_in, expert_out, cotangent):
    weights = tuple((item.astype(jnp.float32) for item in (gain_one, in_proj, conv_weight, conv_bias, x_proj, dt_proj, dt_bias, rate_log, skip, out_proj, gain_two, router, expert_in, expert_out)))

    def one_sequence(totals, pieces):
        seq_tokens, seq_routes, seq_cot = pieces

        def forward(value, params):
            return layer(value, seq_routes[:, 0], params)
        result, pullback = jax.vjp(forward, seq_tokens.astype(jnp.float32), weights)
        input_grad, weight_grads = pullback(seq_cot.astype(jnp.float32))
        totals = jax.tree.map(jnp.add, totals, weight_grads)
        return (totals, (result.astype(jnp.bfloat16), input_grad))
    zeros = jax.tree.map(jnp.zeros_like, weights)
    totals, (outputs, input_grads) = lax.scan(one_sequence, zeros, (tokens, routes, cotangent))
    return (outputs, input_grads, totals[0], totals[1], totals[2], totals[3], totals[4], totals[5], totals[6], totals[7], totals[8], totals[9], totals[10], totals[11], totals[12], totals[13])
```

```python
import functools

import jax
import jax.numpy as jnp
from jax import lax
from jax.experimental import pallas as pl
from jax.experimental.pallas import tpu as pltpu
from jax.sharding import PartitionSpec as P

F32, BF16 = jnp.float32, jnp.bfloat16
SEGS = 8
LANES = 128
LOG2E = 1.4426950408889634
LN2 = 0.6931471805599453
VMEM_LIMIT = 56 * 1024 * 1024


def params(**kw):
    return pltpu.CompilerParams(vmem_limit_bytes=VMEM_LIMIT, **kw)


def softplus(v):
    return jnp.maximum(v, 0.0) + jnp.log1p(jnp.exp(-jnp.abs(v)))


def contract(left, right, left_dim, right_dim):
    return lax.dot_general(
        left, right, (((left_dim,), (right_dim,)), ((), ())), preferred_element_type=F32
    )


def spread_rows(src_ref, first, states, out_ref, steps):
    def one(j, carry):
        tile = src_ref[pl.ds(pl.multiple_of(j * SEGS, SEGS), SEGS), :]
        for n in range(states):
            out_ref[j, n] = jnp.broadcast_to(tile[:, first + n : first + n + 1], (SEGS, LANES))
        return carry

    lax.fori_loop(0, steps, one, 0)


def over_sublanes(row):
    return jnp.broadcast_to(row, (SEGS, LANES))


def ends_kernel(states, steps, forward, *refs):
    if forward:
        pre_ref, in_ref, bc_ref, rate_ref, ends_ref, sums_ref, delta_s, in_s, bb = refs
    else:
        pre_ref, in_ref, bc_ref, rate_ref, ends_ref, delta_s, bb = refs

    @pl.when(pl.program_id(0) == 0)
    def _():
        spread_rows(bc_ref, 0 if forward else states, states, bb, steps)

    delta = softplus(pre_ref[...])
    delta_s[...] = delta
    if forward:
        in_s[...] = delta * in_ref[...].astype(F32)
        sums_ref[...] = jnp.sum(delta.reshape(steps, SEGS, LANES), axis=0)
        source = in_s
    else:
        source = in_ref
    rates = [over_sublanes(rate_ref[n : n + 1, :]) for n in range(states)]

    def one(i, held):
        j = i if forward else steps - 1 - i
        rows = pl.ds(pl.multiple_of(j * SEGS, SEGS), SEGS)
        d, u = delta_s[rows, :], source[rows, :]
        new = []
        for n in range(states):
            a = jnp.exp2(d * rates[n])
            if forward:
                new.append(a * held[n] + u * bb[j, n])
            else:
                new.append(a * (held[n] + u * bb[j, n]))
        return tuple(new)

    zero = jnp.zeros((SEGS, LANES), F32)
    held = lax.fori_loop(0, steps, one, (zero,) * states, unroll=4)
    for n in range(states):
        ends_ref[n] = held[n]


def segment_ends(pre, values, bc, rate2, forward):
    count, width = pre.shape
    states, steps = rate2.shape[0], count // SEGS
    block = pl.BlockSpec((count, LANES), lambda c: (0, c))
    ends_spec = pl.BlockSpec((states, SEGS, LANES), lambda c: (0, 0, c))
    out_shape = [jax.ShapeDtypeStruct((states, SEGS, width), F32)]
    out_specs = [ends_spec]
    scratch = [pltpu.VMEM((count, LANES), F32)]
    if forward:
        out_shape.append(jax.ShapeDtypeStruct((SEGS, width), F32))
        out_specs.append(pl.BlockSpec((SEGS, LANES), lambda c: (0, c)))
        scratch.append(pltpu.VMEM((count, LANES), F32))
    scratch.append(pltpu.VMEM((steps, states, SEGS, LANES), F32))
    return pl.pallas_call(
        functools.partial(ends_kernel, states, steps, forward),
        grid=(width // LANES,),
        out_shape=out_shape,
        in_specs=[
            block,
            block,
            pl.BlockSpec(bc.shape, lambda c: (0, 0)),
            pl.BlockSpec((states, LANES), lambda c: (0, c)),
        ],
        out_specs=out_specs,
        scratch_shapes=scratch,
        compiler_params=params(),
        name="segment_ends",
    )(pre, values, bc, rate2)


def states_kernel(states, steps, *refs):
    (
        pre_ref,
        in_ref,
        bc_ref,
        rate_ref,
        skip_ref,
        start_ref,
        ssm_ref,
        held_ref,
        delta_s,
        in_s,
        bb,
        cb,
    ) = refs

    @pl.when(pl.program_id(0) == 0)
    def _():
        spread_rows(bc_ref, 0, states, bb, steps)
        spread_rows(bc_ref, states, states, cb, steps)

    delta = softplus(pre_ref[...])
    mixed = in_ref[...].astype(F32)
    delta_s[...] = delta
    in_s[...] = delta * mixed
    ssm_ref[...] = skip_ref[...] * mixed
    rates = [over_sublanes(rate_ref[n : n + 1, :]) for n in range(states)]
    start = []
    for n in range(states):
        start.append(start_ref[n])
        held_ref[0, 0, n] = start[n]

    def one(j, held):
        rows = pl.ds(pl.multiple_of(j * SEGS, SEGS), SEGS)
        d, u = delta_s[rows, :], in_s[rows, :]
        total = ssm_ref[rows, :]
        new = []
        for n in range(states):
            h = jnp.exp2(d * rates[n]) * held[n] + u * bb[j, n]
            held_ref[0, j + 1, n] = h
            total = total + cb[j, n] * h
            new.append(h)
        ssm_ref[rows, :] = total
        return tuple(new)

    lax.fori_loop(0, steps, one, tuple(start), unroll=4)


def all_states(pre, mixed, bc, rate2, skip, start):
    count, width = pre.shape
    states, steps = rate2.shape[0], count // SEGS
    block = pl.BlockSpec((count, LANES), lambda c: (0, c))
    spread = pltpu.VMEM((steps, states, SEGS, LANES), F32)
    return pl.pallas_call(
        functools.partial(states_kernel, states, steps),
        grid=(width // LANES,),
        out_shape=[
            jax.ShapeDtypeStruct((count, width), F32),
            jax.ShapeDtypeStruct((width // LANES, steps + 1, states, SEGS, LANES), F32),
        ],
        in_specs=[
            block,
            block,
            pl.BlockSpec(bc.shape, lambda c: (0, 0)),
            pl.BlockSpec((states, LANES), lambda c: (0, c)),
            pl.BlockSpec((1, LANES), lambda c: (0, c)),
            pl.BlockSpec((states, SEGS, LANES), lambda c: (0, 0, c)),
        ],
        out_specs=[
            block,
            pl.BlockSpec((1, steps + 1, states, SEGS, LANES), lambda c: (c, 0, 0, 0, 0)),
        ],
        scratch_shapes=[
            pltpu.VMEM((count, LANES), F32),
            pltpu.VMEM((count, LANES), F32),
            spread,
            spread,
        ],
        compiler_params=params(),
        name="all_states",
    )(pre, mixed, bc, rate2, skip, start)


PAIR = 2


def grads_kernel(states, steps, *refs):
    (
        pre_ref,
        in_ref,
        g_ref,
        bc_ref,
        rate_ref,
        skip_ref,
        later_ref,
        held_ref,
        pre_grad_ref,
        mixed_grad_ref,
        rate_grad_ref,
        skip_grad_ref,
        bias_grad_ref,
        bc_grad_ref,
        delta_s,
        in_s,
        rate_sum,
        in_sum,
        bb,
        cb,
        b_acc,
        c_acc,
    ) = refs
    wide = PAIR * LANES
    step_id = pl.program_id(0)

    @pl.when(step_id == 0)
    def _():
        spread_rows(bc_ref, 0, states, bb, steps)
        spread_rows(bc_ref, states, states, cb, steps)

        def clear(j, carry):
            for n in range(states):
                b_acc[j, n] = jnp.zeros((SEGS, LANES), F32)
                c_acc[j, n] = jnp.zeros((SEGS, LANES), F32)
            return carry

        lax.fori_loop(0, steps, clear, 0)

    delta = softplus(pre_ref[...])
    mixed = in_ref[...].astype(F32)
    delta_s[...] = delta
    in_s[...] = delta * mixed
    rate_sum[...] = jnp.zeros(rate_sum.shape, F32)
    in_sum[...] = jnp.zeros(in_sum.shape, F32)
    part = states // 2
    lanes = [slice(k * LANES, (k + 1) * LANES) for k in range(PAIR)]
    for half in range(2):
        ids = range(half * part, (half + 1) * part)
        rates = [[over_sublanes(rate_ref[n : n + 1, lane]) for lane in lanes] for n in ids]

        def one(i, carry):
            edge, rate_acc = carry
            j = steps - 1 - i
            rows = pl.ds(pl.multiple_of(j * SEGS, SEGS), SEGS)
            d = [delta_s[rows, lane] for lane in lanes]
            u = [in_s[rows, lane] for lane in lanes]
            g = [g_ref[rows, lane] for lane in lanes]
            by_rate = [rate_sum[rows, lane] for lane in lanes]
            by_b = [in_sum[rows, lane] for lane in lanes]
            new_edge, new_acc = [], []
            for at, n in enumerate(ids):
                b, c = bb[j, n], cb[j, n]
                to_b, to_c = b_acc[j, n], c_acc[j, n]
                for k in range(PAIR):
                    q = c * g[k] + edge[at * PAIR + k]
                    e = jnp.exp2(d[k] * rates[at][k]) * q
                    v = e * held_ref[k, j, n]
                    by_rate[k] = by_rate[k] + rates[at][k] * v
                    by_b[k] = by_b[k] + b * q
                    to_b = to_b + q * u[k]
                    to_c = to_c + g[k] * held_ref[k, j + 1, n]
                    new_edge.append(e)
                    new_acc.append(rate_acc[at * PAIR + k] + d[k] * v)
                b_acc[j, n] = to_b
                c_acc[j, n] = to_c
            for k in range(PAIR):
                rate_sum[rows, lanes[k]] = by_rate[k]
                in_sum[rows, lanes[k]] = by_b[k]
            return tuple(new_edge), tuple(new_acc)

        edge = tuple(later_ref[n, :, lane] for n in ids for lane in lanes)
        zero = jnp.zeros((SEGS, LANES), F32)
        _, rate_acc = lax.fori_loop(
            0, steps, one, (edge, (zero,) * (part * PAIR)), unroll=2
        )
        for at, n in enumerate(ids):
            for k in range(PAIR):
                rate_grad_ref[n : n + 1, lanes[k]] = (
                    LN2
                    * rate_ref[n : n + 1, lanes[k]]
                    * jnp.sum(rate_acc[at * PAIR + k], axis=0, keepdims=True)
                )

    g = g_ref[...]
    by_b = in_sum[...]
    pre_grad = (LN2 * rate_sum[...] + mixed * by_b) * jax.nn.sigmoid(pre_ref[...])
    pre_grad_ref[...] = pre_grad.astype(BF16)
    bias_grad_ref[...] = jnp.sum(pre_grad, axis=0, keepdims=True)
    mixed_grad_ref[...] = delta * by_b + skip_ref[...] * g
    skip_grad_ref[...] = jnp.sum(g * mixed, axis=0, keepdims=True)

    @pl.when(step_id == pl.num_programs(0) - 1)
    def _():
        place = lax.broadcasted_iota(jnp.int32, (SEGS, 2 * states), 1)

        def one(j, carry):
            total = jnp.zeros((SEGS, 2 * states), F32)
            for n in range(states):
                total = jnp.where(place == n, jnp.sum(b_acc[j, n], axis=1, keepdims=True), total)
                total = jnp.where(
                    place == states + n, jnp.sum(c_acc[j, n], axis=1, keepdims=True), total
                )
            bc_grad_ref[pl.ds(pl.multiple_of(j * SEGS, SEGS), SEGS), :] = total
            return carry

        lax.fori_loop(0, steps, one, 0)


def state_grads(pre, mixed, ssm_grad, bc, rate2, skip, later, held):
    count, width = pre.shape
    states, steps = rate2.shape[0], count // SEGS
    wide = PAIR * LANES
    block = pl.BlockSpec((count, wide), lambda c: (0, c))
    row = pl.BlockSpec((1, wide), lambda c: (0, c))
    state = pl.BlockSpec((states, wide), lambda c: (0, c))
    whole = pl.BlockSpec(bc.shape, lambda c: (0, 0))
    spread = pltpu.VMEM((steps, states, SEGS, LANES), F32)
    flat = pltpu.VMEM((count, wide), F32)
    return pl.pallas_call(
        functools.partial(grads_kernel, states, steps),
        grid=(width // wide,),
        out_shape=[
            jax.ShapeDtypeStruct((count, width), BF16),
            jax.ShapeDtypeStruct((count, width), F32),
            jax.ShapeDtypeStruct((states, width), F32),
            jax.ShapeDtypeStruct((1, width), F32),
            jax.ShapeDtypeStruct((1, width), F32),
            jax.ShapeDtypeStruct(bc.shape, F32),
        ],
        in_specs=[
            block,
            block,
            block,
            whole,
            state,
            row,
            pl.BlockSpec((states, SEGS, wide), lambda c: (0, 0, c)),
            pl.BlockSpec((PAIR, steps + 1, states, SEGS, LANES), lambda c: (c, 0, 0, 0, 0)),
        ],
        out_specs=[block, block, state, row, row, whole],
        scratch_shapes=[flat, flat, flat, flat, spread, spread, spread, spread],
        compiler_params=params(),
        name="state_grads",
    )(pre, mixed, ssm_grad, bc, rate2, skip, later, held)


def shifted_in(tile, row, forward):
    if forward:
        return jnp.concatenate([row, tile[: SEGS - 1]], axis=0)
    return jnp.concatenate([tile[1:], row], axis=0)


def conv_grads_kernel(reach, grad_ref, inner_ref, before_ref, after_ref, weight_ref, *outs):
    inner_grad_ref, weight_grad_ref, bias_grad_ref, ext_in, ext_grad = outs
    count = grad_ref.shape[0]
    rim = reach * SEGS
    grad = grad_ref[...]
    inner = inner_ref[...].astype(F32)
    for k in range(reach):
        own = inner[count - rim + k * SEGS : count - rim + (k + 1) * SEGS]
        ext_in[k * SEGS : (k + 1) * SEGS, :] = shifted_in(own, before_ref[k : k + 1, :], True)
        own = grad[k * SEGS : (k + 1) * SEGS]
        ext_grad[count + k * SEGS : count + (k + 1) * SEGS, :] = shifted_in(
            own, after_ref[k : k + 1, :], False
        )
    ext_in[rim:, :] = inner
    ext_grad[:count, :] = grad
    bias_grad_ref[...] = jnp.sum(grad, axis=0, keepdims=True)
    total = jnp.zeros_like(grad)
    for k in range(reach + 1):
        total = total + weight_ref[k : k + 1, :] * ext_grad[(reach - k) * SEGS :, :][:count]
        weight_grad_ref[k : k + 1, :] = jnp.sum(
            grad * ext_in[k * SEGS : k * SEGS + count, :], axis=0, keepdims=True
        )
    inner_grad_ref[...] = total.astype(BF16)


def conv_grads(grad, inner, before, after, weight):
    count, width = grad.shape
    reach = weight.shape[0] - 1
    wide = PAIR * LANES
    spec = lambda rows: pl.BlockSpec((rows, wide), lambda c: (0, c))
    return pl.pallas_call(
        functools.partial(conv_grads_kernel, reach),
        grid=(width // wide,),
        out_shape=[
            jax.ShapeDtypeStruct((count, width), BF16),
            jax.ShapeDtypeStruct((reach + 1, width), F32),
            jax.ShapeDtypeStruct((1, width), F32),
        ],
        in_specs=[spec(count), spec(count), spec(reach), spec(reach), spec(reach + 1)],
        out_specs=[spec(count), spec(reach + 1), spec(1)],
        scratch_shapes=[pltpu.VMEM((count + reach * SEGS, wide), F32)] * 2,
        compiler_params=params(),
        name="conv_grads",
    )(grad, inner, before.astype(F32), after, weight)


def segment_starts(ends, sums, rate2, axis, forward):
    states, _, width = ends.shape
    count, me = lax.axis_size(axis), lax.axis_index(axis)
    order = range(SEGS) if forward else range(SEGS - 1, -1, -1)
    decays = jnp.exp2(rate2[:, None, :] * sums[None])
    own = jnp.zeros((states, width), F32)
    for s in order:
        own = decays[:, s] * own + ends[:, s]
    sent = lax.all_gather(own.astype(BF16), axis)
    lengths = lax.all_gather(jnp.sum(sums, axis=0), axis)
    entering = jnp.zeros((states, width), F32)
    for k in range(count) if forward else range(count - 1, -1, -1):
        joined = jnp.exp2(rate2 * lengths[k]) * entering + sent[k].astype(F32)
        entering = jnp.where((k < me) if forward else (k > me), joined, entering)
    starts = [None] * SEGS
    for s in order:
        starts[s] = entering
        entering = decays[:, s] * entering + ends[:, s]
    return jnp.stack(starts, axis=1)


def passed_along(value, axis, steps):
    count = lax.axis_size(axis)
    leading, last = (max(0, -steps), min(count, count - steps))
    return lax.ppermute(value, axis, [(source, source + steps) for source in range(leading, last)])


def exchange(value, axis):
    return lax.all_to_all(value, axis, split_axis=0, concat_axis=0, tiled=True)


def silu(v):
    return v * jax.nn.sigmoid(v)


def silu_slope(v):
    s = jax.nn.sigmoid(v)
    return s * (1.0 + v * (1.0 - s))


def by_segment(value):
    count = value.shape[0]
    return value.reshape(SEGS, count // SEGS, -1).transpose(1, 0, 2).reshape(count, -1)


def by_token(value):
    count = value.shape[0]
    return value.reshape(count // SEGS, SEGS, -1).transpose(1, 0, 2).reshape(count, -1)


def rms_back(values, gain, grad):
    r = lax.rsqrt(jnp.mean(values * values, axis=-1, keepdims=True) + 1e-05)
    u = gain * grad
    mean = jnp.mean(values * u, axis=-1, keepdims=True)
    return r * u - values * (r * r * r) * mean, jnp.sum(grad * values * r, axis=0)


def rms(values, gain):
    return values * lax.rsqrt(jnp.mean(values * values, axis=-1, keepdims=True) + 1e-05) * gain


def per_device(
    tokens,
    routes,
    gain_one,
    in_proj,
    conv_weight,
    conv_bias,
    x_proj,
    dt_proj,
    dt_bias,
    rate_log,
    skip,
    out_proj,
    gain_two,
    router,
    expert_in,
    expert_out,
    cotangent,
):
    count, width = tokens.shape[1], tokens.shape[2]
    steps = count // SEGS
    inner_width = out_proj.shape[0]
    rank = dt_proj.shape[0]
    experts = router.shape[0]
    slots = 5 * count // (4 * experts)
    reach = conv_weight.shape[0] - 1
    rate2 = -jnp.exp(rate_log) * LOG2E
    skip_row = skip[None]

    route = by_segment(routes[0]).reshape(count)
    upstream_low = by_segment(cotangent[0])
    expert_ids = lax.broadcasted_iota(jnp.int32, (experts, count), 0)
    onehot = (expert_ids == route[None]).astype(BF16)
    first = lax.broadcasted_iota(jnp.int32, (count, count), 0)
    second = lax.broadcasted_iota(jnp.int32, (count, count), 1)
    token_of = lambda p: (p % SEGS) * steps + p // SEGS
    earlier = (token_of(first) <= token_of(second)).astype(BF16)
    running = jnp.dot(onehot, earlier, preferred_element_type=F32)
    place = (jnp.sum(running * onehot.astype(F32), axis=0) - 1.0).astype(jnp.int32)
    target = jnp.where(place < slots, route * slots + place, -1)
    slot_ids = lax.broadcasted_iota(jnp.int32, (experts * slots, count), 0)
    dispatch = (slot_ids == target[None]).astype(BF16)

    def to_slots(rows):
        sent = jnp.dot(dispatch, rows, preferred_element_type=F32).astype(BF16)
        return exchange(sent.reshape(experts, slots, width), "expert").reshape(-1, width)

    def to_tokens(rows):
        back = exchange(rows.reshape(experts, slots, width), "expert").reshape(-1, width)
        return contract(dispatch, back, 0, 0)

    slot_upstream = to_slots(upstream_low)

    values = by_segment(tokens[0]).astype(F32)
    normed_one = rms(values, gain_one).astype(BF16)
    both = jnp.dot(normed_one, in_proj, preferred_element_type=F32)
    inner = both[:, :inner_width].astype(BF16)
    gate_z = both[:, inner_width:]
    blocks = inner.reshape(steps, SEGS, inner_width)
    tail = blocks[steps - reach :]
    before = passed_along(tail[:, SEGS - 1], "expert", 1)
    extended = jnp.concatenate(
        [jnp.concatenate([before[:, None], tail[:, : SEGS - 1]], axis=1), blocks], axis=0
    ).astype(F32)
    conv_pre = conv_bias + sum(
        conv_weight[k] * extended[k : k + steps] for k in range(reach + 1)
    )
    conv_pre = conv_pre.reshape(count, inner_width)
    mixed = silu(conv_pre).astype(BF16)
    proj = contract(mixed, x_proj, 1, 1)
    low_rank = proj[:, :rank].astype(BF16)
    bc = proj[:, rank:]
    pre = jnp.dot(low_rank, dt_proj, preferred_element_type=F32) + dt_bias
    ends, sums = segment_ends(pre, mixed, bc, rate2, True)
    start = segment_starts(ends, sums, rate2, "expert", True)
    ssm, held = all_states(pre, mixed, bc, rate2, skip_row, start)
    gated = (ssm * silu(gate_z)).astype(BF16)
    hidden = values + jnp.dot(gated, out_proj, preferred_element_type=F32)
    normed_two = rms(hidden, gain_two).astype(BF16)

    rows = to_slots(normed_two)
    logits = contract(rows, router, 1, 1)
    scores = jnp.exp(logits - jnp.max(logits, axis=1, keepdims=True))
    probs = scores / jnp.sum(scores, axis=1, keepdims=True)
    mine = (
        lax.broadcasted_iota(jnp.int32, probs.shape, 1) == lax.axis_index("expert")
    ).astype(F32)
    gate = jnp.sum(probs * mine, axis=1, keepdims=True)
    pre_hidden = jnp.dot(rows, expert_in[0], preferred_element_type=F32)
    active_f, gelu_back = jax.vjp(lambda v: jax.nn.gelu(v, approximate=False), pre_hidden)
    active = active_f.astype(BF16)
    expert_rows = jnp.dot(active, expert_out[0], preferred_element_type=F32).astype(BF16)
    expert_rows = expert_rows.astype(F32)
    slot_grad = (gate * slot_upstream.astype(F32)).astype(BF16)
    expert_out_local = contract(active, slot_grad, 0, 0)
    active_grad = contract(slot_grad, expert_out[0], 1, 1)
    hidden_pre_grad = gelu_back(active_grad)[0].astype(BF16)
    expert_in_local = contract(rows, hidden_pre_grad, 0, 0)
    row_grad = contract(hidden_pre_grad, expert_in[0], 1, 1)
    picked = jnp.sum(slot_grad.astype(F32) * expert_rows, axis=1, keepdims=True)
    logit_grad = (picked * (mine - probs)).astype(BF16)
    router_local = contract(logit_grad, rows, 0, 0)
    row_grad = (row_grad + jnp.dot(logit_grad, router, preferred_element_type=F32)).astype(BF16)
    normed_two_grad = to_tokens(row_grad)
    output = (hidden + to_tokens((gate * expert_rows).astype(BF16))).astype(BF16)

    hidden_norm, gain_two_local = rms_back(hidden, gain_two, normed_two_grad)
    hidden_grad = upstream_low.astype(F32) + hidden_norm
    branch = hidden_grad.astype(BF16)
    out_proj_local = contract(gated, branch, 0, 0)
    gated_grad = contract(branch, out_proj, 1, 1)
    ssm_grad = gated_grad * silu(gate_z)
    gate_z_grad = (gated_grad * ssm * silu_slope(gate_z)).astype(BF16)

    ends = segment_ends(pre, ssm_grad, bc, rate2, False)[0]
    later = segment_starts(ends, sums, rate2, "expert", False)
    pre_grad, mixed_grad, rate_log_local, skip_local, dt_bias_local, bc_grad = state_grads(
        pre, mixed, ssm_grad, bc, rate2, skip_row, later, held
    )
    dt_proj_local = contract(low_rank, pre_grad, 0, 0)
    low_rank_grad = contract(pre_grad, dt_proj, 1, 1)
    proj_grad = jnp.concatenate([low_rank_grad, bc_grad], axis=1).astype(BF16)
    x_proj_local = contract(proj_grad, mixed, 0, 0)
    mixed_grad = mixed_grad + jnp.dot(proj_grad, x_proj, preferred_element_type=F32)
    conv_grad = mixed_grad * silu_slope(conv_pre)
    head = conv_grad[: reach * SEGS].reshape(reach, SEGS, inner_width)
    after = passed_along(head[:, 0], "expert", -1)
    inner_grad, conv_weight_local, conv_bias_local = conv_grads(
        conv_grad, inner, before, after, conv_weight
    )
    both_grad = jnp.concatenate([inner_grad, gate_z_grad], axis=1)
    in_proj_local = contract(normed_one, both_grad, 0, 0)
    normed_one_grad = contract(both_grad, in_proj, 1, 1)
    values_grad, gain_one_local = rms_back(values, gain_one, normed_one_grad)
    tokens_grad = by_token(values_grad + hidden_grad)

    in_proj_part, out_proj_part = (
        lax.psum_scatter(v.astype(BF16), "expert", scatter_dimension=0, tiled=True).astype(F32)
        for v in (in_proj_local, out_proj_local)
    )
    in_proj_grad, out_proj_grad = (
        lax.psum(v.astype(BF16), "batch").astype(F32) for v in (in_proj_part, out_proj_part)
    )
    small = lax.psum(
        (
            gain_one_local,
            conv_weight_local,
            conv_bias_local[0],
            x_proj_local,
            dt_proj_local,
            dt_bias_local[0],
            rate_log_local,
            skip_local[0],
            gain_two_local,
            router_local,
        ),
        ("batch", "expert"),
    )
    expert_in_grad, expert_out_grad = (
        lax.psum_scatter(v.astype(BF16), "batch", scatter_dimension=0, tiled=True).astype(F32)
        for v in (expert_in_local, expert_out_local)
    )
    return (
        by_token(output)[None],
        tokens_grad[None],
        small[0],
        in_proj_grad,
        *small[1:8],
        out_proj_grad,
        small[8],
        small[9],
        expert_in_grad[None],
        expert_out_grad[None],
    )


def solution(mesh):
    split = P("batch", "expert", None)
    one = P("expert", None, None)
    both = P("expert", "batch", None)
    in_specs = (split, split) + (P(),) * 12 + (one, one, split)
    out_specs = (split, split, P(), P("expert", None)) + (P(),) * 7
    out_specs += (P("expert", None), P(), P(), both, both)
    return jax.shard_map(
        per_device, mesh=mesh, in_specs=in_specs, out_specs=out_specs, check_vma=False
    )
```

```python
import functools

import jax
import jax.numpy as jnp
from jax import lax
from jax.experimental import pallas as pl
from jax.experimental.pallas import tpu as pltpu
from jax.sharding import PartitionSpec as P

F32, BF16 = jnp.float32, jnp.bfloat16
SEGS = 8
LANES = 128
LOG2E = 1.4426950408889634
LN2 = 0.6931471805599453
VMEM_LIMIT = 56 * 1024 * 1024


def params(**kw):
    return pltpu.CompilerParams(vmem_limit_bytes=VMEM_LIMIT, **kw)


def softplus(v):
    return jnp.maximum(v, 0.0) + jnp.log1p(jnp.exp(-jnp.abs(v)))


def contract(left, right, left_dim, right_dim):
    return lax.dot_general(
        left, right, (((left_dim,), (right_dim,)), ((), ())), preferred_element_type=F32
    )


def spread_rows(src_ref, first, states, out_ref, steps):
    def one(j, carry):
        tile = src_ref[pl.ds(pl.multiple_of(j * SEGS, SEGS), SEGS), :]
        for n in range(states):
            out_ref[j, n] = jnp.broadcast_to(tile[:, first + n : first + n + 1], (SEGS, LANES))
        return carry

    lax.fori_loop(0, steps, one, 0)


def over_sublanes(row):
    return jnp.broadcast_to(row, (SEGS, LANES))


def ends_kernel(states, steps, forward, *refs):
    if forward:
        pre_ref, in_ref, bc_ref, rate_ref, ends_ref, sums_ref, delta_s, in_s, bb = refs
    else:
        pre_ref, in_ref, bc_ref, rate_ref, ends_ref, delta_s, bb = refs

    @pl.when(pl.program_id(0) == 0)
    def _():
        spread_rows(bc_ref, 0 if forward else states, states, bb, steps)

    delta = softplus(pre_ref[...])
    delta_s[...] = delta
    if forward:
        in_s[...] = delta * in_ref[...].astype(F32)
        sums_ref[...] = jnp.sum(delta.reshape(steps, SEGS, LANES), axis=0)
        source = in_s
    else:
        source = in_ref
    rates = [over_sublanes(rate_ref[n : n + 1, :]) for n in range(states)]

    def one(i, held):
        j = i if forward else steps - 1 - i
        rows = pl.ds(pl.multiple_of(j * SEGS, SEGS), SEGS)
        d, u = delta_s[rows, :], source[rows, :]
        new = []
        for n in range(states):
            a = jnp.exp2(d * rates[n])
            if forward:
                new.append(a * held[n] + u * bb[j, n])
            else:
                new.append(a * (held[n] + u * bb[j, n]))
        return tuple(new)

    zero = jnp.zeros((SEGS, LANES), F32)
    held = lax.fori_loop(0, steps, one, (zero,) * states, unroll=4)
    for n in range(states):
        ends_ref[n] = held[n]


def segment_ends(pre, values, bc, rate2, forward):
    count, width = pre.shape
    states, steps = rate2.shape[0], count // SEGS
    block = pl.BlockSpec((count, LANES), lambda c: (0, c))
    ends_spec = pl.BlockSpec((states, SEGS, LANES), lambda c: (0, 0, c))
    out_shape = [jax.ShapeDtypeStruct((states, SEGS, width), F32)]
    out_specs = [ends_spec]
    scratch = [pltpu.VMEM((count, LANES), F32)]
    if forward:
        out_shape.append(jax.ShapeDtypeStruct((SEGS, width), F32))
        out_specs.append(pl.BlockSpec((SEGS, LANES), lambda c: (0, c)))
        scratch.append(pltpu.VMEM((count, LANES), F32))
    scratch.append(pltpu.VMEM((steps, states, SEGS, LANES), F32))
    return pl.pallas_call(
        functools.partial(ends_kernel, states, steps, forward),
        grid=(width // LANES,),
        out_shape=out_shape,
        in_specs=[
            block,
            block,
            pl.BlockSpec(bc.shape, lambda c: (0, 0)),
            pl.BlockSpec((states, LANES), lambda c: (0, c)),
        ],
        out_specs=out_specs,
        scratch_shapes=scratch,
        compiler_params=params(),
        name="segment_ends",
    )(pre, values, bc, rate2)


def states_kernel(states, steps, *refs):
    (
        pre_ref,
        in_ref,
        bc_ref,
        rate_ref,
        skip_ref,
        start_ref,
        ssm_ref,
        held_ref,
        delta_s,
        in_s,
        bb,
        cb,
    ) = refs

    @pl.when(pl.program_id(0) == 0)
    def _():
        spread_rows(bc_ref, 0, states, bb, steps)
        spread_rows(bc_ref, states, states, cb, steps)

    delta = softplus(pre_ref[...])
    mixed = in_ref[...].astype(F32)
    delta_s[...] = delta
    in_s[...] = delta * mixed
    ssm_ref[...] = skip_ref[...] * mixed
    rates = [over_sublanes(rate_ref[n : n + 1, :]) for n in range(states)]
    start = []
    for n in range(states):
        start.append(start_ref[n])
        held_ref[0, 0, n] = start[n]

    def one(j, held):
        rows = pl.ds(pl.multiple_of(j * SEGS, SEGS), SEGS)
        d, u = delta_s[rows, :], in_s[rows, :]
        total = ssm_ref[rows, :]
        new = []
        for n in range(states):
            h = jnp.exp2(d * rates[n]) * held[n] + u * bb[j, n]
            held_ref[0, j + 1, n] = h
            total = total + cb[j, n] * h
            new.append(h)
        ssm_ref[rows, :] = total
        return tuple(new)

    lax.fori_loop(0, steps, one, tuple(start), unroll=4)


def all_states(pre, mixed, bc, rate2, skip, start):
    count, width = pre.shape
    states, steps = rate2.shape[0], count // SEGS
    block = pl.BlockSpec((count, LANES), lambda c: (0, c))
    spread = pltpu.VMEM((steps, states, SEGS, LANES), F32)
    return pl.pallas_call(
        functools.partial(states_kernel, states, steps),
        grid=(width // LANES,),
        out_shape=[
            jax.ShapeDtypeStruct((count, width), F32),
            jax.ShapeDtypeStruct((width // LANES, steps + 1, states, SEGS, LANES), F32),
        ],
        in_specs=[
            block,
            block,
            pl.BlockSpec(bc.shape, lambda c: (0, 0)),
            pl.BlockSpec((states, LANES), lambda c: (0, c)),
            pl.BlockSpec((1, LANES), lambda c: (0, c)),
            pl.BlockSpec((states, SEGS, LANES), lambda c: (0, 0, c)),
        ],
        out_specs=[
            block,
            pl.BlockSpec((1, steps + 1, states, SEGS, LANES), lambda c: (c, 0, 0, 0, 0)),
        ],
        scratch_shapes=[
            pltpu.VMEM((count, LANES), F32),
            pltpu.VMEM((count, LANES), F32),
            spread,
            spread,
        ],
        compiler_params=params(),
        name="all_states",
    )(pre, mixed, bc, rate2, skip, start)


PAIR = 2


def grads_kernel(states, steps, *refs):
    (
        pre_ref,
        in_ref,
        g_ref,
        bc_ref,
        rate_ref,
        skip_ref,
        later_ref,
        held_ref,
        pre_grad_ref,
        mixed_grad_ref,
        rate_grad_ref,
        skip_grad_ref,
        bias_grad_ref,
        bc_grad_ref,
        delta_s,
        in_s,
        rate_sum,
        in_sum,
        bb,
        cb,
        b_acc,
        c_acc,
    ) = refs
    wide = PAIR * LANES
    step_id = pl.program_id(0)

    @pl.when(step_id == 0)
    def _():
        spread_rows(bc_ref, 0, states, bb, steps)
        spread_rows(bc_ref, states, states, cb, steps)

        def clear(j, carry):
            for n in range(states):
                b_acc[j, n] = jnp.zeros((SEGS, LANES), F32)
                c_acc[j, n] = jnp.zeros((SEGS, LANES), F32)
            return carry

        lax.fori_loop(0, steps, clear, 0)

    delta = softplus(pre_ref[...])
    mixed = in_ref[...].astype(F32)
    delta_s[...] = delta
    in_s[...] = delta * mixed
    rate_sum[...] = jnp.zeros(rate_sum.shape, F32)
    in_sum[...] = jnp.zeros(in_sum.shape, F32)
    part = states // 2
    lanes = [slice(k * LANES, (k + 1) * LANES) for k in range(PAIR)]
    for half in range(2):
        ids = range(half * part, (half + 1) * part)
        rates = [[over_sublanes(rate_ref[n : n + 1, lane]) for lane in lanes] for n in ids]

        def one(i, carry):
            edge, rate_acc = carry
            j = steps - 1 - i
            rows = pl.ds(pl.multiple_of(j * SEGS, SEGS), SEGS)
            d = [delta_s[rows, lane] for lane in lanes]
            u = [in_s[rows, lane] for lane in lanes]
            g = [g_ref[rows, lane] for lane in lanes]
            by_rate = [rate_sum[rows, lane] for lane in lanes]
            by_b = [in_sum[rows, lane] for lane in lanes]
            new_edge, new_acc = [], []
            for at, n in enumerate(ids):
                b, c = bb[j, n], cb[j, n]
                to_b, to_c = b_acc[j, n], c_acc[j, n]
                for k in range(PAIR):
                    q = c * g[k] + edge[at * PAIR + k]
                    e = jnp.exp2(d[k] * rates[at][k]) * q
                    v = e * held_ref[k, j, n]
                    by_rate[k] = by_rate[k] + rates[at][k] * v
                    by_b[k] = by_b[k] + b * q
                    to_b = to_b + q * u[k]
                    to_c = to_c + g[k] * held_ref[k, j + 1, n]
                    new_edge.append(e)
                    new_acc.append(rate_acc[at * PAIR + k] + d[k] * v)
                b_acc[j, n] = to_b
                c_acc[j, n] = to_c
            for k in range(PAIR):
                rate_sum[rows, lanes[k]] = by_rate[k]
                in_sum[rows, lanes[k]] = by_b[k]
            return tuple(new_edge), tuple(new_acc)

        edge = tuple(later_ref[n, :, lane] for n in ids for lane in lanes)
        zero = jnp.zeros((SEGS, LANES), F32)
        _, rate_acc = lax.fori_loop(
            0, steps, one, (edge, (zero,) * (part * PAIR)), unroll=2
        )
        for at, n in enumerate(ids):
            for k in range(PAIR):
                rate_grad_ref[n : n + 1, lanes[k]] = (
                    LN2
                    * rate_ref[n : n + 1, lanes[k]]
                    * jnp.sum(rate_acc[at * PAIR + k], axis=0, keepdims=True)
                )

    g = g_ref[...]
    by_b = in_sum[...]
    pre_grad = (LN2 * rate_sum[...] + mixed * by_b) * jax.nn.sigmoid(pre_ref[...])
    pre_grad_ref[...] = pre_grad.astype(BF16)
    bias_grad_ref[...] = jnp.sum(pre_grad, axis=0, keepdims=True)
    mixed_grad_ref[...] = delta * by_b + skip_ref[...] * g
    skip_grad_ref[...] = jnp.sum(g * mixed, axis=0, keepdims=True)

    @pl.when(step_id == pl.num_programs(0) - 1)
    def _():
        place = lax.broadcasted_iota(jnp.int32, (SEGS, 2 * states), 1)

        def one(j, carry):
            total = jnp.zeros((SEGS, 2 * states), F32)
            for n in range(states):
                total = jnp.where(place == n, jnp.sum(b_acc[j, n], axis=1, keepdims=True), total)
                total = jnp.where(
                    place == states + n, jnp.sum(c_acc[j, n], axis=1, keepdims=True), total
                )
            bc_grad_ref[pl.ds(pl.multiple_of(j * SEGS, SEGS), SEGS), :] = total
            return carry

        lax.fori_loop(0, steps, one, 0)


def state_grads(pre, mixed, ssm_grad, bc, rate2, skip, later, held):
    count, width = pre.shape
    states, steps = rate2.shape[0], count // SEGS
    wide = PAIR * LANES
    block = pl.BlockSpec((count, wide), lambda c: (0, c))
    row = pl.BlockSpec((1, wide), lambda c: (0, c))
    state = pl.BlockSpec((states, wide), lambda c: (0, c))
    whole = pl.BlockSpec(bc.shape, lambda c: (0, 0))
    spread = pltpu.VMEM((steps, states, SEGS, LANES), F32)
    flat = pltpu.VMEM((count, wide), F32)
    return pl.pallas_call(
        functools.partial(grads_kernel, states, steps),
        grid=(width // wide,),
        out_shape=[
            jax.ShapeDtypeStruct((count, width), BF16),
            jax.ShapeDtypeStruct((count, width), F32),
            jax.ShapeDtypeStruct((states, width), F32),
            jax.ShapeDtypeStruct((1, width), F32),
            jax.ShapeDtypeStruct((1, width), F32),
            jax.ShapeDtypeStruct(bc.shape, F32),
        ],
        in_specs=[
            block,
            block,
            block,
            whole,
            state,
            row,
            pl.BlockSpec((states, SEGS, wide), lambda c: (0, 0, c)),
            pl.BlockSpec((PAIR, steps + 1, states, SEGS, LANES), lambda c: (c, 0, 0, 0, 0)),
        ],
        out_specs=[block, block, state, row, row, whole],
        scratch_shapes=[flat, flat, flat, flat, spread, spread, spread, spread],
        compiler_params=params(),
        name="state_grads",
    )(pre, mixed, ssm_grad, bc, rate2, skip, later, held)


def shifted_in(tile, row, forward):
    if forward:
        return jnp.concatenate([row, tile[: SEGS - 1]], axis=0)
    return jnp.concatenate([tile[1:], row], axis=0)


def conv_grads_kernel(reach, grad_ref, inner_ref, before_ref, after_ref, weight_ref, *outs):
    inner_grad_ref, weight_grad_ref, bias_grad_ref, ext_in, ext_grad = outs
    count = grad_ref.shape[0]
    rim = reach * SEGS
    grad = grad_ref[...]
    inner = inner_ref[...].astype(F32)
    for k in range(reach):
        own = inner[count - rim + k * SEGS : count - rim + (k + 1) * SEGS]
        ext_in[k * SEGS : (k + 1) * SEGS, :] = shifted_in(own, before_ref[k : k + 1, :], True)
        own = grad[k * SEGS : (k + 1) * SEGS]
        ext_grad[count + k * SEGS : count + (k + 1) * SEGS, :] = shifted_in(
            own, after_ref[k : k + 1, :], False
        )
    ext_in[rim:, :] = inner
    ext_grad[:count, :] = grad
    bias_grad_ref[...] = jnp.sum(grad, axis=0, keepdims=True)
    total = jnp.zeros_like(grad)
    for k in range(reach + 1):
        total = total + weight_ref[k : k + 1, :] * ext_grad[(reach - k) * SEGS :, :][:count]
        weight_grad_ref[k : k + 1, :] = jnp.sum(
            grad * ext_in[k * SEGS : k * SEGS + count, :], axis=0, keepdims=True
        )
    inner_grad_ref[...] = total.astype(BF16)


def conv_grads(grad, inner, before, after, weight):
    count, width = grad.shape
    reach = weight.shape[0] - 1
    wide = PAIR * LANES
    spec = lambda rows: pl.BlockSpec((rows, wide), lambda c: (0, c))
    return pl.pallas_call(
        functools.partial(conv_grads_kernel, reach),
        grid=(width // wide,),
        out_shape=[
            jax.ShapeDtypeStruct((count, width), BF16),
            jax.ShapeDtypeStruct((reach + 1, width), F32),
            jax.ShapeDtypeStruct((1, width), F32),
        ],
        in_specs=[spec(count), spec(count), spec(reach), spec(reach), spec(reach + 1)],
        out_specs=[spec(count), spec(reach + 1), spec(1)],
        scratch_shapes=[pltpu.VMEM((count + reach * SEGS, wide), F32)] * 2,
        compiler_params=params(),
        name="conv_grads",
    )(grad, inner, before.astype(F32), after, weight)


def segment_starts(ends, sums, rate2, axis, forward):
    states, _, width = ends.shape
    count, me = lax.axis_size(axis), lax.axis_index(axis)
    order = range(SEGS) if forward else range(SEGS - 1, -1, -1)
    decays = jnp.exp2(rate2[:, None, :] * sums[None])
    own = jnp.zeros((states, width), F32)
    for s in order:
        own = decays[:, s] * own + ends[:, s]
    sent = lax.all_gather(own.astype(BF16), axis)
    lengths = lax.all_gather(jnp.sum(sums, axis=0), axis)
    entering = jnp.zeros((states, width), F32)
    for k in range(count) if forward else range(count - 1, -1, -1):
        joined = jnp.exp2(rate2 * lengths[k]) * entering + sent[k].astype(F32)
        entering = jnp.where((k < me) if forward else (k > me), joined, entering)
    starts = [None] * SEGS
    for s in order:
        starts[s] = entering
        entering = decays[:, s] * entering + ends[:, s]
    return jnp.stack(starts, axis=1)


def passed_along(value, axis, steps):
    count = lax.axis_size(axis)
    leading, last = (max(0, -steps), min(count, count - steps))
    return lax.ppermute(value, axis, [(source, source + steps) for source in range(leading, last)])


def exchange(value, axis):
    return lax.all_to_all(value, axis, split_axis=0, concat_axis=0, tiled=True)


def silu(v):
    return v * jax.nn.sigmoid(v)


def silu_slope(v):
    s = jax.nn.sigmoid(v)
    return s * (1.0 + v * (1.0 - s))


def by_segment(value):
    count = value.shape[0]
    return value.reshape(SEGS, count // SEGS, -1).transpose(1, 0, 2).reshape(count, -1)


def by_token(value):
    count = value.shape[0]
    return value.reshape(count // SEGS, SEGS, -1).transpose(1, 0, 2).reshape(count, -1)


def rms_back(values, gain, grad):
    r = lax.rsqrt(jnp.mean(values * values, axis=-1, keepdims=True) + 1e-05)
    u = gain * grad
    mean = jnp.mean(values * u, axis=-1, keepdims=True)
    return r * u - values * (r * r * r) * mean, jnp.sum(grad * values * r, axis=0)


def rms(values, gain):
    return values * lax.rsqrt(jnp.mean(values * values, axis=-1, keepdims=True) + 1e-05) * gain


MESH = pl.DeviceIdType.MESH


def together(*parts):
    return sum(p.astype(F32) for p in parts)


class Total:
    def __init__(self, local, axis, shared):
        self.local, self.axis, self.shared = local, axis, shared

    def shapes(self, ways):
        pairs = self.local.shape[0]
        chunk = self.local.shape[2:]
        part = list(chunk)
        part[self.axis] //= ways
        return pairs, chunk, tuple(part)


def part_of(ref, lead, axis, size, index):
    start = index * size
    if axis == len(ref.shape) - lead - 1:
        start = pl.multiple_of(start, LANES)
    where = [slice(None)] * len(ref.shape)
    where[lead + axis] = pl.ds(start, size)
    return ref.at[tuple(where)]


def totals_kernel(axes, shared, *refs):
    count = len(axes)
    locals_, outs = refs[:count], refs[count : 2 * count]
    scratch = refs[2 * count :]
    ways, pairs = lax.axis_size("batch"), lax.axis_size("expert") // 2
    group, place = lax.axis_index("batch"), lax.axis_index("expert")
    pair, core = place // 2, lax.rem(place, 2)
    sibling = (group, pair * 2 + 1 - core)
    in_batch = [(lax.rem(group + k, ways), place) for k in range(1, ways)]
    in_pairs = [(group, lax.rem(pair + k, pairs) * 2 + core) for k in range(1, pairs)]
    barrier = pltpu.get_barrier_semaphore()
    for device in [sibling] + in_batch + in_pairs:
        pl.semaphore_signal(barrier, inc=1, device_id=device, device_id_type=MESH)
    pl.semaphore_wait(barrier, 1 + len(in_batch) + len(in_pairs))

    per = 7
    held = [scratch[i * per : (i + 1) * per] for i in range(count)]
    sems = scratch[count * per :]

    def send(src, dst, stage, i, k, device):
        copy = pltpu.make_async_remote_copy(
            src_ref=src,
            dst_ref=dst,
            send_sem=sems[0].at[stage, i, k],
            recv_sem=sems[1].at[stage, i, k],
            device_id=device,
            device_id_type=MESH,
        )
        copy.start()
        return copy

    copies = []
    for i in range(count):
        copies.append([send(locals_[i].at[:, 1 - core], held[i][0], 0, i, 0, sibling)])
    for i in range(count):
        from_core, by_chip, from_batch, by_batch, from_pairs, mine, _ = held[i]
        copies[i][0].wait()

        def add_core(z, carry, i=i, from_core=from_core, by_chip=by_chip):
            by_chip[z] = together(locals_[i][z, core], from_core[z]).astype(BF16)
            return carry

        lax.fori_loop(0, pairs, add_core, 0)
        size = mine.shape[axes[i]]
        copies[i] = [
            send(
                part_of(by_chip, 1, axes[i], size, lax.rem(group + k, ways)),
                from_batch.at[k - 1],
                1,
                i,
                k - 1,
                in_batch[k - 1],
            )
            for k in range(1, ways)
        ]
    for i in range(count):
        from_core, by_chip, from_batch, by_batch, from_pairs, mine, _ = held[i]
        for copy in copies[i]:
            copy.wait()
        size = mine.shape[axes[i]]

        def add_batch(z, carry, i=i, held=held[i], size=size):
            own = part_of(held[1], 1, axes[i], size, group)[z]
            held[3][z] = together(own, *(held[2][k, z] for k in range(ways - 1))).astype(BF16)
            return carry

        lax.fori_loop(0, pairs, add_batch, 0)
        copies[i] = [
            send(
                by_batch.at[lax.rem(pair + k, pairs)],
                from_pairs.at[k - 1],
                2,
                i,
                k - 1,
                in_pairs[k - 1],
            )
            for k in range(1, pairs)
        ]
    for i in range(count):
        from_core, by_chip, from_batch, by_batch, from_pairs, mine, every = held[i]
        for copy in copies[i]:
            copy.wait()
        mine[...] = together(by_batch[pair], *(from_pairs[k] for k in range(pairs - 1))).astype(BF16)
        target = every.at[pair, core] if shared[i] else every
        size = mine.shape[axes[i]]
        own = part_of(target, 0, axes[i], size, group)
        copies[i] = [
            send(mine, own, 3, i, k - 1, in_batch[k - 1]) for k in range(1, ways)
        ]
        own[...] = mine[...]
    for i in range(count):
        every = held[i][6]
        for copy in copies[i]:
            copy.wait()
        if shared[i]:
            copies[i] = [
                send(
                    every.at[pair, core], every.at[pair, core], 4, i, k - 1, in_pairs[k - 1]
                )
                for k in range(1, pairs)
            ]
        else:
            outs[i][...] = every[...].astype(F32)
    for i in range(count):
        if shared[i]:
            every = held[i][6]
            for copy in copies[i]:
                copy.wait()
            send(every.at[:, core], every.at[:, core], 5, i, 0, sibling).wait()
            outs[i][...] = every[...].astype(F32)


def totals(items, collective_id):
    ways, pairs = lax.axis_size("batch"), lax.axis_size("expert") // 2
    out_shape, scratch = [], []
    for item in items:
        _, chunk, part = item.shapes(ways)
        whole = item.local.shape if item.shared else chunk
        out_shape.append(jax.ShapeDtypeStruct(whole, F32))
        scratch += [
            pltpu.VMEM((pairs, *chunk), BF16),
            pltpu.VMEM((pairs, *chunk), BF16),
            pltpu.VMEM((ways - 1, pairs, *part), BF16),
            pltpu.VMEM((pairs, *part), BF16),
            pltpu.VMEM((pairs - 1, *part), BF16),
            pltpu.VMEM(part, BF16),
            pltpu.VMEM(whole, BF16),
        ]
    most = max(ways, pairs) - 1
    scratch += [pltpu.SemaphoreType.DMA((6, len(items), most))] * 2
    return pl.pallas_call(
        functools.partial(
            totals_kernel, tuple(item.axis for item in items), tuple(item.shared for item in items)
        ),
        out_shape=out_shape,
        in_specs=[pl.BlockSpec(memory_space=pltpu.VMEM)] * len(items),
        out_specs=[pl.BlockSpec(memory_space=pltpu.VMEM)] * len(items),
        scratch_shapes=scratch,
        compiler_params=params(collective_id=collective_id, has_side_effects=True),
        name="totals",
    )(*(item.local for item in items))


def pack_small(pieces, width, places):
    flat = jnp.concatenate([p.reshape(-1, width) for p in pieces], axis=0).astype(BF16)
    rows = -(-flat.shape[0] // 16)
    across = width // LANES
    blocks = jnp.pad(flat, ((0, rows * 16 - flat.shape[0]), (0, 0)))
    blocks = blocks.reshape(rows, 16, across, LANES).transpose(0, 2, 1, 3)
    blocks = blocks.reshape(rows * across, 16, LANES)
    ways, experts = places
    each = -(-rows * across // (ways * experts))
    blocks = jnp.pad(blocks, ((0, each * ways * experts - rows * across), (0, 0), (0, 0)))
    return blocks.reshape(experts // 2, 2, ways * each, 16, LANES)


def unpack_small(packed, pieces, width):
    across = width // LANES
    count = sum(p.size for p in pieces) // width
    rows = -(-count // 16)
    blocks = packed.reshape(-1, 16, LANES)[: rows * across]
    flat = blocks.reshape(rows, across, 16, LANES).transpose(0, 2, 1, 3).reshape(rows * 16, width)
    outs, at = [], 0
    for p in pieces:
        step = p.size // width
        outs.append(flat[at : at + step].reshape(p.shape))
        at += step
    return outs


def per_device(
    tokens,
    routes,
    gain_one,
    in_proj,
    conv_weight,
    conv_bias,
    x_proj,
    dt_proj,
    dt_bias,
    rate_log,
    skip,
    out_proj,
    gain_two,
    router,
    expert_in,
    expert_out,
    cotangent,
):
    count, width = tokens.shape[1], tokens.shape[2]
    steps = count // SEGS
    inner_width = out_proj.shape[0]
    rank = dt_proj.shape[0]
    experts = router.shape[0]
    slots = 5 * count // (4 * experts)
    reach = conv_weight.shape[0] - 1
    rate2 = -jnp.exp(rate_log) * LOG2E
    skip_row = skip[None]

    route = by_segment(routes[0]).reshape(count)
    upstream_low = by_segment(cotangent[0])
    expert_ids = lax.broadcasted_iota(jnp.int32, (experts, count), 0)
    onehot = (expert_ids == route[None]).astype(BF16)
    first = lax.broadcasted_iota(jnp.int32, (count, count), 0)
    second = lax.broadcasted_iota(jnp.int32, (count, count), 1)
    token_of = lambda p: (p % SEGS) * steps + p // SEGS
    earlier = (token_of(first) <= token_of(second)).astype(BF16)
    running = jnp.dot(onehot, earlier, preferred_element_type=F32)
    place = (jnp.sum(running * onehot.astype(F32), axis=0) - 1.0).astype(jnp.int32)
    target = jnp.where(place < slots, route * slots + place, -1)
    slot_ids = lax.broadcasted_iota(jnp.int32, (experts * slots, count), 0)
    dispatch = (slot_ids == target[None]).astype(BF16)

    def to_slots(rows):
        sent = jnp.dot(dispatch, rows, preferred_element_type=F32).astype(BF16)
        return exchange(sent.reshape(experts, slots, width), "expert").reshape(-1, width)

    def to_tokens(rows):
        back = exchange(rows.reshape(experts, slots, width), "expert").reshape(-1, width)
        return contract(dispatch, back, 0, 0)

    slot_upstream = to_slots(upstream_low)

    values = by_segment(tokens[0]).astype(F32)
    normed_one = rms(values, gain_one).astype(BF16)
    both = jnp.dot(normed_one, in_proj, preferred_element_type=F32)
    inner = both[:, :inner_width].astype(BF16)
    gate_z = both[:, inner_width:]
    blocks = inner.reshape(steps, SEGS, inner_width)
    tail = blocks[steps - reach :]
    before = passed_along(tail[:, SEGS - 1], "expert", 1)
    extended = jnp.concatenate(
        [jnp.concatenate([before[:, None], tail[:, : SEGS - 1]], axis=1), blocks], axis=0
    ).astype(F32)
    conv_pre = conv_bias + sum(
        conv_weight[k] * extended[k : k + steps] for k in range(reach + 1)
    )
    conv_pre = conv_pre.reshape(count, inner_width)
    mixed = silu(conv_pre).astype(BF16)
    proj = contract(mixed, x_proj, 1, 1)
    low_rank = proj[:, :rank].astype(BF16)
    bc = proj[:, rank:]
    pre = jnp.dot(low_rank, dt_proj, preferred_element_type=F32) + dt_bias
    ends, sums = segment_ends(pre, mixed, bc, rate2, True)
    start = segment_starts(ends, sums, rate2, "expert", True)
    ssm, held = all_states(pre, mixed, bc, rate2, skip_row, start)
    gated = (ssm * silu(gate_z)).astype(BF16)
    hidden = values + jnp.dot(gated, out_proj, preferred_element_type=F32)
    normed_two = rms(hidden, gain_two).astype(BF16)

    rows = to_slots(normed_two)
    logits = contract(rows, router, 1, 1)
    scores = jnp.exp(logits - jnp.max(logits, axis=1, keepdims=True))
    probs = scores / jnp.sum(scores, axis=1, keepdims=True)
    mine = (
        lax.broadcasted_iota(jnp.int32, probs.shape, 1) == lax.axis_index("expert")
    ).astype(F32)
    gate = jnp.sum(probs * mine, axis=1, keepdims=True)
    pre_hidden = jnp.dot(rows, expert_in[0], preferred_element_type=F32)
    active_f, gelu_back = jax.vjp(lambda v: jax.nn.gelu(v, approximate=False), pre_hidden)
    active = active_f.astype(BF16)
    expert_rows = jnp.dot(active, expert_out[0], preferred_element_type=F32).astype(BF16)
    expert_rows = expert_rows.astype(F32)
    slot_grad = (gate * slot_upstream.astype(F32)).astype(BF16)
    expert_out_local = contract(active, slot_grad, 0, 0)
    active_grad = contract(slot_grad, expert_out[0], 1, 1)
    hidden_pre_grad = gelu_back(active_grad)[0].astype(BF16)
    expert_in_local = contract(rows, hidden_pre_grad, 0, 0)
    row_grad = contract(hidden_pre_grad, expert_in[0], 1, 1)
    picked = jnp.sum(slot_grad.astype(F32) * expert_rows, axis=1, keepdims=True)
    logit_grad = (picked * (mine - probs)).astype(BF16)
    router_local = contract(logit_grad, rows, 0, 0)
    row_grad = (row_grad + jnp.dot(logit_grad, router, preferred_element_type=F32)).astype(BF16)
    normed_two_grad = to_tokens(row_grad)
    output = (hidden + to_tokens((gate * expert_rows).astype(BF16))).astype(BF16)

    hidden_norm, gain_two_local = rms_back(hidden, gain_two, normed_two_grad)
    hidden_grad = upstream_low.astype(F32) + hidden_norm
    branch = hidden_grad.astype(BF16)
    out_proj_local = contract(gated, branch, 0, 0)
    gated_grad = contract(branch, out_proj, 1, 1)
    ssm_grad = gated_grad * silu(gate_z)
    gate_z_grad = (gated_grad * ssm * silu_slope(gate_z)).astype(BF16)

    ends = segment_ends(pre, ssm_grad, bc, rate2, False)[0]
    later = segment_starts(ends, sums, rate2, "expert", False)
    pre_grad, mixed_grad, rate_log_local, skip_local, dt_bias_local, bc_grad = state_grads(
        pre, mixed, ssm_grad, bc, rate2, skip_row, later, held
    )
    dt_proj_local = contract(low_rank, pre_grad, 0, 0)
    low_rank_grad = contract(pre_grad, dt_proj, 1, 1)
    proj_grad = jnp.concatenate([low_rank_grad, bc_grad], axis=1).astype(BF16)
    x_proj_local = contract(proj_grad, mixed, 0, 0)
    mixed_grad = mixed_grad + jnp.dot(proj_grad, x_proj, preferred_element_type=F32)
    conv_grad = mixed_grad * silu_slope(conv_pre)
    head = conv_grad[: reach * SEGS].reshape(reach, SEGS, inner_width)
    after = passed_along(head[:, 0], "expert", -1)
    inner_grad, conv_weight_local, conv_bias_local = conv_grads(
        conv_grad, inner, before, after, conv_weight
    )
    both_grad = jnp.concatenate([inner_grad, gate_z_grad], axis=1)
    in_proj_local = contract(normed_one, both_grad, 0, 0)
    normed_one_grad = contract(both_grad, in_proj, 1, 1)
    values_grad, gain_one_local = rms_back(values, gain_one, normed_one_grad)
    tokens_grad = by_token(values_grad + hidden_grad)

    pieces = [
        x_proj_local,
        dt_proj_local,
        rate_log_local,
        conv_weight_local,
        conv_bias_local,
        dt_bias_local,
        skip_local,
        router_local,
        jnp.stack([gain_one_local, gain_two_local]),
    ]
    ways = lax.axis_size("batch")
    pairs = experts // 2
    in_proj_grad, out_proj_grad, small = totals(
        [
            Total(in_proj_local.astype(BF16).reshape(pairs, 2, width // experts, -1), 1, False),
            Total(
                out_proj_local.astype(BF16).reshape(
                    pairs, 2, ways, inner_width // (experts * ways), width
                ),
                0,
                False,
            ),
            Total(pack_small(pieces, inner_width, (ways, experts)), 0, True),
        ],
        1,
    )
    out_proj_grad = out_proj_grad.reshape(-1, width)
    small = unpack_small(small, pieces, inner_width)
    expert_in_grad, expert_out_grad = (
        lax.psum_scatter(v.astype(BF16), "batch", scatter_dimension=0, tiled=True).astype(F32)
        for v in (expert_in_local, expert_out_local)
    )
    x_proj_grad, dt_proj_grad, rate_log_grad, conv_weight_grad = small[:4]
    conv_bias_grad, dt_bias_grad, skip_grad, router_grad, gains = small[4:]
    return (
        by_token(output)[None],
        tokens_grad[None],
        gains[0],
        in_proj_grad,
        conv_weight_grad,
        conv_bias_grad[0],
        x_proj_grad,
        dt_proj_grad,
        dt_bias_grad[0],
        rate_log_grad,
        skip_grad[0],
        out_proj_grad,
        gains[1],
        router_grad,
        expert_in_grad[None],
        expert_out_grad[None],
    )


def solution(mesh):
    split = P("batch", "expert", None)
    one = P("expert", None, None)
    both = P("expert", "batch", None)
    in_specs = (split, split) + (P(),) * 12 + (one, one, split)
    out_specs = (split, split, P(), P("expert", None)) + (P(),) * 7
    out_specs += (P("expert", None), P(), P(), both, both)
    return jax.shard_map(
        per_device, mesh=mesh, in_specs=in_specs, out_specs=out_specs, check_vma=False
    )
```

```python
import functools

import jax
import jax.numpy as jnp
from jax import lax
from jax.experimental import pallas as pl
from jax.experimental.pallas import tpu as pltpu
from jax.sharding import PartitionSpec as P

F32, BF16 = jnp.float32, jnp.bfloat16
SEGS = 8
LANES = 128
LOG2E = 1.4426950408889634
LN2 = 0.6931471805599453
VMEM_LIMIT = 56 * 1024 * 1024
MESH = pl.DeviceIdType.MESH


def params(**kw):
    return pltpu.CompilerParams(vmem_limit_bytes=VMEM_LIMIT, **kw)


def softplus(v):
    return jnp.maximum(v, 0.0) + jnp.log1p(jnp.exp(-jnp.abs(v)))


def contract(left, right, left_dim, right_dim):
    return lax.dot_general(
        left, right, (((left_dim,), (right_dim,)), ((), ())), preferred_element_type=F32
    )


def over_sublanes(row):
    return jnp.broadcast_to(row, (SEGS, LANES))


def over_lanes(column):
    return jnp.broadcast_to(column, (SEGS, LANES))


def tile_rows(j):
    return pl.ds(pl.multiple_of(j * SEGS, SEGS), SEGS)


def run_of_segments(a, b, forward):
    at = lax.broadcasted_iota(jnp.int32, (SEGS, LANES), 0)
    for step in (1, 2, 4):
        if forward:
            inside, turn = at >= step, step
        else:
            inside, turn = at < SEGS - step, SEGS - step
        before_a = jnp.where(inside, pltpu.roll(a, turn, 0), 1.0)
        before_b = jnp.where(inside, pltpu.roll(b, turn, 0), 0.0)
        a, b = a * before_a, a * before_b + b
    return a, b


class Carries:
    groups = 2

    def __init__(self, states, blocks, forward, own, lengths, got, got_lengths, sems):
        self.states, self.blocks, self.forward = states, blocks, forward
        self.own, self.lengths, self.got, self.got_lengths = own, lengths, got, got_lengths
        self.sems = sems
        self.count, self.me = lax.axis_size("expert"), lax.axis_index("expert")
        self.per = blocks // self.groups

    @staticmethod
    def scratch(states, blocks, count):
        per = blocks // Carries.groups
        assert blocks % Carries.groups == 0 and per <= SEGS
        return [
            pltpu.VMEM((blocks, states, LANES), BF16),
            pltpu.VMEM((Carries.groups, SEGS, LANES), F32),
            pltpu.VMEM((count, blocks, states, LANES), BF16),
            pltpu.VMEM((count, Carries.groups, SEGS, LANES), F32),
            pltpu.SemaphoreType.DMA((2, 2, Carries.groups, count)),
        ]

    def greet(self):
        barrier = pltpu.get_barrier_semaphore()
        for k in range(1, self.count):
            pl.semaphore_signal(barrier, inc=1, device_id=self.other(k), device_id_type=MESH)
        pl.semaphore_wait(barrier, self.count - 1)

    def other(self, k):
        return (lax.axis_index("batch"), lax.rem(self.me + k, self.count))

    def copies(self, group):
        blocks = pl.ds(group * self.per, self.per)
        found = []
        for k in range(1, self.count):
            pairs = (
                (self.own.at[blocks], self.got.at[k - 1, blocks]),
                (self.lengths.at[group], self.got_lengths.at[k - 1, group]),
            )
            for i, (src, dst) in enumerate(pairs):
                found.append(
                    pltpu.make_async_remote_copy(
                        src_ref=src,
                        dst_ref=dst,
                        send_sem=self.sems.at[0, i, group, k - 1],
                        recv_sem=self.sems.at[1, i, group, k - 1],
                        device_id=self.other(k),
                        device_id_type=MESH,
                    )
                )
        return found

    def put(self, block, ends, sums, rates, run_a, run_b):
        edge = SEGS - 1 if self.forward else 0
        rows = []
        for n in range(self.states):
            a, b = run_of_segments(jnp.exp2(rates[n] * sums), ends[n], self.forward)
            run_a[block, n] = a
            run_b[block, n] = b
            rows.append(b[edge : edge + 1])
        end = jnp.concatenate(rows, axis=0).astype(BF16)
        total = jnp.sum(sums, axis=0, keepdims=True)
        last = self.count - 1
        self.own[block] = end
        self.got[last, block] = end
        for group in range(self.groups):

            @pl.when(block // self.per == group)
            def _():
                row = pl.ds(lax.rem(block, self.per), 1)
                self.lengths[group, row, :] = total
                self.got_lengths[last, group, row, :] = total

            @pl.when(block == (group + 1) * self.per - 1)
            def _():
                for copy in self.copies(group):
                    copy.start()

    def await_group(self, block):
        for group in range(self.groups):

            @pl.when(block == group * self.per)
            def _():
                for copy in self.copies(group):
                    copy.wait()

    def starts(self, block, rate_ref, run_a, run_b):
        group, row = block // self.per, pl.ds(lax.rem(block, self.per), 1)
        rate = rate_ref[...]
        entering = jnp.zeros((self.states, LANES), F32)
        order = range(self.count) if self.forward else range(self.count - 1, -1, -1)
        for place in order:
            slot = lax.rem(self.me - place - 1 + 2 * self.count, self.count)
            length = self.got_lengths[slot, group, row, :]
            joined = jnp.exp2(rate * length) * entering + self.got[slot, block].astype(F32)
            ahead = (place < self.me) if self.forward else (place > self.me)
            entering = jnp.where(ahead, joined, entering)
        found = []
        for n in range(self.states):
            first = entering[n : n + 1]
            after = run_a[block, n] * over_sublanes(first) + run_b[block, n]
            found.append(shifted_in(after, first, self.forward))
        return found


def forward_kernel(states, steps, *refs):
    delta_ref, in_ref, bc_ref, rate_ref, skip_ref, ssm_ref, held_ref = refs[:7]
    in_s, bb, cb, run_a, run_b = refs[7:12]
    phase, block = pl.program_id(0), pl.program_id(1)
    carries = Carries(states, refs[14].shape[1], True, *refs[12:])
    rates = [over_sublanes(rate_ref[n : n + 1, :]) for n in range(states)]

    @pl.when((phase == 0) & (block == 0))
    def _():
        carries.greet()

    def ends(first):
        in_s[...] = delta_ref[...] * in_ref[...].astype(F32)
        sums = jnp.sum(delta_ref[...].reshape(steps, SEGS, LANES), axis=0)

        def one(j, held):
            d, u = delta_ref[tile_rows(j), :], in_s[tile_rows(j), :]
            tile = bc_ref[tile_rows(j), :] if first else None
            new = []
            for n in range(states):
                if first:
                    b = over_lanes(tile[:, n : n + 1])
                    bb[j, n] = b
                    cb[j, n] = over_lanes(tile[:, states + n : states + n + 1])
                else:
                    b = bb[j, n]
                new.append(jnp.exp2(d * rates[n]) * held[n] + u * b)
            return tuple(new)

        zero = jnp.zeros((SEGS, LANES), F32)
        held = lax.fori_loop(0, steps, one, (zero,) * states, unroll=4)
        carries.put(block, held, sums, rates, run_a, run_b)

    @pl.when((phase == 0) & (block == 0))
    def _():
        ends(True)

    @pl.when((phase == 0) & (block > 0))
    def _():
        ends(False)

    @pl.when(phase == 1)
    def _():
        carries.await_group(block)
        start = carries.starts(block, rate_ref, run_a, run_b)
        mixed = in_ref[...].astype(F32)
        in_s[...] = delta_ref[...] * mixed
        ssm_ref[...] = skip_ref[...] * mixed
        for n in range(states):
            held_ref[0, 0, n] = start[n]

        def one(j, held):
            rows = tile_rows(j)
            d, u = delta_ref[rows, :], in_s[rows, :]
            total = ssm_ref[rows, :]
            new = []
            for n in range(states):
                h = jnp.exp2(d * rates[n]) * held[n] + u * bb[j, n]
                held_ref[0, j + 1, n] = h
                total = total + cb[j, n] * h
                new.append(h)
            ssm_ref[rows, :] = total
            return tuple(new)

        lax.fori_loop(0, steps, one, tuple(start), unroll=4)


def mixer_states(delta, mixed, bc, rate2, skip, collective_id):
    count, width = delta.shape
    states, steps, blocks = rate2.shape[0], count // SEGS, width // LANES
    block = pl.BlockSpec((count, LANES), lambda p, c: (0, c))
    spread = pltpu.VMEM((steps, states, SEGS, LANES), F32)
    run = pltpu.VMEM((blocks, states, SEGS, LANES), F32)
    return pl.pallas_call(
        functools.partial(forward_kernel, states, steps),
        grid=(2, blocks),
        out_shape=[
            jax.ShapeDtypeStruct((count, width), F32),
            jax.ShapeDtypeStruct((blocks, steps + 1, states, SEGS, LANES), F32),
        ],
        in_specs=[
            block,
            block,
            pl.BlockSpec(bc.shape, lambda p, c: (0, 0)),
            pl.BlockSpec((states, LANES), lambda p, c: (0, c)),
            pl.BlockSpec((1, LANES), lambda p, c: (0, c)),
        ],
        out_specs=[
            pl.BlockSpec((count, LANES), lambda p, c: (0, p * c)),
            pl.BlockSpec((1, steps + 1, states, SEGS, LANES), lambda p, c: (p * c, 0, 0, 0, 0)),
        ],
        scratch_shapes=[pltpu.VMEM((count, LANES), F32), spread, spread, run, run]
        + Carries.scratch(states, blocks, lax.axis_size("expert")),
        compiler_params=params(collective_id=collective_id, has_side_effects=True),
        name="mixer_states",
    )(delta, mixed, bc, rate2, skip)


def backward_kernel(states, steps, *refs):
    pre_ref, delta_ref, in_ref, g_ref, bc_ref, rate_ref, skip_ref, held_ref = refs[:8]
    pre_grad_ref, mixed_grad_ref, rate_grad_ref, skip_grad_ref, bias_grad_ref, bc_grad_ref = refs[
        8:14
    ]
    in_s, rate_sum, in_sum, bb, cb, b_acc, c_acc, run_a, run_b = refs[14:23]
    phase, block = pl.program_id(0), pl.program_id(1)
    blocks = refs[25].shape[1]
    carries = Carries(states, blocks, False, *refs[23:])
    rates = [over_sublanes(rate_ref[n : n + 1, :]) for n in range(states)]
    zero = jnp.zeros((SEGS, LANES), F32)

    @pl.when((phase == 0) & (block == 0))
    def _():
        carries.greet()

    def ends(first):
        sums = jnp.sum(delta_ref[...].reshape(steps, SEGS, LANES), axis=0)

        def one(i, held):
            j = steps - 1 - i
            d, g = delta_ref[tile_rows(j), :], g_ref[tile_rows(j), :]
            tile = bc_ref[tile_rows(j), :] if first else None
            new = []
            for n in range(states):
                if first:
                    c = over_lanes(tile[:, states + n : states + n + 1])
                    bb[j, n] = over_lanes(tile[:, n : n + 1])
                    cb[j, n] = c
                else:
                    c = cb[j, n]
                new.append(jnp.exp2(d * rates[n]) * (held[n] + g * c))
            return tuple(new)

        held = lax.fori_loop(0, steps, one, (zero,) * states, unroll=4)
        carries.put(block, held, sums, rates, run_a, run_b)

    @pl.when((phase == 0) & (block == 0))
    def _():
        ends(True)

    @pl.when((phase == 0) & (block > 0))
    def _():
        ends(False)

    def grads(first, last):
        start = carries.starts(block, rate_ref, run_a, run_b)
        delta, g = delta_ref[...], g_ref[...]
        mixed = in_ref[...].astype(F32)
        in_s[...] = delta * mixed
        place = lax.broadcasted_iota(jnp.int32, (SEGS, LANES), 1)

        def one(i, carry):
            edge, rate_acc = carry
            j = steps - 1 - i
            rows = tile_rows(j)
            d, u, g = delta_ref[rows, :], in_s[rows, :], g_ref[rows, :]
            by_rate = by_b = sums = zero
            new_edge, new_acc = [], []
            for n in range(states):
                b, c = bb[j, n], cb[j, n]
                q = c * g + edge[n]
                e = jnp.exp2(d * rates[n]) * q
                v = e * held_ref[0, j, n]
                by_rate = by_rate + rates[n] * v
                by_b = by_b + b * q
                to_b = q * u
                to_c = g * held_ref[0, j + 1, n]
                if not first:
                    to_b = b_acc[j, n] + to_b
                    to_c = c_acc[j, n] + to_c
                if last:
                    sums = jnp.where(place == n, jnp.sum(to_b, axis=1, keepdims=True), sums)
                    to_c = jnp.sum(to_c, axis=1, keepdims=True)
                    sums = jnp.where(place == states + n, to_c, sums)
                else:
                    b_acc[j, n] = to_b
                    c_acc[j, n] = to_c
                new_edge.append(e)
                new_acc.append(rate_acc[n] + d * v)
            rate_sum[rows, :] = by_rate
            in_sum[rows, :] = by_b
            if last:
                bc_grad_ref[rows, :] = sums
            return tuple(new_edge), tuple(new_acc)

        _, rate_acc = lax.fori_loop(
            0, steps, one, (tuple(start), (zero,) * states), unroll=2
        )
        for n in range(states):
            rate_grad_ref[n : n + 1, :] = (
                LN2 * rate_ref[n : n + 1, :] * jnp.sum(rate_acc[n], axis=0, keepdims=True)
            )
        by_b = in_sum[...]
        pre_grad = (LN2 * rate_sum[...] + mixed * by_b) * jax.nn.sigmoid(pre_ref[...])
        pre_grad_ref[...] = pre_grad.astype(BF16)
        bias_grad_ref[...] = jnp.sum(pre_grad, axis=0, keepdims=True)
        mixed_grad_ref[...] = delta * by_b + skip_ref[...] * g
        skip_grad_ref[...] = jnp.sum(g * mixed, axis=0, keepdims=True)

    @pl.when(phase == 1)
    def _():
        carries.await_group(block)

    @pl.when((phase == 1) & (block == 0))
    def _():
        grads(True, False)

    @pl.when((phase == 1) & (block > 0) & (block < blocks - 1))
    def _():
        grads(False, False)

    @pl.when((phase == 1) & (block == blocks - 1))
    def _():
        grads(False, True)


def mixer_grads(pre, delta, mixed, ssm_grad, bc, rate2, skip, held, collective_id):
    count, width = delta.shape
    states, steps, blocks = rate2.shape[0], count // SEGS, width // LANES
    block = pl.BlockSpec((count, LANES), lambda p, c: (0, c))
    late = lambda rows: pl.BlockSpec((rows, LANES), lambda p, c: (0, p * c))
    spread = pltpu.VMEM((steps, states, SEGS, LANES), F32)
    run = pltpu.VMEM((blocks, states, SEGS, LANES), F32)
    flat = pltpu.VMEM((count, LANES), F32)
    *outs, bc_grad = pl.pallas_call(
        functools.partial(backward_kernel, states, steps),
        grid=(2, blocks),
        out_shape=[
            jax.ShapeDtypeStruct((count, width), BF16),
            jax.ShapeDtypeStruct((count, width), F32),
            jax.ShapeDtypeStruct((states, width), F32),
            jax.ShapeDtypeStruct((1, width), F32),
            jax.ShapeDtypeStruct((1, width), F32),
            jax.ShapeDtypeStruct((count, LANES), F32),
        ],
        in_specs=[
            late(count),
            block,
            late(count),
            block,
            pl.BlockSpec(bc.shape, lambda p, c: (0, 0)),
            pl.BlockSpec((states, LANES), lambda p, c: (0, c)),
            late(1),
            pl.BlockSpec((1, steps + 1, states, SEGS, LANES), lambda p, c: (p * c, 0, 0, 0, 0)),
        ],
        out_specs=[late(count), late(count), late(states), late(1), late(1)]
        + [pl.BlockSpec((count, LANES), lambda p, c: (0, 0))],
        scratch_shapes=[flat, flat, flat, spread, spread, spread, spread, run, run]
        + Carries.scratch(states, blocks, lax.axis_size("expert")),
        compiler_params=params(collective_id=collective_id, has_side_effects=True),
        name="mixer_grads",
    )(pre, delta, mixed, ssm_grad, bc, rate2, skip, held)
    return *outs, bc_grad[:, : 2 * states]


PAIR = 2


def shifted_in(tile, row, forward):
    if forward:
        return jnp.concatenate([row, tile[: SEGS - 1]], axis=0)
    return jnp.concatenate([tile[1:], row], axis=0)


def conv_grads_kernel(reach, grad_ref, inner_ref, before_ref, after_ref, weight_ref, *outs):
    inner_grad_ref, weight_grad_ref, bias_grad_ref, ext_in, ext_grad = outs
    count = grad_ref.shape[0]
    rim = reach * SEGS
    grad = grad_ref[...]
    inner = inner_ref[...].astype(F32)
    for k in range(reach):
        own = inner[count - rim + k * SEGS : count - rim + (k + 1) * SEGS]
        ext_in[k * SEGS : (k + 1) * SEGS, :] = shifted_in(own, before_ref[k : k + 1, :], True)
        own = grad[k * SEGS : (k + 1) * SEGS]
        ext_grad[count + k * SEGS : count + (k + 1) * SEGS, :] = shifted_in(
            own, after_ref[k : k + 1, :], False
        )
    ext_in[rim:, :] = inner
    ext_grad[:count, :] = grad
    bias_grad_ref[...] = jnp.sum(grad, axis=0, keepdims=True)
    total = jnp.zeros_like(grad)
    for k in range(reach + 1):
        total = total + weight_ref[k : k + 1, :] * ext_grad[(reach - k) * SEGS :, :][:count]
        weight_grad_ref[k : k + 1, :] = jnp.sum(
            grad * ext_in[k * SEGS : k * SEGS + count, :], axis=0, keepdims=True
        )
    inner_grad_ref[...] = total.astype(BF16)


def conv_grads(grad, inner, before, after, weight):
    count, width = grad.shape
    reach = weight.shape[0] - 1
    wide = PAIR * LANES
    spec = lambda rows: pl.BlockSpec((rows, wide), lambda c: (0, c))
    return pl.pallas_call(
        functools.partial(conv_grads_kernel, reach),
        grid=(width // wide,),
        out_shape=[
            jax.ShapeDtypeStruct((count, width), BF16),
            jax.ShapeDtypeStruct((reach + 1, width), F32),
            jax.ShapeDtypeStruct((1, width), F32),
        ],
        in_specs=[spec(count), spec(count), spec(reach), spec(reach), spec(reach + 1)],
        out_specs=[spec(count), spec(reach + 1), spec(1)],
        scratch_shapes=[pltpu.VMEM((count + reach * SEGS, wide), F32)] * 2,
        compiler_params=params(),
        name="conv_grads",
    )(grad, inner, before.astype(F32), after, weight)


def passed_along(value, axis, steps):
    count = lax.axis_size(axis)
    leading, last = (max(0, -steps), min(count, count - steps))
    return lax.ppermute(value, axis, [(source, source + steps) for source in range(leading, last)])


def exchange(value, axis):
    return lax.all_to_all(value, axis, split_axis=0, concat_axis=0, tiled=True)


def silu(v):
    return v * jax.nn.sigmoid(v)


def silu_slope(v):
    s = jax.nn.sigmoid(v)
    return s * (1.0 + v * (1.0 - s))


def by_segment(value):
    count = value.shape[0]
    return value.reshape(SEGS, count // SEGS, -1).transpose(1, 0, 2).reshape(count, -1)


def by_token(value):
    count = value.shape[0]
    return value.reshape(count // SEGS, SEGS, -1).transpose(1, 0, 2).reshape(count, -1)


def rms_back(values, gain, grad):
    r = lax.rsqrt(jnp.mean(values * values, axis=-1, keepdims=True) + 1e-05)
    u = gain * grad
    mean = jnp.mean(values * u, axis=-1, keepdims=True)
    return r * u - values * (r * r * r) * mean, jnp.sum(grad * values * r, axis=0)


def rms(values, gain):
    return values * lax.rsqrt(jnp.mean(values * values, axis=-1, keepdims=True) + 1e-05) * gain


def together(*parts):
    return sum(p.astype(F32) for p in parts)


class Total:
    def __init__(self, local, axis, shared):
        self.local, self.axis, self.shared = local, axis, shared

    def shapes(self, ways):
        pairs = self.local.shape[0]
        chunk = self.local.shape[2:]
        part = list(chunk)
        part[self.axis] //= ways
        return pairs, chunk, tuple(part)


def part_of(ref, lead, axis, size, index):
    start = index * size
    if axis == len(ref.shape) - lead - 1:
        start = pl.multiple_of(start, LANES)
    where = [slice(None)] * len(ref.shape)
    where[lead + axis] = pl.ds(start, size)
    return ref.at[tuple(where)]


def totals_kernel(axes, shared, *refs):
    count = len(axes)
    locals_, outs = refs[:count], refs[count : 2 * count]
    scratch = refs[2 * count :]
    ways, pairs = lax.axis_size("batch"), lax.axis_size("expert") // 2
    group, place = lax.axis_index("batch"), lax.axis_index("expert")
    pair, core = place // 2, lax.rem(place, 2)
    sibling = (group, pair * 2 + 1 - core)
    in_batch = [(lax.rem(group + k, ways), place) for k in range(1, ways)]
    in_pairs = [(group, lax.rem(pair + k, pairs) * 2 + core) for k in range(1, pairs)]
    barrier = pltpu.get_barrier_semaphore()
    for device in [sibling] + in_batch + in_pairs:
        pl.semaphore_signal(barrier, inc=1, device_id=device, device_id_type=MESH)
    pl.semaphore_wait(barrier, 1 + len(in_batch) + len(in_pairs))

    per = 7
    held = [scratch[i * per : (i + 1) * per] for i in range(count)]
    sems = scratch[count * per :]

    def send(src, dst, stage, i, k, device):
        copy = pltpu.make_async_remote_copy(
            src_ref=src,
            dst_ref=dst,
            send_sem=sems[0].at[stage, i, k],
            recv_sem=sems[1].at[stage, i, k],
            device_id=device,
            device_id_type=MESH,
        )
        copy.start()
        return copy

    copies = []
    for i in range(count):
        copies.append([send(locals_[i].at[:, 1 - core], held[i][0], 0, i, 0, sibling)])
    for i in range(count):
        from_core, by_chip, from_batch, by_batch, from_pairs, mine, _ = held[i]
        copies[i][0].wait()

        def add_core(z, carry, i=i, from_core=from_core, by_chip=by_chip):
            by_chip[z] = together(locals_[i][z, core], from_core[z]).astype(BF16)
            return carry

        lax.fori_loop(0, pairs, add_core, 0)
        size = mine.shape[axes[i]]
        copies[i] = [
            send(
                part_of(by_chip, 1, axes[i], size, lax.rem(group + k, ways)),
                from_batch.at[k - 1],
                1,
                i,
                k - 1,
                in_batch[k - 1],
            )
            for k in range(1, ways)
        ]
    for i in range(count):
        from_core, by_chip, from_batch, by_batch, from_pairs, mine, _ = held[i]
        for copy in copies[i]:
            copy.wait()
        size = mine.shape[axes[i]]

        def add_batch(z, carry, i=i, held=held[i], size=size):
            own = part_of(held[1], 1, axes[i], size, group)[z]
            held[3][z] = together(own, *(held[2][k, z] for k in range(ways - 1))).astype(BF16)
            return carry

        lax.fori_loop(0, pairs, add_batch, 0)
        copies[i] = [
            send(
                by_batch.at[lax.rem(pair + k, pairs)],
                from_pairs.at[k - 1],
                2,
                i,
                k - 1,
                in_pairs[k - 1],
            )
            for k in range(1, pairs)
        ]
    for i in range(count):
        from_core, by_chip, from_batch, by_batch, from_pairs, mine, every = held[i]
        for copy in copies[i]:
            copy.wait()
        mine[...] = together(by_batch[pair], *(from_pairs[k] for k in range(pairs - 1))).astype(BF16)
        target = every.at[pair, core] if shared[i] else every
        size = mine.shape[axes[i]]
        own = part_of(target, 0, axes[i], size, group)
        copies[i] = [
            send(mine, own, 3, i, k - 1, in_batch[k - 1]) for k in range(1, ways)
        ]
        own[...] = mine[...]
    for i in range(count):
        every = held[i][6]
        for copy in copies[i]:
            copy.wait()
        if shared[i]:
            copies[i] = [
                send(
                    every.at[pair, core], every.at[pair, core], 4, i, k - 1, in_pairs[k - 1]
                )
                for k in range(1, pairs)
            ]
        else:
            outs[i][...] = every[...].astype(F32)
    for i in range(count):
        if shared[i]:
            every = held[i][6]
            for copy in copies[i]:
                copy.wait()
            send(every.at[:, core], every.at[:, core], 5, i, 0, sibling).wait()
            outs[i][...] = every[...].astype(F32)


def totals(items, collective_id):
    ways, pairs = lax.axis_size("batch"), lax.axis_size("expert") // 2
    out_shape, scratch = [], []
    for item in items:
        _, chunk, part = item.shapes(ways)
        whole = item.local.shape if item.shared else chunk
        out_shape.append(jax.ShapeDtypeStruct(whole, F32))
        scratch += [
            pltpu.VMEM((pairs, *chunk), BF16),
            pltpu.VMEM((pairs, *chunk), BF16),
            pltpu.VMEM((ways - 1, pairs, *part), BF16),
            pltpu.VMEM((pairs, *part), BF16),
            pltpu.VMEM((pairs - 1, *part), BF16),
            pltpu.VMEM(part, BF16),
            pltpu.VMEM(whole, BF16),
        ]
    most = max(ways, pairs) - 1
    scratch += [pltpu.SemaphoreType.DMA((6, len(items), most))] * 2
    return pl.pallas_call(
        functools.partial(
            totals_kernel, tuple(item.axis for item in items), tuple(item.shared for item in items)
        ),
        out_shape=out_shape,
        in_specs=[pl.BlockSpec(memory_space=pltpu.VMEM)] * len(items),
        out_specs=[pl.BlockSpec(memory_space=pltpu.VMEM)] * len(items),
        scratch_shapes=scratch,
        compiler_params=params(collective_id=collective_id, has_side_effects=True),
        name="totals",
    )(*(item.local for item in items))


def pack_small(pieces, width, places):
    flat = jnp.concatenate([p.reshape(-1, width) for p in pieces], axis=0).astype(BF16)
    rows = -(-flat.shape[0] // 16)
    across = width // LANES
    blocks = jnp.pad(flat, ((0, rows * 16 - flat.shape[0]), (0, 0)))
    blocks = blocks.reshape(rows, 16, across, LANES).transpose(0, 2, 1, 3)
    blocks = blocks.reshape(rows * across, 16, LANES)
    ways, experts = places
    each = -(-rows * across // (ways * experts))
    blocks = jnp.pad(blocks, ((0, each * ways * experts - rows * across), (0, 0), (0, 0)))
    return blocks.reshape(experts // 2, 2, ways * each, 16, LANES)


def unpack_small(packed, pieces, width):
    across = width // LANES
    count = sum(p.size for p in pieces) // width
    rows = -(-count // 16)
    blocks = packed.reshape(-1, 16, LANES)[: rows * across]
    flat = blocks.reshape(rows, across, 16, LANES).transpose(0, 2, 1, 3).reshape(rows * 16, width)
    outs, at = [], 0
    for p in pieces:
        step = p.size // width
        outs.append(flat[at : at + step].reshape(p.shape))
        at += step
    return outs


def per_device(
    tokens,
    routes,
    gain_one,
    in_proj,
    conv_weight,
    conv_bias,
    x_proj,
    dt_proj,
    dt_bias,
    rate_log,
    skip,
    out_proj,
    gain_two,
    router,
    expert_in,
    expert_out,
    cotangent,
):
    count, width = tokens.shape[1], tokens.shape[2]
    steps = count // SEGS
    inner_width = out_proj.shape[0]
    rank = dt_proj.shape[0]
    experts = router.shape[0]
    slots = 5 * count // (4 * experts)
    reach = conv_weight.shape[0] - 1
    rate2 = -jnp.exp(rate_log) * LOG2E
    skip_row = skip[None]

    route = by_segment(routes[0]).reshape(count)
    upstream_low = by_segment(cotangent[0])
    expert_ids = lax.broadcasted_iota(jnp.int32, (experts, count), 0)
    onehot = (expert_ids == route[None]).astype(BF16)
    first = lax.broadcasted_iota(jnp.int32, (count, count), 0)
    second = lax.broadcasted_iota(jnp.int32, (count, count), 1)
    token_of = lambda p: (p % SEGS) * steps + p // SEGS
    earlier = (token_of(first) <= token_of(second)).astype(BF16)
    running = jnp.dot(onehot, earlier, preferred_element_type=F32)
    place = (jnp.sum(running * onehot.astype(F32), axis=0) - 1.0).astype(jnp.int32)
    target = jnp.where(place < slots, route * slots + place, -1)
    slot_ids = lax.broadcasted_iota(jnp.int32, (experts * slots, count), 0)
    dispatch = (slot_ids == target[None]).astype(BF16)

    def to_slots(rows):
        sent = jnp.dot(dispatch, rows, preferred_element_type=F32).astype(BF16)
        return exchange(sent.reshape(experts, slots, width), "expert").reshape(-1, width)

    def to_tokens(rows):
        back = exchange(rows.reshape(experts, slots, width), "expert").reshape(-1, width)
        return contract(dispatch, back, 0, 0)

    slot_upstream = to_slots(upstream_low)

    values = by_segment(tokens[0]).astype(F32)
    normed_one = rms(values, gain_one).astype(BF16)
    both = jnp.dot(normed_one, in_proj, preferred_element_type=F32)
    inner = both[:, :inner_width].astype(BF16)
    gate_z = both[:, inner_width:]
    blocks = inner.reshape(steps, SEGS, inner_width)
    tail = blocks[steps - reach :]
    before = passed_along(tail[:, SEGS - 1], "expert", 1)
    extended = jnp.concatenate(
        [jnp.concatenate([before[:, None], tail[:, : SEGS - 1]], axis=1), blocks], axis=0
    ).astype(F32)
    conv_pre = conv_bias + sum(
        conv_weight[k] * extended[k : k + steps] for k in range(reach + 1)
    )
    conv_pre = conv_pre.reshape(count, inner_width)
    mixed = silu(conv_pre).astype(BF16)
    proj = contract(mixed, x_proj, 1, 1)
    low_rank = proj[:, :rank].astype(BF16)
    bc = proj[:, rank:]
    pre = jnp.dot(low_rank, dt_proj, preferred_element_type=F32) + dt_bias
    delta = softplus(pre)
    ssm, held = mixer_states(delta, mixed, bc, rate2, skip_row, 2)
    gated = (ssm * silu(gate_z)).astype(BF16)
    hidden = values + jnp.dot(gated, out_proj, preferred_element_type=F32)
    normed_two = rms(hidden, gain_two).astype(BF16)

    rows = to_slots(normed_two)
    logits = contract(rows, router, 1, 1)
    scores = jnp.exp(logits - jnp.max(logits, axis=1, keepdims=True))
    probs = scores / jnp.sum(scores, axis=1, keepdims=True)
    mine = (
        lax.broadcasted_iota(jnp.int32, probs.shape, 1) == lax.axis_index("expert")
    ).astype(F32)
    gate = jnp.sum(probs * mine, axis=1, keepdims=True)
    pre_hidden = jnp.dot(rows, expert_in[0], preferred_element_type=F32)
    active_f, gelu_back = jax.vjp(lambda v: jax.nn.gelu(v, approximate=False), pre_hidden)
    active = active_f.astype(BF16)
    expert_rows = jnp.dot(active, expert_out[0], preferred_element_type=F32).astype(BF16)
    expert_rows = expert_rows.astype(F32)
    slot_grad = (gate * slot_upstream.astype(F32)).astype(BF16)
    expert_out_local = contract(active, slot_grad, 0, 0)
    active_grad = contract(slot_grad, expert_out[0], 1, 1)
    hidden_pre_grad = gelu_back(active_grad)[0].astype(BF16)
    expert_in_local = contract(rows, hidden_pre_grad, 0, 0)
    row_grad = contract(hidden_pre_grad, expert_in[0], 1, 1)
    picked = jnp.sum(slot_grad.astype(F32) * expert_rows, axis=1, keepdims=True)
    logit_grad = (picked * (mine - probs)).astype(BF16)
    router_local = contract(logit_grad, rows, 0, 0)
    row_grad = (row_grad + jnp.dot(logit_grad, router, preferred_element_type=F32)).astype(BF16)
    normed_two_grad = to_tokens(row_grad)
    output = (hidden + to_tokens((gate * expert_rows).astype(BF16))).astype(BF16)

    hidden_norm, gain_two_local = rms_back(hidden, gain_two, normed_two_grad)
    hidden_grad = upstream_low.astype(F32) + hidden_norm
    branch = hidden_grad.astype(BF16)
    out_proj_local = contract(gated, branch, 0, 0)
    gated_grad = contract(branch, out_proj, 1, 1)
    ssm_grad = gated_grad * silu(gate_z)
    gate_z_grad = (gated_grad * ssm * silu_slope(gate_z)).astype(BF16)

    pre_grad, mixed_grad, rate_log_local, skip_local, dt_bias_local, bc_grad = mixer_grads(
        pre, delta, mixed, ssm_grad, bc, rate2, skip_row, held, 3
    )
    dt_proj_local = contract(low_rank, pre_grad, 0, 0)
    low_rank_grad = contract(pre_grad, dt_proj, 1, 1)
    proj_grad = jnp.concatenate([low_rank_grad, bc_grad], axis=1).astype(BF16)
    x_proj_local = contract(proj_grad, mixed, 0, 0)
    mixed_grad = mixed_grad + jnp.dot(proj_grad, x_proj, preferred_element_type=F32)
    conv_grad = mixed_grad * silu_slope(conv_pre)
    head = conv_grad[: reach * SEGS].reshape(reach, SEGS, inner_width)
    after = passed_along(head[:, 0], "expert", -1)
    inner_grad, conv_weight_local, conv_bias_local = conv_grads(
        conv_grad, inner, before, after, conv_weight
    )
    both_grad = jnp.concatenate([inner_grad, gate_z_grad], axis=1)
    in_proj_local = contract(normed_one, both_grad, 0, 0)
    normed_one_grad = contract(both_grad, in_proj, 1, 1)
    values_grad, gain_one_local = rms_back(values, gain_one, normed_one_grad)
    tokens_grad = by_token(values_grad + hidden_grad)

    pieces = [
        x_proj_local,
        dt_proj_local,
        rate_log_local,
        conv_weight_local,
        conv_bias_local,
        dt_bias_local,
        skip_local,
        router_local,
        jnp.stack([gain_one_local, gain_two_local]),
    ]
    ways = lax.axis_size("batch")
    pairs = experts // 2
    in_proj_grad, out_proj_grad, small = totals(
        [
            Total(in_proj_local.astype(BF16).reshape(pairs, 2, width // experts, -1), 1, False),
            Total(
                out_proj_local.astype(BF16).reshape(
                    pairs, 2, ways, inner_width // (experts * ways), width
                ),
                0,
                False,
            ),
            Total(pack_small(pieces, inner_width, (ways, experts)), 0, True),
        ],
        1,
    )
    out_proj_grad = out_proj_grad.reshape(-1, width)
    small = unpack_small(small, pieces, inner_width)
    expert_in_grad, expert_out_grad = (
        lax.psum_scatter(v.astype(BF16), "batch", scatter_dimension=0, tiled=True).astype(F32)
        for v in (expert_in_local, expert_out_local)
    )
    x_proj_grad, dt_proj_grad, rate_log_grad, conv_weight_grad = small[:4]
    conv_bias_grad, dt_bias_grad, skip_grad, router_grad, gains = small[4:]
    return (
        by_token(output)[None],
        tokens_grad[None],
        gains[0],
        in_proj_grad,
        conv_weight_grad,
        conv_bias_grad[0],
        x_proj_grad,
        dt_proj_grad,
        dt_bias_grad[0],
        rate_log_grad,
        skip_grad[0],
        out_proj_grad,
        gains[1],
        router_grad,
        expert_in_grad[None],
        expert_out_grad[None],
    )


def solution(mesh):
    split = P("batch", "expert", None)
    one = P("expert", None, None)
    both = P("expert", "batch", None)
    in_specs = (split, split) + (P(),) * 12 + (one, one, split)
    out_specs = (split, split, P(), P("expert", None)) + (P(),) * 7
    out_specs += (P("expert", None), P(), P(), both, both)
    return jax.shard_map(
        per_device, mesh=mesh, in_specs=in_specs, out_specs=out_specs, check_vma=False
    )
```

```python
import functools

import jax
import jax.numpy as jnp
from jax import lax
from jax.experimental import pallas as pl
from jax.experimental.pallas import tpu as pltpu
from jax.sharding import PartitionSpec as P

F32, BF16 = jnp.float32, jnp.bfloat16
SEGS = 8
LANES = 128
LOG2E = 1.4426950408889634
LN2 = 0.6931471805599453
VMEM_LIMIT = 56 * 1024 * 1024
MESH = pl.DeviceIdType.MESH


def params(**kw):
    return pltpu.CompilerParams(vmem_limit_bytes=VMEM_LIMIT, **kw)


def softplus(v):
    return jnp.maximum(v, 0.0) + jnp.log1p(jnp.exp(-jnp.abs(v)))


def contract(left, right, left_dim, right_dim):
    return lax.dot_general(
        left, right, (((left_dim,), (right_dim,)), ((), ())), preferred_element_type=F32
    )


def over_sublanes(row):
    return jnp.broadcast_to(row, (SEGS, LANES))


def over_lanes(column):
    return jnp.broadcast_to(column, (SEGS, LANES))


def tile_rows(j):
    return pl.ds(pl.multiple_of(j * SEGS, SEGS), SEGS)


def run_of_segments(a, b, forward):
    at = lax.broadcasted_iota(jnp.int32, (SEGS, LANES), 0)
    for step in (1, 2, 4):
        if forward:
            inside, turn = at >= step, step
        else:
            inside, turn = at < SEGS - step, SEGS - step
        before_a = jnp.where(inside, pltpu.roll(a, turn, 0), 1.0)
        before_b = jnp.where(inside, pltpu.roll(b, turn, 0), 0.0)
        a, b = a * before_a, a * before_b + b
    return a, b


class Carries:
    groups = 2

    def __init__(self, states, blocks, forward, own, lengths, got, got_lengths, sems):
        self.states, self.blocks, self.forward = states, blocks, forward
        self.own, self.lengths, self.got, self.got_lengths = own, lengths, got, got_lengths
        self.sems = sems
        self.count, self.me = lax.axis_size("expert"), lax.axis_index("expert")
        self.per = blocks // self.groups

    @staticmethod
    def scratch(states, blocks, count):
        per = blocks // Carries.groups
        assert blocks % Carries.groups == 0 and per <= SEGS
        return [
            pltpu.VMEM((blocks, states, LANES), BF16),
            pltpu.VMEM((Carries.groups, SEGS, LANES), F32),
            pltpu.VMEM((count, blocks, states, LANES), BF16),
            pltpu.VMEM((count, Carries.groups, SEGS, LANES), F32),
            pltpu.SemaphoreType.DMA((2, 2, Carries.groups, count)),
        ]

    def other(self, k):
        return (lax.axis_index("batch"), lax.rem(self.me + k, self.count))

    def copies(self, group):
        blocks = pl.ds(group * self.per, self.per)
        found = []
        for k in range(1, self.count):
            pairs = (
                (self.own.at[blocks], self.got.at[k - 1, blocks]),
                (self.lengths.at[group], self.got_lengths.at[k - 1, group]),
            )
            for i, (src, dst) in enumerate(pairs):
                found.append(
                    pltpu.make_async_remote_copy(
                        src_ref=src,
                        dst_ref=dst,
                        send_sem=self.sems.at[0, i, group, k - 1],
                        recv_sem=self.sems.at[1, i, group, k - 1],
                        device_id=self.other(k),
                        device_id_type=MESH,
                    )
                )
        return found

    def put(self, block, ends, sums, rates, run_a, run_b):
        edge = SEGS - 1 if self.forward else 0
        rows = []
        for n in range(self.states):
            a, b = run_of_segments(jnp.exp2(rates[n] * sums), ends[n], self.forward)
            run_a[block, n] = a
            run_b[block, n] = b
            rows.append(b[edge : edge + 1])
        end = jnp.concatenate(rows, axis=0).astype(BF16)
        total = jnp.sum(sums, axis=0, keepdims=True)
        last = self.count - 1
        self.own[block] = end
        self.got[last, block] = end
        for group in range(self.groups):

            @pl.when(block // self.per == group)
            def _():
                row = pl.ds(lax.rem(block, self.per), 1)
                self.lengths[group, row, :] = total
                self.got_lengths[last, group, row, :] = total

            @pl.when(block == (group + 1) * self.per - 1)
            def _():
                for copy in self.copies(group):
                    copy.start()

    def await_group(self, block):
        for group in range(self.groups):

            @pl.when(block == group * self.per)
            def _():
                for copy in self.copies(group):
                    copy.wait()

    def starts(self, block, rate_ref, run_a, run_b):
        group, row = block // self.per, pl.ds(lax.rem(block, self.per), 1)
        rate = rate_ref[...]
        entering = jnp.zeros((self.states, LANES), F32)
        order = range(self.count) if self.forward else range(self.count - 1, -1, -1)
        for place in order:
            slot = lax.rem(self.me - place - 1 + 2 * self.count, self.count)
            length = self.got_lengths[slot, group, row, :]
            joined = jnp.exp2(rate * length) * entering + self.got[slot, block].astype(F32)
            ahead = (place < self.me) if self.forward else (place > self.me)
            entering = jnp.where(ahead, joined, entering)
        found = []
        for n in range(self.states):
            first = entering[n : n + 1]
            after = run_a[block, n] * over_sublanes(first) + run_b[block, n]
            found.append(shifted_in(after, first, self.forward))
        return found


def together(*parts):
    return sum(p.astype(F32) for p in parts)


class Total:
    def __init__(self, local, axis, shared, chunk=None):
        self.local, self.axis, self.shared = local, axis, shared
        self.pairs, self.chunk = local.shape[0], chunk or local.shape[2:]
        part = list(self.chunk)
        part[axis] //= lax.axis_size("batch")
        self.part = tuple(part)
        self.whole = local.shape if shared else self.chunk
        self.taken_up = chunk is not None

    def kind(self):
        return self.axis, self.shared, self.part, self.taken_up

    def out_shape(self):
        return jax.ShapeDtypeStruct(self.whole, F32)

    def spread_shape(self):
        return jax.ShapeDtypeStruct((self.pairs, *self.part), BF16)

    def resumed(self, spread):
        return Total(spread, self.axis, self.shared, self.chunk)

    def spread_scratch(self):
        ways, pairs = lax.axis_size("batch"), self.pairs
        return [
            pltpu.VMEM((2, pairs, *self.chunk), BF16),
            pltpu.VMEM((pairs, *self.chunk), BF16),
            pltpu.VMEM((ways - 1, pairs, *self.part), BF16),
            pltpu.SemaphoreType.DMA((2, 2, max(ways, pairs))),
        ]

    def gather_scratch(self):
        ways, pairs = lax.axis_size("batch"), self.pairs
        return [
            pltpu.VMEM((pairs - 1, *self.part), BF16),
            pltpu.VMEM(self.part, BF16),
            pltpu.VMEM(self.whole, BF16),
            pltpu.SemaphoreType.DMA((2, 6, max(ways, pairs))),
        ]

    def scratch(self):
        if self.taken_up:
            return self.gather_scratch()
        own = [pltpu.VMEM((self.pairs, *self.part), BF16)]
        return self.spread_scratch() + own + self.gather_scratch()


def part_of(ref, lead, axis, size, index):
    start = index * size
    if axis == len(ref.shape) - lead - 1:
        start = pl.multiple_of(start, LANES)
    where = [slice(None)] * len(ref.shape)
    where[lead + axis] = pl.ds(start, size)
    return ref.at[tuple(where)]


class Summing:
    def __init__(self, kind, local, out, scratch):
        self.axis, self.shared, part, self.taken_up = kind
        self.local, self.out = local, out
        if self.taken_up:
            self.by_batch = local
        else:
            self.both, self.by_chip, self.from_batch, self.spread_sems = scratch[:4]
            self.by_batch = out if len(scratch) == 4 else scratch[4]
        if len(scratch) >= 4 and (self.taken_up or len(scratch) > 4):
            self.from_pairs, self.mine, self.every, self.sems = scratch[-4:]
        self.ways, self.pairs = lax.axis_size("batch"), lax.axis_size("expert") // 2
        self.group, place = lax.axis_index("batch"), lax.axis_index("expert")
        self.pair, self.core = place // 2, lax.rem(place, 2)
        self.sibling = (self.group, self.pair * 2 + 1 - self.core)
        self.in_batch = [
            (lax.rem(self.group + k, self.ways), place) for k in range(1, self.ways)
        ]
        self.in_pairs = [
            (self.group, lax.rem(self.pair + k, self.pairs) * 2 + self.core)
            for k in range(1, self.pairs)
        ]
        self.size = part[self.axis]

    def share(self, ref, lead, index):
        return part_of(ref, lead, self.axis, self.size, index)

    def remote(self, src, dst, stage, k, device):
        sems = self.spread_sems if stage < 2 else self.sems
        return pltpu.make_async_remote_copy(
            src_ref=src,
            dst_ref=dst,
            send_sem=sems.at[0, stage, k],
            recv_sem=sems.at[1, stage, k],
            device_id=device,
            device_id_type=MESH,
        )

    def copies(self, stage):
        batch, pairs = range(1, self.ways), range(1, self.pairs)
        if stage == 0:
            own = pltpu.make_async_copy(
                self.local.at[:, self.core], self.both.at[0], self.spread_sems.at[0, 0, 1]
            )
            away = self.local.at[:, 1 - self.core]
            return [own, self.remote(away, self.both.at[1], 0, 0, self.sibling)]
        if stage == 1:
            to = [lax.rem(self.group + k, self.ways) for k in batch]
            return [
                self.remote(
                    self.share(self.by_chip, 1, to[k - 1]),
                    self.from_batch.at[k - 1],
                    1,
                    k,
                    self.in_batch[k - 1],
                )
                for k in batch
            ]
        if stage == 2:
            to = [lax.rem(self.pair + k, self.pairs) for k in pairs]
            return [
                self.remote(
                    self.by_batch.at[to[k - 1]],
                    self.from_pairs.at[k - 1],
                    2,
                    k,
                    self.in_pairs[k - 1],
                )
                for k in pairs
            ]
        if stage == 3:
            own = self.own_share()
            return [self.remote(self.mine, own, 3, k, self.in_batch[k - 1]) for k in batch]
        if stage == 4:
            own = self.every.at[self.pair, self.core]
            return [self.remote(own, own, 4, k, self.in_pairs[k - 1]) for k in pairs]
        own = self.every.at[:, self.core]
        return [self.remote(own, own, 5, 0, self.sibling)]

    def own_share(self):
        target = self.every.at[self.pair, self.core] if self.shared else self.every
        return self.share(target, 0, self.group)

    def start(self, stage):
        for copy in self.copies(stage):
            copy.start()

    def wait(self, stage):
        for copy in self.copies(stage):
            copy.wait()

    def add(self, stage):
        if stage == 0:

            def over_cores(z, carry):
                self.by_chip[z] = together(self.both[0, z], self.both[1, z]).astype(BF16)
                return carry

            lax.fori_loop(0, self.pairs, over_cores, 0)
        elif stage == 1:
            own = self.share(self.by_chip, 1, self.group)

            def over_batch(z, carry):
                others = (self.from_batch[k, z] for k in range(self.ways - 1))
                self.by_batch[z] = together(own[z], *others).astype(BF16)
                return carry

            lax.fori_loop(0, self.pairs, over_batch, 0)
        elif stage == 2:
            others = (self.from_pairs[k] for k in range(self.pairs - 1))
            total = together(self.by_batch[self.pair], *others).astype(BF16)
            self.mine[...] = total
            self.own_share()[...] = total

    def stages(self):
        return 6 if self.shared else 4

    def advance(self, stage):
        if stage >= self.stages():
            return
        self.wait(stage)
        self.add(stage)
        if stage + 1 < self.stages():
            self.start(stage + 1)
        else:
            self.out[...] = self.every[...].astype(F32)


    def begin(self):
        self.start(2 if self.taken_up else 0)

    def first(self):
        return 2 if self.taken_up else 0


def summings(kinds, ins, outs, scratch):
    found, at = [], 0
    for (kind, many), local, out in zip(kinds, ins, outs):
        found.append(Summing(kind, local, out, scratch[at : at + many]))
        at += many
    return found


def totals_kernel(kinds, *refs):
    count = len(kinds)
    found = summings(kinds, refs[:count], refs[count : 2 * count], refs[2 * count :])
    greet_others()
    for item in found:
        item.begin()
    for stage in range(6):
        for item in found:
            if stage >= item.first():
                item.advance(stage)


def totals(items, collective_id):
    scratch = [item.scratch() for item in items]
    kinds = tuple((item.kind(), len(refs)) for item, refs in zip(items, scratch))
    vmem, hbm = (pl.BlockSpec(memory_space=m) for m in (pltpu.VMEM, pl.ANY))
    return pl.pallas_call(
        functools.partial(totals_kernel, kinds),
        out_shape=[item.out_shape() for item in items],
        in_specs=[vmem if item.taken_up else hbm for item in items],
        out_specs=[vmem] * len(items),
        scratch_shapes=[ref for refs in scratch for ref in refs],
        compiler_params=params(collective_id=collective_id, has_side_effects=True),
        name="totals",
    )(*(item.local for item in items))


class Side:
    def __init__(self, src, dst, sems):
        self.src, self.dst, self.sems = src, dst, sems
        self.count, self.me = lax.axis_size("expert"), lax.axis_index("expert")

    @staticmethod
    def scratch(count):
        return pltpu.SemaphoreType.DMA((2, count))

    def copy(self, k):
        to = lax.rem(self.me + k, self.count)
        return pltpu.make_async_remote_copy(
            src_ref=self.src.at[to],
            dst_ref=self.dst.at[self.me],
            send_sem=self.sems.at[0, k],
            recv_sem=self.sems.at[1, k],
            device_id=(lax.axis_index("batch"), to),
            device_id_type=MESH,
        )

    def own(self):
        return pltpu.make_async_copy(
            self.src.at[self.me], self.dst.at[self.me], self.sems.at[0, 0]
        )

    def start(self, part=0, parts=((0, 1),)):
        if part == 0:
            self.own().start()
        least, most = (1 + round(share * (self.count - 1)) for share in parts[part])
        for k in range(least, most):
            self.copy(k).start()

    def wait(self):
        self.own().wait()
        for k in range(1, self.count):
            self.copy(k).wait()


def greet_others():
    barrier = pltpu.get_barrier_semaphore()
    group, place = lax.axis_index("batch"), lax.axis_index("expert")
    ways, count = lax.axis_size("batch"), lax.axis_size("expert")
    others = [(group, lax.rem(place + k, count)) for k in range(1, count)]
    others += [(lax.rem(group + k, ways), place) for k in range(1, ways)]
    for device in others:
        pl.semaphore_signal(barrier, inc=1, device_id=device, device_id_type=MESH)
    pl.semaphore_wait(barrier, len(others))


def greet_experts():
    barrier = pltpu.get_barrier_semaphore()
    count, me = lax.axis_size("expert"), lax.axis_index("expert")
    for k in range(1, count):
        device = (lax.axis_index("batch"), lax.rem(me + k, count))
        pl.semaphore_signal(barrier, inc=1, device_id=device, device_id_type=MESH)
    pl.semaphore_wait(barrier, count - 1)


def gelu_parts(v):
    size = jnp.abs(v) * 0.7071067811865476
    t = 1.0 / (1.0 + 0.3275911 * size)
    bell = jnp.exp2(v * v * (-0.5 * LOG2E))
    poly = t * (
        0.127414796
        + t * (-0.142248368 + t * (0.7107068705 + t * (-0.7265760135 + t * 0.5307027145)))
    )
    tail = poly * bell
    phi = jnp.where(v >= 0.0, 1.0 - tail, tail)
    return v * phi, phi + v * (bell * 0.3989422804014327)


FF_TILE = 512


def experts_kernel(slots, tile, *refs):
    normed_ref, row_ref, col_ref, router_ref, upstream_ref, in_hbm, out_hbm = refs[:7]
    grad_ref, result_ref, in_grad_hbm, out_grad_hbm, router_grad_ref = refs[7:12]
    w_in, w_out, sent, got, home, slot_grad, active, hid_grad, row_grad = refs[12:21]
    in_grad, out_grad, there_sems, back_sems, load_sems, store_sems = refs[21:]
    back, rows = sent, row_grad
    count, me = lax.axis_size("expert"), lax.axis_index("expert")
    width, hidden = w_in.shape
    total = count * slots
    tiles = hidden // tile
    loads = [
        pltpu.make_async_copy(in_hbm.at[0], w_in, load_sems.at[0]),
        pltpu.make_async_copy(out_hbm.at[0], w_out, load_sems.at[1]),
    ]
    for load in loads:
        load.start()
    greet_experts()
    there = Side(sent, got, there_sems)
    returning = Side(back, home, back_sems)
    tokens = normed_ref.shape[0]
    slot_id = lax.broadcasted_iota(jnp.int32, (slots, tokens), 0)

    def dispatch(k, carry):
        to = lax.rem(me + k, count)
        picked = (slot_id + to * slots == row_ref[...]).astype(F32).astype(BF16)
        chunk = jnp.dot(picked, normed_ref[...], preferred_element_type=F32).astype(BF16)
        sent[to] = chunk

        @pl.when(k < count)
        def _():
            there.copy(k).start()

        @pl.when(k == count)
        def _():
            got[me] = chunk

        return carry

    lax.fori_loop(1, count + 1, dispatch, 0)
    for k in range(1, count):
        there.copy(k).wait()

    x = got[...].reshape(total, width)
    logits = lax.dot_general(
        x, router_ref[...], (((1,), (1,)), ((), ())), preferred_element_type=F32
    )
    lane = lax.broadcasted_iota(jnp.int32, logits.shape, 1)
    logits = jnp.where(lane < count, logits, -1e30)
    scores = jnp.exp(logits - jnp.max(logits, axis=1, keepdims=True))
    probs = scores / jnp.sum(scores, axis=1, keepdims=True)
    mine = (lane == me).astype(F32)
    gate = jnp.sum(probs * mine, axis=1, keepdims=True)
    slot_grad[...] = (gate * upstream_ref[...].reshape(total, width).astype(F32)).astype(BF16)
    row_grad[...] = jnp.zeros(row_grad.shape, F32)
    for load in loads:
        load.wait()

    def inward(t, picked):
        at = pl.ds(pl.multiple_of(t * tile, tile), tile)
        pre = jnp.dot(
            got[...].reshape(total, width), w_in[:, at], preferred_element_type=F32
        )
        act_grad = lax.dot_general(
            slot_grad[...], w_out[at, :], (((1,), (1,)), ((), ())), preferred_element_type=F32
        )
        value, slope = gelu_parts(pre)
        active[:, at] = value.astype(BF16)
        low = (act_grad * slope).astype(BF16)
        hid_grad[:, at] = low
        row_grad[...] += lax.dot_general(
            low, w_in[:, at], (((1,), (1,)), ((), ())), preferred_element_type=F32
        )
        return picked + jnp.sum(value * act_grad, axis=1, keepdims=True)

    picked = lax.fori_loop(0, tiles, inward, jnp.zeros((total, 1), F32))
    logit_grad = (picked * (mine - probs)).astype(BF16)
    whole = row_grad[...] + jnp.dot(logit_grad, router_ref[...], preferred_element_type=F32)
    back[...] = whole.astype(BF16).reshape(count, slots, width)
    home[me] = back[me]
    for k in range(1, count):
        returning.copy(k).start()

    router_grad_ref[...] = lax.dot_general(
        logit_grad,
        got[...].reshape(total, width),
        (((0,), (0,)), ((), ())),
        preferred_element_type=F32,
    )
    rows[...] = jnp.zeros(rows.shape, F32)

    def stores(t):
        at = pl.ds(pl.multiple_of(t * tile, tile), tile)
        return (
            pltpu.make_async_copy(in_grad.at[:, at], in_grad_hbm.at[:, at], store_sems.at[0, t]),
            pltpu.make_async_copy(out_grad.at[at], out_grad_hbm.at[at], store_sems.at[1, t]),
        )

    def outward(t, carry):
        at = pl.ds(pl.multiple_of(t * tile, tile), tile)
        over_rows = (((0,), (0,)), ((), ()))
        in_grad[:, at] = lax.dot_general(
            got[...].reshape(total, width), hid_grad[:, at], over_rows, preferred_element_type=F32
        ).astype(BF16)
        out_grad[at, :] = lax.dot_general(
            active[:, at], slot_grad[...], over_rows, preferred_element_type=F32
        ).astype(BF16)
        for store in stores(t):
            store.start()
        rows[...] += jnp.dot(active[:, at], w_out[at, :], preferred_element_type=F32)
        return carry

    lax.fori_loop(0, tiles, outward, 0)
    result_ref[...] = (gate * rows[...]).astype(BF16).reshape(count, slots, width)
    for k in range(1, count):
        returning.copy(k).wait()
    slot_id = lax.broadcasted_iota(jnp.int32, (tokens, total), 1)
    chosen = (slot_id == col_ref[...]).astype(F32).astype(BF16)
    grad_ref[...] = jnp.dot(
        chosen, home[...].reshape(total, width), preferred_element_type=F32
    )
    for t in range(tiles):
        for store in stores(t):
            store.wait()


def run_experts(normed, target, router, upstream, expert_in, expert_out, slots, collective_id):
    tokens, width = normed.shape
    count = lax.axis_size("expert")
    hidden = expert_in.shape[2]
    tile = FF_TILE if hidden % FF_TILE == 0 else hidden
    total = count * slots
    exchanged = (count, slots, width)
    padded = jnp.pad(router, ((0, LANES - router.shape[0]), (0, 0)))
    vmem = pl.BlockSpec(memory_space=pltpu.VMEM)
    hbm = pl.BlockSpec(memory_space=pl.ANY)
    grad, result, in_grad, out_grad, router_grad = pl.pallas_call(
        functools.partial(experts_kernel, slots, tile),
        out_shape=[
            jax.ShapeDtypeStruct((tokens, width), F32),
            jax.ShapeDtypeStruct(exchanged, BF16),
            jax.ShapeDtypeStruct((width, hidden), BF16),
            jax.ShapeDtypeStruct((hidden, width), BF16),
            jax.ShapeDtypeStruct((LANES, width), F32),
        ],
        in_specs=[vmem] * 5 + [hbm] * 2,
        out_specs=[vmem, vmem, hbm, hbm, vmem],
        scratch_shapes=[
            pltpu.VMEM((width, hidden), BF16),
            pltpu.VMEM((hidden, width), BF16),
            pltpu.VMEM(exchanged, BF16),
            pltpu.VMEM(exchanged, BF16),
            pltpu.VMEM(exchanged, BF16),
            pltpu.VMEM((total, width), BF16),
            pltpu.VMEM((total, hidden), BF16),
            pltpu.VMEM((total, hidden), BF16),
            pltpu.VMEM((total, width), F32),
            pltpu.VMEM((width, hidden), BF16),
            pltpu.VMEM((hidden, width), BF16),
            Side.scratch(count),
            Side.scratch(count),
            pltpu.SemaphoreType.DMA((2,)),
            pltpu.SemaphoreType.DMA((2, hidden // tile)),
        ],
        compiler_params=params(collective_id=collective_id, has_side_effects=True),
        name="experts",
    )(normed, target[None], target[:, None], padded, upstream, expert_in, expert_out)
    return grad, result, in_grad, out_grad, router_grad[: router.shape[0]]


def forward_kernel(states, steps, *refs):
    delta_ref, in_ref, bc_ref, rate_ref, skip_ref, side_in, ssm_ref, held_ref, side_out = refs[:9]
    in_s, bb, cb, run_a, run_b, side_sems = refs[9:15]
    phase, block = pl.program_id(0), pl.program_id(1)
    blocks = refs[17].shape[1]
    carries = Carries(states, blocks, True, *refs[15:])
    side = Side(side_in, side_out, side_sems)
    rates = [over_sublanes(rate_ref[n : n + 1, :]) for n in range(states)]

    parts = ((0, 2 / 7), (2 / 7, 3 / 7), (3 / 7, 1))
    for part, (at_phase, at_block) in enumerate(((0, 0), (0, blocks // 2), (1, 1))):

        @pl.when((phase == at_phase) & (block == at_block))
        def _():
            if part == 0:
                greet_experts()
            side.start(part, parts)

    def ends(first):
        in_s[...] = delta_ref[...] * in_ref[...].astype(F32)
        sums = jnp.sum(delta_ref[...].reshape(steps, SEGS, LANES), axis=0)

        def one(j, held):
            d, u = delta_ref[tile_rows(j), :], in_s[tile_rows(j), :]
            tile = bc_ref[tile_rows(j), :] if first else None
            new = []
            for n in range(states):
                if first:
                    b = over_lanes(tile[:, n : n + 1])
                    bb[j, n] = b
                    cb[j, n] = over_lanes(tile[:, states + n : states + n + 1])
                else:
                    b = bb[j, n]
                new.append(jnp.exp2(d * rates[n]) * held[n] + u * b)
            return tuple(new)

        zero = jnp.zeros((SEGS, LANES), F32)
        held = lax.fori_loop(0, steps, one, (zero,) * states, unroll=4)
        carries.put(block, held, sums, rates, run_a, run_b)

    @pl.when((phase == 0) & (block == 0))
    def _():
        ends(True)

    @pl.when((phase == 0) & (block > 0))
    def _():
        ends(False)

    @pl.when(phase == 1)
    def _():
        carries.await_group(block)
        start = carries.starts(block, rate_ref, run_a, run_b)
        mixed = in_ref[...].astype(F32)
        in_s[...] = delta_ref[...] * mixed
        ssm_ref[...] = skip_ref[...] * mixed
        for n in range(states):
            held_ref[0, 0, n] = start[n]

        def one(j, held):
            rows = tile_rows(j)
            d, u = delta_ref[rows, :], in_s[rows, :]
            total = ssm_ref[rows, :]
            new = []
            for n in range(states):
                h = jnp.exp2(d * rates[n]) * held[n] + u * bb[j, n]
                held_ref[0, j + 1, n] = h
                total = total + cb[j, n] * h
                new.append(h)
            ssm_ref[rows, :] = total
            return tuple(new)

        lax.fori_loop(0, steps, one, tuple(start), unroll=4)

    @pl.when((phase == 1) & (block == blocks - 1))
    def _():
        side.wait()


def mixer_states(delta, mixed, bc, rate2, skip, beside, collective_id):
    count, width = delta.shape
    states, steps, blocks = rate2.shape[0], count // SEGS, width // LANES
    block = pl.BlockSpec((count, LANES), lambda p, c: (0, c))
    spread = pltpu.VMEM((steps, states, SEGS, LANES), F32)
    run = pltpu.VMEM((blocks, states, SEGS, LANES), F32)
    return pl.pallas_call(
        functools.partial(forward_kernel, states, steps),
        grid=(2, blocks),
        out_shape=[
            jax.ShapeDtypeStruct((count, width), F32),
            jax.ShapeDtypeStruct((blocks, steps + 1, states, SEGS, LANES), F32),
            jax.ShapeDtypeStruct(beside.shape, beside.dtype),
        ],
        in_specs=[
            block,
            block,
            pl.BlockSpec(bc.shape, lambda p, c: (0, 0)),
            pl.BlockSpec((states, LANES), lambda p, c: (0, c)),
            pl.BlockSpec((1, LANES), lambda p, c: (0, c)),
            pl.BlockSpec(memory_space=pl.ANY),
        ],
        out_specs=[
            pl.BlockSpec((count, LANES), lambda p, c: (0, p * c)),
            pl.BlockSpec((1, steps + 1, states, SEGS, LANES), lambda p, c: (p * c, 0, 0, 0, 0)),
            pl.BlockSpec(memory_space=pl.ANY),
        ],
        scratch_shapes=[pltpu.VMEM((count, LANES), F32), spread, spread, run, run]
        + [Side.scratch(lax.axis_size("expert"))]
        + Carries.scratch(states, blocks, lax.axis_size("expert")),
        compiler_params=params(collective_id=collective_id, has_side_effects=True),
        name="mixer_states",
    )(delta, mixed, bc, rate2, skip, beside)


def backward_kernel(states, steps, kinds, *refs):
    many = len(kinds)
    sum_in, refs = refs[:many], refs[many:]
    pre_ref, delta_ref, in_ref, g_ref, bc_ref, rate_ref, skip_ref, held_ref, side_in = refs[:9]
    sum_out, refs = refs[9 : 9 + many], refs[9 + many :]
    pre_grad_ref, mixed_grad_ref, rate_grad_ref, skip_grad_ref, bias_grad_ref = refs[:5]
    bc_grad_ref, side_out = refs[5:7]
    in_s, rate_sum, in_sum, bb, cb, b_acc, c_acc, run_a, run_b, side_sems = refs[7:17]
    carry_refs, sum_refs = refs[17:22], refs[22:]
    phase, block = pl.program_id(0), pl.program_id(1)
    blocks = carry_refs[2].shape[1]
    carries = Carries(states, blocks, False, *carry_refs)
    sums = summings(kinds, sum_in, sum_out, sum_refs)
    side = Side(side_in, side_out, side_sems)
    rates = [over_sublanes(rate_ref[n : n + 1, :]) for n in range(states)]
    zero = jnp.zeros((SEGS, LANES), F32)

    @pl.when((phase == 0) & (block == 0))
    def _():
        greet_others()
        for item in sums:
            item.start(0)

    @pl.when((phase == 1) & (block == 1))
    def _():
        side.start()

    @pl.when((phase == 0) & (block == blocks - 3))
    def _():
        for item in sums:
            item.advance(0)

    def ends(first):
        sums = jnp.sum(delta_ref[...].reshape(steps, SEGS, LANES), axis=0)

        def one(i, held):
            j = steps - 1 - i
            d, g = delta_ref[tile_rows(j), :], g_ref[tile_rows(j), :]
            tile = bc_ref[tile_rows(j), :] if first else None
            new = []
            for n in range(states):
                if first:
                    c = over_lanes(tile[:, states + n : states + n + 1])
                    bb[j, n] = over_lanes(tile[:, n : n + 1])
                    cb[j, n] = c
                else:
                    c = cb[j, n]
                new.append(jnp.exp2(d * rates[n]) * (held[n] + g * c))
            return tuple(new)

        held = lax.fori_loop(0, steps, one, (zero,) * states, unroll=4)
        carries.put(block, held, sums, rates, run_a, run_b)

    @pl.when((phase == 0) & (block == 0))
    def _():
        ends(True)

    @pl.when((phase == 0) & (block > 0))
    def _():
        ends(False)

    def grads(first, last):
        start = carries.starts(block, rate_ref, run_a, run_b)
        delta, g = delta_ref[...], g_ref[...]
        mixed = in_ref[...].astype(F32)
        in_s[...] = delta * mixed
        place = lax.broadcasted_iota(jnp.int32, (SEGS, LANES), 1)

        def one(i, carry):
            edge, rate_acc = carry
            j = steps - 1 - i
            rows = tile_rows(j)
            d, u, g = delta_ref[rows, :], in_s[rows, :], g_ref[rows, :]
            by_rate = by_b = sums = zero
            new_edge, new_acc = [], []
            for n in range(states):
                b, c = bb[j, n], cb[j, n]
                q = c * g + edge[n]
                e = jnp.exp2(d * rates[n]) * q
                v = e * held_ref[0, j, n]
                by_rate = by_rate + rates[n] * v
                by_b = by_b + b * q
                to_b = q * u
                to_c = g * held_ref[0, j + 1, n]
                if not first:
                    to_b = b_acc[j, n] + to_b
                    to_c = c_acc[j, n] + to_c
                if last:
                    sums = jnp.where(place == n, jnp.sum(to_b, axis=1, keepdims=True), sums)
                    to_c = jnp.sum(to_c, axis=1, keepdims=True)
                    sums = jnp.where(place == states + n, to_c, sums)
                else:
                    b_acc[j, n] = to_b
                    c_acc[j, n] = to_c
                new_edge.append(e)
                new_acc.append(rate_acc[n] + d * v)
            rate_sum[rows, :] = by_rate
            in_sum[rows, :] = by_b
            if last:
                bc_grad_ref[rows, :] = sums
            return tuple(new_edge), tuple(new_acc)

        _, rate_acc = lax.fori_loop(
            0, steps, one, (tuple(start), (zero,) * states), unroll=2
        )
        for n in range(states):
            rate_grad_ref[n : n + 1, :] = (
                LN2 * rate_ref[n : n + 1, :] * jnp.sum(rate_acc[n], axis=0, keepdims=True)
            )
        by_b = in_sum[...]
        pre_grad = (LN2 * rate_sum[...] + mixed * by_b) * jax.nn.sigmoid(pre_ref[...])
        pre_grad_ref[...] = pre_grad.astype(BF16)
        bias_grad_ref[...] = jnp.sum(pre_grad, axis=0, keepdims=True)
        mixed_grad_ref[...] = delta * by_b + skip_ref[...] * g
        skip_grad_ref[...] = jnp.sum(g * mixed, axis=0, keepdims=True)

    @pl.when(phase == 1)
    def _():
        carries.await_group(block)

    @pl.when((phase == 1) & (block == 0))
    def _():
        grads(True, False)

    @pl.when((phase == 1) & (block > 0) & (block < blocks - 1))
    def _():
        grads(False, False)

    @pl.when((phase == 1) & (block == blocks - 1))
    def _():
        grads(False, True)
        side.wait()
        for item in sums:
            item.wait(1)
            item.add(1)


def mixer_grads(
    pre, delta, mixed, ssm_grad, bc, rate2, skip, held, beside, items, collective_id
):
    count, width = delta.shape
    states, steps, blocks = rate2.shape[0], count // SEGS, width // LANES
    block = pl.BlockSpec((count, LANES), lambda p, c: (0, c))
    late = lambda rows: pl.BlockSpec((rows, LANES), lambda p, c: (0, p * c))
    spread = pltpu.VMEM((steps, states, SEGS, LANES), F32)
    run = pltpu.VMEM((blocks, states, SEGS, LANES), F32)
    flat = pltpu.VMEM((count, LANES), F32)
    sum_scratch = [item.spread_scratch() for item in items]
    kinds = tuple((item.kind(), len(refs)) for item, refs in zip(items, sum_scratch))
    spread_specs = [
        pl.BlockSpec(item.spread_shape().shape, lambda p, c, rank=len(item.part) + 1: (0,) * rank)
        for item in items
    ]
    outs = pl.pallas_call(
        functools.partial(backward_kernel, states, steps, kinds),
        grid=(2, blocks),
        out_shape=[item.spread_shape() for item in items]
        + [
            jax.ShapeDtypeStruct((count, width), BF16),
            jax.ShapeDtypeStruct((count, width), F32),
            jax.ShapeDtypeStruct((states, width), F32),
            jax.ShapeDtypeStruct((1, width), F32),
            jax.ShapeDtypeStruct((1, width), F32),
            jax.ShapeDtypeStruct((count, LANES), F32),
            jax.ShapeDtypeStruct(beside.shape, beside.dtype),
        ],
        in_specs=[pl.BlockSpec(memory_space=pl.ANY)] * len(items)
        + [
            late(count),
            block,
            late(count),
            block,
            pl.BlockSpec(bc.shape, lambda p, c: (0, 0)),
            pl.BlockSpec((states, LANES), lambda p, c: (0, c)),
            late(1),
            pl.BlockSpec((1, steps + 1, states, SEGS, LANES), lambda p, c: (p * c, 0, 0, 0, 0)),
            pl.BlockSpec(memory_space=pl.ANY),
        ],
        out_specs=spread_specs
        + [late(count), late(count), late(states), late(1), late(1)]
        + [pl.BlockSpec((count, LANES), lambda p, c: (0, 0)), pl.BlockSpec(memory_space=pl.ANY)],
        scratch_shapes=[flat, flat, flat, spread, spread, spread, spread, run, run]
        + [Side.scratch(lax.axis_size("expert"))]
        + Carries.scratch(states, blocks, lax.axis_size("expert"))
        + [ref for refs in sum_scratch for ref in refs],
        compiler_params=params(collective_id=collective_id, has_side_effects=True),
        name="mixer_grads",
    )(*(item.local for item in items), pre, delta, mixed, ssm_grad, bc, rate2, skip, held, beside)
    *outs, bc_grad, beside = outs
    return *outs, bc_grad[:, : 2 * states], beside


PAIR = 2


def shifted_in(tile, row, forward):
    if forward:
        return jnp.concatenate([row, tile[: SEGS - 1]], axis=0)
    return jnp.concatenate([tile[1:], row], axis=0)


def conv_grads_kernel(reach, grad_ref, inner_ref, before_ref, after_ref, weight_ref, *outs):
    inner_grad_ref, weight_grad_ref, bias_grad_ref, ext_in, ext_grad = outs
    count = grad_ref.shape[0]
    rim = reach * SEGS
    grad = grad_ref[...]
    inner = inner_ref[...].astype(F32)
    for k in range(reach):
        own = inner[count - rim + k * SEGS : count - rim + (k + 1) * SEGS]
        ext_in[k * SEGS : (k + 1) * SEGS, :] = shifted_in(own, before_ref[k : k + 1, :], True)
        own = grad[k * SEGS : (k + 1) * SEGS]
        ext_grad[count + k * SEGS : count + (k + 1) * SEGS, :] = shifted_in(
            own, after_ref[k : k + 1, :], False
        )
    ext_in[rim:, :] = inner
    ext_grad[:count, :] = grad
    bias_grad_ref[...] = jnp.sum(grad, axis=0, keepdims=True)
    total = jnp.zeros_like(grad)
    for k in range(reach + 1):
        total = total + weight_ref[k : k + 1, :] * ext_grad[(reach - k) * SEGS :, :][:count]
        weight_grad_ref[k : k + 1, :] = jnp.sum(
            grad * ext_in[k * SEGS : k * SEGS + count, :], axis=0, keepdims=True
        )
    inner_grad_ref[...] = total.astype(BF16)


def conv_grads(grad, inner, before, after, weight):
    count, width = grad.shape
    reach = weight.shape[0] - 1
    wide = PAIR * LANES
    spec = lambda rows: pl.BlockSpec((rows, wide), lambda c: (0, c))
    return pl.pallas_call(
        functools.partial(conv_grads_kernel, reach),
        grid=(width // wide,),
        out_shape=[
            jax.ShapeDtypeStruct((count, width), BF16),
            jax.ShapeDtypeStruct((reach + 1, width), F32),
            jax.ShapeDtypeStruct((1, width), F32),
        ],
        in_specs=[spec(count), spec(count), spec(reach), spec(reach), spec(reach + 1)],
        out_specs=[spec(count), spec(reach + 1), spec(1)],
        scratch_shapes=[pltpu.VMEM((count + reach * SEGS, wide), F32)] * 2,
        compiler_params=params(),
        name="conv_grads",
    )(grad, inner, before.astype(F32), after, weight)


def passed_along(value, axis, steps):
    count = lax.axis_size(axis)
    leading, last = (max(0, -steps), min(count, count - steps))
    return lax.ppermute(value, axis, [(source, source + steps) for source in range(leading, last)])


def silu(v):
    return v * jax.nn.sigmoid(v)


def silu_slope(v):
    s = jax.nn.sigmoid(v)
    return s * (1.0 + v * (1.0 - s))


def by_segment(value):
    count = value.shape[0]
    return value.reshape(SEGS, count // SEGS, -1).transpose(1, 0, 2).reshape(count, -1)


def by_token(value):
    count = value.shape[0]
    return value.reshape(count // SEGS, SEGS, -1).transpose(1, 0, 2).reshape(count, -1)


def rms_back(values, gain, grad):
    r = lax.rsqrt(jnp.mean(values * values, axis=-1, keepdims=True) + 1e-05)
    u = gain * grad
    mean = jnp.mean(values * u, axis=-1, keepdims=True)
    return r * u - values * (r * r * r) * mean, jnp.sum(grad * values * r, axis=0)


def rms(values, gain):
    return values * lax.rsqrt(jnp.mean(values * values, axis=-1, keepdims=True) + 1e-05) * gain


def pack_small(pieces, width, places):
    flat = jnp.concatenate([p.reshape(-1, width) for p in pieces], axis=0).astype(BF16)
    rows = -(-flat.shape[0] // 16)
    across = width // LANES
    blocks = jnp.pad(flat, ((0, rows * 16 - flat.shape[0]), (0, 0)))
    blocks = blocks.reshape(rows, 16, across, LANES).transpose(0, 2, 1, 3)
    blocks = blocks.reshape(rows * across, 16, LANES)
    ways, experts = places
    each = -(-rows * across // (ways * experts))
    blocks = jnp.pad(blocks, ((0, each * ways * experts - rows * across), (0, 0), (0, 0)))
    return blocks.reshape(experts // 2, 2, ways * each, 16, LANES)


def unpack_small(packed, pieces, width):
    across = width // LANES
    count = sum(p.size for p in pieces) // width
    rows = -(-count // 16)
    blocks = packed.reshape(-1, 16, LANES)[: rows * across]
    flat = blocks.reshape(rows, across, 16, LANES).transpose(0, 2, 1, 3).reshape(rows * 16, width)
    outs, at = [], 0
    for p in pieces:
        step = p.size // width
        outs.append(flat[at : at + step].reshape(p.shape))
        at += step
    return outs


def per_device(
    tokens,
    routes,
    gain_one,
    in_proj,
    conv_weight,
    conv_bias,
    x_proj,
    dt_proj,
    dt_bias,
    rate_log,
    skip,
    out_proj,
    gain_two,
    router,
    expert_in,
    expert_out,
    cotangent,
):
    count, width = tokens.shape[1], tokens.shape[2]
    steps = count // SEGS
    inner_width = out_proj.shape[0]
    rank = dt_proj.shape[0]
    experts = router.shape[0]
    capacity = 5 * count // (4 * experts)
    slots = -(-capacity // 16) * 16
    reach = conv_weight.shape[0] - 1
    rate2 = -jnp.exp(rate_log) * LOG2E
    skip_row = skip[None]

    route = by_segment(routes[0]).reshape(count)
    upstream_low = by_segment(cotangent[0])
    expert_ids = lax.broadcasted_iota(jnp.int32, (experts, count), 0)
    onehot = (expert_ids == route[None]).astype(BF16)
    first = lax.broadcasted_iota(jnp.int32, (count, count), 0)
    second = lax.broadcasted_iota(jnp.int32, (count, count), 1)
    token_of = lambda p: (p % SEGS) * steps + p // SEGS
    earlier = (token_of(first) <= token_of(second)).astype(BF16)
    running = jnp.dot(onehot, earlier, preferred_element_type=F32)
    place = (jnp.sum(running * onehot.astype(F32), axis=0) - 1.0).astype(jnp.int32)
    target = jnp.where(place < capacity, route * slots + place, -1)
    slot_ids = lax.broadcasted_iota(jnp.int32, (experts * slots, count), 0)
    dispatch = (slot_ids == target[None]).astype(BF16)

    upstream_rows = jnp.dot(dispatch, upstream_low, preferred_element_type=F32).astype(BF16)
    upstream_rows = upstream_rows.reshape(experts, slots, width)

    values = by_segment(tokens[0]).astype(F32)
    normed_one = rms(values, gain_one).astype(BF16)
    both = jnp.dot(normed_one, in_proj, preferred_element_type=F32)
    inner = both[:, :inner_width].astype(BF16)
    gate_z = both[:, inner_width:]
    blocks = inner.reshape(steps, SEGS, inner_width)
    tail = blocks[steps - reach :]
    before = passed_along(tail[:, SEGS - 1], "expert", 1)
    extended = jnp.concatenate(
        [jnp.concatenate([before[:, None], tail[:, : SEGS - 1]], axis=1), blocks], axis=0
    ).astype(F32)
    conv_pre = conv_bias + sum(
        conv_weight[k] * extended[k : k + steps] for k in range(reach + 1)
    )
    conv_pre = conv_pre.reshape(count, inner_width)
    mixed = silu(conv_pre).astype(BF16)
    proj = contract(mixed, x_proj, 1, 1)
    low_rank = proj[:, :rank].astype(BF16)
    bc = proj[:, rank:]
    pre = jnp.dot(low_rank, dt_proj, preferred_element_type=F32) + dt_bias
    delta = softplus(pre)
    ssm, held, slot_upstream = mixer_states(
        delta, mixed, bc, rate2, skip_row, upstream_rows, 2
    )
    gated = (ssm * silu(gate_z)).astype(BF16)
    hidden = values + jnp.dot(gated, out_proj, preferred_element_type=F32)
    normed_two = rms(hidden, gain_two).astype(BF16)

    normed_two_grad, results, expert_in_local, expert_out_local, router_local = run_experts(
        normed_two, target, router, slot_upstream, expert_in, expert_out, slots, 4
    )

    hidden_norm, gain_two_local = rms_back(hidden, gain_two, normed_two_grad)
    hidden_grad = upstream_low.astype(F32) + hidden_norm
    branch = hidden_grad.astype(BF16)
    out_proj_local = contract(gated, branch, 0, 0)
    gated_grad = contract(branch, out_proj, 1, 1)
    ssm_grad = gated_grad * silu(gate_z)
    gate_z_grad = (gated_grad * ssm * silu_slope(gate_z)).astype(BF16)

    ways, pairs = lax.axis_size("batch"), experts // 2
    in_proj_gate_local = contract(normed_one, gate_z_grad, 0, 0)
    early = [
        Total(
            in_proj_gate_local.astype(BF16).reshape(pairs, 2, width // experts, inner_width),
            1,
            False,
        ),
        Total(
            out_proj_local.astype(BF16).reshape(
                pairs, 2, ways, inner_width // (experts * ways), width
            ),
            0,
            False,
        ),
    ]
    (
        in_proj_gate_spread,
        out_proj_spread,
        pre_grad,
        mixed_grad,
        rate_log_local,
        skip_local,
        dt_bias_local,
        bc_grad,
        returned,
    ) = mixer_grads(
        pre, delta, mixed, ssm_grad, bc, rate2, skip_row, held, results, early, 3
    )
    output = hidden + contract(dispatch, returned.reshape(-1, width), 0, 0)
    output = output.astype(BF16)
    dt_proj_local = contract(low_rank, pre_grad, 0, 0)
    low_rank_grad = contract(pre_grad, dt_proj, 1, 1)
    proj_grad = jnp.concatenate([low_rank_grad, bc_grad], axis=1).astype(BF16)
    x_proj_local = contract(proj_grad, mixed, 0, 0)
    mixed_grad = mixed_grad + jnp.dot(proj_grad, x_proj, preferred_element_type=F32)
    conv_grad = mixed_grad * silu_slope(conv_pre)
    head = conv_grad[: reach * SEGS].reshape(reach, SEGS, inner_width)
    after = passed_along(head[:, 0], "expert", -1)
    inner_grad, conv_weight_local, conv_bias_local = conv_grads(
        conv_grad, inner, before, after, conv_weight
    )
    both_grad = jnp.concatenate([inner_grad, gate_z_grad], axis=1)
    in_proj_inner_local = contract(normed_one, inner_grad, 0, 0)
    normed_one_grad = contract(both_grad, in_proj, 1, 1)
    values_grad, gain_one_local = rms_back(values, gain_one, normed_one_grad)
    tokens_grad = by_token(values_grad + hidden_grad)

    pieces = [
        x_proj_local,
        dt_proj_local,
        rate_log_local,
        conv_weight_local,
        conv_bias_local,
        dt_bias_local,
        skip_local,
        router_local,
        jnp.stack([gain_one_local, gain_two_local]),
    ]
    in_proj_gate_grad, out_proj_grad, in_proj_inner_grad, small = totals(
        [
            early[0].resumed(in_proj_gate_spread),
            early[1].resumed(out_proj_spread),
            Total(
                in_proj_inner_local.astype(BF16).reshape(pairs, 2, width // experts, inner_width),
                1,
                False,
            ),
            Total(pack_small(pieces, inner_width, (ways, experts)), 0, True),
        ],
        1,
    )
    in_proj_grad = jnp.concatenate([in_proj_inner_grad, in_proj_gate_grad], axis=1)
    out_proj_grad = out_proj_grad.reshape(-1, width)
    small = unpack_small(small, pieces, inner_width)
    expert_in_grad, expert_out_grad = (
        lax.psum_scatter(v, "batch", scatter_dimension=0, tiled=True).astype(F32)
        for v in (expert_in_local, expert_out_local)
    )
    x_proj_grad, dt_proj_grad, rate_log_grad, conv_weight_grad = small[:4]
    conv_bias_grad, dt_bias_grad, skip_grad, router_grad, gains = small[4:]
    return (
        by_token(output)[None],
        tokens_grad[None],
        gains[0],
        in_proj_grad,
        conv_weight_grad,
        conv_bias_grad[0],
        x_proj_grad,
        dt_proj_grad,
        dt_bias_grad[0],
        rate_log_grad,
        skip_grad[0],
        out_proj_grad,
        gains[1],
        router_grad,
        expert_in_grad[None],
        expert_out_grad[None],
    )


def solution(mesh):
    split = P("batch", "expert", None)
    one = P("expert", None, None)
    both = P("expert", "batch", None)
    in_specs = (split, split) + (P(),) * 12 + (one, one, split)
    out_specs = (split, split, P(), P("expert", None)) + (P(),) * 7
    out_specs += (P("expert", None), P(), P(), both, both)
    return jax.shard_map(
        per_device, mesh=mesh, in_specs=in_specs, out_specs=out_specs, check_vma=False
    )
```

```python
import functools

import jax
import jax.numpy as jnp
from jax import lax
from jax.experimental import pallas as pl
from jax.experimental.pallas import tpu as pltpu
from jax.sharding import PartitionSpec as P

F32, BF16 = jnp.float32, jnp.bfloat16
SEGS = 8
LANES = 128
LOG2E = 1.4426950408889634
LN2 = 0.6931471805599453
VMEM_LIMIT = 56 * 1024 * 1024
MESH = pl.DeviceIdType.MESH


def params(**kw):
    return pltpu.CompilerParams(vmem_limit_bytes=VMEM_LIMIT, **kw)


def softplus(v):
    return jnp.maximum(v, 0.0) + jnp.log1p(jnp.exp(-jnp.abs(v)))


def contract(left, right, left_dim, right_dim):
    return lax.dot_general(
        left, right, (((left_dim,), (right_dim,)), ((), ())), preferred_element_type=F32
    )


def over_sublanes(row):
    return jnp.broadcast_to(row, (SEGS, LANES))


def over_lanes(column):
    return jnp.broadcast_to(column, (SEGS, LANES))


def tile_rows(j):
    return pl.ds(pl.multiple_of(j * SEGS, SEGS), SEGS)


def run_of_segments(a, b, forward):
    at = lax.broadcasted_iota(jnp.int32, (SEGS, LANES), 0)
    for step in (1, 2, 4):
        if forward:
            inside, turn = at >= step, step
        else:
            inside, turn = at < SEGS - step, SEGS - step
        before_a = jnp.where(inside, pltpu.roll(a, turn, 0), 1.0)
        before_b = jnp.where(inside, pltpu.roll(b, turn, 0), 0.0)
        a, b = a * before_a, a * before_b + b
    return a, b


class Carries:
    groups = 2

    def __init__(self, states, blocks, forward, own, lengths, got, got_lengths, sems):
        self.states, self.blocks, self.forward = states, blocks, forward
        self.own, self.lengths, self.got, self.got_lengths = own, lengths, got, got_lengths
        self.sems = sems
        self.count, self.me = lax.axis_size("expert"), lax.axis_index("expert")
        self.per = blocks // self.groups

    @staticmethod
    def scratch(states, blocks, count):
        per = blocks // Carries.groups
        assert blocks % Carries.groups == 0 and per <= SEGS
        return [
            pltpu.VMEM((blocks, states, LANES), BF16),
            pltpu.VMEM((Carries.groups, SEGS, LANES), F32),
            pltpu.VMEM((count, blocks, states, LANES), BF16),
            pltpu.VMEM((count, Carries.groups, SEGS, LANES), F32),
            pltpu.SemaphoreType.DMA((2, 2, Carries.groups, count)),
        ]

    def other(self, k):
        return (lax.axis_index("batch"), lax.rem(self.me + k, self.count))

    def copies(self, group):
        blocks = pl.ds(group * self.per, self.per)
        found = []
        for k in range(1, self.count):
            pairs = (
                (self.own.at[blocks], self.got.at[k - 1, blocks]),
                (self.lengths.at[group], self.got_lengths.at[k - 1, group]),
            )
            for i, (src, dst) in enumerate(pairs):
                found.append(
                    pltpu.make_async_remote_copy(
                        src_ref=src,
                        dst_ref=dst,
                        send_sem=self.sems.at[0, i, group, k - 1],
                        recv_sem=self.sems.at[1, i, group, k - 1],
                        device_id=self.other(k),
                        device_id_type=MESH,
                    )
                )
        return found

    def put(self, block, ends, sums, rates, run_a, run_b):
        edge = SEGS - 1 if self.forward else 0
        rows = []
        for n in range(self.states):
            a, b = run_of_segments(jnp.exp2(rates[n] * sums), ends[n], self.forward)
            run_a[block, n] = a
            run_b[block, n] = b
            rows.append(b[edge : edge + 1])
        end = jnp.concatenate(rows, axis=0).astype(BF16)
        total = jnp.sum(sums, axis=0, keepdims=True)
        last = self.count - 1
        self.own[block] = end
        self.got[last, block] = end
        for group in range(self.groups):

            @pl.when(block // self.per == group)
            def _():
                row = pl.ds(lax.rem(block, self.per), 1)
                self.lengths[group, row, :] = total
                self.got_lengths[last, group, row, :] = total

            @pl.when(block == (group + 1) * self.per - 1)
            def _():
                for copy in self.copies(group):
                    copy.start()

    def await_group(self, block):
        for group in range(self.groups):

            @pl.when(block == group * self.per)
            def _():
                for copy in self.copies(group):
                    copy.wait()

    def starts(self, block, rate_ref, run_a, run_b):
        group, row = block // self.per, pl.ds(lax.rem(block, self.per), 1)
        rate = rate_ref[...]
        entering = jnp.zeros((self.states, LANES), F32)
        order = range(self.count) if self.forward else range(self.count - 1, -1, -1)
        for place in order:
            slot = lax.rem(self.me - place - 1 + 2 * self.count, self.count)
            length = self.got_lengths[slot, group, row, :]
            joined = jnp.exp2(rate * length) * entering + self.got[slot, block].astype(F32)
            ahead = (place < self.me) if self.forward else (place > self.me)
            entering = jnp.where(ahead, joined, entering)
        found = []
        for n in range(self.states):
            first = entering[n : n + 1]
            after = run_a[block, n] * over_sublanes(first) + run_b[block, n]
            found.append(shifted_in(after, first, self.forward))
        return found


def together(*parts):
    return sum(p.astype(F32) for p in parts)


class Total:
    def __init__(self, local, axis, pairs_first=False, chunk=None):
        self.local, self.axis, self.pairs_first = local, axis, pairs_first
        self.ways = lax.axis_size("batch")
        self.taken_up = chunk is not None
        self.pairs, self.chunk = lax.axis_size("expert") // 2, chunk or local.shape[2:]
        part = list(self.chunk)
        part[axis] //= self.ways
        self.part = tuple(part)

    def kind(self):
        return self.axis, self.pairs_first, self.part, self.taken_up

    def spread_shape(self):
        shape = self.chunk if self.pairs_first else (self.pairs, *self.part)
        return jax.ShapeDtypeStruct(shape, BF16)

    def resumed(self, spread):
        return Total(spread, self.axis, self.pairs_first, self.chunk)

    def first_scratch(self):
        first = (self.pairs - 1, *self.chunk)
        if not self.pairs_first:
            first = (self.ways - 1, self.pairs, *self.part)
        return [
            pltpu.VMEM((2, self.pairs, *self.chunk), BF16),
            pltpu.VMEM((self.pairs, *self.chunk), BF16),
            pltpu.VMEM(first, BF16),
            pltpu.SemaphoreType.DMA((2, 2, max(self.ways, self.pairs))),
        ]

    def second_scratch(self):
        second = self.ways - 1 if self.pairs_first else self.pairs - 1
        return [
            pltpu.VMEM((second, *self.part), BF16),
            pltpu.VMEM(self.part, BF16),
            pltpu.VMEM(self.chunk, BF16),
            pltpu.SemaphoreType.DMA((2, 4, max(self.ways, self.pairs))),
        ]

    def scratch(self):
        if self.taken_up:
            return self.second_scratch()
        spread = self.spread_shape()
        return self.first_scratch() + [pltpu.VMEM(spread.shape, BF16)] + self.second_scratch()


def part_of(ref, lead, axis, size, index):
    start = index * size
    if axis == len(ref.shape) - lead - 1:
        start = pl.multiple_of(start, LANES)
    where = [slice(None)] * len(ref.shape)
    where[lead + axis] = pl.ds(start, size)
    return ref.at[tuple(where)]


class Peers:
    def __init__(self):
        self.ways, self.pairs = lax.axis_size("batch"), lax.axis_size("expert") // 2
        self.group, place = lax.axis_index("batch"), lax.axis_index("expert")
        self.pair, self.core = place // 2, lax.rem(place, 2)
        self.sibling = (self.group, self.pair * 2 + 1 - self.core)
        self.to_batch = [lax.rem(self.group + k, self.ways) for k in range(1, self.ways)]
        self.to_pairs = [lax.rem(self.pair + k, self.pairs) for k in range(1, self.pairs)]
        self.in_batch = [(to, place) for to in self.to_batch]
        self.in_pairs = [(self.group, to * 2 + self.core) for to in self.to_pairs]

    def remote(self, src, dst, sems, stage, k, device):
        return pltpu.make_async_remote_copy(
            src_ref=src,
            dst_ref=dst,
            send_sem=sems.at[0, stage, k],
            recv_sem=sems.at[1, stage, k],
            device_id=device,
            device_id_type=MESH,
        )

    def start(self, stage):
        for copy in self.copies(stage):
            copy.start()

    def wait(self, stage):
        for copy in self.copies(stage):
            copy.wait()

    def advance(self, stage):
        self.wait(stage)
        self.add(stage)
        if stage < self.last:
            self.start(stage + 1)


class Summing(Peers):
    last = 3

    def __init__(self, kind, local, out, scratch):
        super().__init__()
        self.axis, self.pairs_first, part, self.taken_up = kind
        self.local, self.out, self.size = local, out, part[self.axis]
        if self.taken_up:
            self.spread = local
            self.from_second, self.mine, self.every, self.late_sems = scratch
        else:
            self.both, self.by_chip, self.from_first, self.sems = scratch[:4]
            self.spread = out
            if len(scratch) > 4:
                self.spread, self.from_second, self.mine, self.every, self.late_sems = scratch[4:]

    def share(self, ref, lead, index):
        return part_of(ref, lead, self.axis, self.size, index)

    def copies(self, stage):
        if stage == 0:
            own = pltpu.make_async_copy(
                self.local.at[:, self.core], self.both.at[0], self.sems.at[0, 0, 1]
            )
            away = self.local.at[:, 1 - self.core]
            return [own, self.remote(away, self.both.at[1], self.sems, 0, 0, self.sibling)]
        if stage == 3:
            own, devices = self.share(self.every, 0, self.group), self.in_batch
            pieces = [(self.mine, own) for _ in devices]
        elif (stage == 1) == self.pairs_first:
            devices = self.in_pairs
            src, dst = (self.by_chip, self.from_first) if stage == 1 else (self.spread, self.from_second)
            pieces = [(src.at[to], dst.at[k]) for k, to in enumerate(self.to_pairs)]
        else:
            devices = self.in_batch
            src, dst = (self.by_chip, self.from_first) if stage == 1 else (self.spread, self.from_second)
            lead = 1 if stage == 1 else 0
            pieces = [
                (self.share(src, lead, to), dst.at[k]) for k, to in enumerate(self.to_batch)
            ]
        sems = self.sems if stage == 1 else self.late_sems
        return [
            self.remote(src, dst, sems, stage, k, devices[k]) for k, (src, dst) in enumerate(pieces)
        ]

    def add(self, stage):
        if stage == 0:

            def over_cores(z, carry):
                self.by_chip[z] = together(self.both[0, z], self.both[1, z]).astype(BF16)
                return carry

            lax.fori_loop(0, self.pairs, over_cores, 0)
        elif stage == 1 and self.pairs_first:
            others = (self.from_first[k] for k in range(self.pairs - 1))
            self.spread[...] = together(self.by_chip[self.pair], *others).astype(BF16)
        elif stage == 1:
            own = self.share(self.by_chip, 1, self.group)

            def over_batch(z, carry):
                others = (self.from_first[k, z] for k in range(self.ways - 1))
                self.spread[z] = together(own[z], *others).astype(BF16)
                return carry

            lax.fori_loop(0, self.pairs, over_batch, 0)
        elif stage == 2:
            if self.pairs_first:
                own, count = self.share(self.spread, 0, self.group)[...], self.ways
            else:
                own, count = self.spread[self.pair], self.pairs
            others = (self.from_second[k] for k in range(count - 1))
            total = together(own, *others).astype(BF16)
            self.mine[...] = total
            self.share(self.every, 0, self.group)[...] = total
        else:
            self.out[...] = self.every[...].astype(F32)

    def begin(self):
        self.start(2 if self.taken_up else 0)


class SmallSum(Peers):
    last = 4

    def __init__(self, pack, from_core, half, from_pairs, by_group, every, sems):
        super().__init__()
        self.pack, self.from_core, self.half, self.from_pairs = pack, from_core, half, from_pairs
        self.by_group, self.every, self.sems = by_group, every, sems

    @staticmethod
    def scratch(pairs, ways, tiles):
        tile = (tiles, 16, LANES)
        shapes = ((2, pairs), (pairs,), (pairs,), (pairs - 1,), (ways,), (2, pairs))
        found = [pltpu.VMEM((*lead, *tile), BF16) for lead in shapes]
        return found + [pltpu.SemaphoreType.DMA((2, 5, max(pairs, ways)))]

    def copies(self, stage):
        if stage == 0:
            pieces = [(self.pack.at[1 - self.core], self.from_core, self.sibling)]
        elif stage == 1:
            pieces = [
                (self.half.at[to], self.from_pairs.at[k], self.in_pairs[k])
                for k, to in enumerate(self.to_pairs)
            ]
        elif stage == 2:
            own = self.by_group.at[self.group]
            pieces = [(own, own, device) for device in self.in_batch]
        elif stage == 3:
            own = self.every.at[self.core, self.pair]
            pieces = [(own, own, device) for device in self.in_pairs]
        else:
            own = self.every.at[self.core]
            pieces = [(own, own, self.sibling)]
        return [
            self.remote(src, dst, self.sems, stage, k, device)
            for k, (src, dst, device) in enumerate(pieces)
        ]

    def add(self, stage):
        if stage == 0:
            self.half[...] = together(self.pack[self.core], self.from_core[...]).astype(BF16)
        elif stage == 1:
            others = (self.from_pairs[k] for k in range(self.pairs - 1))
            self.by_group[self.group] = together(self.half[self.pair], *others).astype(BF16)
        elif stage == 2:
            total = together(*(self.by_group[k] for k in range(self.ways)))
            self.every[self.core, self.pair] = total.astype(BF16)


def summings(kinds, ins, outs, scratch):
    found, at = [], 0
    for (kind, many), local, out in zip(kinds, ins, outs):
        found.append(Summing(kind, local, out, scratch[at : at + many]))
        at += many
    return found


class Side:
    def __init__(self, src, dst, sems):
        self.src, self.dst, self.sems = src, dst, sems
        self.count, self.me = lax.axis_size("expert"), lax.axis_index("expert")

    @staticmethod
    def scratch(count):
        return pltpu.SemaphoreType.DMA((2, count))

    def copy(self, k):
        to = lax.rem(self.me + k, self.count)
        return pltpu.make_async_remote_copy(
            src_ref=self.src.at[to],
            dst_ref=self.dst.at[self.me],
            send_sem=self.sems.at[0, k],
            recv_sem=self.sems.at[1, k],
            device_id=(lax.axis_index("batch"), to),
            device_id_type=MESH,
        )

    def own(self):
        return pltpu.make_async_copy(
            self.src.at[self.me], self.dst.at[self.me], self.sems.at[0, 0]
        )

    def start(self, part=0, parts=((0, 1),)):
        if part == 0:
            self.own().start()
        least, most = (1 + round(share * (self.count - 1)) for share in parts[part])
        for k in range(least, most):
            self.copy(k).start()

    def wait(self):
        self.own().wait()
        for k in range(1, self.count):
            self.copy(k).wait()


def greet_others():
    barrier = pltpu.get_barrier_semaphore()
    group, place = lax.axis_index("batch"), lax.axis_index("expert")
    ways, count = lax.axis_size("batch"), lax.axis_size("expert")
    others = [(group, lax.rem(place + k, count)) for k in range(1, count)]
    others += [(lax.rem(group + k, ways), place) for k in range(1, ways)]
    for device in others:
        pl.semaphore_signal(barrier, inc=1, device_id=device, device_id_type=MESH)
    pl.semaphore_wait(barrier, len(others))


def greet_experts():
    barrier = pltpu.get_barrier_semaphore()
    count, me = lax.axis_size("expert"), lax.axis_index("expert")
    for k in range(1, count):
        device = (lax.axis_index("batch"), lax.rem(me + k, count))
        pl.semaphore_signal(barrier, inc=1, device_id=device, device_id_type=MESH)
    pl.semaphore_wait(barrier, count - 1)


def gelu_parts(v):
    size = jnp.abs(v) * 0.7071067811865476
    t = 1.0 / (1.0 + 0.3275911 * size)
    bell = jnp.exp2(v * v * (-0.5 * LOG2E))
    poly = t * (
        0.127414796
        + t * (-0.142248368 + t * (0.7107068705 + t * (-0.7265760135 + t * 0.5307027145)))
    )
    tail = poly * bell
    phi = jnp.where(v >= 0.0, 1.0 - tail, tail)
    return v * phi, phi + v * (bell * 0.3989422804014327)


FF_TILE = 512


def experts_kernel(slots, tile, *refs):
    normed_ref, row_ref, col_ref, router_ref, upstream_ref, in_hbm, out_hbm = refs[:7]
    grad_ref, result_ref, in_grad_hbm, out_grad_hbm, router_grad_ref = refs[7:12]
    w_in, w_out, sent, got, home, slot_grad, active, hid_grad, row_grad = refs[12:21]
    in_grad, out_grad, there_sems, back_sems, load_sems, store_sems = refs[21:]
    back, rows = sent, row_grad
    count, me = lax.axis_size("expert"), lax.axis_index("expert")
    width, hidden = w_in.shape
    total = count * slots
    tiles = hidden // tile
    loads = [
        pltpu.make_async_copy(in_hbm.at[0], w_in, load_sems.at[0]),
        pltpu.make_async_copy(out_hbm.at[0], w_out, load_sems.at[1]),
    ]
    for load in loads:
        load.start()
    greet_experts()
    there = Side(sent, got, there_sems)
    returning = Side(back, home, back_sems)
    tokens = normed_ref.shape[0]
    slot_id = lax.broadcasted_iota(jnp.int32, (slots, tokens), 0)

    def dispatch(k, carry):
        to = lax.rem(me + k, count)
        picked = (slot_id + to * slots == row_ref[...]).astype(F32).astype(BF16)
        chunk = jnp.dot(picked, normed_ref[...], preferred_element_type=F32).astype(BF16)
        sent[to] = chunk

        @pl.when(k < count)
        def _():
            there.copy(k).start()

        @pl.when(k == count)
        def _():
            got[me] = chunk

        return carry

    lax.fori_loop(1, count + 1, dispatch, 0)
    for k in range(1, count):
        there.copy(k).wait()

    x = got[...].reshape(total, width)
    logits = lax.dot_general(
        x, router_ref[...], (((1,), (1,)), ((), ())), preferred_element_type=F32
    )
    lane = lax.broadcasted_iota(jnp.int32, logits.shape, 1)
    logits = jnp.where(lane < count, logits, -1e30)
    scores = jnp.exp(logits - jnp.max(logits, axis=1, keepdims=True))
    probs = scores / jnp.sum(scores, axis=1, keepdims=True)
    mine = (lane == me).astype(F32)
    gate = jnp.sum(probs * mine, axis=1, keepdims=True)
    slot_grad[...] = (gate * upstream_ref[...].reshape(total, width).astype(F32)).astype(BF16)
    row_grad[...] = jnp.zeros(row_grad.shape, F32)
    for load in loads:
        load.wait()

    def inward(t, picked):
        at = pl.ds(pl.multiple_of(t * tile, tile), tile)
        pre = jnp.dot(
            got[...].reshape(total, width), w_in[:, at], preferred_element_type=F32
        )
        act_grad = lax.dot_general(
            slot_grad[...], w_out[at, :], (((1,), (1,)), ((), ())), preferred_element_type=F32
        )
        value, slope = gelu_parts(pre)
        active[:, at] = value.astype(BF16)
        low = (act_grad * slope).astype(BF16)
        hid_grad[:, at] = low
        row_grad[...] += lax.dot_general(
            low, w_in[:, at], (((1,), (1,)), ((), ())), preferred_element_type=F32
        )
        return picked + jnp.sum(value * act_grad, axis=1, keepdims=True)

    picked = lax.fori_loop(0, tiles, inward, jnp.zeros((total, 1), F32))
    logit_grad = (picked * (mine - probs)).astype(BF16)
    whole = row_grad[...] + jnp.dot(logit_grad, router_ref[...], preferred_element_type=F32)
    back[...] = whole.astype(BF16).reshape(count, slots, width)
    home[me] = back[me]
    for k in range(1, count):
        returning.copy(k).start()

    router_grad_ref[...] = lax.dot_general(
        logit_grad,
        got[...].reshape(total, width),
        (((0,), (0,)), ((), ())),
        preferred_element_type=F32,
    )
    rows[...] = jnp.zeros(rows.shape, F32)

    def stores(t):
        at = pl.ds(pl.multiple_of(t * tile, tile), tile)
        return (
            pltpu.make_async_copy(in_grad.at[:, at], in_grad_hbm.at[:, at], store_sems.at[0, t]),
            pltpu.make_async_copy(out_grad.at[at], out_grad_hbm.at[at], store_sems.at[1, t]),
        )

    def outward(t, carry):
        at = pl.ds(pl.multiple_of(t * tile, tile), tile)
        over_rows = (((0,), (0,)), ((), ()))
        in_grad[:, at] = lax.dot_general(
            got[...].reshape(total, width), hid_grad[:, at], over_rows, preferred_element_type=F32
        ).astype(BF16)
        out_grad[at, :] = lax.dot_general(
            active[:, at], slot_grad[...], over_rows, preferred_element_type=F32
        ).astype(BF16)
        for store in stores(t):
            store.start()
        rows[...] += jnp.dot(active[:, at], w_out[at, :], preferred_element_type=F32)
        return carry

    lax.fori_loop(0, tiles, outward, 0)
    result_ref[...] = (gate * rows[...]).astype(BF16).reshape(count, slots, width)
    for k in range(1, count):
        returning.copy(k).wait()
    slot_id = lax.broadcasted_iota(jnp.int32, (tokens, total), 1)
    chosen = (slot_id == col_ref[...]).astype(F32).astype(BF16)
    grad_ref[...] = jnp.dot(
        chosen, home[...].reshape(total, width), preferred_element_type=F32
    )
    for t in range(tiles):
        for store in stores(t):
            store.wait()


def run_experts(normed, target, router, upstream, expert_in, expert_out, slots, collective_id):
    tokens, width = normed.shape
    count = lax.axis_size("expert")
    hidden = expert_in.shape[2]
    tile = FF_TILE if hidden % FF_TILE == 0 else hidden
    total = count * slots
    exchanged = (count, slots, width)
    padded = jnp.pad(router, ((0, LANES - router.shape[0]), (0, 0)))
    vmem = pl.BlockSpec(memory_space=pltpu.VMEM)
    hbm = pl.BlockSpec(memory_space=pl.ANY)
    grad, result, in_grad, out_grad, router_grad = pl.pallas_call(
        functools.partial(experts_kernel, slots, tile),
        out_shape=[
            jax.ShapeDtypeStruct((tokens, width), F32),
            jax.ShapeDtypeStruct(exchanged, BF16),
            jax.ShapeDtypeStruct((width, hidden), BF16),
            jax.ShapeDtypeStruct((hidden, width), BF16),
            jax.ShapeDtypeStruct((LANES, width), F32),
        ],
        in_specs=[vmem] * 5 + [hbm] * 2,
        out_specs=[vmem, vmem, hbm, hbm, vmem],
        scratch_shapes=[
            pltpu.VMEM((width, hidden), BF16),
            pltpu.VMEM((hidden, width), BF16),
            pltpu.VMEM(exchanged, BF16),
            pltpu.VMEM(exchanged, BF16),
            pltpu.VMEM(exchanged, BF16),
            pltpu.VMEM((total, width), BF16),
            pltpu.VMEM((total, hidden), BF16),
            pltpu.VMEM((total, hidden), BF16),
            pltpu.VMEM((total, width), F32),
            pltpu.VMEM((width, hidden), BF16),
            pltpu.VMEM((hidden, width), BF16),
            Side.scratch(count),
            Side.scratch(count),
            pltpu.SemaphoreType.DMA((2,)),
            pltpu.SemaphoreType.DMA((2, hidden // tile)),
        ],
        compiler_params=params(collective_id=collective_id, has_side_effects=True),
        name="experts",
    )(normed, target[None], target[:, None], padded, upstream, expert_in, expert_out)
    return grad, result, in_grad, out_grad, router_grad[: router.shape[0]]


def forward_kernel(states, steps, rank, *refs):
    delta_ref, in_ref, bc_ref, rate_ref, skip_ref, side_in, ssm_ref, held_ref, side_out = refs[:9]
    in_s, bb, cb, run_a, run_b, side_sems = refs[9:15]
    phase, block = pl.program_id(0), pl.program_id(1)
    blocks = refs[17].shape[1]
    carries = Carries(states, blocks, True, *refs[15:])
    side = Side(side_in, side_out, side_sems)
    rates = [over_sublanes(rate_ref[n : n + 1, :]) for n in range(states)]

    parts = ((0, 2 / 7), (2 / 7, 3 / 7), (3 / 7, 1))
    for part, (at_phase, at_block) in enumerate(((0, 0), (0, blocks // 2), (1, 1))):

        @pl.when((phase == at_phase) & (block == at_block))
        def _():
            if part == 0:
                greet_experts()
            side.start(part, parts)

    def ends(first):
        in_s[...] = delta_ref[...] * in_ref[...].astype(F32)
        sums = jnp.sum(delta_ref[...].reshape(steps, SEGS, LANES), axis=0)

        def one(j, held):
            d, u = delta_ref[tile_rows(j), :], in_s[tile_rows(j), :]
            tile = bc_ref[tile_rows(j), :] if first else None
            new = []
            for n in range(states):
                if first:
                    b = over_lanes(tile[:, rank + n : rank + n + 1])
                    bb[j, n] = b
                    cb[j, n] = over_lanes(tile[:, rank + states + n : rank + states + n + 1])
                else:
                    b = bb[j, n]
                new.append(jnp.exp2(d * rates[n]) * held[n] + u * b)
            return tuple(new)

        zero = jnp.zeros((SEGS, LANES), F32)
        held = lax.fori_loop(0, steps, one, (zero,) * states, unroll=4)
        carries.put(block, held, sums, rates, run_a, run_b)

    @pl.when((phase == 0) & (block == 0))
    def _():
        ends(True)

    @pl.when((phase == 0) & (block > 0))
    def _():
        ends(False)

    @pl.when(phase == 1)
    def _():
        carries.await_group(block)
        start = carries.starts(block, rate_ref, run_a, run_b)
        mixed = in_ref[...].astype(F32)
        in_s[...] = delta_ref[...] * mixed
        ssm_ref[...] = skip_ref[...] * mixed
        for n in range(states):
            held_ref[0, 0, n] = start[n]

        def one(j, held):
            rows = tile_rows(j)
            d, u = delta_ref[rows, :], in_s[rows, :]
            total = ssm_ref[rows, :]
            new = []
            for n in range(states):
                h = jnp.exp2(d * rates[n]) * held[n] + u * bb[j, n]
                held_ref[0, j + 1, n] = h
                total = total + cb[j, n] * h
                new.append(h)
            ssm_ref[rows, :] = total
            return tuple(new)

        lax.fori_loop(0, steps, one, tuple(start), unroll=4)

    @pl.when((phase == 1) & (block == blocks - 1))
    def _():
        side.wait()


def mixer_states(delta, mixed, bc, rate2, skip, beside, rank, collective_id):
    count, width = delta.shape
    states, steps, blocks = rate2.shape[0], count // SEGS, width // LANES
    block = pl.BlockSpec((count, LANES), lambda p, c: (0, c))
    spread = pltpu.VMEM((steps, states, SEGS, LANES), F32)
    run = pltpu.VMEM((blocks, states, SEGS, LANES), F32)
    return pl.pallas_call(
        functools.partial(forward_kernel, states, steps, rank),
        grid=(2, blocks),
        out_shape=[
            jax.ShapeDtypeStruct((count, width), F32),
            jax.ShapeDtypeStruct((blocks, steps + 1, states, SEGS, LANES), F32),
            jax.ShapeDtypeStruct(beside.shape, beside.dtype),
        ],
        in_specs=[
            block,
            block,
            pl.BlockSpec(bc.shape, lambda p, c: (0, 0)),
            pl.BlockSpec((states, LANES), lambda p, c: (0, c)),
            pl.BlockSpec((1, LANES), lambda p, c: (0, c)),
            pl.BlockSpec(memory_space=pl.ANY),
        ],
        out_specs=[
            pl.BlockSpec((count, LANES), lambda p, c: (0, p * c)),
            pl.BlockSpec((1, steps + 1, states, SEGS, LANES), lambda p, c: (p * c, 0, 0, 0, 0)),
            pl.BlockSpec(memory_space=pl.ANY),
        ],
        scratch_shapes=[pltpu.VMEM((count, LANES), F32), spread, spread, run, run]
        + [Side.scratch(lax.axis_size("expert"))]
        + Carries.scratch(states, blocks, lax.axis_size("expert")),
        compiler_params=params(collective_id=collective_id, has_side_effects=True),
        name="mixer_states",
    )(delta, mixed, bc, rate2, skip, beside)


def backward_kernel(states, steps, rank, kinds, *refs):
    many = len(kinds)
    sum_in, refs = refs[:many], refs[many:]
    pre_ref, delta_ref, in_ref, g_ref, bc_ref, rate_ref, skip_ref, held_ref, side_in = refs[:9]
    sum_out, refs = refs[9 : 9 + many], refs[9 + many :]
    pre_grad_ref, mixed_grad_ref, rate_grad_ref, skip_grad_ref, bias_grad_ref = refs[:5]
    bc_grad_ref, side_out = refs[5:7]
    in_s, rate_sum, in_sum, bb, cb, b_acc, c_acc, run_a, run_b, side_sems = refs[7:17]
    carry_refs, sum_refs = refs[17:22], refs[22:]
    phase, block = pl.program_id(0), pl.program_id(1)
    blocks = carry_refs[2].shape[1]
    carries = Carries(states, blocks, False, *carry_refs)
    sums = summings(kinds, sum_in, sum_out, sum_refs)
    side = Side(side_in, side_out, side_sems)
    rates = [over_sublanes(rate_ref[n : n + 1, :]) for n in range(states)]
    zero = jnp.zeros((SEGS, LANES), F32)

    @pl.when((phase == 0) & (block == 0))
    def _():
        greet_others()
        for item in sums:
            item.start(0)

    @pl.when((phase == 0) & (block == blocks - 3))
    def _():
        for item in sums:
            if not item.pairs_first:
                item.advance(0)

    @pl.when((phase == 1) & (block == 1))
    def _():
        for item in sums:
            if item.pairs_first:
                item.advance(0)

    @pl.when((phase == 1) & (block == blocks // 2 - 1))
    def _():
        side.start()

    def ends(first):
        sums = jnp.sum(delta_ref[...].reshape(steps, SEGS, LANES), axis=0)

        def one(i, held):
            j = steps - 1 - i
            d, g = delta_ref[tile_rows(j), :], g_ref[tile_rows(j), :]
            tile = bc_ref[tile_rows(j), :] if first else None
            new = []
            for n in range(states):
                if first:
                    c = over_lanes(tile[:, rank + states + n : rank + states + n + 1])
                    bb[j, n] = over_lanes(tile[:, rank + n : rank + n + 1])
                    cb[j, n] = c
                else:
                    c = cb[j, n]
                new.append(jnp.exp2(d * rates[n]) * (held[n] + g * c))
            return tuple(new)

        held = lax.fori_loop(0, steps, one, (zero,) * states, unroll=4)
        carries.put(block, held, sums, rates, run_a, run_b)

    @pl.when((phase == 0) & (block == 0))
    def _():
        ends(True)

    @pl.when((phase == 0) & (block > 0))
    def _():
        ends(False)

    def grads(first, last):
        start = carries.starts(block, rate_ref, run_a, run_b)
        delta, g = delta_ref[...], g_ref[...]
        mixed = in_ref[...].astype(F32)
        in_s[...] = delta * mixed
        place = lax.broadcasted_iota(jnp.int32, (SEGS, LANES), 1)

        def one(i, carry):
            edge, rate_acc = carry
            j = steps - 1 - i
            rows = tile_rows(j)
            d, u, g = delta_ref[rows, :], in_s[rows, :], g_ref[rows, :]
            by_rate = by_b = sums = zero
            new_edge, new_acc = [], []
            for n in range(states):
                b, c = bb[j, n], cb[j, n]
                q = c * g + edge[n]
                e = jnp.exp2(d * rates[n]) * q
                v = e * held_ref[0, j, n]
                by_rate = by_rate + rates[n] * v
                by_b = by_b + b * q
                to_b = q * u
                to_c = g * held_ref[0, j + 1, n]
                if not first:
                    to_b = b_acc[j, n] + to_b
                    to_c = c_acc[j, n] + to_c
                if last:
                    sums = jnp.where(place == rank + n, jnp.sum(to_b, axis=1, keepdims=True), sums)
                    to_c = jnp.sum(to_c, axis=1, keepdims=True)
                    sums = jnp.where(place == rank + states + n, to_c, sums)
                else:
                    b_acc[j, n] = to_b
                    c_acc[j, n] = to_c
                new_edge.append(e)
                new_acc.append(rate_acc[n] + d * v)
            rate_sum[rows, :] = by_rate
            in_sum[rows, :] = by_b
            if last:
                bc_grad_ref[rows, :] = sums
            return tuple(new_edge), tuple(new_acc)

        _, rate_acc = lax.fori_loop(
            0, steps, one, (tuple(start), (zero,) * states), unroll=2
        )
        for n in range(states):
            rate_grad_ref[n : n + 1, :] = (
                LN2 * rate_ref[n : n + 1, :] * jnp.sum(rate_acc[n], axis=0, keepdims=True)
            )
        by_b = in_sum[...]
        pre_grad = (LN2 * rate_sum[...] + mixed * by_b) * jax.nn.sigmoid(pre_ref[...])
        pre_grad_ref[...] = pre_grad.astype(BF16)
        bias_grad_ref[...] = jnp.sum(pre_grad, axis=0, keepdims=True)
        mixed_grad_ref[...] = delta * by_b + skip_ref[...] * g
        skip_grad_ref[...] = jnp.sum(g * mixed, axis=0, keepdims=True)

    @pl.when(phase == 1)
    def _():
        carries.await_group(block)

    @pl.when((phase == 1) & (block == 0))
    def _():
        grads(True, False)

    @pl.when((phase == 1) & (block > 0) & (block < blocks - 1))
    def _():
        grads(False, False)

    @pl.when((phase == 1) & (block == blocks - 1))
    def _():
        grads(False, True)
        side.wait()
        for item in sums:
            item.wait(1)
            item.add(1)


def mixer_grads(
    pre, delta, mixed, ssm_grad, bc, rate2, skip, held, beside, rank, items, collective_id
):
    count, width = delta.shape
    states, steps, blocks = rate2.shape[0], count // SEGS, width // LANES
    block = pl.BlockSpec((count, LANES), lambda p, c: (0, c))
    late = lambda rows: pl.BlockSpec((rows, LANES), lambda p, c: (0, p * c))
    spread = pltpu.VMEM((steps, states, SEGS, LANES), F32)
    run = pltpu.VMEM((blocks, states, SEGS, LANES), F32)
    flat = pltpu.VMEM((count, LANES), F32)
    sum_scratch = [item.first_scratch() for item in items]
    kinds = tuple((item.kind(), len(refs)) for item, refs in zip(items, sum_scratch))
    spread_specs = [
        pl.BlockSpec(item.spread_shape().shape, lambda p, c, rank=len(item.spread_shape().shape): (0,) * rank)
        for item in items
    ]
    outs = pl.pallas_call(
        functools.partial(backward_kernel, states, steps, rank, kinds),
        grid=(2, blocks),
        out_shape=[item.spread_shape() for item in items]
        + [
            jax.ShapeDtypeStruct((count, width), BF16),
            jax.ShapeDtypeStruct((count, width), F32),
            jax.ShapeDtypeStruct((states, width), F32),
            jax.ShapeDtypeStruct((1, width), F32),
            jax.ShapeDtypeStruct((1, width), F32),
            jax.ShapeDtypeStruct((count, LANES), F32),
            jax.ShapeDtypeStruct(beside.shape, beside.dtype),
        ],
        in_specs=[pl.BlockSpec(memory_space=pl.ANY)] * len(items)
        + [
            late(count),
            block,
            late(count),
            block,
            pl.BlockSpec(bc.shape, lambda p, c: (0, 0)),
            pl.BlockSpec((states, LANES), lambda p, c: (0, c)),
            late(1),
            pl.BlockSpec((1, steps + 1, states, SEGS, LANES), lambda p, c: (p * c, 0, 0, 0, 0)),
            pl.BlockSpec(memory_space=pl.ANY),
        ],
        out_specs=spread_specs
        + [late(count), late(count), late(states), late(1), late(1)]
        + [pl.BlockSpec((count, LANES), lambda p, c: (0, 0)), pl.BlockSpec(memory_space=pl.ANY)],
        scratch_shapes=[flat, flat, flat, spread, spread, spread, spread, run, run]
        + [Side.scratch(lax.axis_size("expert"))]
        + Carries.scratch(states, blocks, lax.axis_size("expert"))
        + [ref for refs in sum_scratch for ref in refs],
        compiler_params=params(collective_id=collective_id, has_side_effects=True),
        name="mixer_grads",
    )(*(item.local for item in items), pre, delta, mixed, ssm_grad, bc, rate2, skip, held, beside)
    return outs


def shifted_in(tile, row, forward):
    if forward:
        return jnp.concatenate([row, tile[: SEGS - 1]], axis=0)
    return jnp.concatenate([tile[1:], row], axis=0)


WIDE = 2 * LANES


def over_blocks(width, size, body):
    def one(n, carry):
        body(pl.ds(pl.multiple_of(n * size, size), size))
        return carry

    lax.fori_loop(0, width // size, one, 0)


def put_by_token(out_ref, value, turn):
    steps = value.shape[0] // SEGS
    for lane in range(turn.shape[0]):
        lanes = slice(lane * LANES, (lane + 1) * LANES)
        turn[lane] = value[:, lanes]
        for s in range(SEGS):
            rows = turn[lane, pl.ds(s, steps, stride=SEGS), :]
            out_ref[s * steps : (s + 1) * steps, lanes] = rows.astype(out_ref.dtype)


def tile_places(pack, flat):
    _, pairs, each = pack.shape[:3]
    across = flat.shape[1] // LANES
    for t in range(2 * pairs * each):
        row, lane = t // across * 16, t % across * LANES
        inside = (slice(row, row + 16), slice(lane, lane + LANES)) if row < flat.shape[0] else None
        yield (t // (pairs * each), t // each % pairs, t % each), inside


def put_tiles(pack, flat):
    for tile, inside in tile_places(pack, flat):
        if inside is None:
            pack[tile] = jnp.zeros((16, LANES), BF16)
        else:
            pack[tile] = flat[inside].astype(BF16)


def get_tiles(flat, pack):
    for tile, inside in tile_places(pack, flat):
        if inside is not None:
            flat[inside] = pack[tile].astype(F32)


def finish_kernel(rank, states, kinds, *refs):
    loads_hbm, refs = refs[:11], refs[11:]
    bc_grad_ref, low_ref, x_proj_ref, dt_proj_ref, conv_ref, bias_ref = refs[:6]
    before_ref, gain_ref, rate_ref, dt_bias_ref, skip_ref, gain_two_ref, router_ref = refs[6:13]
    col_ref, gate_spread, out_spread = refs[13:16]
    (
        output_ref,
        tokens_grad_ref,
        gain_out,
        in_proj_out,
        conv_out,
        bias_out,
        x_proj_out,
        dt_proj_out,
        dt_bias_out,
        rate_out,
        skip_out,
        out_proj_out,
        gain_two_out,
        router_out,
    ) = refs[16:30]
    refs = refs[30:]
    loaded, refs = refs[:11], refs[11:]
    pre_grad, mixed_part, mixed, inner, normed, in_proj, gate_grad, tokens, hidden_grad = loaded[:9]
    hidden, home = loaded[9:]
    ext_in, ext_grad, inner_grad, proj_grad, flat, last_flat, rows, head, after = refs[:9]
    turn, load_sems, halo_sems = refs[9:12]
    small, last_small = SmallSum(*refs[12:19]), SmallSum(*refs[19:26])
    parts, refs = len(kinds) - 2, refs[26:]
    locals_, sum_refs = refs[:parts], refs[parts:]
    count, width = tokens.shape
    inner_width = inner.shape[1]
    reach = conv_ref.shape[0] - 1
    rim = reach * SEGS
    experts, me = lax.axis_size("expert"), lax.axis_index("expert")
    group = lax.axis_index("batch")
    half = inner_width

    loads = [
        pltpu.make_async_copy(src, dst, load_sems.at[i])
        for i, (src, dst) in enumerate(zip(loads_hbm, loaded))
    ]
    for load in loads:
        load.start()
    ends = [0]
    for ref in locals_:
        ends.append(ends[-1] + ref.shape[2])
    inner_rows = [slice(ends[i], ends[i + 1]) for i in range(parts)]
    gate_sum, out_sum, *inner_sums = summings(
        kinds,
        (gate_spread, out_spread, *locals_),
        (in_proj_out.at[:, half:], out_proj_out)
        + tuple(in_proj_out.at[at, :half] for at in inner_rows),
        sum_refs,
    )
    greet_others()
    gate_sum.begin()
    out_sum.begin()
    flat[...] = jnp.zeros(flat.shape, F32)
    last_flat[...] = jnp.zeros(last_flat.shape, F32)

    loads[0].wait()
    over_inner = (((1,), (1,)), ((), ()))
    over_rows = (((0,), (0,)), ((), ()))
    low_grad = lax.dot_general(
        pre_grad[...], dt_proj_ref[...], over_inner, preferred_element_type=F32
    )
    proj_grad[...] = (low_grad + bc_grad_ref[...]).astype(BF16)

    for load in loads[1:4]:
        load.wait()

    def before_silu(at):
        own = inner[:, at].astype(F32)
        for k in range(reach):
            tile = own[count - rim + k * SEGS : count - rim + (k + 1) * SEGS]
            ext_in[k * SEGS : (k + 1) * SEGS, at] = shifted_in(tile, before_ref[k : k + 1, at], True)
        ext_in[rim:, at] = own
        total = jnp.dot(proj_grad[...], x_proj_ref[:, at], preferred_element_type=F32)
        total = total + mixed_part[:, at]
        conv_pre = jnp.broadcast_to(bias_ref[:, at], total.shape)
        for k in range(reach + 1):
            conv_pre = conv_pre + conv_ref[k : k + 1, at] * ext_in[k * SEGS : k * SEGS + count, at]
        total = total * silu_slope(conv_pre)
        ext_grad[:count, at] = total
        for k in range(reach):
            head[k : k + 1, at] = total[k * SEGS : k * SEGS + 1]

    over_blocks(inner_width, WIDE, before_silu)
    halo = pltpu.make_async_remote_copy(
        src_ref=head,
        dst_ref=after,
        send_sem=halo_sems.at[0],
        recv_sem=halo_sems.at[1],
        device_id=(group, lax.rem(me + experts - 1, experts)),
        device_id_type=MESH,
    )

    @pl.when(me > 0)
    def _():
        halo.start()

    @pl.when(me == experts - 1)
    def _():
        after[...] = jnp.zeros(after.shape, F32)

    at_dt = rank + 2 * states
    x_local = lax.dot_general(proj_grad[...], mixed[...], over_rows, preferred_element_type=F32)
    flat[:at_dt, :] = x_local[:at_dt]
    dt_local = lax.dot_general(low_ref[...], pre_grad[...], over_rows, preferred_element_type=F32)
    flat[at_dt : at_dt + rank, :] = dt_local[:rank]
    at = at_dt + rank + states
    flat[at_dt + rank : at, :] = rate_ref[...]
    flat[at : at + 1, :] = dt_bias_ref[...]
    flat[at + 1 : at + 2, :] = skip_ref[...]
    flat[at + 2 : at + 3, :width] = gain_two_ref[...]
    fold = router_ref.shape[0] // 2
    flat[at + 3 : at + 3 + fold, :width] = router_ref[:fold, :]
    flat[at + 3 : at + 3 + fold, width:] = router_ref[fold:, :]
    put_tiles(small.pack, flat)
    small.start(0)
    for load in loads[4:7]:
        load.wait()
    rows[...] = lax.dot_general(
        gate_grad[...], in_proj[:, half:], over_inner, preferred_element_type=F32
    )

    @pl.when(me > 0)
    def _():
        halo.wait_send()

    @pl.when(me < experts - 1)
    def _():
        halo.wait_recv()

    def before_taps(at):
        for k in range(reach):
            tile = ext_grad[k * SEGS : (k + 1) * SEGS, at]
            ext_grad[count + k * SEGS : count + (k + 1) * SEGS, at] = shifted_in(
                tile, after[k : k + 1, at], False
            )
        total = conv_ref[0:1, at] * ext_grad[rim : rim + count, at]
        for k in range(1, reach + 1):
            first = (reach - k) * SEGS
            total = total + conv_ref[k : k + 1, at] * ext_grad[first : first + count, at]
        inner_grad[:, at] = total.astype(BF16)

    over_blocks(inner_width, WIDE, before_taps)
    chunk = width // experts
    share = inner_width // lax.axis_size("batch")

    def to_in_proj(at):
        total = lax.dot_general(
            normed[...], inner_grad[:, at], over_rows, preferred_element_type=F32
        ).astype(BF16)
        for e in range(experts):
            own = total[e * chunk : (e + 1) * chunk]
            for ref, rows_at in zip(locals_, inner_rows):
                ref[e // 2, e % 2, :, at] = own[rows_at]

    over_blocks(inner_width, share, to_in_proj)
    for item in inner_sums:
        item.begin()
    small.advance(0)


    def to_taps(at):
        grad = ext_grad[:count, at]
        for k in range(reach + 1):
            last_flat[k : k + 1, at] = jnp.sum(
                grad * ext_in[k * SEGS : k * SEGS + count, at], axis=0, keepdims=True
            )
        last_flat[reach + 1 : reach + 2, at] = jnp.sum(grad, axis=0, keepdims=True)

    for item in inner_sums:
        item.advance(0)
    over_blocks(inner_width, WIDE, to_taps)
    for load in loads[7:]:
        load.wait()
    grad = rows[...] + lax.dot_general(
        inner_grad[...], in_proj[:, :half], over_inner, preferred_element_type=F32
    )
    values = tokens[...].astype(F32)
    to_values, to_gain = rms_back(values, gain_ref[...], grad)
    put_by_token(tokens_grad_ref, to_values + hidden_grad[...], turn)

    last_flat[reach + 2 : reach + 3, :width] = to_gain[None]
    put_tiles(last_small.pack, last_flat)
    last_small.start(0)
    gate_sum.advance(2)
    out_sum.advance(2)
    small.advance(1)
    last_small.advance(0)
    for item in inner_sums:
        item.advance(1)
    last_small.advance(1)
    small.advance(2)

    slots = home.shape[1]
    slot_id = lax.broadcasted_iota(jnp.int32, (count, experts * slots), 1)
    chosen = (slot_id == col_ref[...]).astype(F32).astype(BF16)
    returned = jnp.dot(
        chosen, home[...].reshape(experts * slots, width), preferred_element_type=F32
    )
    put_by_token(output_ref, hidden[...] + returned, turn)

    last_small.advance(2)
    gate_sum.advance(3)
    out_sum.advance(3)
    for item in inner_sums:
        item.advance(2)
    small.advance(3)
    last_small.advance(3)
    small.advance(4)
    get_tiles(flat, small.every)
    x_proj_out[...] = flat[:at_dt, :]
    dt_proj_out[...] = flat[at_dt : at_dt + rank, :]
    rate_out[...] = flat[at_dt + rank : at, :]
    dt_bias_out[...] = flat[at : at + 1, :]
    skip_out[...] = flat[at + 1 : at + 2, :]
    gain_two_out[...] = flat[at + 2 : at + 3, :width]
    router_out[:fold, :] = flat[at + 3 : at + 3 + fold, :width]
    router_out[fold:, :] = flat[at + 3 : at + 3 + fold, width:]
    for item in inner_sums:
        item.advance(3)
    last_small.advance(4)
    get_tiles(last_flat, last_small.every)
    conv_out[...] = last_flat[: reach + 1, :]
    bias_out[...] = last_flat[reach + 1 : reach + 2, :]
    gain_out[...] = last_flat[reach + 2 : reach + 3, :width]


def finish(loaded, small, early, rank, states, collective_id):
    pre_grad, in_proj, tokens = loaded[0], loaded[5], loaded[7]
    conv_weight, router_local = small[4], small[12]
    count, inner_width = pre_grad.shape
    width = tokens.shape[1]
    experts, ways = lax.axis_size("expert"), lax.axis_size("batch")
    pairs, chunk = experts // 2, width // experts
    taps = conv_weight.shape[0]
    vmem, hbm = (pl.BlockSpec(memory_space=m) for m in (pltpu.VMEM, pl.ANY))
    split = (chunk * 2 // 3, chunk // 3) if chunk % 48 == 0 else (chunk,)
    locals_ = [jax.ShapeDtypeStruct((pairs, 2, part, inner_width), BF16) for part in split]
    items = early + [Total(local, 1, i == 1) for i, local in enumerate(locals_)]
    scratch = [item.scratch() for item in items]
    kinds = tuple((item.kind(), len(refs)) for item, refs in zip(items, scratch))
    used = 2 * rank + 3 * states + 3 + router_local.shape[0] // 2
    high, low = (-(-rows // 16) * 16 for rows in (used, taps + 2))
    tiles = [-(-(rows // 16 * inner_width // LANES) // (2 * pairs)) for rows in (high, low)]
    f32 = lambda *shape: jax.ShapeDtypeStruct(shape, F32)
    halo = pltpu.VMEM((SEGS, inner_width), F32)
    rim = (taps - 1) * SEGS
    return pl.pallas_call(
        functools.partial(finish_kernel, rank, states, kinds),
        out_shape=[
            jax.ShapeDtypeStruct((count, width), BF16),
            f32(count, width),
            f32(1, width),
            f32(chunk, 2 * inner_width),
            f32(taps, inner_width),
            f32(1, inner_width),
            f32(rank + 2 * states, inner_width),
            f32(rank, inner_width),
            f32(1, inner_width),
            f32(states, inner_width),
            f32(1, inner_width),
            f32(*early[1].chunk),
            f32(1, width),
            f32(*router_local.shape),
        ],
        in_specs=[hbm] * len(loaded) + [vmem] * (len(small) + len(early)),
        out_specs=[vmem] * 14,
        scratch_shapes=[pltpu.VMEM(a.shape, a.dtype) for a in loaded]
        + [
            pltpu.VMEM((count + rim, inner_width), F32),
            pltpu.VMEM((count + rim, inner_width), F32),
            pltpu.VMEM((count, inner_width), BF16),
            pltpu.VMEM((count, LANES), BF16),
            pltpu.VMEM((high, inner_width), F32),
            pltpu.VMEM((low, inner_width), F32),
            pltpu.VMEM((count, width), F32),
            halo,
            halo,
            pltpu.VMEM((width // LANES, count, LANES), F32),
            pltpu.SemaphoreType.DMA((len(loaded),)),
            pltpu.SemaphoreType.DMA((2,)),
        ]
        + SmallSum.scratch(pairs, ways, tiles[0])
        + SmallSum.scratch(pairs, ways, tiles[1])
        + [pltpu.VMEM(local.shape, BF16) for local in locals_]
        + [ref for refs in scratch for ref in refs],
        compiler_params=params(collective_id=collective_id, has_side_effects=True),
        name="finish",
    )(*loaded, *small, *(item.local for item in early))


def passed_along(value, axis, steps):
    count = lax.axis_size(axis)
    leading, last = (max(0, -steps), min(count, count - steps))
    return lax.ppermute(value, axis, [(source, source + steps) for source in range(leading, last)])


def silu(v):
    return v * jax.nn.sigmoid(v)


def silu_slope(v):
    s = jax.nn.sigmoid(v)
    return s * (1.0 + v * (1.0 - s))


def by_segment(value):
    count = value.shape[0]
    return value.reshape(SEGS, count // SEGS, -1).transpose(1, 0, 2).reshape(count, -1)


def rms_back(values, gain, grad):
    r = lax.rsqrt(jnp.mean(values * values, axis=-1, keepdims=True) + 1e-05)
    u = gain * grad
    mean = jnp.mean(values * u, axis=-1, keepdims=True)
    return r * u - values * (r * r * r) * mean, jnp.sum(grad * values * r, axis=0)


def rms(values, gain):
    return values * lax.rsqrt(jnp.mean(values * values, axis=-1, keepdims=True) + 1e-05) * gain


def per_device(
    tokens,
    routes,
    gain_one,
    in_proj,
    conv_weight,
    conv_bias,
    x_proj,
    dt_proj,
    dt_bias,
    rate_log,
    skip,
    out_proj,
    gain_two,
    router,
    expert_in,
    expert_out,
    cotangent,
):
    count, width = tokens.shape[1], tokens.shape[2]
    steps = count // SEGS
    inner_width = out_proj.shape[0]
    rank = dt_proj.shape[0]
    experts = router.shape[0]
    capacity = 5 * count // (4 * experts)
    slots = -(-capacity // 16) * 16
    reach = conv_weight.shape[0] - 1
    rate2 = -jnp.exp(rate_log) * LOG2E
    skip_row = skip[None]

    route = by_segment(routes[0]).reshape(count)
    upstream_low = by_segment(cotangent[0])
    expert_ids = lax.broadcasted_iota(jnp.int32, (experts, count), 0)
    onehot = (expert_ids == route[None]).astype(BF16)
    first = lax.broadcasted_iota(jnp.int32, (count, count), 0)
    second = lax.broadcasted_iota(jnp.int32, (count, count), 1)
    token_of = lambda p: (p % SEGS) * steps + p // SEGS
    earlier = (token_of(first) <= token_of(second)).astype(BF16)
    running = jnp.dot(onehot, earlier, preferred_element_type=F32)
    place = (jnp.sum(running * onehot.astype(F32), axis=0) - 1.0).astype(jnp.int32)
    target = jnp.where(place < capacity, route * slots + place, -1)
    slot_ids = lax.broadcasted_iota(jnp.int32, (experts * slots, count), 0)
    dispatch = (slot_ids == target[None]).astype(BF16)

    upstream_rows = jnp.dot(dispatch, upstream_low, preferred_element_type=F32).astype(BF16)
    upstream_rows = upstream_rows.reshape(experts, slots, width)

    tokens_low = by_segment(tokens[0])
    values = tokens_low.astype(F32)
    normed_one = rms(values, gain_one).astype(BF16)
    both = jnp.dot(normed_one, in_proj, preferred_element_type=F32)
    inner = both[:, :inner_width].astype(BF16)
    gate_z = both[:, inner_width:]
    blocks = inner.reshape(steps, SEGS, inner_width)
    tail = blocks[steps - reach :]
    before = passed_along(tail[:, SEGS - 1], "expert", 1)
    extended = jnp.concatenate(
        [jnp.concatenate([before[:, None], tail[:, : SEGS - 1]], axis=1), blocks], axis=0
    ).astype(F32)
    conv_pre = conv_bias + sum(
        conv_weight[k] * extended[k : k + steps] for k in range(reach + 1)
    )
    conv_pre = conv_pre.reshape(count, inner_width)
    mixed = silu(conv_pre).astype(BF16)
    states = rate_log.shape[0]
    x_proj = jnp.pad(x_proj, ((0, LANES - x_proj.shape[0]), (0, 0)))
    dt_proj = jnp.pad(dt_proj, ((0, LANES - rank), (0, 0)))
    proj = contract(mixed, x_proj, 1, 1)
    low_rank = proj.astype(BF16)
    pre = jnp.dot(low_rank, dt_proj, preferred_element_type=F32) + dt_bias
    delta = softplus(pre)
    ssm, held, slot_upstream = mixer_states(
        delta, mixed, proj, rate2, skip_row, upstream_rows, rank, 2
    )
    gated = (ssm * silu(gate_z)).astype(BF16)
    hidden = values + jnp.dot(gated, out_proj, preferred_element_type=F32)
    normed_two = rms(hidden, gain_two).astype(BF16)

    normed_two_grad, results, expert_in_local, expert_out_local, router_local = run_experts(
        normed_two, target, router, slot_upstream, expert_in, expert_out, slots, 4
    )

    hidden_norm, gain_two_local = rms_back(hidden, gain_two, normed_two_grad)
    hidden_grad = upstream_low.astype(F32) + hidden_norm
    branch = hidden_grad.astype(BF16)
    out_proj_local = contract(gated, branch, 0, 0)
    gated_grad = contract(branch, out_proj, 1, 1)
    ssm_grad = gated_grad * silu(gate_z)
    gate_z_grad = (gated_grad * ssm * silu_slope(gate_z)).astype(BF16)

    ways, pairs = lax.axis_size("batch"), experts // 2
    in_proj_gate_local = contract(normed_one, gate_z_grad, 0, 0)
    early = [
        Total(
            in_proj_gate_local.astype(BF16).reshape(pairs, 2, width // experts, inner_width),
            1,
        ),
        Total(
            out_proj_local.astype(BF16).reshape(
                pairs, 2, ways, inner_width // (experts * ways), width
            ),
            0,
            True,
        ),
    ]
    (
        in_proj_gate_spread,
        out_proj_spread,
        pre_grad,
        mixed_grad,
        rate_log_local,
        skip_local,
        dt_bias_local,
        bc_grad,
        returned,
    ) = mixer_grads(
        pre, delta, mixed, ssm_grad, proj, rate2, skip_row, held, results, rank, early, 3
    )
    early = [early[0].resumed(in_proj_gate_spread), early[1].resumed(out_proj_spread)]
    outs = finish(
        [
            pre_grad,
            mixed_grad,
            mixed,
            inner,
            normed_one,
            in_proj,
            gate_z_grad,
            tokens_low,
            hidden_grad,
            hidden,
            returned,
        ],
        [
            bc_grad,
            low_rank,
            x_proj,
            dt_proj,
            conv_weight,
            conv_bias[None],
            before.astype(F32),
            gain_one[None],
            rate_log_local,
            dt_bias_local,
            skip_local,
            gain_two_local[None],
            router_local,
            target[:, None],
        ],
        early,
        rank,
        states,
        1,
    )
    expert_in_grad, expert_out_grad = (
        lax.psum_scatter(v, "batch", scatter_dimension=0, tiled=True).astype(F32)
        for v in (expert_in_local, expert_out_local)
    )
    output, tokens_grad, gain_one_grad, in_proj_grad, conv_weight_grad, conv_bias_grad = outs[:6]
    x_proj_grad, dt_proj_grad, dt_bias_grad, rate_log_grad, skip_grad, out_proj_grad = outs[6:12]
    gain_two_grad, router_grad = outs[12:]
    return (
        output[None],
        tokens_grad[None],
        gain_one_grad[0],
        in_proj_grad,
        conv_weight_grad,
        conv_bias_grad[0],
        x_proj_grad,
        dt_proj_grad,
        dt_bias_grad[0],
        rate_log_grad,
        skip_grad[0],
        out_proj_grad.reshape(-1, width),
        gain_two_grad[0],
        router_grad,
        expert_in_grad[None],
        expert_out_grad[None],
    )


def solution(mesh):
    split = P("batch", "expert", None)
    one = P("expert", None, None)
    both = P("expert", "batch", None)
    in_specs = (split, split) + (P(),) * 12 + (one, one, split)
    out_specs = (split, split, P(), P("expert", None)) + (P(),) * 7
    out_specs += (P("expert", None), P(), P(), both, both)
    return jax.shard_map(
        per_device, mesh=mesh, in_specs=in_specs, out_specs=out_specs, check_vma=False
    )
```

```python
import functools

import jax
import jax.numpy as jnp
from jax import lax
from jax.experimental import pallas as pl
from jax.experimental.pallas import tpu as pltpu
from jax.sharding import PartitionSpec as P

F32, BF16 = jnp.float32, jnp.bfloat16
SEGS = 8
LANES = 128
LOG2E = 1.4426950408889634
LN2 = 0.6931471805599453
VMEM_LIMIT = 60 * 1024 * 1024
MESH = pl.DeviceIdType.MESH


def params(**kw):
    return pltpu.CompilerParams(vmem_limit_bytes=VMEM_LIMIT, **kw)


def softplus(v):
    return jnp.maximum(v, 0.0) + jnp.log1p(jnp.exp(-jnp.abs(v)))


def as_row(ref):
    return ref[...].reshape(1, ref.shape[0])


def padded_rows(ref, high):
    low = jnp.zeros((high - ref.shape[0], ref.shape[1]), F32)
    return jnp.concatenate([ref[...].astype(F32), low], axis=0).astype(BF16)


def over_sublanes(row):
    return jnp.broadcast_to(row, (SEGS, LANES))


def over_lanes(column):
    return jnp.broadcast_to(column, (SEGS, LANES))


def tile_rows(j):
    return pl.ds(pl.multiple_of(j * SEGS, SEGS), SEGS)


def run_of_segments(a, b, forward):
    at = lax.broadcasted_iota(jnp.int32, (SEGS, LANES), 0)
    for step in (1, 2, 4):
        if forward:
            inside, turn = at >= step, step
        else:
            inside, turn = at < SEGS - step, SEGS - step
        before_a = jnp.where(inside, pltpu.roll(a, turn, 0), 1.0)
        before_b = jnp.where(inside, pltpu.roll(b, turn, 0), 0.0)
        a, b = a * before_a, a * before_b + b
    return a, b


class Carries:
    groups = 2

    def __init__(self, states, blocks, forward, own, lengths, got, got_lengths, sems):
        self.states, self.blocks, self.forward = states, blocks, forward
        self.own, self.lengths, self.got, self.got_lengths = own, lengths, got, got_lengths
        self.sems = sems
        self.count, self.me = lax.axis_size("expert"), lax.axis_index("expert")
        self.per = blocks // self.groups

    @staticmethod
    def scratch(states, blocks, count):
        per = blocks // Carries.groups
        assert blocks % Carries.groups == 0 and per <= SEGS
        return [
            pltpu.VMEM((blocks, states, LANES), BF16),
            pltpu.VMEM((Carries.groups, SEGS, LANES), F32),
            pltpu.VMEM((count, blocks, states, LANES), BF16),
            pltpu.VMEM((count, Carries.groups, SEGS, LANES), F32),
            pltpu.SemaphoreType.DMA((2, 2, Carries.groups, count)),
        ]

    def other(self, k):
        return (lax.axis_index("batch"), lax.rem(self.me + k, self.count))

    def copies(self, group):
        blocks = pl.ds(group * self.per, self.per)
        found = []
        for k in range(1, self.count):
            pairs = (
                (self.own.at[blocks], self.got.at[k - 1, blocks]),
                (self.lengths.at[group], self.got_lengths.at[k - 1, group]),
            )
            for i, (src, dst) in enumerate(pairs):
                found.append(
                    pltpu.make_async_remote_copy(
                        src_ref=src,
                        dst_ref=dst,
                        send_sem=self.sems.at[0, i, group, k - 1],
                        recv_sem=self.sems.at[1, i, group, k - 1],
                        device_id=self.other(k),
                        device_id_type=MESH,
                    )
                )
        return found

    def put(self, block, ends, sums, rates, run_a, run_b):
        edge = SEGS - 1 if self.forward else 0
        rows = []
        for n in range(self.states):
            a, b = run_of_segments(jnp.exp2(rates[n] * sums), ends[n], self.forward)
            run_a[block, n] = a
            run_b[block, n] = b
            rows.append(b[edge : edge + 1])
        end = jnp.concatenate(rows, axis=0).astype(BF16)
        total = jnp.sum(sums, axis=0, keepdims=True)
        last = self.count - 1
        self.own[block] = end
        self.got[last, block] = end
        for group in range(self.groups):

            @pl.when(block // self.per == group)
            def _():
                row = pl.ds(lax.rem(block, self.per), 1)
                self.lengths[group, row, :] = total
                self.got_lengths[last, group, row, :] = total

            @pl.when(block == (group + 1) * self.per - 1)
            def _():
                for copy in self.copies(group):
                    copy.start()

    def await_group(self, block):
        for group in range(self.groups):

            @pl.when(block == group * self.per)
            def _():
                for copy in self.copies(group):
                    copy.wait()

    def starts(self, block, rate, run_a, run_b):
        group, row = block // self.per, pl.ds(lax.rem(block, self.per), 1)
        entering = jnp.zeros((self.states, LANES), F32)
        order = range(self.count) if self.forward else range(self.count - 1, -1, -1)
        for place in order:
            slot = lax.rem(self.me - place - 1 + 2 * self.count, self.count)
            length = self.got_lengths[slot, group, row, :]
            joined = jnp.exp2(rate * length) * entering + self.got[slot, block].astype(F32)
            ahead = (place < self.me) if self.forward else (place > self.me)
            entering = jnp.where(ahead, joined, entering)
        found = []
        for n in range(self.states):
            first = entering[n : n + 1]
            after = run_a[block, n] * over_sublanes(first) + run_b[block, n]
            found.append(shifted_in(after, first, self.forward))
        return found


def together(*parts):
    return sum(p.astype(F32) for p in parts)


class Total:
    def __init__(self, local, axis, pairs_first=False, chunk=None):
        self.local, self.axis, self.pairs_first = local, axis, pairs_first
        self.ways = lax.axis_size("batch")
        self.taken_up = chunk is not None
        self.pairs, self.chunk = lax.axis_size("expert") // 2, chunk or local.shape[2:]
        part = list(self.chunk)
        part[axis] //= self.ways
        self.part = tuple(part)

    def kind(self):
        return self.axis, self.pairs_first, self.part, self.taken_up

    def spread_shape(self):
        shape = self.chunk if self.pairs_first else (self.pairs, *self.part)
        return jax.ShapeDtypeStruct(shape, BF16)

    def resumed(self, spread):
        return Total(spread, self.axis, self.pairs_first, self.chunk)

    def first_scratch(self):
        first = (self.pairs - 1, *self.chunk)
        if not self.pairs_first:
            first = (self.ways - 1, self.pairs, *self.part)
        return [
            pltpu.VMEM((2, self.pairs, *self.chunk), BF16),
            pltpu.VMEM((self.pairs, *self.chunk), BF16),
            pltpu.VMEM(first, BF16),
            pltpu.SemaphoreType.DMA((2, 2, max(self.ways, self.pairs))),
        ]

    def second_scratch(self):
        second = self.ways - 1 if self.pairs_first else self.pairs - 1
        return [
            pltpu.VMEM((second, *self.part), BF16),
            pltpu.VMEM(self.part, BF16),
            pltpu.VMEM(self.chunk, BF16),
            pltpu.SemaphoreType.DMA((2, 4, max(self.ways, self.pairs))),
        ]

    def scratch(self):
        if self.taken_up:
            return self.second_scratch()
        spread = self.spread_shape()
        return self.first_scratch() + [pltpu.VMEM(spread.shape, BF16)] + self.second_scratch()


def part_of(ref, lead, axis, size, index):
    start = index * size
    if axis == len(ref.shape) - lead - 1:
        start = pl.multiple_of(start, LANES)
    where = [slice(None)] * len(ref.shape)
    where[lead + axis] = pl.ds(start, size)
    return ref.at[tuple(where)]


class Peers:
    def __init__(self):
        self.ways, self.pairs = lax.axis_size("batch"), lax.axis_size("expert") // 2
        self.group, place = lax.axis_index("batch"), lax.axis_index("expert")
        self.pair, self.core = place // 2, lax.rem(place, 2)
        self.sibling = (self.group, self.pair * 2 + 1 - self.core)
        self.to_batch = [lax.rem(self.group + k, self.ways) for k in range(1, self.ways)]
        self.to_pairs = [lax.rem(self.pair + k, self.pairs) for k in range(1, self.pairs)]
        self.in_batch = [(to, place) for to in self.to_batch]
        self.in_pairs = [(self.group, to * 2 + self.core) for to in self.to_pairs]

    def remote(self, src, dst, sems, stage, k, device):
        return pltpu.make_async_remote_copy(
            src_ref=src,
            dst_ref=dst,
            send_sem=sems.at[0, stage, k],
            recv_sem=sems.at[1, stage, k],
            device_id=device,
            device_id_type=MESH,
        )

    def start(self, stage):
        for copy in self.copies(stage):
            copy.start()

    def wait(self, stage):
        for copy in self.copies(stage):
            copy.wait()

    def advance(self, stage):
        self.wait(stage)
        self.add(stage)
        if stage < self.last:
            self.start(stage + 1)


class Summing(Peers):
    last = 3

    def __init__(self, kind, local, out, scratch):
        super().__init__()
        self.axis, self.pairs_first, part, self.taken_up = kind
        self.local, self.out, self.size = local, out, part[self.axis]
        if self.taken_up:
            self.spread = local
            self.from_second, self.mine, self.every, self.late_sems = scratch
        else:
            self.both, self.by_chip, self.from_first, self.sems = scratch[:4]
            self.spread = out
            if len(scratch) > 4:
                self.spread, self.from_second, self.mine, self.every, self.late_sems = scratch[4:]

    def share(self, ref, lead, index):
        return part_of(ref, lead, self.axis, self.size, index)

    def copies(self, stage):
        if stage == 0:
            own = pltpu.make_async_copy(
                self.local.at[:, self.core], self.both.at[0], self.sems.at[0, 0, 1]
            )
            away = self.local.at[:, 1 - self.core]
            return [own, self.remote(away, self.both.at[1], self.sems, 0, 0, self.sibling)]
        if stage == 3:
            own, devices = self.share(self.every, 0, self.group), self.in_batch
            pieces = [(self.mine, own) for _ in devices]
        elif (stage == 1) == self.pairs_first:
            devices = self.in_pairs
            src, dst = (self.by_chip, self.from_first) if stage == 1 else (self.spread, self.from_second)
            pieces = [(src.at[to], dst.at[k]) for k, to in enumerate(self.to_pairs)]
        else:
            devices = self.in_batch
            src, dst = (self.by_chip, self.from_first) if stage == 1 else (self.spread, self.from_second)
            lead = 1 if stage == 1 else 0
            pieces = [
                (self.share(src, lead, to), dst.at[k]) for k, to in enumerate(self.to_batch)
            ]
        sems = self.sems if stage == 1 else self.late_sems
        return [
            self.remote(src, dst, sems, stage, k, devices[k]) for k, (src, dst) in enumerate(pieces)
        ]

    def add(self, stage):
        if stage == 0:

            def over_cores(z, carry):
                self.by_chip[z] = together(self.both[0, z], self.both[1, z]).astype(BF16)
                return carry

            lax.fori_loop(0, self.pairs, over_cores, 0)
        elif stage == 1 and self.pairs_first:
            others = (self.from_first[k] for k in range(self.pairs - 1))
            self.spread[...] = together(self.by_chip[self.pair], *others).astype(BF16)
        elif stage == 1:
            own = self.share(self.by_chip, 1, self.group)

            def over_batch(z, carry):
                others = (self.from_first[k, z] for k in range(self.ways - 1))
                self.spread[z] = together(own[z], *others).astype(BF16)
                return carry

            lax.fori_loop(0, self.pairs, over_batch, 0)
        elif stage == 2:
            if self.pairs_first:
                own, count = self.share(self.spread, 0, self.group)[...], self.ways
            else:
                own, count = self.spread[self.pair], self.pairs
            others = (self.from_second[k] for k in range(count - 1))
            total = together(own, *others).astype(BF16)
            self.mine[...] = total
            self.share(self.every, 0, self.group)[...] = total
        else:
            self.out[...] = self.every[...].astype(self.out.dtype)

    def begin(self):
        self.start(2 if self.taken_up else 0)


class SmallSum(Peers):
    last = 4

    def __init__(self, pack, from_core, half, from_pairs, by_group, every, sems):
        super().__init__()
        self.pack, self.from_core, self.half, self.from_pairs = pack, from_core, half, from_pairs
        self.by_group, self.every, self.sems = by_group, every, sems

    @staticmethod
    def scratch(pairs, ways, tiles):
        tile = (tiles, 16, LANES)
        shapes = ((2, pairs), (pairs,), (pairs,), (pairs - 1,), (ways,), (2, pairs))
        found = [pltpu.VMEM((*lead, *tile), BF16) for lead in shapes]
        return found + [pltpu.SemaphoreType.DMA((2, 5, max(pairs, ways)))]

    def copies(self, stage):
        if stage == 0:
            pieces = [(self.pack.at[1 - self.core], self.from_core, self.sibling)]
        elif stage == 1:
            pieces = [
                (self.half.at[to], self.from_pairs.at[k], self.in_pairs[k])
                for k, to in enumerate(self.to_pairs)
            ]
        elif stage == 2:
            own = self.by_group.at[self.group]
            pieces = [(own, own, device) for device in self.in_batch]
        elif stage == 3:
            own = self.every.at[self.core, self.pair]
            pieces = [(own, own, device) for device in self.in_pairs]
        else:
            own = self.every.at[self.core]
            pieces = [(own, own, self.sibling)]
        return [
            self.remote(src, dst, self.sems, stage, k, device)
            for k, (src, dst, device) in enumerate(pieces)
        ]

    def add(self, stage):
        if stage == 0:
            self.half[...] = together(self.pack[self.core], self.from_core[...]).astype(BF16)
        elif stage == 1:
            others = (self.from_pairs[k] for k in range(self.pairs - 1))
            self.by_group[self.group] = together(self.half[self.pair], *others).astype(BF16)
        elif stage == 2:
            total = together(*(self.by_group[k] for k in range(self.ways)))
            self.every[self.core, self.pair] = total.astype(BF16)


def summings(kinds, ins, outs, scratch):
    found, at = [], 0
    for (kind, many), local, out in zip(kinds, ins, outs):
        found.append(Summing(kind, local, out, scratch[at : at + many]))
        at += many
    return found


class Side:
    def __init__(self, src, dst, sems):
        self.src, self.dst, self.sems = src, dst, sems
        self.count, self.me = lax.axis_size("expert"), lax.axis_index("expert")

    @staticmethod
    def scratch(count):
        return pltpu.SemaphoreType.DMA((2, count))

    def copy(self, k):
        to = lax.rem(self.me + k, self.count)
        return pltpu.make_async_remote_copy(
            src_ref=self.src.at[to],
            dst_ref=self.dst.at[self.me],
            send_sem=self.sems.at[0, k],
            recv_sem=self.sems.at[1, k],
            device_id=(lax.axis_index("batch"), to),
            device_id_type=MESH,
        )

    def own(self):
        return pltpu.make_async_copy(
            self.src.at[self.me], self.dst.at[self.me], self.sems.at[0, 0]
        )

    def start(self, part=0, parts=((0, 1),)):
        if part == 0:
            self.own().start()
        least, most = (1 + round(share * (self.count - 1)) for share in parts[part])
        for k in range(least, most):
            self.copy(k).start()

    def wait(self):
        self.own().wait()
        for k in range(1, self.count):
            self.copy(k).wait()


def greet_others():
    barrier = pltpu.get_barrier_semaphore()
    group, place = lax.axis_index("batch"), lax.axis_index("expert")
    ways, count = lax.axis_size("batch"), lax.axis_size("expert")
    others = [(group, lax.rem(place + k, count)) for k in range(1, count)]
    others += [(lax.rem(group + k, ways), place) for k in range(1, ways)]
    for device in others:
        pl.semaphore_signal(barrier, inc=1, device_id=device, device_id_type=MESH)
    pl.semaphore_wait(barrier, len(others))


def greet_experts():
    barrier = pltpu.get_barrier_semaphore()
    count, me = lax.axis_size("expert"), lax.axis_index("expert")
    for k in range(1, count):
        device = (lax.axis_index("batch"), lax.rem(me + k, count))
        pl.semaphore_signal(barrier, inc=1, device_id=device, device_id_type=MESH)
    pl.semaphore_wait(barrier, count - 1)


def gelu_parts(v):
    size = jnp.abs(v) * 0.7071067811865476
    t = 1.0 / (1.0 + 0.3275911 * size)
    bell = jnp.exp2(v * v * (-0.5 * LOG2E))
    poly = t * (
        0.127414796
        + t * (-0.142248368 + t * (0.7107068705 + t * (-0.7265760135 + t * 0.5307027145)))
    )
    tail = poly * bell
    phi = jnp.where(v >= 0.0, 1.0 - tail, tail)
    return v * phi, phi + v * (bell * 0.3989422804014327)


FF_TILE = 512


def experts_kernel(slots, tile, *refs):
    normed_ref, row_ref, col_ref, router_ref, upstream_ref, in_hbm, out_hbm = refs[:7]
    grad_ref, result_ref, in_grad_hbm, out_grad_hbm, router_grad_ref = refs[7:12]
    w_in, w_out, sent, got, home, slot_grad, active, hid_grad, row_grad = refs[12:21]
    in_grad, out_grad, there_sems, back_sems, load_sems, store_sems, router = refs[21:]
    back, rows = sent, row_grad
    count, me = lax.axis_size("expert"), lax.axis_index("expert")
    width, hidden = w_in.shape
    total = count * slots
    tiles = hidden // tile
    router[...] = padded_rows(router_ref, LANES)
    loads = [
        pltpu.make_async_copy(in_hbm.at[0], w_in, load_sems.at[0]),
        pltpu.make_async_copy(out_hbm.at[0], w_out, load_sems.at[1]),
    ]
    for load in loads:
        load.start()
    greet_experts()
    there = Side(sent, got, there_sems)
    returning = Side(back, home, back_sems)
    tokens = normed_ref.shape[0]
    slot_id = lax.broadcasted_iota(jnp.int32, (slots, tokens), 0)

    def dispatch(k, carry):
        to = lax.rem(me + k, count)
        picked = (slot_id + to * slots == row_ref[...]).astype(F32).astype(BF16)
        chunk = jnp.dot(picked, normed_ref[...], preferred_element_type=F32).astype(BF16)
        sent[to] = chunk

        @pl.when(k < count)
        def _():
            there.copy(k).start()

        @pl.when(k == count)
        def _():
            got[me] = chunk

        return carry

    lax.fori_loop(1, count + 1, dispatch, 0)
    for k in range(1, count):
        there.copy(k).wait()

    x = got[...].reshape(total, width)
    logits = lax.dot_general(
        x, router[...], (((1,), (1,)), ((), ())), preferred_element_type=F32
    )
    lane = lax.broadcasted_iota(jnp.int32, logits.shape, 1)
    logits = jnp.where(lane < count, logits, -1e30)
    scores = jnp.exp(logits - jnp.max(logits, axis=1, keepdims=True))
    probs = scores / jnp.sum(scores, axis=1, keepdims=True)
    mine = (lane == me).astype(F32)
    gate = jnp.sum(probs * mine, axis=1, keepdims=True)
    slot_grad[...] = (gate * upstream_ref[...].reshape(total, width).astype(F32)).astype(BF16)
    row_grad[...] = jnp.zeros(row_grad.shape, F32)
    for load in loads:
        load.wait()

    def inward(t, picked):
        at = pl.ds(pl.multiple_of(t * tile, tile), tile)
        pre = jnp.dot(
            got[...].reshape(total, width), w_in[:, at], preferred_element_type=F32
        )
        act_grad = lax.dot_general(
            slot_grad[...], w_out[at, :], (((1,), (1,)), ((), ())), preferred_element_type=F32
        )
        value, slope = gelu_parts(pre)
        active[:, at] = value.astype(BF16)
        low = (act_grad * slope).astype(BF16)
        hid_grad[:, at] = low
        row_grad[...] += lax.dot_general(
            low, w_in[:, at], (((1,), (1,)), ((), ())), preferred_element_type=F32
        )
        return picked + jnp.sum(value * act_grad, axis=1, keepdims=True)

    picked = lax.fori_loop(0, tiles, inward, jnp.zeros((total, 1), F32))
    logit_grad = (picked * (mine - probs)).astype(BF16)
    whole = row_grad[...] + jnp.dot(logit_grad, router[...], preferred_element_type=F32)
    back[...] = whole.astype(BF16).reshape(count, slots, width)
    home[me] = back[me]
    for k in range(1, count):
        returning.copy(k).start()

    router_grad = lax.dot_general(
        logit_grad,
        got[...].reshape(total, width),
        (((0,), (0,)), ((), ())),
        preferred_element_type=F32,
    )
    router_grad_ref[...] = router_grad[:count]
    rows[...] = jnp.zeros(rows.shape, F32)

    def stores(t):
        at = pl.ds(pl.multiple_of(t * tile, tile), tile)
        return (
            pltpu.make_async_copy(in_grad.at[:, at], in_grad_hbm.at[:, at], store_sems.at[0, t]),
            pltpu.make_async_copy(out_grad.at[at], out_grad_hbm.at[at], store_sems.at[1, t]),
        )

    def outward(t, carry):
        at = pl.ds(pl.multiple_of(t * tile, tile), tile)
        over_rows = (((0,), (0,)), ((), ()))
        in_grad[:, at] = lax.dot_general(
            got[...].reshape(total, width), hid_grad[:, at], over_rows, preferred_element_type=F32
        ).astype(BF16)
        out_grad[at, :] = lax.dot_general(
            active[:, at], slot_grad[...], over_rows, preferred_element_type=F32
        ).astype(BF16)
        for store in stores(t):
            store.start()
        rows[...] += jnp.dot(active[:, at], w_out[at, :], preferred_element_type=F32)
        return carry

    lax.fori_loop(0, tiles, outward, 0)
    result_ref[...] = (gate * rows[...]).astype(BF16).reshape(count, slots, width)
    for k in range(1, count):
        returning.copy(k).wait()
    slot_id = lax.broadcasted_iota(jnp.int32, (tokens, total), 1)
    chosen = (slot_id == col_ref[...]).astype(F32).astype(BF16)
    grad_ref[...] = jnp.dot(
        chosen, home[...].reshape(total, width), preferred_element_type=F32
    )
    for t in range(tiles):
        for store in stores(t):
            store.wait()


def run_experts(
    normed, row, col, router, upstream, expert_in, expert_out, slots, collective_id
):
    tokens, width = normed.shape
    count = lax.axis_size("expert")
    hidden = expert_in.shape[2]
    tile = FF_TILE if hidden % FF_TILE == 0 else hidden
    total = count * slots
    exchanged = (count, slots, width)
    vmem = pl.BlockSpec(memory_space=pltpu.VMEM)
    hbm = pl.BlockSpec(memory_space=pl.ANY)
    grad, result, in_grad, out_grad, router_grad = pl.pallas_call(
        functools.partial(experts_kernel, slots, tile),
        out_shape=[
            jax.ShapeDtypeStruct((tokens, width), F32),
            jax.ShapeDtypeStruct(exchanged, BF16),
            jax.ShapeDtypeStruct((width, hidden), BF16),
            jax.ShapeDtypeStruct((hidden, width), BF16),
            jax.ShapeDtypeStruct(router.shape, F32),
        ],
        in_specs=[vmem] * 5 + [hbm] * 2,
        out_specs=[vmem, vmem, hbm, hbm, vmem],
        scratch_shapes=[
            pltpu.VMEM((width, hidden), BF16),
            pltpu.VMEM((hidden, width), BF16),
            pltpu.VMEM(exchanged, BF16),
            pltpu.VMEM(exchanged, BF16),
            pltpu.VMEM(exchanged, BF16),
            pltpu.VMEM((total, width), BF16),
            pltpu.VMEM((total, hidden), BF16),
            pltpu.VMEM((total, hidden), BF16),
            pltpu.VMEM((total, width), F32),
            pltpu.VMEM((width, hidden), BF16),
            pltpu.VMEM((hidden, width), BF16),
            Side.scratch(count),
            Side.scratch(count),
            pltpu.SemaphoreType.DMA((2,)),
            pltpu.SemaphoreType.DMA((2, hidden // tile)),
            pltpu.VMEM((LANES, width), BF16),
        ],
        compiler_params=params(collective_id=collective_id, has_side_effects=True),
        name="experts",
    )(normed, row, col, router, upstream, expert_in, expert_out)
    return grad, result, in_grad, out_grad, router_grad


def in_segments(value_ref, turn):
    steps = value_ref.shape[0] // SEGS
    parts = []
    for lane in range(turn.shape[0]):
        lanes = slice(lane * LANES, (lane + 1) * LANES)
        for s in range(SEGS):
            rows = value_ref[s * steps : (s + 1) * steps, lanes].astype(F32)
            turn[lane, pl.ds(s, steps, stride=SEGS), :] = rows
        parts.append(turn[lane].astype(BF16))
    return jnp.concatenate(parts, axis=1)


def over_blocks(width, size, body):
    def one(n, carry):
        body(pl.ds(pl.multiple_of(n * size, size), size))
        return carry

    lax.fori_loop(0, width // size, one, 0)


def slot_targets(route, experts, capacity, slots):
    count = route.shape[1]
    steps = count // SEGS
    high = max(experts, 16)
    onehot = lax.broadcasted_iota(jnp.int32, (high, count), 0) == route
    onehot = onehot.astype(F32)
    token_of = lambda p: (p % SEGS) * steps + p // SEGS
    first = token_of(lax.broadcasted_iota(jnp.int32, (count, count), 0))
    second = token_of(lax.broadcasted_iota(jnp.int32, (count, count), 1))
    earlier = (first <= second).astype(F32).astype(BF16)
    running = jnp.dot(onehot.astype(BF16), earlier, preferred_element_type=F32)
    place = (jnp.sum(running * onehot, axis=0, keepdims=True) - 1.0).astype(jnp.int32)
    return jnp.where(place < capacity, route * slots + place, -1)


def forward_kernel(sizes, *refs):
    states, steps, rank, capacity = sizes
    tokens_hbm, upstream_hbm, in_proj_hbm, out_proj_hbm = refs[:4]
    route_ref, gain_ref, gain_two_ref, conv_ref, bias_ref, x_proj_ref, dt_proj_ref = refs[4:11]
    dt_bias_ref, skip_ref, rate_log_ref = refs[11:14]
    ssm_ref, held_ref, gated_ref, hidden_ref, normed_two_ref, row_ref, col_ref, before_ref = refs[14:22]
    side_out = refs[22]
    kept_hbm, refs = refs[23:32], refs[32:]
    tokens_in, upstream_in, in_proj, out_proj, turn, ext_in, tail, sent = refs[:8]
    kept, refs = refs[8:17], refs[17:]
    tokens, upstream, normed, inner, gate_z, mixed, pre, delta, proj = kept
    in_s, bb, cb, run_a, run_b, side_sems, load_sems, keep_sems, halo_sems = refs[:9]
    x_proj, dt_proj, small, before, carry_refs = *refs[9:13], refs[13:]
    phase, block = pl.program_id(0), pl.program_id(1)
    blocks = carry_refs[2].shape[1]
    carries = Carries(states, blocks, True, *carry_refs)
    side = Side(sent, side_out, side_sems)
    parts = ((0, 2 / 7), (2 / 7, 3 / 7), (3 / 7, 1))
    rate2 = -jnp.exp(rate_log_ref[...]) * LOG2E
    rates = [over_sublanes(rate2[n : n + 1, :]) for n in range(states)]
    here = pl.ds(pl.multiple_of(block * LANES, LANES), LANES)
    count, width = tokens.shape
    inner_width = inner.shape[1]
    reach = conv_ref.shape[0] - 1
    rim = reach * SEGS
    experts, me = lax.axis_size("expert"), lax.axis_index("expert")
    slots = sent.shape[1]
    half = inner_width
    loads = [
        pltpu.make_async_copy(src, dst, load_sems.at[i])
        for i, (src, dst) in enumerate(
            (
                (tokens_hbm.at[0], tokens_in),
                (in_proj_hbm.at[:, :half], in_proj.at[:, :half]),
                (in_proj_hbm.at[:, half:], in_proj.at[:, half:]),
                (upstream_hbm.at[0], upstream_in),
                (out_proj_hbm, out_proj),
            )
        )
    ]
    keeps = [
        pltpu.make_async_copy(src, dst, keep_sems.at[i])
        for i, (src, dst) in enumerate(zip(kept, kept_hbm))
    ]

    def front():
        for load in loads:
            load.start()
        small[0:1, :] = as_row(skip_ref)
        small[1:2, :] = as_row(bias_ref)
        small[2:3, :] = as_row(dt_bias_ref)
        x_proj[...] = padded_rows(x_proj_ref, LANES)
        dt_proj[...] = padded_rows(dt_proj_ref, LANES)
        loads[0].wait()
        tokens[...] = in_segments(tokens_in, turn)
        normed[...] = rms(tokens[...].astype(F32), as_row(gain_ref)).astype(BF16)
        loads[1].wait()

        def to_inner(at):
            inner[:, at] = jnp.dot(
                normed[...], in_proj[:, at], preferred_element_type=F32
            ).astype(BF16)

        over_blocks(inner_width, 4 * LANES, to_inner)
        last = inner[count - rim - rim % 16 :, :].astype(F32)[rim % 16 :]
        for k in range(reach):
            tail[k : k + 1, :] = last[(k + 1) * SEGS - 1 : (k + 1) * SEGS]
        greet_experts()
        halo = pltpu.make_async_remote_copy(
            src_ref=tail,
            dst_ref=before,
            send_sem=halo_sems.at[0],
            recv_sem=halo_sems.at[1],
            device_id=(lax.axis_index("batch"), lax.rem(me + 1, experts)),
            device_id_type=MESH,
        )

        @pl.when(me < experts - 1)
        def _():
            halo.start()

        @pl.when(me == 0)
        def _():
            before[...] = jnp.zeros(before.shape, F32)

        loads[2].wait()

        def to_gate(at):
            lanes = pl.ds(pl.multiple_of(half + at.start, LANES), at.size)
            gate_z[:, at] = jnp.dot(normed[...], in_proj[:, lanes], preferred_element_type=F32)

        over_blocks(inner_width, 4 * LANES, to_gate)
        for keep in keeps[2:5]:
            keep.start()
        keeps[0].start()
        loads[3].wait()
        upstream[...] = in_segments(upstream_in, turn)
        keeps[1].start()
        target = slot_targets(route_ref[...], experts, capacity, slots)
        row_ref[...] = target
        wide = jnp.broadcast_to(target.astype(F32), (SEGS, count))
        col_ref[...] = jnp.transpose(wide)[:, :1].astype(jnp.int32)
        slot_id = lax.broadcasted_iota(jnp.int32, (slots, count), 0)

        def dispatch(e, carry):
            picked = (slot_id + e * slots == row_ref[...]).astype(F32).astype(BF16)
            sent[e] = jnp.dot(picked, upstream[...], preferred_element_type=F32).astype(BF16)
            return carry

        lax.fori_loop(0, experts, dispatch, 0)
        side.start(0, parts)

        @pl.when(me < experts - 1)
        def _():
            halo.wait_send()

        @pl.when(me > 0)
        def _():
            halo.wait_recv()

        before_ref[...] = before[...]

        def to_mixed(at):
            own = inner[:, at].astype(F32)
            for k in range(reach):
                tile = own[count - rim + k * SEGS : count - rim + (k + 1) * SEGS]
                ext_in[k * SEGS : (k + 1) * SEGS, at] = shifted_in(
                    tile, before[k : k + 1, at], True
                )
            ext_in[rim:, at] = own
            total = jnp.broadcast_to(small[1:2, at], own.shape)
            for k in range(reach + 1):
                total = total + conv_ref[k : k + 1, at] * ext_in[k * SEGS : k * SEGS + count, at]
            mixed[:, at] = silu(total).astype(BF16)

        over_blocks(inner_width, 2 * LANES, to_mixed)
        keeps[5].start()
        proj[...] = lax.dot_general(
            mixed[...], x_proj[...], (((1,), (1,)), ((), ())), preferred_element_type=F32
        )
        keeps[8].start()

        def to_delta(at):
            own = jnp.dot(
                proj[...].astype(BF16), dt_proj[:, at], preferred_element_type=F32
            )
            own = own + small[2:3, at]
            pre[:, at] = own
            delta[:, at] = softplus(own)

        over_blocks(inner_width, 2 * LANES, to_delta)
        keeps[6].start()
        keeps[7].start()

    @pl.when((phase == 0) & (block == 0))
    def _():
        front()

    for part, (at_phase, at_block) in enumerate(((0, blocks // 2), (1, 1))):

        @pl.when((phase == at_phase) & (block == at_block))
        def _():
            side.start(part + 1, parts)

    def ends(first):
        in_s[...] = delta[:, here] * mixed[:, here].astype(F32)
        sums = jnp.sum(delta[:, here].reshape(steps, SEGS, LANES), axis=0)

        def one(j, held):
            rows = tile_rows(j)
            d, u = delta[rows, here], in_s[rows, :]
            tile = proj[rows, :] if first else None
            new = []
            for n in range(states):
                if first:
                    b = over_lanes(tile[:, rank + n : rank + n + 1])
                    bb[j, n] = b
                    cb[j, n] = over_lanes(tile[:, rank + states + n : rank + states + n + 1])
                else:
                    b = bb[j, n]
                new.append(jnp.exp2(d * rates[n]) * held[n] + u * b)
            return tuple(new)

        zero = jnp.zeros((SEGS, LANES), F32)
        held = lax.fori_loop(0, steps, one, (zero,) * states, unroll=4)
        carries.put(block, held, sums, rates, run_a, run_b)

    @pl.when((phase == 0) & (block == 0))
    def _():
        ends(True)

    @pl.when((phase == 0) & (block > 0))
    def _():
        ends(False)

    @pl.when(phase == 1)
    def _():
        carries.await_group(block)
        start = carries.starts(block, rate2, run_a, run_b)
        own = mixed[:, here].astype(F32)
        in_s[...] = delta[:, here] * own
        ssm_ref[...] = small[0:1, here] * own
        for n in range(states):
            held_ref[0, 0, n] = start[n]

        def one(j, held):
            rows = tile_rows(j)
            d, u = delta[rows, here], in_s[rows, :]
            total = ssm_ref[rows, :]
            new = []
            for n in range(states):
                h = jnp.exp2(d * rates[n]) * held[n] + u * bb[j, n]
                held_ref[0, j + 1, n] = h
                total = total + cb[j, n] * h
                new.append(h)
            ssm_ref[rows, :] = total
            return tuple(new)

        lax.fori_loop(0, steps, one, tuple(start), unroll=4)
        gated_ref[:, here] = (ssm_ref[...] * silu(gate_z[:, here])).astype(BF16)

    @pl.when((phase == 1) & (block == blocks - 1))
    def _():
        loads[4].wait()
        hidden = tokens[...].astype(F32) + jnp.dot(
            gated_ref[...], out_proj[...], preferred_element_type=F32
        )
        hidden_ref[...] = hidden
        normed_two_ref[...] = rms(hidden, as_row(gain_two_ref)).astype(BF16)
        side.wait()
        for keep in keeps:
            keep.wait()


def forward(
    tokens,
    upstream,
    in_proj,
    out_proj,
    route,
    gain_one,
    gain_two,
    conv_weight,
    conv_bias,
    x_proj,
    dt_proj,
    dt_bias,
    skip,
    rate_log,
    sizes,
    collective_id,
):
    rank, capacity, slots = sizes
    count, width = tokens.shape[1:]
    inner_width = out_proj.shape[0]
    states, steps, blocks = rate_log.shape[0], count // SEGS, inner_width // LANES
    experts = lax.axis_size("expert")
    rim = (conv_weight.shape[0] - 1) * SEGS
    vmem, hbm = (pl.BlockSpec(memory_space=m) for m in (pltpu.VMEM, pl.ANY))
    spread = pltpu.VMEM((steps, states, SEGS, LANES), F32)
    run = pltpu.VMEM((blocks, states, SEGS, LANES), F32)
    whole = lambda *shape: pl.BlockSpec(shape, lambda p, c: (0,) * len(shape))
    shape_of = jax.ShapeDtypeStruct
    kept = [
        shape_of((count, width), BF16),
        shape_of((count, width), BF16),
        shape_of((count, width), BF16),
        shape_of((count, inner_width), BF16),
        shape_of((count, inner_width), F32),
        shape_of((count, inner_width), BF16),
        shape_of((count, inner_width), F32),
        shape_of((count, inner_width), F32),
        shape_of((count, LANES), F32),
    ]
    exchanged = (experts, slots, width)
    out = pl.pallas_call(
        functools.partial(forward_kernel, (states, steps, rank, capacity)),
        grid=(2, blocks),
        out_shape=[
            shape_of((count, inner_width), F32),
            shape_of((blocks, steps + 1, states, SEGS, LANES), F32),
            shape_of((count, inner_width), BF16),
            shape_of((count, width), F32),
            shape_of((count, width), BF16),
            shape_of((1, count), jnp.int32),
            shape_of((count, 1), jnp.int32),
            shape_of((SEGS, inner_width), F32),
            shape_of(exchanged, BF16),
        ]
        + kept,
        in_specs=[hbm] * 4
        + [vmem] * 9
        + [pl.BlockSpec((states, LANES), lambda p, c: (0, c))],
        out_specs=[
            pl.BlockSpec((count, LANES), lambda p, c: (0, p * c)),
            pl.BlockSpec((1, steps + 1, states, SEGS, LANES), lambda p, c: (p * c, 0, 0, 0, 0)),
            whole(count, inner_width),
            whole(count, width),
            whole(count, width),
            whole(1, count),
            whole(count, 1),
            vmem,
            hbm,
        ]
        + [hbm] * len(kept),
        scratch_shapes=[
            pltpu.VMEM((count, width), BF16),
            pltpu.VMEM((count, width), BF16),
            pltpu.VMEM(in_proj.shape, BF16),
            pltpu.VMEM(out_proj.shape, BF16),
            pltpu.VMEM((width // LANES, count, LANES), F32),
            pltpu.VMEM((count + rim, inner_width), F32),
            pltpu.VMEM((SEGS, inner_width), F32),
            pltpu.VMEM(exchanged, BF16),
        ]
        + [pltpu.VMEM(k.shape, k.dtype) for k in kept]
        + [
            pltpu.VMEM((count, LANES), F32),
            spread,
            spread,
            run,
            run,
            Side.scratch(experts),
            pltpu.SemaphoreType.DMA((5,)),
            pltpu.SemaphoreType.DMA((len(kept),)),
            pltpu.SemaphoreType.DMA((2,)),
            pltpu.VMEM((LANES, inner_width), BF16),
            pltpu.VMEM((LANES, inner_width), BF16),
            pltpu.VMEM((SEGS, inner_width), F32),
            pltpu.VMEM((SEGS, inner_width), F32),
        ]
        + Carries.scratch(states, blocks, experts),
        compiler_params=params(collective_id=collective_id, has_side_effects=True),
        name="forward",
    )(
        tokens,
        upstream,
        in_proj,
        out_proj,
        route,
        gain_one,
        gain_two,
        conv_weight,
        conv_bias,
        x_proj,
        dt_proj,
        dt_bias,
        skip,
        rate_log,
    )
    return out[:9], out[9:]


def backward_kernel(states, steps, rank, kinds, *refs):
    many = len(kinds)
    sum_in, refs = refs[:many], refs[many:]
    pre_ref, delta_ref, in_ref, g_ref, bc_ref, rate_ref, skip_ref, held_ref, side_in = refs[:9]
    sum_out, refs = refs[9 : 9 + many], refs[9 + many :]
    pre_grad_ref, mixed_grad_ref, rate_grad_ref, skip_grad_ref, bias_grad_ref = refs[:5]
    bc_grad_ref, side_out = refs[5:7]
    in_s, rate_sum, in_sum, bb, cb, b_acc, c_acc, run_a, run_b, side_sems = refs[7:17]
    skip_row, carry_refs, sum_refs = refs[17], refs[18:23], refs[23:]
    phase, block = pl.program_id(0), pl.program_id(1)
    here = pl.ds(pl.multiple_of(block * LANES, LANES), LANES)
    blocks = carry_refs[2].shape[1]
    carries = Carries(states, blocks, False, *carry_refs)
    sums = summings(kinds, sum_in, sum_out, sum_refs)
    side = Side(side_in, side_out, side_sems)
    rate2 = -jnp.exp(rate_ref[...]) * LOG2E
    rates = [over_sublanes(rate2[n : n + 1, :]) for n in range(states)]
    zero = jnp.zeros((SEGS, LANES), F32)

    @pl.when((phase == 0) & (block == 0))
    def _():
        skip_row[...] = as_row(skip_ref)
        greet_others()
        for item in sums:
            item.start(0)

    @pl.when((phase == 0) & (block == blocks - 3))
    def _():
        for item in sums:
            if not item.pairs_first:
                item.advance(0)

    @pl.when((phase == 1) & (block == 1))
    def _():
        for item in sums:
            if item.pairs_first:
                item.advance(0)

    @pl.when((phase == 1) & (block == blocks // 2 - 1))
    def _():
        side.start()

    def ends(first):
        sums = jnp.sum(delta_ref[...].reshape(steps, SEGS, LANES), axis=0)

        def one(i, held):
            j = steps - 1 - i
            d, g = delta_ref[tile_rows(j), :], g_ref[tile_rows(j), :]
            tile = bc_ref[tile_rows(j), :] if first else None
            new = []
            for n in range(states):
                if first:
                    c = over_lanes(tile[:, rank + states + n : rank + states + n + 1])
                    bb[j, n] = over_lanes(tile[:, rank + n : rank + n + 1])
                    cb[j, n] = c
                else:
                    c = cb[j, n]
                new.append(jnp.exp2(d * rates[n]) * (held[n] + g * c))
            return tuple(new)

        held = lax.fori_loop(0, steps, one, (zero,) * states, unroll=4)
        carries.put(block, held, sums, rates, run_a, run_b)

    @pl.when((phase == 0) & (block == 0))
    def _():
        ends(True)

    @pl.when((phase == 0) & (block > 0))
    def _():
        ends(False)

    def grads(first, last):
        start = carries.starts(block, rate2, run_a, run_b)
        delta, g = delta_ref[...], g_ref[...]
        mixed = in_ref[...].astype(F32)
        in_s[...] = delta * mixed
        place = lax.broadcasted_iota(jnp.int32, (SEGS, LANES), 1)

        def one(i, carry):
            edge, rate_acc = carry
            j = steps - 1 - i
            rows = tile_rows(j)
            d, u, g = delta_ref[rows, :], in_s[rows, :], g_ref[rows, :]
            by_rate = by_b = sums = zero
            new_edge, new_acc = [], []
            for n in range(states):
                b, c = bb[j, n], cb[j, n]
                q = c * g + edge[n]
                e = jnp.exp2(d * rates[n]) * q
                v = e * held_ref[0, j, n]
                by_rate = by_rate + rates[n] * v
                by_b = by_b + b * q
                to_b = q * u
                to_c = g * held_ref[0, j + 1, n]
                if not first:
                    to_b = b_acc[j, n] + to_b
                    to_c = c_acc[j, n] + to_c
                if last:
                    sums = jnp.where(place == rank + n, jnp.sum(to_b, axis=1, keepdims=True), sums)
                    to_c = jnp.sum(to_c, axis=1, keepdims=True)
                    sums = jnp.where(place == rank + states + n, to_c, sums)
                else:
                    b_acc[j, n] = to_b
                    c_acc[j, n] = to_c
                new_edge.append(e)
                new_acc.append(rate_acc[n] + d * v)
            rate_sum[rows, :] = by_rate
            in_sum[rows, :] = by_b
            if last:
                bc_grad_ref[rows, :] = sums
            return tuple(new_edge), tuple(new_acc)

        _, rate_acc = lax.fori_loop(
            0, steps, one, (tuple(start), (zero,) * states), unroll=2
        )
        for n in range(states):
            rate_grad_ref[n : n + 1, :] = (
                LN2 * rate2[n : n + 1, :] * jnp.sum(rate_acc[n], axis=0, keepdims=True)
            )
        by_b = in_sum[...]
        pre_grad = (LN2 * rate_sum[...] + mixed * by_b) * jax.nn.sigmoid(pre_ref[...])
        pre_grad_ref[...] = pre_grad.astype(BF16)
        bias_grad_ref[...] = jnp.sum(pre_grad, axis=0, keepdims=True)
        mixed_grad_ref[...] = delta * by_b + skip_row[:, here] * g
        skip_grad_ref[...] = jnp.sum(g * mixed, axis=0, keepdims=True)

    @pl.when(phase == 1)
    def _():
        carries.await_group(block)

    @pl.when((phase == 1) & (block == 0))
    def _():
        grads(True, False)

    @pl.when((phase == 1) & (block > 0) & (block < blocks - 1))
    def _():
        grads(False, False)

    @pl.when((phase == 1) & (block == blocks - 1))
    def _():
        grads(False, True)
        side.wait()
        for item in sums:
            item.wait(1)
            item.add(1)


def mixer_grads(
    pre, delta, mixed, ssm_grad, bc, rate_log, skip, held, beside, rank, items, collective_id
):
    count, width = delta.shape
    states, steps, blocks = rate_log.shape[0], count // SEGS, width // LANES
    block = pl.BlockSpec((count, LANES), lambda p, c: (0, c))
    late = lambda rows: pl.BlockSpec((rows, LANES), lambda p, c: (0, p * c))
    spread = pltpu.VMEM((steps, states, SEGS, LANES), F32)
    run = pltpu.VMEM((blocks, states, SEGS, LANES), F32)
    flat = pltpu.VMEM((count, LANES), F32)
    sum_scratch = [item.first_scratch() for item in items]
    kinds = tuple((item.kind(), len(refs)) for item, refs in zip(items, sum_scratch))
    spread_specs = [
        pl.BlockSpec(item.spread_shape().shape, lambda p, c, rank=len(item.spread_shape().shape): (0,) * rank)
        for item in items
    ]
    outs = pl.pallas_call(
        functools.partial(backward_kernel, states, steps, rank, kinds),
        grid=(2, blocks),
        out_shape=[item.spread_shape() for item in items]
        + [
            jax.ShapeDtypeStruct((count, width), BF16),
            jax.ShapeDtypeStruct((count, width), F32),
            jax.ShapeDtypeStruct((states, width), F32),
            jax.ShapeDtypeStruct((1, width), F32),
            jax.ShapeDtypeStruct((1, width), F32),
            jax.ShapeDtypeStruct((count, LANES), F32),
            jax.ShapeDtypeStruct(beside.shape, beside.dtype),
        ],
        in_specs=[pl.BlockSpec(memory_space=pl.ANY)] * len(items)
        + [
            late(count),
            block,
            late(count),
            block,
            pl.BlockSpec(bc.shape, lambda p, c: (0, 0)),
            pl.BlockSpec((states, LANES), lambda p, c: (0, c)),
            pl.BlockSpec(memory_space=pltpu.VMEM),
            pl.BlockSpec((1, steps + 1, states, SEGS, LANES), lambda p, c: (p * c, 0, 0, 0, 0)),
            pl.BlockSpec(memory_space=pl.ANY),
        ],
        out_specs=spread_specs
        + [late(count), late(count), late(states), late(1), late(1)]
        + [pl.BlockSpec((count, LANES), lambda p, c: (0, 0)), pl.BlockSpec(memory_space=pl.ANY)],
        scratch_shapes=[flat, flat, flat, spread, spread, spread, spread, run, run]
        + [Side.scratch(lax.axis_size("expert")), pltpu.VMEM((1, width), F32)]
        + Carries.scratch(states, blocks, lax.axis_size("expert"))
        + [ref for refs in sum_scratch for ref in refs],
        compiler_params=params(collective_id=collective_id, has_side_effects=True),
        name="mixer_grads",
    )(*(item.local for item in items), pre, delta, mixed, ssm_grad, bc, rate_log, skip, held, beside)
    return outs


def shifted_in(tile, row, forward):
    if forward:
        return jnp.concatenate([row, tile[: SEGS - 1]], axis=0)
    return jnp.concatenate([tile[1:], row], axis=0)


def middle_kernel(*refs):
    hidden_ref, grad_ref, upstream_ref, gain_ref, normed_ref = refs[:5]
    gated_ref, ssm_ref, gate_ref, out_proj_ref = refs[5:9]
    hidden_grad_ref, gain_out, ssm_grad_ref, gate_grad_ref, out_local_ref, gate_local_ref = refs[9:15]
    branch = refs[15]

    @pl.when(pl.program_id(0) == 0)
    def _():
        to_hidden, to_gain = rms_back(hidden_ref[...], as_row(gain_ref), grad_ref[...])
        total = upstream_ref[...].astype(F32) + to_hidden
        hidden_grad_ref[...] = total
        branch[...] = total.astype(BF16)
        gain_out[...] = to_gain[None]

    over_rows = (((0,), (0,)), ((), ()))
    out_local_ref[...] = lax.dot_general(
        gated_ref[...], branch[...], over_rows, preferred_element_type=F32
    ).astype(BF16)
    gated_grad = lax.dot_general(
        branch[...], out_proj_ref[...], (((1,), (1,)), ((), ())), preferred_element_type=F32
    )
    gate = gate_ref[...]
    s = jax.nn.sigmoid(gate)
    ssm_grad_ref[...] = gated_grad * (gate * s)
    low = (gated_grad * ssm_ref[...] * (s * (1.0 + gate * (1.0 - s)))).astype(BF16)
    gate_grad_ref[...] = low
    gate_local_ref[...] = lax.dot_general(
        normed_ref[...], low, over_rows, preferred_element_type=F32
    ).astype(BF16)


def middle(hidden, grad, upstream, gain, normed, gated, ssm, gate_z, out_proj):
    count, width = hidden.shape
    inner_width = out_proj.shape[0]
    wide = 2 * LANES
    vmem = pl.BlockSpec(memory_space=pltpu.VMEM)
    whole = lambda *shape: pl.BlockSpec(shape, lambda c: (0,) * len(shape))
    lanes = lambda rows: pl.BlockSpec((rows, wide), lambda c: (0, c))
    rows = pl.BlockSpec((wide, width), lambda c: (c, 0))
    shape_of = jax.ShapeDtypeStruct
    return pl.pallas_call(
        middle_kernel,
        grid=(inner_width // wide,),
        out_shape=[
            shape_of((count, width), F32),
            shape_of((1, width), F32),
            shape_of((count, inner_width), F32),
            shape_of((count, inner_width), BF16),
            shape_of((inner_width, width), BF16),
            shape_of((width, inner_width), BF16),
        ],
        in_specs=[vmem] * 5 + [lanes(count)] * 3 + [rows],
        out_specs=[whole(count, width), whole(1, width), lanes(count), lanes(count), rows]
        + [lanes(width)],
        scratch_shapes=[pltpu.VMEM((count, width), BF16)],
        compiler_params=params(),
        name="middle",
    )(hidden, grad, upstream, gain, normed, gated, ssm, gate_z, out_proj)


WIDE = 2 * LANES


def put_by_token(out_ref, value, turn):
    steps = value.shape[0] // SEGS
    for lane in range(turn.shape[0]):
        lanes = slice(lane * LANES, (lane + 1) * LANES)
        turn[lane] = value[:, lanes]
        for s in range(SEGS):
            rows = turn[lane, pl.ds(s, steps, stride=SEGS), :]
            out_ref[s * steps : (s + 1) * steps, lanes] = rows.astype(out_ref.dtype)


def tile_places(pack, flat):
    _, pairs, each = pack.shape[:3]
    across = flat.shape[1] // LANES
    for t in range(2 * pairs * each):
        row, lane = t // across * 16, t % across * LANES
        inside = (slice(row, row + 16), slice(lane, lane + LANES)) if row < flat.shape[0] else None
        yield (t // (pairs * each), t // each % pairs, t % each), inside


def put_tiles(pack, flat):
    for tile, inside in tile_places(pack, flat):
        if inside is None:
            pack[tile] = jnp.zeros((16, LANES), BF16)
        else:
            pack[tile] = flat[inside].astype(BF16)


def get_tiles(flat, pack):
    for tile, inside in tile_places(pack, flat):
        if inside is not None:
            flat[inside] = pack[tile].astype(F32)


def finish_kernel(rank, states, kinds, *refs):
    loads_hbm, refs = refs[:11], refs[11:]
    bc_grad_ref, low_ref, x_proj_ref, dt_proj_ref, conv_ref, bias_ref = refs[:6]
    before_ref, gain_ref, rate_ref, dt_bias_ref, skip_ref, gain_two_ref, router_ref = refs[6:13]
    col_ref, gate_spread, out_spread = refs[13:16]
    output_ref, tokens_grad_ref, in_proj_out, out_proj_out, flat, last_flat = refs[16:22]
    refs = refs[22:]
    loaded, refs = refs[:11], refs[11:]
    pre_grad, mixed_part, mixed, inner, normed, in_proj, gate_grad, tokens, hidden_grad = loaded[:9]
    hidden, home = loaded[9:]
    ext_in, ext_grad, inner_grad, proj_grad, rows, head, after = refs[:7]
    turn, load_sems, halo_sems = refs[7:10]
    small, last_small = SmallSum(*refs[10:17]), SmallSum(*refs[17:24])
    x_proj, dt_proj, bias_row = refs[24:27]
    parts, refs = len(kinds) - 2, refs[27:]
    locals_, sum_refs = refs[:parts], refs[parts:]
    count, width = tokens.shape
    inner_width = inner.shape[1]
    reach = conv_ref.shape[0] - 1
    rim = reach * SEGS
    experts, me = lax.axis_size("expert"), lax.axis_index("expert")
    group = lax.axis_index("batch")
    half = inner_width

    loads = [
        pltpu.make_async_copy(src, dst, load_sems.at[i])
        for i, (src, dst) in enumerate(zip(loads_hbm, loaded))
    ]
    for load in loads:
        load.start()
    ends = [0]
    for ref in locals_:
        ends.append(ends[-1] + ref.shape[2])
    inner_rows = [slice(ends[i], ends[i + 1]) for i in range(parts)]
    gate_sum, out_sum, *inner_sums = summings(
        kinds,
        (gate_spread, out_spread, *locals_),
        (in_proj_out.at[:, half:], out_proj_out)
        + tuple(in_proj_out.at[at, :half] for at in inner_rows),
        sum_refs,
    )
    greet_others()
    gate_sum.begin()
    out_sum.begin()
    x_proj[...] = padded_rows(x_proj_ref, LANES)
    dt_proj[...] = padded_rows(dt_proj_ref, LANES)
    bias_row[...] = as_row(bias_ref)
    low = low_ref[...].astype(BF16)
    flat[...] = jnp.zeros(flat.shape, F32)
    last_flat[...] = jnp.zeros(last_flat.shape, F32)

    loads[0].wait()
    over_inner = (((1,), (1,)), ((), ()))
    over_rows = (((0,), (0,)), ((), ()))
    low_grad = lax.dot_general(
        pre_grad[...], dt_proj[...], over_inner, preferred_element_type=F32
    )
    proj_grad[...] = (low_grad + bc_grad_ref[...]).astype(BF16)

    for load in loads[1:4]:
        load.wait()

    def before_silu(at):
        own = inner[:, at].astype(F32)
        for k in range(reach):
            tile = own[count - rim + k * SEGS : count - rim + (k + 1) * SEGS]
            ext_in[k * SEGS : (k + 1) * SEGS, at] = shifted_in(tile, before_ref[k : k + 1, at], True)
        ext_in[rim:, at] = own
        total = jnp.dot(proj_grad[...], x_proj[:, at], preferred_element_type=F32)
        total = total + mixed_part[:, at]
        conv_pre = jnp.broadcast_to(bias_row[:, at], total.shape)
        for k in range(reach + 1):
            conv_pre = conv_pre + conv_ref[k : k + 1, at] * ext_in[k * SEGS : k * SEGS + count, at]
        total = total * silu_slope(conv_pre)
        ext_grad[:count, at] = total
        for k in range(reach):
            head[k : k + 1, at] = total[k * SEGS : k * SEGS + 1]

    over_blocks(inner_width, WIDE, before_silu)
    halo = pltpu.make_async_remote_copy(
        src_ref=head,
        dst_ref=after,
        send_sem=halo_sems.at[0],
        recv_sem=halo_sems.at[1],
        device_id=(group, lax.rem(me + experts - 1, experts)),
        device_id_type=MESH,
    )

    @pl.when(me > 0)
    def _():
        halo.start()

    @pl.when(me == experts - 1)
    def _():
        after[...] = jnp.zeros(after.shape, F32)

    at_dt = rank + 2 * states
    x_local = lax.dot_general(proj_grad[...], mixed[...], over_rows, preferred_element_type=F32)
    flat[:at_dt, :] = x_local[:at_dt]
    dt_local = lax.dot_general(low, pre_grad[...], over_rows, preferred_element_type=F32)
    flat[at_dt : at_dt + rank, :] = dt_local[:rank]
    at = at_dt + rank + states
    flat[at_dt + rank : at, :] = rate_ref[...]
    flat[at : at + 1, :] = dt_bias_ref[...]
    flat[at + 1 : at + 2, :] = skip_ref[...]
    flat[at + 2 : at + 3, :width] = gain_two_ref[...]
    fold = router_ref.shape[0] // 2
    flat[at + 3 : at + 3 + fold, :width] = router_ref[:fold, :]
    flat[at + 3 : at + 3 + fold, width:] = router_ref[fold:, :]
    put_tiles(small.pack, flat)
    small.start(0)
    for load in loads[4:7]:
        load.wait()
    rows[...] = lax.dot_general(
        gate_grad[...], in_proj[:, half:], over_inner, preferred_element_type=F32
    )

    @pl.when(me > 0)
    def _():
        halo.wait_send()

    @pl.when(me < experts - 1)
    def _():
        halo.wait_recv()

    def before_taps(at):
        for k in range(reach):
            tile = ext_grad[k * SEGS : (k + 1) * SEGS, at]
            ext_grad[count + k * SEGS : count + (k + 1) * SEGS, at] = shifted_in(
                tile, after[k : k + 1, at], False
            )
        total = conv_ref[0:1, at] * ext_grad[rim : rim + count, at]
        for k in range(1, reach + 1):
            first = (reach - k) * SEGS
            total = total + conv_ref[k : k + 1, at] * ext_grad[first : first + count, at]
        inner_grad[:, at] = total.astype(BF16)

    over_blocks(inner_width, WIDE, before_taps)
    chunk = width // experts
    share = inner_width // lax.axis_size("batch")

    def to_in_proj(at):
        total = lax.dot_general(
            normed[...], inner_grad[:, at], over_rows, preferred_element_type=F32
        ).astype(BF16)
        for e in range(experts):
            own = total[e * chunk : (e + 1) * chunk]
            for ref, rows_at in zip(locals_, inner_rows):
                ref[e // 2, e % 2, :, at] = own[rows_at]

    over_blocks(inner_width, share, to_in_proj)
    for item in inner_sums:
        item.begin()
    small.advance(0)


    def to_taps(at):
        grad = ext_grad[:count, at]
        for k in range(reach + 1):
            last_flat[k : k + 1, at] = jnp.sum(
                grad * ext_in[k * SEGS : k * SEGS + count, at], axis=0, keepdims=True
            )
        last_flat[reach + 1 : reach + 2, at] = jnp.sum(grad, axis=0, keepdims=True)

    for item in inner_sums:
        item.advance(0)
    over_blocks(inner_width, WIDE, to_taps)
    for load in loads[7:]:
        load.wait()
    grad = rows[...] + lax.dot_general(
        inner_grad[...], in_proj[:, :half], over_inner, preferred_element_type=F32
    )
    values = tokens[...].astype(F32)
    to_values, to_gain = rms_back(values, as_row(gain_ref), grad)
    put_by_token(tokens_grad_ref, to_values + hidden_grad[...], turn)

    last_flat[reach + 2 : reach + 3, :width] = to_gain[None]
    put_tiles(last_small.pack, last_flat)
    last_small.start(0)
    gate_sum.advance(2)
    out_sum.advance(2)
    small.advance(1)
    last_small.advance(0)
    for item in inner_sums:
        item.advance(1)
    last_small.advance(1)
    small.advance(2)

    slots = home.shape[1]
    slot_id = lax.broadcasted_iota(jnp.int32, (count, experts * slots), 1)
    chosen = (slot_id == col_ref[...]).astype(F32).astype(BF16)
    returned = jnp.dot(
        chosen, home[...].reshape(experts * slots, width), preferred_element_type=F32
    )
    put_by_token(output_ref, hidden[...] + returned, turn)

    last_small.advance(2)
    gate_sum.advance(3)
    out_sum.advance(3)
    for item in inner_sums:
        item.advance(2)
    small.advance(3)
    last_small.advance(3)
    small.advance(4)
    get_tiles(flat, small.every)
    for item in inner_sums:
        item.advance(3)
    last_small.advance(4)
    get_tiles(last_flat, last_small.every)


def finish(loaded, small, early, rank, states, collective_id):
    pre_grad, in_proj, tokens = loaded[0], loaded[5], loaded[7]
    conv_weight, router_local = small[4], small[12]
    count, inner_width = pre_grad.shape
    width = tokens.shape[1]
    experts, ways = lax.axis_size("expert"), lax.axis_size("batch")
    pairs, chunk = experts // 2, width // experts
    taps = conv_weight.shape[0]
    vmem, hbm = (pl.BlockSpec(memory_space=m) for m in (pltpu.VMEM, pl.ANY))
    split = (chunk * 2 // 3, chunk // 3) if chunk % 48 == 0 else (chunk,)
    locals_ = [jax.ShapeDtypeStruct((pairs, 2, part, inner_width), BF16) for part in split]
    items = early + [Total(local, 1, i == 1) for i, local in enumerate(locals_)]
    scratch = [item.scratch() for item in items]
    kinds = tuple((item.kind(), len(refs)) for item, refs in zip(items, scratch))
    used = 2 * rank + 3 * states + 3 + router_local.shape[0] // 2
    high, low = (-(-rows // 16) * 16 for rows in (used, taps + 2))
    tiles = [-(-(rows // 16 * inner_width // LANES) // (2 * pairs)) for rows in (high, low)]
    f32 = lambda *shape: jax.ShapeDtypeStruct(shape, F32)
    halo = pltpu.VMEM((SEGS, inner_width), F32)
    rim = (taps - 1) * SEGS
    return pl.pallas_call(
        functools.partial(finish_kernel, rank, states, kinds),
        out_shape=[
            jax.ShapeDtypeStruct((count, width), BF16),
            f32(count, width),
            jax.ShapeDtypeStruct((chunk, 2 * inner_width), BF16),
            jax.ShapeDtypeStruct(early[1].chunk, BF16),
            f32(high, inner_width),
            f32(low, inner_width),
        ],
        in_specs=[hbm] * len(loaded) + [vmem] * (len(small) + len(early)),
        out_specs=[vmem] * 6,
        scratch_shapes=[pltpu.VMEM(a.shape, a.dtype) for a in loaded]
        + [
            pltpu.VMEM((count + rim, inner_width), F32),
            pltpu.VMEM((count + rim, inner_width), F32),
            pltpu.VMEM((count, inner_width), BF16),
            pltpu.VMEM((count, LANES), BF16),
            pltpu.VMEM((count, width), F32),
            halo,
            halo,
            pltpu.VMEM((width // LANES, count, LANES), F32),
            pltpu.SemaphoreType.DMA((len(loaded),)),
            pltpu.SemaphoreType.DMA((2,)),
        ]
        + SmallSum.scratch(pairs, ways, tiles[0])
        + SmallSum.scratch(pairs, ways, tiles[1])
        + [
            pltpu.VMEM((LANES, inner_width), BF16),
            pltpu.VMEM((LANES, inner_width), BF16),
            pltpu.VMEM((1, inner_width), F32),
        ]
        + [pltpu.VMEM(local.shape, BF16) for local in locals_]
        + [ref for refs in scratch for ref in refs],
        compiler_params=params(collective_id=collective_id, has_side_effects=True),
        name="finish",
    )(*loaded, *small, *(item.local for item in early))


def deliver_kernel(*refs):
    output_in, tokens_grad_in, in_proj, out_proj, flat, last, expert_in, expert_out = refs[:8]
    output, tokens_grad, gain, in_proj_out, conv, bias, x_proj, dt_proj, dt_bias, rate = refs[8:18]
    skip, out_proj_out, gain_two, router, expert_in_out, expert_out_out = refs[18:]
    output[0] = output_in[...]
    tokens_grad[0] = tokens_grad_in[...]
    at, width = 0, gain.shape[0]
    for ref in (x_proj, dt_proj, rate):
        ref[...] = flat[at : at + ref.shape[0], :]
        at += ref.shape[0]
    fold = router.shape[0] // 2
    dt_bias[...] = flat[at : at + 1, :].reshape(dt_bias.shape)
    skip[...] = flat[at + 1 : at + 2, :].reshape(skip.shape)
    gain_two[...] = flat[at + 2 : at + 3, :width].reshape(gain_two.shape)
    router[:fold, :] = flat[at + 3 : at + 3 + fold, :width]
    router[fold:, :] = flat[at + 3 : at + 3 + fold, width:]
    taps = conv.shape[0]
    conv[...] = last[:taps, :]
    bias[...] = last[taps : taps + 1, :].reshape(bias.shape)
    gain[...] = last[taps + 1 : taps + 2, :width].reshape(gain.shape)
    in_proj_out[...] = in_proj[...].astype(F32)
    out_proj_out[...] = out_proj[...].astype(F32)
    expert_in_out[0] = expert_in[...].astype(F32)
    expert_out_out[0] = expert_out[...].astype(F32)


def deliver(made, expert_in, expert_out, shapes):
    vmem = pl.BlockSpec(memory_space=pltpu.VMEM)
    output, tokens_grad, in_proj, out_proj, flat, last = made
    f32 = lambda *shape: jax.ShapeDtypeStruct(shape, F32)
    outs = [
        jax.ShapeDtypeStruct((1, *output.shape), BF16),
        f32(1, *tokens_grad.shape),
        shapes[0],
        f32(*in_proj.shape),
        *shapes[1:8],
        f32(*out_proj.shape),
        *shapes[8:],
        f32(1, *expert_in.shape),
        f32(1, *expert_out.shape),
    ]
    return pl.pallas_call(
        deliver_kernel,
        out_shape=outs,
        in_specs=[vmem] * 8,
        out_specs=[vmem] * len(outs),
        compiler_params=params(),
        name="deliver",
    )(*made, expert_in, expert_out)


def silu(v):
    return v * jax.nn.sigmoid(v)


def silu_slope(v):
    s = jax.nn.sigmoid(v)
    return s * (1.0 + v * (1.0 - s))


def rms_back(values, gain, grad):
    r = lax.rsqrt(jnp.mean(values * values, axis=-1, keepdims=True) + 1e-05)
    u = gain * grad
    mean = jnp.mean(values * u, axis=-1, keepdims=True)
    return r * u - values * (r * r * r) * mean, jnp.sum(grad * values * r, axis=0)


def rms(values, gain):
    return values * lax.rsqrt(jnp.mean(values * values, axis=-1, keepdims=True) + 1e-05) * gain


def per_device(
    tokens,
    routes,
    gain_one,
    in_proj,
    conv_weight,
    conv_bias,
    x_proj,
    dt_proj,
    dt_bias,
    rate_log,
    skip,
    out_proj,
    gain_two,
    router,
    expert_in,
    expert_out,
    cotangent,
):
    count, width = tokens.shape[1], tokens.shape[2]
    steps = count // SEGS
    inner_width = out_proj.shape[0]
    rank = dt_proj.shape[0]
    experts = router.shape[0]
    capacity = 5 * count // (4 * experts)
    slots = -(-capacity // 16) * 16
    states = rate_log.shape[0]
    route = routes.reshape(SEGS, steps).T.reshape(1, count)
    made, kept = forward(
        tokens,
        cotangent,
        in_proj,
        out_proj,
        route,
        gain_one,
        gain_two,
        conv_weight,
        conv_bias,
        x_proj,
        dt_proj,
        dt_bias,
        skip,
        rate_log,
        (rank, capacity, slots),
        2,
    )
    ssm, held, gated, hidden, normed_two, row, col, before, slot_upstream = made
    tokens_low, upstream_low, normed_one, inner, gate_z, mixed, pre, delta, proj = kept

    normed_two_grad, results, expert_in_local, expert_out_local, router_local = run_experts(
        normed_two, row, col, router, slot_upstream, expert_in, expert_out, slots, 4
    )

    hidden_grad, gain_two_local, ssm_grad, gate_z_grad, out_proj_local, in_proj_gate_local = middle(
        hidden, normed_two_grad, upstream_low, gain_two, normed_one, gated, ssm, gate_z, out_proj
    )
    ways, pairs = lax.axis_size("batch"), experts // 2
    early = [
        Total(
            in_proj_gate_local.reshape(pairs, 2, width // experts, inner_width),
            1,
        ),
        Total(
            out_proj_local.reshape(
                pairs, 2, ways, inner_width // (experts * ways), width
            ),
            0,
            True,
        ),
    ]
    (
        in_proj_gate_spread,
        out_proj_spread,
        pre_grad,
        mixed_grad,
        rate_log_local,
        skip_local,
        dt_bias_local,
        bc_grad,
        returned,
    ) = mixer_grads(
        pre, delta, mixed, ssm_grad, proj, rate_log, skip, held, results, rank, early, 3
    )
    early = [early[0].resumed(in_proj_gate_spread), early[1].resumed(out_proj_spread)]
    outs = finish(
        [
            pre_grad,
            mixed_grad,
            mixed,
            inner,
            normed_one,
            in_proj,
            gate_z_grad,
            tokens_low,
            hidden_grad,
            hidden,
            returned,
        ],
        [
            bc_grad,
            proj,
            x_proj,
            dt_proj,
            conv_weight,
            conv_bias,
            before,
            gain_one,
            rate_log_local,
            dt_bias_local,
            skip_local,
            gain_two_local,
            router_local,
            col,
        ],
        early,
        rank,
        states,
        1,
    )
    expert_in_grad, expert_out_grad = (
        lax.psum_scatter(v, "batch", scatter_dimension=0, tiled=True)
        for v in (expert_in_local, expert_out_local)
    )
    outs = (*outs[:3], outs[3].reshape(-1, width), *outs[4:])
    weights = (gain_one, conv_weight, conv_bias, x_proj, dt_proj, dt_bias, rate_log, skip)
    shapes = [jax.ShapeDtypeStruct(w.shape, F32) for w in (*weights, gain_two, router)]
    return tuple(deliver(outs, expert_in_grad, expert_out_grad, shapes))


def solution(mesh):
    split = P("batch", "expert", None)
    one = P("expert", None, None)
    both = P("expert", "batch", None)
    in_specs = (split, split) + (P(),) * 12 + (one, one, split)
    out_specs = (split, split, P(), P("expert", None)) + (P(),) * 7
    out_specs += (P("expert", None), P(), P(), both, both)
    return jax.shard_map(
        per_device, mesh=mesh, in_specs=in_specs, out_specs=out_specs, check_vma=False
    )
```

```python
import functools

import jax
import jax.numpy as jnp
from jax import lax
from jax.experimental import pallas as pl
from jax.experimental.pallas import tpu as pltpu
from jax.sharding import PartitionSpec as P

F32, BF16 = jnp.float32, jnp.bfloat16
SEGS = 8
LANES = 128
LOG2E = 1.4426950408889634
LN2 = 0.6931471805599453
VMEM_LIMIT = 60 * 1024 * 1024
MESH = pl.DeviceIdType.MESH


def params(**kw):
    return pltpu.CompilerParams(vmem_limit_bytes=VMEM_LIMIT, **kw)


def softplus(v):
    return jnp.maximum(v, 0.0) + jnp.log1p(jnp.exp(-jnp.abs(v)))


def as_row(ref):
    return ref[...].reshape(1, ref.shape[0])


def padded_rows(ref, high):
    low = jnp.zeros((high - ref.shape[0], ref.shape[1]), F32)
    return jnp.concatenate([ref[...].astype(F32), low], axis=0).astype(BF16)


def over_sublanes(row):
    return jnp.broadcast_to(row, (SEGS, LANES))


def over_lanes(column):
    return jnp.broadcast_to(column, (SEGS, LANES))


def tile_rows(j):
    return pl.ds(pl.multiple_of(j * SEGS, SEGS), SEGS)


def run_of_segments(a, b, forward):
    at = lax.broadcasted_iota(jnp.int32, (SEGS, LANES), 0)
    for step in (1, 2, 4):
        if forward:
            inside, turn = at >= step, step
        else:
            inside, turn = at < SEGS - step, SEGS - step
        before_a = jnp.where(inside, pltpu.roll(a, turn, 0), 1.0)
        before_b = jnp.where(inside, pltpu.roll(b, turn, 0), 0.0)
        a, b = a * before_a, a * before_b + b
    return a, b


class Carries:
    groups = 2

    def __init__(self, states, blocks, forward, own, lengths, got, got_lengths, sems):
        self.states, self.blocks, self.forward = states, blocks, forward
        self.own, self.lengths, self.got, self.got_lengths = own, lengths, got, got_lengths
        self.sems = sems
        self.count, self.me = lax.axis_size("expert"), lax.axis_index("expert")
        self.per = blocks // self.groups

    @staticmethod
    def scratch(states, blocks, count):
        per = blocks // Carries.groups
        assert blocks % Carries.groups == 0 and per <= SEGS
        return [
            pltpu.VMEM((blocks, states, LANES), BF16),
            pltpu.VMEM((Carries.groups, SEGS, LANES), F32),
            pltpu.VMEM((count, blocks, states, LANES), BF16),
            pltpu.VMEM((count, Carries.groups, SEGS, LANES), F32),
            pltpu.SemaphoreType.DMA((2, 2, Carries.groups, count)),
        ]

    def other(self, k):
        return (lax.axis_index("batch"), lax.rem(self.me + k, self.count))

    def copies(self, group):
        blocks = pl.ds(group * self.per, self.per)
        found = []
        for k in range(1, self.count):
            pairs = (
                (self.own.at[blocks], self.got.at[k - 1, blocks]),
                (self.lengths.at[group], self.got_lengths.at[k - 1, group]),
            )
            for i, (src, dst) in enumerate(pairs):
                found.append(
                    pltpu.make_async_remote_copy(
                        src_ref=src,
                        dst_ref=dst,
                        send_sem=self.sems.at[0, i, group, k - 1],
                        recv_sem=self.sems.at[1, i, group, k - 1],
                        device_id=self.other(k),
                        device_id_type=MESH,
                    )
                )
        return found

    def put(self, block, ends, sums, rates, run_a, run_b):
        edge = SEGS - 1 if self.forward else 0
        rows = []
        for n in range(self.states):
            a, b = run_of_segments(jnp.exp2(rates[n] * sums), ends[n], self.forward)
            run_a[block, n] = a
            run_b[block, n] = b
            rows.append(b[edge : edge + 1])
        end = jnp.concatenate(rows, axis=0).astype(BF16)
        total = jnp.sum(sums, axis=0, keepdims=True)
        last = self.count - 1
        self.own[block] = end
        self.got[last, block] = end
        for group in range(self.groups):

            @pl.when(block // self.per == group)
            def _():
                row = pl.ds(lax.rem(block, self.per), 1)
                self.lengths[group, row, :] = total
                self.got_lengths[last, group, row, :] = total

            @pl.when(block == (group + 1) * self.per - 1)
            def _():
                for copy in self.copies(group):
                    copy.start()

    def await_group(self, block):
        for group in range(self.groups):

            @pl.when(block == group * self.per)
            def _():
                for copy in self.copies(group):
                    copy.wait()

    def starts(self, block, rate, run_a, run_b):
        group, row = block // self.per, pl.ds(lax.rem(block, self.per), 1)
        entering = jnp.zeros((self.states, LANES), F32)
        order = range(self.count) if self.forward else range(self.count - 1, -1, -1)
        for place in order:
            slot = lax.rem(self.me - place - 1 + 2 * self.count, self.count)
            length = self.got_lengths[slot, group, row, :]
            joined = jnp.exp2(rate * length) * entering + self.got[slot, block].astype(F32)
            ahead = (place < self.me) if self.forward else (place > self.me)
            entering = jnp.where(ahead, joined, entering)
        found = []
        for n in range(self.states):
            first = entering[n : n + 1]
            after = run_a[block, n] * over_sublanes(first) + run_b[block, n]
            found.append(shifted_in(after, first, self.forward))
        return found


def together(*parts):
    return sum(p.astype(F32) for p in parts)


class Total:
    def __init__(self, local, axis, pairs_first=False, chunk=None):
        self.local, self.axis, self.pairs_first = local, axis, pairs_first
        self.ways = lax.axis_size("batch")
        self.taken_up = chunk is not None
        self.pairs, self.chunk = lax.axis_size("expert") // 2, chunk or local.shape[2:]
        part = list(self.chunk)
        part[axis] //= self.ways
        self.part = tuple(part)

    def kind(self):
        return self.axis, self.pairs_first, self.part, self.taken_up

    def spread_shape(self):
        shape = self.chunk if self.pairs_first else (self.pairs, *self.part)
        return jax.ShapeDtypeStruct(shape, BF16)

    def resumed(self, spread):
        return Total(spread, self.axis, self.pairs_first, self.chunk)

    def first_scratch(self):
        first = (self.pairs - 1, *self.chunk)
        if not self.pairs_first:
            first = (self.ways - 1, self.pairs, *self.part)
        return [
            pltpu.VMEM((2, self.pairs, *self.chunk), BF16),
            pltpu.VMEM((self.pairs, *self.chunk), BF16),
            pltpu.VMEM(first, BF16),
            pltpu.SemaphoreType.DMA((2, 2, max(self.ways, self.pairs))),
        ]

    def second_scratch(self):
        second = self.ways - 1 if self.pairs_first else self.pairs - 1
        return [
            pltpu.VMEM((second, *self.part), BF16),
            pltpu.VMEM(self.part, BF16),
            pltpu.VMEM(self.chunk, BF16),
            pltpu.SemaphoreType.DMA((2, 4, max(self.ways, self.pairs))),
        ]

    def scratch(self):
        if self.taken_up:
            return self.second_scratch()
        spread = self.spread_shape()
        return self.first_scratch() + [pltpu.VMEM(spread.shape, BF16)] + self.second_scratch()


def part_of(ref, lead, axis, size, index):
    start = index * size
    if axis == len(ref.shape) - lead - 1:
        start = pl.multiple_of(start, LANES)
    where = [slice(None)] * len(ref.shape)
    where[lead + axis] = pl.ds(start, size)
    return ref.at[tuple(where)]


class Peers:
    def __init__(self):
        self.ways, self.pairs = lax.axis_size("batch"), lax.axis_size("expert") // 2
        self.group, place = lax.axis_index("batch"), lax.axis_index("expert")
        self.pair, self.core = place // 2, lax.rem(place, 2)
        self.sibling = (self.group, self.pair * 2 + 1 - self.core)
        self.to_batch = [lax.rem(self.group + k, self.ways) for k in range(1, self.ways)]
        self.to_pairs = [lax.rem(self.pair + k, self.pairs) for k in range(1, self.pairs)]
        self.in_batch = [(to, place) for to in self.to_batch]
        self.in_pairs = [(self.group, to * 2 + self.core) for to in self.to_pairs]

    def remote(self, src, dst, sems, stage, k, device):
        return pltpu.make_async_remote_copy(
            src_ref=src,
            dst_ref=dst,
            send_sem=sems.at[0, stage, k],
            recv_sem=sems.at[1, stage, k],
            device_id=device,
            device_id_type=MESH,
        )

    def start(self, stage):
        for copy in self.copies(stage):
            copy.start()

    def wait(self, stage):
        for copy in self.copies(stage):
            copy.wait()

    def advance(self, stage):
        self.wait(stage)
        self.add(stage)
        if stage < self.last:
            self.start(stage + 1)


class Summing(Peers):
    last = 3

    def __init__(self, kind, local, out, scratch):
        super().__init__()
        self.axis, self.pairs_first, part, self.taken_up = kind
        self.local, self.out, self.size = local, out, part[self.axis]
        if self.taken_up:
            self.spread = local
            self.from_second, self.mine, self.every, self.late_sems = scratch
        else:
            self.both, self.by_chip, self.from_first, self.sems = scratch[:4]
            self.spread = out
            if len(scratch) > 4:
                self.spread, self.from_second, self.mine, self.every, self.late_sems = scratch[4:]

    def share(self, ref, lead, index):
        return part_of(ref, lead, self.axis, self.size, index)

    def copies(self, stage):
        if stage == 0:
            own = pltpu.make_async_copy(
                self.local.at[:, self.core], self.both.at[0], self.sems.at[0, 0, 1]
            )
            away = self.local.at[:, 1 - self.core]
            return [own, self.remote(away, self.both.at[1], self.sems, 0, 0, self.sibling)]
        if stage == 3:
            own, devices = self.share(self.every, 0, self.group), self.in_batch
            pieces = [(self.mine, own) for _ in devices]
        elif (stage == 1) == self.pairs_first:
            devices = self.in_pairs
            src, dst = (self.by_chip, self.from_first) if stage == 1 else (self.spread, self.from_second)
            pieces = [(src.at[to], dst.at[k]) for k, to in enumerate(self.to_pairs)]
        else:
            devices = self.in_batch
            src, dst = (self.by_chip, self.from_first) if stage == 1 else (self.spread, self.from_second)
            lead = 1 if stage == 1 else 0
            pieces = [
                (self.share(src, lead, to), dst.at[k]) for k, to in enumerate(self.to_batch)
            ]
        sems = self.sems if stage == 1 else self.late_sems
        return [
            self.remote(src, dst, sems, stage, k, devices[k]) for k, (src, dst) in enumerate(pieces)
        ]

    def add(self, stage):
        if stage == 0:

            def over_cores(z, carry):
                self.by_chip[z] = together(self.both[0, z], self.both[1, z]).astype(BF16)
                return carry

            lax.fori_loop(0, self.pairs, over_cores, 0)
        elif stage == 1 and self.pairs_first:
            others = (self.from_first[k] for k in range(self.pairs - 1))
            self.spread[...] = together(self.by_chip[self.pair], *others).astype(BF16)
        elif stage == 1:
            own = self.share(self.by_chip, 1, self.group)

            def over_batch(z, carry):
                others = (self.from_first[k, z] for k in range(self.ways - 1))
                self.spread[z] = together(own[z], *others).astype(BF16)
                return carry

            lax.fori_loop(0, self.pairs, over_batch, 0)
        elif stage == 2:
            if self.pairs_first:
                own, count = self.share(self.spread, 0, self.group)[...], self.ways
            else:
                own, count = self.spread[self.pair], self.pairs
            others = (self.from_second[k] for k in range(count - 1))
            total = together(own, *others).astype(BF16)
            self.mine[...] = total
            self.share(self.every, 0, self.group)[...] = total
        else:
            self.out[...] = self.every[...].astype(self.out.dtype)

    def begin(self):
        self.start(2 if self.taken_up else 0)


class SmallSum(Peers):
    last = 4

    def __init__(self, pack, from_core, half, from_pairs, by_group, every, sems):
        super().__init__()
        self.pack, self.from_core, self.half, self.from_pairs = pack, from_core, half, from_pairs
        self.by_group, self.every, self.sems = by_group, every, sems

    @staticmethod
    def scratch(pairs, ways, tiles):
        tile = (tiles, 16, LANES)
        shapes = ((2, pairs), (pairs,), (pairs,), (pairs - 1,), (ways,), (2, pairs))
        found = [pltpu.VMEM((*lead, *tile), BF16) for lead in shapes]
        return found + [pltpu.SemaphoreType.DMA((2, 5, max(pairs, ways)))]

    def copies(self, stage):
        if stage == 0:
            pieces = [(self.pack.at[1 - self.core], self.from_core, self.sibling)]
        elif stage == 1:
            pieces = [
                (self.half.at[to], self.from_pairs.at[k], self.in_pairs[k])
                for k, to in enumerate(self.to_pairs)
            ]
        elif stage == 2:
            own = self.by_group.at[self.group]
            pieces = [(own, own, device) for device in self.in_batch]
        elif stage == 3:
            own = self.every.at[self.core, self.pair]
            pieces = [(own, own, device) for device in self.in_pairs]
        else:
            own = self.every.at[self.core]
            pieces = [(own, own, self.sibling)]
        return [
            self.remote(src, dst, self.sems, stage, k, device)
            for k, (src, dst, device) in enumerate(pieces)
        ]

    def add(self, stage):
        if stage == 0:
            self.half[...] = together(self.pack[self.core], self.from_core[...]).astype(BF16)
        elif stage == 1:
            others = (self.from_pairs[k] for k in range(self.pairs - 1))
            self.by_group[self.group] = together(self.half[self.pair], *others).astype(BF16)
        elif stage == 2:
            total = together(*(self.by_group[k] for k in range(self.ways)))
            self.every[self.core, self.pair] = total.astype(BF16)


def summings(kinds, ins, outs, scratch):
    found, at = [], 0
    for (kind, many), local, out in zip(kinds, ins, outs):
        found.append(Summing(kind, local, out, scratch[at : at + many]))
        at += many
    return found


class Halving:
    def __init__(self, local, x_first, sems=None):
        assert lax.axis_size("batch") == 4
        group, self.place = lax.axis_index("batch"), lax.axis_index("expert")
        by_x = group + 1 - 2 * lax.rem(group, 2)
        by_y = group + 2 - 4 * (group // 2)
        self.local, self.sems, self.group, self.across = local, sems, group, 3 - group
        self.near, self.far = (by_x, by_y) if x_first else (by_y, by_x)
        self.rows = local.shape[0] // 4

    def chunk(self, index):
        return self.local.at[pl.ds(pl.multiple_of(index * self.rows, self.rows), self.rows)]

    def copy(self, src, dst, k, device):
        return pltpu.make_async_remote_copy(
            src_ref=src,
            dst_ref=dst,
            send_sem=self.sems.at[0, k],
            recv_sem=self.sems.at[1, k],
            device_id=(device, self.place),
            device_id_type=MESH,
        )

    def first(self, landing):
        return [
            self.copy(self.chunk(index), landing.at[k], k, self.near)
            for k, index in enumerate((self.near, self.across))
        ]

    def second(self, src, landing):
        return self.copy(src, landing, 0, self.far)


class Side:
    def __init__(self, src, dst, sems):
        self.src, self.dst, self.sems = src, dst, sems
        self.count, self.me = lax.axis_size("expert"), lax.axis_index("expert")

    @staticmethod
    def scratch(count):
        return pltpu.SemaphoreType.DMA((2, count))

    def copy(self, k):
        return self.copy_to(lax.rem(self.me + k, self.count))

    def copy_to(self, to):
        return pltpu.make_async_remote_copy(
            src_ref=self.src.at[to],
            dst_ref=self.dst.at[self.me],
            send_sem=self.sems.at[0, to],
            recv_sem=self.sems.at[1, self.me],
            device_id=(lax.axis_index("batch"), to),
            device_id_type=MESH,
        )

    def brought(self, place):
        return pltpu.make_async_remote_copy(
            src_ref=self.src.at[place],
            dst_ref=self.dst.at[place],
            send_sem=self.sems.at[0, place],
            recv_sem=self.sems.at[1, place],
            device_id=(lax.axis_index("batch"), place),
            device_id_type=MESH,
        )

    def own(self):
        return pltpu.make_async_copy(
            self.src.at[self.me], self.dst.at[self.me], self.sems.at[0, self.me]
        )

    def start(self, part=0, parts=((0, 1),)):
        if part == 0:
            self.own().start()
        least, most = (1 + round(share * (self.count - 1)) for share in parts[part])
        for k in range(least, most):
            self.copy(k).start()

    def wait(self):
        self.own().wait()
        self.wait_others()

    def wait_others(self):
        for k in range(1, self.count):
            place = lax.rem(self.me + k, self.count)
            self.copy_to(place).wait_send()
            self.brought(place).wait_recv()


def greet_others():
    barrier = pltpu.get_barrier_semaphore()
    group, place = lax.axis_index("batch"), lax.axis_index("expert")
    ways, count = lax.axis_size("batch"), lax.axis_size("expert")
    others = [(group, lax.rem(place + k, count)) for k in range(1, count)]
    others += [(lax.rem(group + k, ways), place) for k in range(1, ways)]
    for device in others:
        pl.semaphore_signal(barrier, inc=1, device_id=device, device_id_type=MESH)
    pl.semaphore_wait(barrier, len(others))


def greet_experts():
    barrier = pltpu.get_barrier_semaphore()
    count, me = lax.axis_size("expert"), lax.axis_index("expert")
    for k in range(1, count):
        device = (lax.axis_index("batch"), lax.rem(me + k, count))
        pl.semaphore_signal(barrier, inc=1, device_id=device, device_id_type=MESH)
    pl.semaphore_wait(barrier, count - 1)


def gelu_parts(v):
    size = jnp.abs(v) * 0.7071067811865476
    t = 1.0 / (1.0 + 0.3275911 * size)
    bell = jnp.exp2(v * v * (-0.5 * LOG2E))
    poly = t * (
        0.127414796
        + t * (-0.142248368 + t * (0.7107068705 + t * (-0.7265760135 + t * 0.5307027145)))
    )
    tail = poly * bell
    phi = jnp.where(v >= 0.0, 1.0 - tail, tail)
    return v * phi, phi + v * (bell * 0.3989422804014327)


FF_TILE = 512


def experts_kernel(slots, tile, *refs):
    normed_ref, row_ref, col_ref, router_ref, upstream_ref, in_hbm, out_hbm = refs[:7]
    grad_ref, result_ref, in_grad_hbm, out_grad_hbm, router_grad_ref = refs[7:12]
    w_in, w_out, sent, got, home, slot_grad, active, hid_grad, row_grad = refs[12:21]
    in_grad, out_grad, there_sems, back_sems, load_sems, store_sems, router = refs[21:28]
    gates, logit_grads, back = refs[28:]
    rows = row_grad
    count, me = lax.axis_size("expert"), lax.axis_index("expert")
    width, hidden = w_in.shape
    total = count * slots
    tiles = hidden // tile
    router[...] = padded_rows(router_ref, LANES)
    loads = [
        pltpu.make_async_copy(in_hbm.at[0], w_in, load_sems.at[0]),
        pltpu.make_async_copy(out_hbm.at[0], w_out, load_sems.at[1]),
    ]
    for load in loads:
        load.start()
    greet_experts()
    there = Side(sent, got, there_sems)
    returning = Side(back, home, back_sems)
    tokens = normed_ref.shape[0]
    slot_id = lax.broadcasted_iota(jnp.int32, (slots, tokens), 0)

    upper = me // (count // 2)
    quarter = count // 4
    groups = (
        (upper * 2 * quarter, 2 * quarter),
        ((2 - upper) * quarter, quarter),
        ((3 - 3 * upper) * quarter, quarter),
    )

    def dispatch(to, carry):
        picked = (slot_id + to * slots == row_ref[...]).astype(F32).astype(BF16)
        chunk = jnp.dot(picked, normed_ref[...], preferred_element_type=F32).astype(BF16)
        sent[to] = chunk

        @pl.when(to != me)
        def _():
            there.copy_to(to).start()

        @pl.when(to == me)
        def _():
            got[me] = chunk

        return carry

    for first, many in groups:
        lax.fori_loop(first, first + many, dispatch, 0)
    over_inner = (((1,), (1,)), ((), ()))
    for load in loads:
        load.wait()
    for first, many in groups:

        def arrive(place, carry):
            @pl.when(place != me)
            def _():
                there.brought(place).wait_recv()

            return carry

        lax.fori_loop(first, first + many, arrive, 0)
        high = many * slots
        places = pl.ds(first, many)
        at_rows = pl.ds(pl.multiple_of(first * slots, 16), high)
        x = got[places].reshape(high, width)
        logits = lax.dot_general(x, router[...], over_inner, preferred_element_type=F32)
        lane = lax.broadcasted_iota(jnp.int32, logits.shape, 1)
        logits = jnp.where(lane < count, logits, -1e30)
        scores = jnp.exp(logits - jnp.max(logits, axis=1, keepdims=True))
        probs = scores / jnp.sum(scores, axis=1, keepdims=True)
        mine = (lane == me).astype(F32)
        gate = jnp.sum(probs * mine, axis=1, keepdims=True)
        gates[at_rows, :] = jnp.broadcast_to(gate, (high, LANES))
        upstream = upstream_ref[places].reshape(high, width).astype(F32)
        slot_grad[at_rows, :] = (gate * upstream).astype(BF16)
        row_grad[at_rows, :] = jnp.zeros((high, width), F32)

        def inward(t, picked, x=x, at_rows=at_rows):
            at = pl.ds(pl.multiple_of(t * tile, tile), tile)
            pre = jnp.dot(x, w_in[:, at], preferred_element_type=F32)
            act_grad = lax.dot_general(
                slot_grad[at_rows, :], w_out[at, :], over_inner, preferred_element_type=F32
            )
            value, slope = gelu_parts(pre)
            active[at_rows, at] = value.astype(BF16)
            low = (act_grad * slope).astype(BF16)
            hid_grad[at_rows, at] = low
            row_grad[at_rows, :] += lax.dot_general(
                low, w_in[:, at], over_inner, preferred_element_type=F32
            )
            return picked + jnp.sum(value * act_grad, axis=1, keepdims=True)

        picked = lax.fori_loop(0, tiles, inward, jnp.zeros((high, 1), F32))
        logit_grad = (picked * (mine - probs)).astype(BF16)
        logit_grads[at_rows, :] = logit_grad
        whole = row_grad[at_rows, :] + jnp.dot(logit_grad, router[...], preferred_element_type=F32)
        back[places] = whole.astype(BF16).reshape(many, slots, width)

        def give_back(place, carry):
            @pl.when(place != me)
            def _():
                returning.copy_to(place).start()

            @pl.when(place == me)
            def _():
                home[me] = back[me]

            return carry

        lax.fori_loop(first, first + many, give_back, 0)

    router_grad = lax.dot_general(
        logit_grads[...],
        got[...].reshape(total, width),
        (((0,), (0,)), ((), ())),
        preferred_element_type=F32,
    )
    router_grad_ref[...] = router_grad[:count]
    rows[...] = jnp.zeros(rows.shape, F32)

    def stores(t):
        at = pl.ds(pl.multiple_of(t * tile, tile), tile)
        return (
            pltpu.make_async_copy(in_grad.at[:, at], in_grad_hbm.at[:, at], store_sems.at[0, t]),
            pltpu.make_async_copy(out_grad.at[at], out_grad_hbm.at[at], store_sems.at[1, t]),
        )

    def outward(t, carry):
        at = pl.ds(pl.multiple_of(t * tile, tile), tile)
        over_rows = (((0,), (0,)), ((), ()))
        in_grad[:, at] = lax.dot_general(
            got[...].reshape(total, width), hid_grad[:, at], over_rows, preferred_element_type=F32
        ).astype(BF16)
        out_grad[at, :] = lax.dot_general(
            active[:, at], slot_grad[...], over_rows, preferred_element_type=F32
        ).astype(BF16)
        for store in stores(t):
            store.start()
        rows[...] += jnp.dot(active[:, at], w_out[at, :], preferred_element_type=F32)
        return carry

    lax.fori_loop(0, tiles, outward, 0)
    result_ref[...] = (gates[:, :1] * rows[...]).astype(BF16).reshape(count, slots, width)
    returning.wait_others()
    for k in range(1, count):
        there.copy(k).wait_send()
    slot_id = lax.broadcasted_iota(jnp.int32, (tokens, total), 1)
    chosen = (slot_id == col_ref[...]).astype(F32).astype(BF16)
    grad_ref[...] = jnp.dot(
        chosen, home[...].reshape(total, width), preferred_element_type=F32
    )
    for t in range(tiles):
        for store in stores(t):
            store.wait()


def run_experts(
    normed, row, col, router, upstream, expert_in, expert_out, slots, collective_id
):
    tokens, width = normed.shape
    count = lax.axis_size("expert")
    hidden = expert_in.shape[2]
    tile = FF_TILE if hidden % FF_TILE == 0 else hidden
    total = count * slots
    exchanged = (count, slots, width)
    vmem = pl.BlockSpec(memory_space=pltpu.VMEM)
    hbm = pl.BlockSpec(memory_space=pl.ANY)
    grad, result, in_grad, out_grad, router_grad = pl.pallas_call(
        functools.partial(experts_kernel, slots, tile),
        out_shape=[
            jax.ShapeDtypeStruct((tokens, width), F32),
            jax.ShapeDtypeStruct(exchanged, BF16),
            jax.ShapeDtypeStruct((width, hidden), BF16),
            jax.ShapeDtypeStruct((hidden, width), BF16),
            jax.ShapeDtypeStruct(router.shape, F32),
        ],
        in_specs=[vmem] * 5 + [hbm] * 2,
        out_specs=[vmem, vmem, hbm, hbm, vmem],
        scratch_shapes=[
            pltpu.VMEM((width, hidden), BF16),
            pltpu.VMEM((hidden, width), BF16),
            pltpu.VMEM(exchanged, BF16),
            pltpu.VMEM(exchanged, BF16),
            pltpu.VMEM(exchanged, BF16),
            pltpu.VMEM((total, width), BF16),
            pltpu.VMEM((total, hidden), BF16),
            pltpu.VMEM((total, hidden), BF16),
            pltpu.VMEM((total, width), F32),
            pltpu.VMEM((width, hidden), BF16),
            pltpu.VMEM((hidden, width), BF16),
            Side.scratch(count),
            Side.scratch(count),
            pltpu.SemaphoreType.DMA((2,)),
            pltpu.SemaphoreType.DMA((2, hidden // tile)),
            pltpu.VMEM((LANES, width), BF16),
            pltpu.VMEM((total, LANES), F32),
            pltpu.VMEM((total, LANES), BF16),
            pltpu.VMEM(exchanged, BF16),
        ],
        compiler_params=params(collective_id=collective_id, has_side_effects=True),
        name="experts",
    )(normed, row, col, router, upstream, expert_in, expert_out)
    return grad, result, in_grad, out_grad, router_grad


def in_segments(value_ref, turn):
    steps = value_ref.shape[0] // SEGS
    parts = []
    for lane in range(turn.shape[0]):
        lanes = slice(lane * LANES, (lane + 1) * LANES)
        for s in range(SEGS):
            rows = value_ref[s * steps : (s + 1) * steps, lanes].astype(F32)
            turn[lane, pl.ds(s, steps, stride=SEGS), :] = rows
        parts.append(turn[lane].astype(BF16))
    return jnp.concatenate(parts, axis=1)


def over_blocks(width, size, body):
    def one(n, carry):
        body(pl.ds(pl.multiple_of(n * size, size), size))
        return carry

    lax.fori_loop(0, width // size, one, 0)


def slot_targets(route, experts, capacity, slots):
    count = route.shape[1]
    steps = count // SEGS
    high = max(experts, 16)
    onehot = lax.broadcasted_iota(jnp.int32, (high, count), 0) == route
    onehot = onehot.astype(F32)
    token_of = lambda p: (p % SEGS) * steps + p // SEGS
    first = token_of(lax.broadcasted_iota(jnp.int32, (count, count), 0))
    second = token_of(lax.broadcasted_iota(jnp.int32, (count, count), 1))
    earlier = (first <= second).astype(F32).astype(BF16)
    running = jnp.dot(onehot.astype(BF16), earlier, preferred_element_type=F32)
    place = (jnp.sum(running * onehot, axis=0, keepdims=True) - 1.0).astype(jnp.int32)
    return jnp.where(place < capacity, route * slots + place, -1)


def forward_kernel(sizes, *refs):
    states, steps, rank, capacity = sizes
    tokens_hbm, upstream_hbm, in_proj_hbm, out_proj_hbm = refs[:4]
    route_ref, gain_ref, gain_two_ref, conv_ref, bias_ref, x_proj_ref, dt_proj_ref = refs[4:11]
    dt_bias_ref, skip_ref, rate_log_ref = refs[11:14]
    ssm_ref, held_ref, gated_ref, hidden_ref, normed_two_ref, row_ref, col_ref, before_ref = refs[14:22]
    side_out = refs[22]
    kept_hbm, refs = refs[23:32], refs[32:]
    tokens_in, upstream_in, in_proj, out_proj, turn, ext_in, tail, sent = refs[:8]
    kept, refs = refs[8:17], refs[17:]
    tokens, upstream, normed, inner, gate_z, mixed, pre, delta, proj = kept
    in_s, bb, cb, run_a, run_b, side_sems, load_sems, keep_sems, halo_sems = refs[:9]
    x_proj, dt_proj, small, before, carry_refs = *refs[9:13], refs[13:]
    phase, block = pl.program_id(0), pl.program_id(1)
    blocks = carry_refs[2].shape[1]
    carries = Carries(states, blocks, True, *carry_refs)
    side = Side(sent, side_out, side_sems)
    parts = ((0, 2 / 7), (2 / 7, 3 / 7), (3 / 7, 1))
    rate2 = -jnp.exp(rate_log_ref[...]) * LOG2E
    rates = [over_sublanes(rate2[n : n + 1, :]) for n in range(states)]
    here = pl.ds(pl.multiple_of(block * LANES, LANES), LANES)
    count, width = tokens.shape
    inner_width = inner.shape[1]
    reach = conv_ref.shape[0] - 1
    rim = reach * SEGS
    experts, me = lax.axis_size("expert"), lax.axis_index("expert")
    slots = sent.shape[1]
    half = inner_width
    loads = [
        pltpu.make_async_copy(src, dst, load_sems.at[i])
        for i, (src, dst) in enumerate(
            (
                (tokens_hbm.at[0], tokens_in),
                (in_proj_hbm.at[:, :half], in_proj.at[:, :half]),
                (in_proj_hbm.at[:, half:], in_proj.at[:, half:]),
                (upstream_hbm.at[0], upstream_in),
                (out_proj_hbm, out_proj),
            )
        )
    ]
    keeps = [
        pltpu.make_async_copy(src, dst, keep_sems.at[i])
        for i, (src, dst) in enumerate(zip(kept, kept_hbm))
    ]

    def front():
        for load in loads:
            load.start()
        small[0:1, :] = as_row(skip_ref)
        small[1:2, :] = as_row(bias_ref)
        small[2:3, :] = as_row(dt_bias_ref)
        x_proj[...] = padded_rows(x_proj_ref, LANES)
        dt_proj[...] = padded_rows(dt_proj_ref, LANES)
        loads[0].wait()
        tokens[...] = in_segments(tokens_in, turn)
        normed[...] = rms(tokens[...].astype(F32), as_row(gain_ref)).astype(BF16)
        loads[1].wait()

        def to_inner(at):
            inner[:, at] = jnp.dot(
                normed[...], in_proj[:, at], preferred_element_type=F32
            ).astype(BF16)

        over_blocks(inner_width, 4 * LANES, to_inner)
        last = inner[count - rim - rim % 16 :, :].astype(F32)[rim % 16 :]
        for k in range(reach):
            tail[k : k + 1, :] = last[(k + 1) * SEGS - 1 : (k + 1) * SEGS]
        greet_experts()
        halo = pltpu.make_async_remote_copy(
            src_ref=tail,
            dst_ref=before,
            send_sem=halo_sems.at[0],
            recv_sem=halo_sems.at[1],
            device_id=(lax.axis_index("batch"), lax.rem(me + 1, experts)),
            device_id_type=MESH,
        )

        @pl.when(me < experts - 1)
        def _():
            halo.start()

        @pl.when(me == 0)
        def _():
            before[...] = jnp.zeros(before.shape, F32)

        loads[2].wait()

        def to_gate(at):
            lanes = pl.ds(pl.multiple_of(half + at.start, LANES), at.size)
            gate_z[:, at] = jnp.dot(normed[...], in_proj[:, lanes], preferred_element_type=F32)

        over_blocks(inner_width, 4 * LANES, to_gate)
        for keep in keeps[2:5]:
            keep.start()
        keeps[0].start()
        loads[3].wait()
        upstream[...] = in_segments(upstream_in, turn)
        keeps[1].start()
        target = slot_targets(route_ref[...], experts, capacity, slots)
        row_ref[...] = target
        wide = jnp.broadcast_to(target.astype(F32), (SEGS, count))
        col_ref[...] = jnp.transpose(wide)[:, :1].astype(jnp.int32)
        slot_id = lax.broadcasted_iota(jnp.int32, (slots, count), 0)

        def dispatch(e, carry):
            picked = (slot_id + e * slots == row_ref[...]).astype(F32).astype(BF16)
            sent[e] = jnp.dot(picked, upstream[...], preferred_element_type=F32).astype(BF16)
            return carry

        lax.fori_loop(0, experts, dispatch, 0)
        side.start(0, parts)

        @pl.when(me < experts - 1)
        def _():
            halo.wait_send()

        @pl.when(me > 0)
        def _():
            halo.wait_recv()

        before_ref[...] = before[...]

        def to_mixed(at):
            own = inner[:, at].astype(F32)
            for k in range(reach):
                tile = own[count - rim + k * SEGS : count - rim + (k + 1) * SEGS]
                ext_in[k * SEGS : (k + 1) * SEGS, at] = shifted_in(
                    tile, before[k : k + 1, at], True
                )
            ext_in[rim:, at] = own
            total = jnp.broadcast_to(small[1:2, at], own.shape)
            for k in range(reach + 1):
                total = total + conv_ref[k : k + 1, at] * ext_in[k * SEGS : k * SEGS + count, at]
            mixed[:, at] = silu(total).astype(BF16)

        over_blocks(inner_width, 2 * LANES, to_mixed)
        keeps[5].start()
        proj[...] = lax.dot_general(
            mixed[...], x_proj[...], (((1,), (1,)), ((), ())), preferred_element_type=F32
        )
        keeps[8].start()

        def to_delta(at):
            own = jnp.dot(
                proj[...].astype(BF16), dt_proj[:, at], preferred_element_type=F32
            )
            own = own + small[2:3, at]
            pre[:, at] = own
            delta[:, at] = softplus(own)

        over_blocks(inner_width, 2 * LANES, to_delta)
        keeps[6].start()
        keeps[7].start()

    @pl.when((phase == 0) & (block == 0))
    def _():
        front()

    for part, (at_phase, at_block) in enumerate(((0, blocks // 2), (1, 1))):

        @pl.when((phase == at_phase) & (block == at_block))
        def _():
            side.start(part + 1, parts)

    def ends(first):
        in_s[...] = delta[:, here] * mixed[:, here].astype(F32)
        sums = jnp.sum(delta[:, here].reshape(steps, SEGS, LANES), axis=0)

        def one(j, held):
            rows = tile_rows(j)
            d, u = delta[rows, here], in_s[rows, :]
            tile = proj[rows, :] if first else None
            new = []
            for n in range(states):
                if first:
                    b = over_lanes(tile[:, rank + n : rank + n + 1])
                    bb[j, n] = b
                    cb[j, n] = over_lanes(tile[:, rank + states + n : rank + states + n + 1])
                else:
                    b = bb[j, n]
                new.append(jnp.exp2(d * rates[n]) * held[n] + u * b)
            return tuple(new)

        zero = jnp.zeros((SEGS, LANES), F32)
        held = lax.fori_loop(0, steps, one, (zero,) * states, unroll=4)
        carries.put(block, held, sums, rates, run_a, run_b)

    @pl.when((phase == 0) & (block == 0))
    def _():
        ends(True)

    @pl.when((phase == 0) & (block > 0))
    def _():
        ends(False)

    @pl.when(phase == 1)
    def _():
        carries.await_group(block)
        start = carries.starts(block, rate2, run_a, run_b)
        own = mixed[:, here].astype(F32)
        in_s[...] = delta[:, here] * own
        ssm_ref[...] = small[0:1, here] * own
        for n in range(states):
            held_ref[0, 0, n] = start[n]

        def one(j, held):
            rows = tile_rows(j)
            d, u = delta[rows, here], in_s[rows, :]
            total = ssm_ref[rows, :]
            new = []
            for n in range(states):
                h = jnp.exp2(d * rates[n]) * held[n] + u * bb[j, n]
                held_ref[0, j + 1, n] = h
                total = total + cb[j, n] * h
                new.append(h)
            ssm_ref[rows, :] = total
            return tuple(new)

        lax.fori_loop(0, steps, one, tuple(start), unroll=4)
        gated_ref[:, here] = (ssm_ref[...] * silu(gate_z[:, here])).astype(BF16)

    @pl.when((phase == 1) & (block == blocks - 1))
    def _():
        loads[4].wait()
        hidden = tokens[...].astype(F32) + jnp.dot(
            gated_ref[...], out_proj[...], preferred_element_type=F32
        )
        hidden_ref[...] = hidden
        normed_two_ref[...] = rms(hidden, as_row(gain_two_ref)).astype(BF16)
        side.wait()
        for keep in keeps:
            keep.wait()


def forward(
    tokens,
    upstream,
    in_proj,
    out_proj,
    route,
    gain_one,
    gain_two,
    conv_weight,
    conv_bias,
    x_proj,
    dt_proj,
    dt_bias,
    skip,
    rate_log,
    sizes,
    collective_id,
):
    rank, capacity, slots = sizes
    count, width = tokens.shape[1:]
    inner_width = out_proj.shape[0]
    states, steps, blocks = rate_log.shape[0], count // SEGS, inner_width // LANES
    experts = lax.axis_size("expert")
    rim = (conv_weight.shape[0] - 1) * SEGS
    vmem, hbm = (pl.BlockSpec(memory_space=m) for m in (pltpu.VMEM, pl.ANY))
    spread = pltpu.VMEM((steps, states, SEGS, LANES), F32)
    run = pltpu.VMEM((blocks, states, SEGS, LANES), F32)
    whole = lambda *shape: pl.BlockSpec(shape, lambda p, c: (0,) * len(shape))
    shape_of = jax.ShapeDtypeStruct
    kept = [
        shape_of((count, width), BF16),
        shape_of((count, width), BF16),
        shape_of((count, width), BF16),
        shape_of((count, inner_width), BF16),
        shape_of((count, inner_width), F32),
        shape_of((count, inner_width), BF16),
        shape_of((count, inner_width), F32),
        shape_of((count, inner_width), F32),
        shape_of((count, LANES), F32),
    ]
    exchanged = (experts, slots, width)
    out = pl.pallas_call(
        functools.partial(forward_kernel, (states, steps, rank, capacity)),
        grid=(2, blocks),
        out_shape=[
            shape_of((count, inner_width), F32),
            shape_of((blocks, steps + 1, states, SEGS, LANES), F32),
            shape_of((count, inner_width), BF16),
            shape_of((count, width), F32),
            shape_of((count, width), BF16),
            shape_of((1, count), jnp.int32),
            shape_of((count, 1), jnp.int32),
            shape_of((SEGS, inner_width), F32),
            shape_of(exchanged, BF16),
        ]
        + kept,
        in_specs=[hbm] * 4
        + [vmem] * 9
        + [pl.BlockSpec((states, LANES), lambda p, c: (0, c))],
        out_specs=[
            pl.BlockSpec((count, LANES), lambda p, c: (0, p * c)),
            pl.BlockSpec((1, steps + 1, states, SEGS, LANES), lambda p, c: (p * c, 0, 0, 0, 0)),
            whole(count, inner_width),
            whole(count, width),
            whole(count, width),
            whole(1, count),
            whole(count, 1),
            vmem,
            hbm,
        ]
        + [hbm] * len(kept),
        scratch_shapes=[
            pltpu.VMEM((count, width), BF16),
            pltpu.VMEM((count, width), BF16),
            pltpu.VMEM(in_proj.shape, BF16),
            pltpu.VMEM(out_proj.shape, BF16),
            pltpu.VMEM((width // LANES, count, LANES), F32),
            pltpu.VMEM((count + rim, inner_width), F32),
            pltpu.VMEM((SEGS, inner_width), F32),
            pltpu.VMEM(exchanged, BF16),
        ]
        + [pltpu.VMEM(k.shape, k.dtype) for k in kept]
        + [
            pltpu.VMEM((count, LANES), F32),
            spread,
            spread,
            run,
            run,
            Side.scratch(experts),
            pltpu.SemaphoreType.DMA((5,)),
            pltpu.SemaphoreType.DMA((len(kept),)),
            pltpu.SemaphoreType.DMA((2,)),
            pltpu.VMEM((LANES, inner_width), BF16),
            pltpu.VMEM((LANES, inner_width), BF16),
            pltpu.VMEM((SEGS, inner_width), F32),
            pltpu.VMEM((SEGS, inner_width), F32),
        ]
        + Carries.scratch(states, blocks, experts),
        compiler_params=params(collective_id=collective_id, has_side_effects=True),
        name="forward",
    )(
        tokens,
        upstream,
        in_proj,
        out_proj,
        route,
        gain_one,
        gain_two,
        conv_weight,
        conv_bias,
        x_proj,
        dt_proj,
        dt_bias,
        skip,
        rate_log,
    )
    return out[:9], out[9:]


def backward_kernel(states, steps, rank, kinds, *refs):
    many = len(kinds)
    expert_hbm, sum_in, refs = refs[:2], refs[2 : 2 + many], refs[2 + many :]
    delta_hbm, g_hbm, in_hbm, pre_hbm, bc_ref, rate_ref, skip_ref, held_ref, side_in = refs[:9]
    sum_out, refs = refs[9 : 9 + many], refs[9 + many :]
    pre_grad_ref, mixed_grad_ref, rate_grad_ref, skip_grad_ref, bias_grad_ref = refs[:5]
    bc_grad_ref, side_out = refs[5:7]
    landings, refs = refs[7:9], refs[9:]
    in_s, rate_sum, in_sum, bb, cb, b_acc, c_acc, run_a, run_b, side_sems = refs[:10]
    skip_row, halving_sems, refs = refs[10], refs[11:13], refs[13:]
    delta_ref, g_ref, in_ref, pre_ref, load_sems = refs[:5]
    carry_refs, sum_refs = refs[5:10], refs[10:]
    loads = [
        pltpu.make_async_copy(src, dst, load_sems.at[i])
        for i, (src, dst) in enumerate(
            ((delta_hbm, delta_ref), (g_hbm, g_ref), (in_hbm, in_ref), (pre_hbm, pre_ref))
        )
    ]
    halvings = [Halving(expert_hbm[i], i == 0, halving_sems[i]) for i in range(2)]
    phase, block = pl.program_id(0), pl.program_id(1)
    here = pl.ds(pl.multiple_of(block * LANES, LANES), LANES)
    blocks = carry_refs[2].shape[1]
    carries = Carries(states, blocks, False, *carry_refs)
    sums = summings(kinds, sum_in, sum_out, sum_refs)
    side = Side(side_in, side_out, side_sems)
    rate2 = -jnp.exp(rate_ref[:, here]) * LOG2E
    rates = [over_sublanes(rate2[n : n + 1, :]) for n in range(states)]
    zero = jnp.zeros((SEGS, LANES), F32)

    @pl.when((phase == 0) & (block == 0))
    def _():
        for load in loads:
            load.start()
        skip_row[...] = as_row(skip_ref)
        greet_others()
        for item in sums:
            item.start(0)
        for halving, landing in zip(halvings, landings):
            for copy in halving.first(landing):
                copy.start()
        for load in loads[:2]:
            load.wait()

    @pl.when((phase == 1) & (block == 0))
    def _():
        for load in loads[2:]:
            load.wait()

    @pl.when((phase == 0) & (block == blocks - 3))
    def _():
        for item in sums:
            if not item.pairs_first:
                item.advance(0)

    @pl.when((phase == 1) & (block == 1))
    def _():
        for item in sums:
            if item.pairs_first:
                item.advance(0)

    @pl.when((phase == 1) & (block == blocks // 2 - 1))
    def _():
        side.start()

    def ends(first):
        sums = jnp.sum(delta_ref[:, here].reshape(steps, SEGS, LANES), axis=0)

        def one(i, held):
            j = steps - 1 - i
            d, g = delta_ref[tile_rows(j), here], g_ref[tile_rows(j), here]
            tile = bc_ref[tile_rows(j), :] if first else None
            new = []
            for n in range(states):
                if first:
                    c = over_lanes(tile[:, rank + states + n : rank + states + n + 1])
                    bb[j, n] = over_lanes(tile[:, rank + n : rank + n + 1])
                    cb[j, n] = c
                else:
                    c = cb[j, n]
                new.append(jnp.exp2(d * rates[n]) * (held[n] + g * c))
            return tuple(new)

        held = lax.fori_loop(0, steps, one, (zero,) * states, unroll=4)
        carries.put(block, held, sums, rates, run_a, run_b)

    @pl.when((phase == 0) & (block == 0))
    def _():
        ends(True)

    @pl.when((phase == 0) & (block > 0))
    def _():
        ends(False)

    def grads(first, last):
        start = carries.starts(block, rate2, run_a, run_b)
        delta, g = delta_ref[:, here], g_ref[:, here]
        mixed = in_ref[:, here].astype(F32)
        in_s[...] = delta * mixed
        place = lax.broadcasted_iota(jnp.int32, (SEGS, LANES), 1)

        def one(i, carry):
            edge, rate_acc = carry
            j = steps - 1 - i
            rows = tile_rows(j)
            d, u, g = delta_ref[rows, here], in_s[rows, :], g_ref[rows, here]
            by_rate = by_b = sums = zero
            new_edge, new_acc = [], []
            for n in range(states):
                b, c = bb[j, n], cb[j, n]
                q = c * g + edge[n]
                e = jnp.exp2(d * rates[n]) * q
                v = e * held_ref[0, j, n]
                by_rate = by_rate + rates[n] * v
                by_b = by_b + b * q
                to_b = q * u
                to_c = g * held_ref[0, j + 1, n]
                if not first:
                    to_b = b_acc[j, n] + to_b
                    to_c = c_acc[j, n] + to_c
                if last:
                    sums = jnp.where(place == rank + n, jnp.sum(to_b, axis=1, keepdims=True), sums)
                    to_c = jnp.sum(to_c, axis=1, keepdims=True)
                    sums = jnp.where(place == rank + states + n, to_c, sums)
                else:
                    b_acc[j, n] = to_b
                    c_acc[j, n] = to_c
                new_edge.append(e)
                new_acc.append(rate_acc[n] + d * v)
            rate_sum[rows, :] = by_rate
            in_sum[rows, :] = by_b
            if last:
                bc_grad_ref[rows, :] = sums
            return tuple(new_edge), tuple(new_acc)

        _, rate_acc = lax.fori_loop(
            0, steps, one, (tuple(start), (zero,) * states), unroll=4
        )
        for n in range(states):
            rate_grad_ref[n : n + 1, here] = (
                LN2 * rate2[n : n + 1, :] * jnp.sum(rate_acc[n], axis=0, keepdims=True)
            )
        by_b = in_sum[...]
        pre_grad = (LN2 * rate_sum[...] + mixed * by_b) * jax.nn.sigmoid(pre_ref[:, here])
        pre_grad_ref[:, here] = pre_grad.astype(BF16)
        bias_grad_ref[:, here] = jnp.sum(pre_grad, axis=0, keepdims=True)
        mixed_grad_ref[:, here] = delta * by_b + skip_row[:, here] * g
        skip_grad_ref[:, here] = jnp.sum(g * mixed, axis=0, keepdims=True)

    @pl.when(phase == 1)
    def _():
        carries.await_group(block)

    @pl.when((phase == 1) & (block == 0))
    def _():
        grads(True, False)

    @pl.when((phase == 1) & (block > 0) & (block < blocks - 1))
    def _():
        grads(False, False)

    @pl.when((phase == 1) & (block == blocks - 1))
    def _():
        grads(False, True)
        side.wait()
        for item in sums:
            item.wait(1)
            item.add(1)
        for halving, landing in zip(halvings, landings):
            for copy in halving.first(landing):
                copy.wait()


def mixer_grads(
    pre, delta, mixed, ssm_grad, bc, rate_log, skip, held, beside, experts, rank, items, collective_id
):
    count, width = delta.shape
    states, steps, blocks = rate_log.shape[0], count // SEGS, width // LANES
    spread = pltpu.VMEM((steps, states, SEGS, LANES), F32)
    run = pltpu.VMEM((blocks, states, SEGS, LANES), F32)
    flat = pltpu.VMEM((count, LANES), F32)
    sum_scratch = [item.first_scratch() for item in items]
    kinds = tuple((item.kind(), len(refs)) for item, refs in zip(items, sum_scratch))
    spread_specs = [
        pl.BlockSpec(item.spread_shape().shape, lambda p, c, rank=len(item.spread_shape().shape): (0,) * rank)
        for item in items
    ]
    outs = pl.pallas_call(
        functools.partial(backward_kernel, states, steps, rank, kinds),
        grid=(2, blocks),
        out_shape=[item.spread_shape() for item in items]
        + [
            jax.ShapeDtypeStruct((count, width), BF16),
            jax.ShapeDtypeStruct((count, width), F32),
            jax.ShapeDtypeStruct((states, width), F32),
            jax.ShapeDtypeStruct((1, width), F32),
            jax.ShapeDtypeStruct((1, width), F32),
            jax.ShapeDtypeStruct((count, LANES), F32),
            jax.ShapeDtypeStruct(beside.shape, beside.dtype),
        ]
        + [jax.ShapeDtypeStruct((2, e.shape[0] // 4, e.shape[1]), BF16) for e in experts],
        in_specs=[pl.BlockSpec(memory_space=pl.ANY)] * (2 + len(items))
        + [pl.BlockSpec(memory_space=pl.ANY)] * 4
        + [pl.BlockSpec(memory_space=pltpu.VMEM)] * 3
        + [
            pl.BlockSpec((1, steps + 1, states, SEGS, LANES), lambda p, c: (p * c, 0, 0, 0, 0)),
            pl.BlockSpec(memory_space=pl.ANY),
        ],
        out_specs=spread_specs
        + [pl.BlockSpec(memory_space=pltpu.VMEM)] * 6
        + [pl.BlockSpec(memory_space=pl.ANY)] * 3,
        scratch_shapes=[flat, flat, flat, spread, spread, spread, spread, run, run]
        + [Side.scratch(lax.axis_size("expert")), pltpu.VMEM((1, width), F32)]
        + [pltpu.SemaphoreType.DMA((2, 2))] * 2
        + [pltpu.VMEM((count, width), kind) for kind in (F32, F32, BF16, F32)]
        + [pltpu.SemaphoreType.DMA((4,))]
        + Carries.scratch(states, blocks, lax.axis_size("expert"))
        + [ref for refs in sum_scratch for ref in refs],
        compiler_params=params(collective_id=collective_id, has_side_effects=True),
        name="mixer_grads",
    )(*experts, *(item.local for item in items), delta, ssm_grad, mixed, pre, bc, rate_log, skip, held, beside)
    return outs


def shifted_in(tile, row, forward):
    if forward:
        return jnp.concatenate([row, tile[: SEGS - 1]], axis=0)
    return jnp.concatenate([tile[1:], row], axis=0)


def middle_kernel(*refs):
    hidden_ref, grad_ref, upstream_ref, gain_ref, normed_ref = refs[:5]
    gated_ref, ssm_ref, gate_ref, out_proj_ref = refs[5:9]
    hidden_grad_ref, gain_out, ssm_grad_ref, gate_grad_ref, out_local_ref, gate_local_ref = refs[9:15]
    branch = refs[15]

    @pl.when(pl.program_id(0) == 0)
    def _():
        to_hidden, to_gain = rms_back(hidden_ref[...], as_row(gain_ref), grad_ref[...])
        total = upstream_ref[...].astype(F32) + to_hidden
        hidden_grad_ref[...] = total
        branch[...] = total.astype(BF16)
        gain_out[...] = to_gain[None]

    over_rows = (((0,), (0,)), ((), ()))
    out_local_ref[...] = lax.dot_general(
        gated_ref[...], branch[...], over_rows, preferred_element_type=F32
    ).astype(BF16)
    gated_grad = lax.dot_general(
        branch[...], out_proj_ref[...], (((1,), (1,)), ((), ())), preferred_element_type=F32
    )
    gate = gate_ref[...]
    s = jax.nn.sigmoid(gate)
    ssm_grad_ref[...] = gated_grad * (gate * s)
    low = (gated_grad * ssm_ref[...] * (s * (1.0 + gate * (1.0 - s)))).astype(BF16)
    gate_grad_ref[...] = low
    gate_local_ref[...] = lax.dot_general(
        normed_ref[...], low, over_rows, preferred_element_type=F32
    ).astype(BF16)


def middle(hidden, grad, upstream, gain, normed, gated, ssm, gate_z, out_proj):
    count, width = hidden.shape
    inner_width = out_proj.shape[0]
    wide = 2 * LANES
    vmem = pl.BlockSpec(memory_space=pltpu.VMEM)
    whole = lambda *shape: pl.BlockSpec(shape, lambda c: (0,) * len(shape))
    lanes = lambda rows: pl.BlockSpec((rows, wide), lambda c: (0, c))
    rows = pl.BlockSpec((wide, width), lambda c: (c, 0))
    shape_of = jax.ShapeDtypeStruct
    return pl.pallas_call(
        middle_kernel,
        grid=(inner_width // wide,),
        out_shape=[
            shape_of((count, width), F32),
            shape_of((1, width), F32),
            shape_of((count, inner_width), F32),
            shape_of((count, inner_width), BF16),
            shape_of((inner_width, width), BF16),
            shape_of((width, inner_width), BF16),
        ],
        in_specs=[vmem] * 5 + [lanes(count)] * 3 + [rows],
        out_specs=[whole(count, width), whole(1, width), lanes(count), lanes(count), rows]
        + [lanes(width)],
        scratch_shapes=[pltpu.VMEM((count, width), BF16)],
        compiler_params=params(),
        name="middle",
    )(hidden, grad, upstream, gain, normed, gated, ssm, gate_z, out_proj)


WIDE = 2 * LANES


def put_by_token(out_ref, value, turn):
    steps = value.shape[0] // SEGS
    for lane in range(turn.shape[0]):
        lanes = slice(lane * LANES, (lane + 1) * LANES)
        turn[lane] = value[:, lanes]
        for s in range(SEGS):
            rows = turn[lane, pl.ds(s, steps, stride=SEGS), :]
            out_ref[s * steps : (s + 1) * steps, lanes] = rows.astype(out_ref.dtype)


def tile_places(pack, flat):
    _, pairs, each = pack.shape[:3]
    across = flat.shape[1] // LANES
    for t in range(2 * pairs * each):
        row, lane = t // across * 16, t % across * LANES
        inside = (slice(row, row + 16), slice(lane, lane + LANES)) if row < flat.shape[0] else None
        yield (t // (pairs * each), t // each % pairs, t % each), inside


def put_tiles(pack, flat):
    for tile, inside in tile_places(pack, flat):
        if inside is None:
            pack[tile] = jnp.zeros((16, LANES), BF16)
        else:
            pack[tile] = flat[inside].astype(BF16)


def get_tiles(flat, pack):
    for tile, inside in tile_places(pack, flat):
        if inside is not None:
            flat[inside] = pack[tile].astype(F32)


def finish_kernel(rank, states, kinds, *refs):
    loads_hbm, expert_hbm, landed_hbm, refs = refs[:11], refs[11:13], refs[13:15], refs[15:]
    bc_grad_ref, low_ref, x_proj_ref, dt_proj_ref, conv_ref, bias_ref = refs[:6]
    before_ref, gain_ref, rate_ref, dt_bias_ref, skip_ref, gain_two_ref, router_ref = refs[6:13]
    col_ref, gate_spread, out_spread = refs[13:16]
    output_ref, tokens_grad_ref, in_proj_out, out_proj_out, flat, last_flat = refs[16:22]
    second_hbm, refs = refs[22:24], refs[24:]
    halving_refs, halving_sems, refs = refs[:4], refs[4:8], refs[8:]
    halvings = [Halving(expert_hbm[i], i == 0, halving_sems[i]) for i in range(2)]
    loaded, refs = refs[:11], refs[11:]
    pre_grad, mixed_part, mixed, inner, normed, in_proj, gate_grad, tokens, hidden_grad = loaded[:9]
    hidden, home = loaded[9:]
    ext_in, ext_grad, inner_grad, proj_grad, rows, head, after = refs[:7]
    turn, load_sems, halo_sems = refs[7:10]
    small, last_small = SmallSum(*refs[10:17]), SmallSum(*refs[17:24])
    x_proj, dt_proj, bias_row = refs[24:27]
    parts, refs = len(kinds) - 2, refs[27:]
    locals_, sum_refs = refs[:parts], refs[parts:]
    count, width = tokens.shape
    inner_width = inner.shape[1]
    reach = conv_ref.shape[0] - 1
    rim = reach * SEGS
    experts, me = lax.axis_size("expert"), lax.axis_index("expert")
    group = lax.axis_index("batch")
    half = inner_width

    loads = [
        pltpu.make_async_copy(src, dst, load_sems.at[i])
        for i, (src, dst) in enumerate(zip(loads_hbm, loaded))
    ]
    halving_loads = []
    for i, halving in enumerate(halvings):
        for k, src in enumerate((halving.chunk(halving.far), landed_hbm[i].at[1])):
            halving_loads.append(
                pltpu.make_async_copy(src, halving_refs[2 * i + k], halving_sems[2 + i].at[k])
            )
    for load in loads[:1] + halving_loads + loads[1:]:
        load.start()
    ends = [0]
    for ref in locals_:
        ends.append(ends[-1] + ref.shape[2])
    inner_rows = [slice(ends[i], ends[i + 1]) for i in range(parts)]
    gate_sum, out_sum, *inner_sums = summings(
        kinds,
        (gate_spread, out_spread, *locals_),
        (in_proj_out.at[:, half:], out_proj_out)
        + tuple(in_proj_out.at[at, :half] for at in inner_rows),
        sum_refs,
    )
    greet_others()
    gate_sum.begin()
    out_sum.begin()
    x_proj[...] = padded_rows(x_proj_ref, LANES)
    dt_proj[...] = padded_rows(dt_proj_ref, LANES)
    bias_row[...] = as_row(bias_ref)
    low = low_ref[...].astype(BF16)
    flat[...] = jnp.zeros(flat.shape, F32)
    last_flat[...] = jnp.zeros(last_flat.shape, F32)

    seconds = []
    for i, halving in enumerate(halvings):
        own, brought = halving_refs[2 * i : 2 * i + 2]
        for load in halving_loads[2 * i : 2 * i + 2]:
            load.wait()

        def join(n, carry, own=own, brought=brought):
            at = pl.ds(pl.multiple_of(n * 16, 16), 16)
            own[at, :] = together(own[at, :], brought[at, :]).astype(BF16)
            return carry

        lax.fori_loop(0, own.shape[0] // 16, join, 0)
        seconds.append(halving.second(own, second_hbm[i]))
        seconds[i].start()

    loads[0].wait()
    over_inner = (((1,), (1,)), ((), ()))
    over_rows = (((0,), (0,)), ((), ()))
    low_grad = lax.dot_general(
        pre_grad[...], dt_proj[...], over_inner, preferred_element_type=F32
    )
    proj_grad[...] = (low_grad + bc_grad_ref[...]).astype(BF16)

    for load in loads[1:4]:
        load.wait()

    def before_silu(at):
        own = inner[:, at].astype(F32)
        for k in range(reach):
            tile = own[count - rim + k * SEGS : count - rim + (k + 1) * SEGS]
            ext_in[k * SEGS : (k + 1) * SEGS, at] = shifted_in(tile, before_ref[k : k + 1, at], True)
        ext_in[rim:, at] = own
        total = jnp.dot(proj_grad[...], x_proj[:, at], preferred_element_type=F32)
        total = total + mixed_part[:, at]
        conv_pre = jnp.broadcast_to(bias_row[:, at], total.shape)
        for k in range(reach + 1):
            conv_pre = conv_pre + conv_ref[k : k + 1, at] * ext_in[k * SEGS : k * SEGS + count, at]
        total = total * silu_slope(conv_pre)
        ext_grad[:count, at] = total
        for k in range(reach):
            head[k : k + 1, at] = total[k * SEGS : k * SEGS + 1]

    over_blocks(inner_width, WIDE, before_silu)
    halo = pltpu.make_async_remote_copy(
        src_ref=head,
        dst_ref=after,
        send_sem=halo_sems.at[0],
        recv_sem=halo_sems.at[1],
        device_id=(group, lax.rem(me + experts - 1, experts)),
        device_id_type=MESH,
    )

    @pl.when(me > 0)
    def _():
        halo.start()

    @pl.when(me == experts - 1)
    def _():
        after[...] = jnp.zeros(after.shape, F32)

    at_dt = rank + 2 * states
    x_local = lax.dot_general(proj_grad[...], mixed[...], over_rows, preferred_element_type=F32)
    flat[:at_dt, :] = x_local[:at_dt]
    dt_local = lax.dot_general(low, pre_grad[...], over_rows, preferred_element_type=F32)
    flat[at_dt : at_dt + rank, :] = dt_local[:rank]
    at = at_dt + rank + states
    flat[at_dt + rank : at, :] = rate_ref[...]
    flat[at : at + 1, :] = dt_bias_ref[...]
    flat[at + 1 : at + 2, :] = skip_ref[...]
    flat[at + 2 : at + 3, :width] = gain_two_ref[...]
    fold = router_ref.shape[0] // 2
    flat[at + 3 : at + 3 + fold, :width] = router_ref[:fold, :]
    flat[at + 3 : at + 3 + fold, width:] = router_ref[fold:, :]
    put_tiles(small.pack, flat)
    small.start(0)
    for load in loads[4:7]:
        load.wait()
    rows[...] = lax.dot_general(
        gate_grad[...], in_proj[:, half:], over_inner, preferred_element_type=F32
    )

    @pl.when(me > 0)
    def _():
        halo.wait_send()

    @pl.when(me < experts - 1)
    def _():
        halo.wait_recv()

    def before_taps(at):
        for k in range(reach):
            tile = ext_grad[k * SEGS : (k + 1) * SEGS, at]
            ext_grad[count + k * SEGS : count + (k + 1) * SEGS, at] = shifted_in(
                tile, after[k : k + 1, at], False
            )
        total = conv_ref[0:1, at] * ext_grad[rim : rim + count, at]
        for k in range(1, reach + 1):
            first = (reach - k) * SEGS
            total = total + conv_ref[k : k + 1, at] * ext_grad[first : first + count, at]
        inner_grad[:, at] = total.astype(BF16)

    over_blocks(inner_width, WIDE, before_taps)
    chunk = width // experts
    share = inner_width // lax.axis_size("batch")

    def to_in_proj(at):
        total = lax.dot_general(
            normed[...], inner_grad[:, at], over_rows, preferred_element_type=F32
        ).astype(BF16)
        for e in range(experts):
            own = total[e * chunk : (e + 1) * chunk]
            for ref, rows_at in zip(locals_, inner_rows):
                ref[e // 2, e % 2, :, at] = own[rows_at]

    over_blocks(inner_width, share, to_in_proj)
    for item in inner_sums:
        item.begin()
    small.advance(0)


    def to_taps(at):
        grad = ext_grad[:count, at]
        for k in range(reach + 1):
            last_flat[k : k + 1, at] = jnp.sum(
                grad * ext_in[k * SEGS : k * SEGS + count, at], axis=0, keepdims=True
            )
        last_flat[reach + 1 : reach + 2, at] = jnp.sum(grad, axis=0, keepdims=True)

    for item in inner_sums:
        item.advance(0)
    over_blocks(inner_width, WIDE, to_taps)
    for load in loads[7:]:
        load.wait()
    grad = rows[...] + lax.dot_general(
        inner_grad[...], in_proj[:, :half], over_inner, preferred_element_type=F32
    )
    values = tokens[...].astype(F32)
    to_values, to_gain = rms_back(values, as_row(gain_ref), grad)
    put_by_token(tokens_grad_ref, to_values + hidden_grad[...], turn)

    last_flat[reach + 2 : reach + 3, :width] = to_gain[None]
    put_tiles(last_small.pack, last_flat)
    last_small.start(0)
    gate_sum.advance(2)
    out_sum.advance(2)
    small.advance(1)
    last_small.advance(0)
    for item in inner_sums:
        item.advance(1)
    last_small.advance(1)
    small.advance(2)

    slots = home.shape[1]
    slot_id = lax.broadcasted_iota(jnp.int32, (count, experts * slots), 1)
    chosen = (slot_id == col_ref[...]).astype(F32).astype(BF16)
    returned = jnp.dot(
        chosen, home[...].reshape(experts * slots, width), preferred_element_type=F32
    )
    put_by_token(output_ref, hidden[...] + returned, turn)

    last_small.advance(2)
    gate_sum.advance(3)
    out_sum.advance(3)
    for item in inner_sums:
        item.advance(2)
    small.advance(3)
    last_small.advance(3)
    small.advance(4)
    get_tiles(flat, small.every)
    for item in inner_sums:
        item.advance(3)
    last_small.advance(4)
    get_tiles(last_flat, last_small.every)
    for copy in seconds:
        copy.wait()


def finish(loaded, experts, landed, small, early, rank, states, collective_id):
    pre_grad, in_proj, tokens = loaded[0], loaded[5], loaded[7]
    conv_weight, router_local = small[4], small[12]
    count, inner_width = pre_grad.shape
    width = tokens.shape[1]
    count_experts, ways = lax.axis_size("expert"), lax.axis_size("batch")
    pairs, chunk = count_experts // 2, width // count_experts
    chunks = [(e.shape[0] // 4, e.shape[1]) for e in experts]
    taps = conv_weight.shape[0]
    vmem, hbm = (pl.BlockSpec(memory_space=m) for m in (pltpu.VMEM, pl.ANY))
    split = (chunk * 2 // 3, chunk // 3) if chunk % 48 == 0 else (chunk,)
    locals_ = [jax.ShapeDtypeStruct((pairs, 2, part, inner_width), BF16) for part in split]
    items = early + [Total(local, 1, i == 1) for i, local in enumerate(locals_)]
    scratch = [item.scratch() for item in items]
    kinds = tuple((item.kind(), len(refs)) for item, refs in zip(items, scratch))
    used = 2 * rank + 3 * states + 3 + router_local.shape[0] // 2
    high, low = (-(-rows // 16) * 16 for rows in (used, taps + 2))
    tiles = [-(-(rows // 16 * inner_width // LANES) // (2 * pairs)) for rows in (high, low)]
    f32 = lambda *shape: jax.ShapeDtypeStruct(shape, F32)
    halo = pltpu.VMEM((SEGS, inner_width), F32)
    rim = (taps - 1) * SEGS
    return pl.pallas_call(
        functools.partial(finish_kernel, rank, states, kinds),
        out_shape=[
            jax.ShapeDtypeStruct((count, width), BF16),
            f32(count, width),
            jax.ShapeDtypeStruct((chunk, 2 * inner_width), BF16),
            jax.ShapeDtypeStruct(early[1].chunk, BF16),
            f32(high, inner_width),
            f32(low, inner_width),
        ]
        + [jax.ShapeDtypeStruct(shape, BF16) for shape in chunks],
        in_specs=[hbm] * (len(loaded) + 4) + [vmem] * (len(small) + len(early)),
        out_specs=[vmem] * 6 + [hbm] * 2,
        scratch_shapes=[pltpu.VMEM(shape, BF16) for shape in chunks for _ in range(2)]
        + [pltpu.SemaphoreType.DMA((2, 1))] * 2
        + [pltpu.SemaphoreType.DMA((2,))] * 2
        + [pltpu.VMEM(a.shape, a.dtype) for a in loaded]
        + [
            pltpu.VMEM((count + rim, inner_width), F32),
            pltpu.VMEM((count + rim, inner_width), F32),
            pltpu.VMEM((count, inner_width), BF16),
            pltpu.VMEM((count, LANES), BF16),
            pltpu.VMEM((count, width), F32),
            halo,
            halo,
            pltpu.VMEM((width // LANES, count, LANES), F32),
            pltpu.SemaphoreType.DMA((len(loaded),)),
            pltpu.SemaphoreType.DMA((2,)),
        ]
        + SmallSum.scratch(pairs, ways, tiles[0])
        + SmallSum.scratch(pairs, ways, tiles[1])
        + [
            pltpu.VMEM((LANES, inner_width), BF16),
            pltpu.VMEM((LANES, inner_width), BF16),
            pltpu.VMEM((1, inner_width), F32),
        ]
        + [pltpu.VMEM(local.shape, BF16) for local in locals_]
        + [ref for refs in scratch for ref in refs],
        compiler_params=params(collective_id=collective_id, has_side_effects=True),
        name="finish",
    )(*loaded, *experts, *landed, *small, *(item.local for item in early))


def deliver_kernel(*refs):
    output_in, tokens_grad_in, in_proj, out_proj, flat, last = refs[:6]
    expert_hbm, landed_hbm, second_hbm, refs = refs[6:8], refs[8:10], refs[10:12], refs[12:]
    output, tokens_grad, gain, in_proj_out, conv, bias, x_proj, dt_proj, dt_bias, rate = refs[:10]
    skip, out_proj_out, gain_two, router, expert_in_out, expert_out_out = refs[10:16]
    held, sems = refs[16:22], refs[22]
    loads = []
    for i in range(2):
        halving = Halving(expert_hbm[i], i == 0)
        parts = (halving.chunk(halving.group), landed_hbm[i].at[0], second_hbm[i])
        for k, src in enumerate(parts):
            loads.append(pltpu.make_async_copy(src, held[3 * i + k], sems.at[i, k]))
    for load in loads:
        load.start()
    output[0] = output_in[...]
    tokens_grad[0] = tokens_grad_in[...]
    at, width = 0, gain.shape[0]
    for ref in (x_proj, dt_proj, rate):
        ref[...] = flat[at : at + ref.shape[0], :]
        at += ref.shape[0]
    fold = router.shape[0] // 2
    dt_bias[...] = flat[at : at + 1, :].reshape(dt_bias.shape)
    skip[...] = flat[at + 1 : at + 2, :].reshape(skip.shape)
    gain_two[...] = flat[at + 2 : at + 3, :width].reshape(gain_two.shape)
    router[:fold, :] = flat[at + 3 : at + 3 + fold, :width]
    router[fold:, :] = flat[at + 3 : at + 3 + fold, width:]
    taps = conv.shape[0]
    conv[...] = last[:taps, :]
    bias[...] = last[taps : taps + 1, :].reshape(bias.shape)
    gain[...] = last[taps + 1 : taps + 2, :width].reshape(gain.shape)
    in_proj_out[...] = in_proj[...].astype(F32)
    out_proj_out[...] = out_proj[...].astype(F32)
    for i, out in enumerate((expert_in_out, expert_out_out)):
        for load in loads[3 * i : 3 * i + 3]:
            load.wait()
        total = together(*(ref[...] for ref in held[3 * i : 3 * i + 3]))
        out[0] = total.astype(BF16).astype(F32)


def deliver(made, experts, landed, shapes):
    vmem = pl.BlockSpec(memory_space=pltpu.VMEM)
    hbm = pl.BlockSpec(memory_space=pl.ANY)
    output, tokens_grad, in_proj, out_proj, flat, last = made[:6]
    chunks = [(e.shape[0] // 4, e.shape[1]) for e in experts]
    f32 = lambda *shape: jax.ShapeDtypeStruct(shape, F32)
    outs = [
        jax.ShapeDtypeStruct((1, *output.shape), BF16),
        f32(1, *tokens_grad.shape),
        shapes[0],
        f32(*in_proj.shape),
        *shapes[1:8],
        f32(*out_proj.shape),
        *shapes[8:],
        *(f32(1, *shape) for shape in chunks),
    ]
    return pl.pallas_call(
        deliver_kernel,
        out_shape=outs,
        in_specs=[vmem] * 6 + [hbm] * 6,
        out_specs=[vmem] * len(outs),
        scratch_shapes=[pltpu.VMEM(shape, BF16) for shape in chunks for _ in range(3)]
        + [pltpu.SemaphoreType.DMA((2, 3))],
        compiler_params=params(),
        name="deliver",
    )(*made[:6], *experts, *landed, *made[6:])


def silu(v):
    return v * jax.nn.sigmoid(v)


def silu_slope(v):
    s = jax.nn.sigmoid(v)
    return s * (1.0 + v * (1.0 - s))


def rms_back(values, gain, grad):
    r = lax.rsqrt(jnp.mean(values * values, axis=-1, keepdims=True) + 1e-05)
    u = gain * grad
    mean = jnp.mean(values * u, axis=-1, keepdims=True)
    return r * u - values * (r * r * r) * mean, jnp.sum(grad * values * r, axis=0)


def rms(values, gain):
    return values * lax.rsqrt(jnp.mean(values * values, axis=-1, keepdims=True) + 1e-05) * gain


def per_device(
    tokens,
    routes,
    gain_one,
    in_proj,
    conv_weight,
    conv_bias,
    x_proj,
    dt_proj,
    dt_bias,
    rate_log,
    skip,
    out_proj,
    gain_two,
    router,
    expert_in,
    expert_out,
    cotangent,
):
    count, width = tokens.shape[1], tokens.shape[2]
    steps = count // SEGS
    inner_width = out_proj.shape[0]
    rank = dt_proj.shape[0]
    experts = router.shape[0]
    capacity = 5 * count // (4 * experts)
    slots = -(-capacity // 16) * 16
    states = rate_log.shape[0]
    route = routes.reshape(SEGS, steps).T.reshape(1, count)
    made, kept = forward(
        tokens,
        cotangent,
        in_proj,
        out_proj,
        route,
        gain_one,
        gain_two,
        conv_weight,
        conv_bias,
        x_proj,
        dt_proj,
        dt_bias,
        skip,
        rate_log,
        (rank, capacity, slots),
        2,
    )
    ssm, held, gated, hidden, normed_two, row, col, before, slot_upstream = made
    tokens_low, upstream_low, normed_one, inner, gate_z, mixed, pre, delta, proj = kept

    normed_two_grad, results, *expert_grads, router_local = run_experts(
        normed_two, row, col, router, slot_upstream, expert_in, expert_out, slots, 4
    )

    hidden_grad, gain_two_local, ssm_grad, gate_z_grad, out_proj_local, in_proj_gate_local = middle(
        hidden, normed_two_grad, upstream_low, gain_two, normed_one, gated, ssm, gate_z, out_proj
    )
    ways, pairs = lax.axis_size("batch"), experts // 2
    early = [
        Total(
            in_proj_gate_local.reshape(pairs, 2, width // experts, inner_width),
            1,
        ),
        Total(
            out_proj_local.reshape(
                pairs, 2, ways, inner_width // (experts * ways), width
            ),
            0,
            True,
        ),
    ]
    (
        in_proj_gate_spread,
        out_proj_spread,
        pre_grad,
        mixed_grad,
        rate_log_local,
        skip_local,
        dt_bias_local,
        bc_grad,
        returned,
        *landed,
    ) = mixer_grads(
        pre, delta, mixed, ssm_grad, proj, rate_log, skip, held, results, expert_grads, rank, early, 3
    )
    early = [early[0].resumed(in_proj_gate_spread), early[1].resumed(out_proj_spread)]
    outs = finish(
        [
            pre_grad,
            mixed_grad,
            mixed,
            inner,
            normed_one,
            in_proj,
            gate_z_grad,
            tokens_low,
            hidden_grad,
            hidden,
            returned,
        ],
        expert_grads,
        landed,
        [
            bc_grad,
            proj,
            x_proj,
            dt_proj,
            conv_weight,
            conv_bias,
            before,
            gain_one,
            rate_log_local,
            dt_bias_local,
            skip_local,
            gain_two_local,
            router_local,
            col,
        ],
        early,
        rank,
        states,
        1,
    )
    outs = (*outs[:3], outs[3].reshape(-1, width), *outs[4:])
    weights = (gain_one, conv_weight, conv_bias, x_proj, dt_proj, dt_bias, rate_log, skip)
    shapes = [jax.ShapeDtypeStruct(w.shape, F32) for w in (*weights, gain_two, router)]
    return tuple(deliver(outs, expert_grads, landed, shapes))


def solution(mesh):
    split = P("batch", "expert", None)
    one = P("expert", None, None)
    both = P("expert", "batch", None)
    in_specs = (split, split) + (P(),) * 12 + (one, one, split)
    out_specs = (split, split, P(), P("expert", None)) + (P(),) * 7
    out_specs += (P("expert", None), P(), P(), both, both)
    return jax.shard_map(
        per_device, mesh=mesh, in_specs=in_specs, out_specs=out_specs, check_vma=False
    )
```

```python
import functools

import jax
import jax.numpy as jnp
from jax import lax
from jax.experimental import pallas as pl
from jax.experimental.pallas import tpu as pltpu
from jax.sharding import PartitionSpec as P

F32, BF16 = jnp.float32, jnp.bfloat16
SEGS = 8
LANES = 128
LOG2E = 1.4426950408889634
LN2 = 0.6931471805599453
VMEM_LIMIT = 60 * 1024 * 1024
MESH = pl.DeviceIdType.MESH


def params(**kw):
    return pltpu.CompilerParams(vmem_limit_bytes=VMEM_LIMIT, **kw)


def softplus(v):
    return jnp.maximum(v, 0.0) + jnp.log1p(jnp.exp(-jnp.abs(v)))


def as_row(ref):
    return ref[...].reshape(1, ref.shape[0])


def padded_rows(ref, high):
    low = jnp.zeros((high - ref.shape[0], ref.shape[1]), F32)
    return jnp.concatenate([ref[...].astype(F32), low], axis=0).astype(BF16)


def over_sublanes(row):
    return jnp.broadcast_to(row, (SEGS, LANES))


def over_lanes(column):
    return jnp.broadcast_to(column, (SEGS, LANES))


def tile_rows(j):
    return pl.ds(pl.multiple_of(j * SEGS, SEGS), SEGS)


def run_of_segments(a, b, forward):
    at = lax.broadcasted_iota(jnp.int32, (SEGS, LANES), 0)
    for step in (1, 2, 4):
        if forward:
            inside, turn = at >= step, step
        else:
            inside, turn = at < SEGS - step, SEGS - step
        before_a = jnp.where(inside, pltpu.roll(a, turn, 0), 1.0)
        before_b = jnp.where(inside, pltpu.roll(b, turn, 0), 0.0)
        a, b = a * before_a, a * before_b + b
    return a, b


class Carries:
    groups = 2

    def __init__(self, states, blocks, forward, own, lengths, got, got_lengths, sems):
        self.states, self.blocks, self.forward = states, blocks, forward
        self.own, self.lengths, self.got, self.got_lengths = own, lengths, got, got_lengths
        self.sems = sems
        self.count, self.me = lax.axis_size("expert"), lax.axis_index("expert")
        self.per = blocks // self.groups

    @staticmethod
    def scratch(states, blocks, count):
        per = blocks // Carries.groups
        assert blocks % Carries.groups == 0 and per <= SEGS
        return [
            pltpu.VMEM((blocks, states, LANES), BF16),
            pltpu.VMEM((Carries.groups, SEGS, LANES), F32),
            pltpu.VMEM((count, blocks, states, LANES), BF16),
            pltpu.VMEM((count, Carries.groups, SEGS, LANES), F32),
            pltpu.SemaphoreType.DMA((2, 2, Carries.groups, count)),
        ]

    def other(self, k):
        return (lax.axis_index("batch"), lax.rem(self.me + k, self.count))

    def copies(self, group):
        blocks = pl.ds(group * self.per, self.per)
        found = []
        for k in range(1, self.count):
            pairs = (
                (self.own.at[blocks], self.got.at[k - 1, blocks]),
                (self.lengths.at[group], self.got_lengths.at[k - 1, group]),
            )
            for i, (src, dst) in enumerate(pairs):
                found.append(
                    pltpu.make_async_remote_copy(
                        src_ref=src,
                        dst_ref=dst,
                        send_sem=self.sems.at[0, i, group, k - 1],
                        recv_sem=self.sems.at[1, i, group, k - 1],
                        device_id=self.other(k),
                        device_id_type=MESH,
                    )
                )
        return found

    def put(self, block, ends, sums, rates, run_a, run_b):
        edge = SEGS - 1 if self.forward else 0
        rows = []
        for n in range(self.states):
            a, b = run_of_segments(jnp.exp2(rates[n] * sums), ends[n], self.forward)
            run_a[block, n] = a
            run_b[block, n] = b
            rows.append(b[edge : edge + 1])
        end = jnp.concatenate(rows, axis=0).astype(BF16)
        total = jnp.sum(sums, axis=0, keepdims=True)
        last = self.count - 1
        self.own[block] = end
        self.got[last, block] = end
        for group in range(self.groups):

            @pl.when(block // self.per == group)
            def _():
                row = pl.ds(lax.rem(block, self.per), 1)
                self.lengths[group, row, :] = total
                self.got_lengths[last, group, row, :] = total

            @pl.when(block == (group + 1) * self.per - 1)
            def _():
                for copy in self.copies(group):
                    copy.start()

    def await_group(self, block):
        for group in range(self.groups):

            @pl.when(block == group * self.per)
            def _():
                for copy in self.copies(group):
                    copy.wait()

    def starts(self, block, rate, run_a, run_b):
        group, row = block // self.per, pl.ds(lax.rem(block, self.per), 1)
        entering = jnp.zeros((self.states, LANES), F32)
        order = range(self.count) if self.forward else range(self.count - 1, -1, -1)
        for place in order:
            slot = lax.rem(self.me - place - 1 + 2 * self.count, self.count)
            length = self.got_lengths[slot, group, row, :]
            joined = jnp.exp2(rate * length) * entering + self.got[slot, block].astype(F32)
            ahead = (place < self.me) if self.forward else (place > self.me)
            entering = jnp.where(ahead, joined, entering)
        found = []
        for n in range(self.states):
            first = entering[n : n + 1]
            after = run_a[block, n] * over_sublanes(first) + run_b[block, n]
            found.append(shifted_in(after, first, self.forward))
        return found


def together(*parts):
    return sum(p.astype(F32) for p in parts)


class Total:
    def __init__(self, local, axis, pairs_first=False, chunk=None):
        self.local, self.axis, self.pairs_first = local, axis, pairs_first
        self.ways = lax.axis_size("batch")
        self.taken_up = chunk is not None
        self.pairs, self.chunk = lax.axis_size("expert") // 2, chunk or local.shape[2:]
        part = list(self.chunk)
        part[axis] //= self.ways
        self.part = tuple(part)

    def kind(self):
        return self.axis, self.pairs_first, self.part, self.taken_up

    def spread_shape(self):
        shape = self.chunk if self.pairs_first else (self.pairs, *self.part)
        return jax.ShapeDtypeStruct(shape, BF16)

    def resumed(self, spread):
        return Total(spread, self.axis, self.pairs_first, self.chunk)

    def first_scratch(self):
        first = (self.pairs - 1, *self.chunk)
        if not self.pairs_first:
            first = (self.ways - 1, self.pairs, *self.part)
        return [
            pltpu.VMEM((2, self.pairs, *self.chunk), BF16),
            pltpu.VMEM((self.pairs, *self.chunk), BF16),
            pltpu.VMEM(first, BF16),
            pltpu.SemaphoreType.DMA((2, 2, max(self.ways, self.pairs))),
        ]

    def second_scratch(self):
        second = self.ways - 1 if self.pairs_first else self.pairs - 1
        return [
            pltpu.VMEM((second, *self.part), BF16),
            pltpu.VMEM(self.part, BF16),
            pltpu.VMEM(self.chunk, BF16),
            pltpu.SemaphoreType.DMA((2, 4, max(self.ways, self.pairs))),
        ]

    def scratch(self):
        if self.taken_up:
            return self.second_scratch()
        spread = self.spread_shape()
        return self.first_scratch() + [pltpu.VMEM(spread.shape, BF16)] + self.second_scratch()


def part_of(ref, lead, axis, size, index):
    start = index * size
    if axis == len(ref.shape) - lead - 1:
        start = pl.multiple_of(start, LANES)
    where = [slice(None)] * len(ref.shape)
    where[lead + axis] = pl.ds(start, size)
    return ref.at[tuple(where)]


class Peers:
    def __init__(self):
        self.ways, self.pairs = lax.axis_size("batch"), lax.axis_size("expert") // 2
        self.group, place = lax.axis_index("batch"), lax.axis_index("expert")
        self.pair, self.core = place // 2, lax.rem(place, 2)
        self.sibling = (self.group, self.pair * 2 + 1 - self.core)
        self.to_batch = [lax.rem(self.group + k, self.ways) for k in range(1, self.ways)]
        self.to_pairs = [lax.rem(self.pair + k, self.pairs) for k in range(1, self.pairs)]
        self.in_batch = [(to, place) for to in self.to_batch]
        self.in_pairs = [(self.group, to * 2 + self.core) for to in self.to_pairs]

    def remote(self, src, dst, sems, stage, k, device):
        return pltpu.make_async_remote_copy(
            src_ref=src,
            dst_ref=dst,
            send_sem=sems.at[0, stage, k],
            recv_sem=sems.at[1, stage, k],
            device_id=device,
            device_id_type=MESH,
        )

    def start(self, stage):
        for copy in self.copies(stage):
            copy.start()

    def wait(self, stage):
        for copy in self.copies(stage):
            copy.wait()

    def advance(self, stage):
        self.wait(stage)
        self.add(stage)
        if stage < self.last:
            self.start(stage + 1)


class Summing(Peers):
    last = 3

    def __init__(self, kind, local, out, scratch):
        super().__init__()
        self.axis, self.pairs_first, part, self.taken_up = kind
        self.local, self.out, self.size = local, out, part[self.axis]
        if self.taken_up:
            self.spread = local
            self.from_second, self.mine, self.every, self.late_sems = scratch
        else:
            self.both, self.by_chip, self.from_first, self.sems = scratch[:4]
            self.spread = out
            if len(scratch) > 4:
                self.spread, self.from_second, self.mine, self.every, self.late_sems = scratch[4:]

    def share(self, ref, lead, index):
        return part_of(ref, lead, self.axis, self.size, index)

    def copies(self, stage):
        if stage == 0:
            own = pltpu.make_async_copy(
                self.local.at[:, self.core], self.both.at[0], self.sems.at[0, 0, 1]
            )
            away = self.local.at[:, 1 - self.core]
            return [own, self.remote(away, self.both.at[1], self.sems, 0, 0, self.sibling)]
        if stage == 3:
            own, devices = self.share(self.every, 0, self.group), self.in_batch
            pieces = [(self.mine, own) for _ in devices]
        elif (stage == 1) == self.pairs_first:
            devices = self.in_pairs
            src, dst = (self.by_chip, self.from_first) if stage == 1 else (self.spread, self.from_second)
            pieces = [(src.at[to], dst.at[k]) for k, to in enumerate(self.to_pairs)]
        else:
            devices = self.in_batch
            src, dst = (self.by_chip, self.from_first) if stage == 1 else (self.spread, self.from_second)
            lead = 1 if stage == 1 else 0
            pieces = [
                (self.share(src, lead, to), dst.at[k]) for k, to in enumerate(self.to_batch)
            ]
        sems = self.sems if stage == 1 else self.late_sems
        return [
            self.remote(src, dst, sems, stage, k, devices[k]) for k, (src, dst) in enumerate(pieces)
        ]

    def add(self, stage):
        if stage == 0:

            def over_cores(z, carry):
                self.by_chip[z] = together(self.both[0, z], self.both[1, z]).astype(BF16)
                return carry

            lax.fori_loop(0, self.pairs, over_cores, 0)
        elif stage == 1 and self.pairs_first:
            others = (self.from_first[k] for k in range(self.pairs - 1))
            self.spread[...] = together(self.by_chip[self.pair], *others).astype(BF16)
        elif stage == 1:
            own = self.share(self.by_chip, 1, self.group)

            def over_batch(z, carry):
                others = (self.from_first[k, z] for k in range(self.ways - 1))
                self.spread[z] = together(own[z], *others).astype(BF16)
                return carry

            lax.fori_loop(0, self.pairs, over_batch, 0)
        elif stage == 2:
            if self.pairs_first:
                own, count = self.share(self.spread, 0, self.group)[...], self.ways
            else:
                own, count = self.spread[self.pair], self.pairs
            others = (self.from_second[k] for k in range(count - 1))
            total = together(own, *others).astype(BF16)
            self.mine[...] = total
            self.share(self.every, 0, self.group)[...] = total
        else:
            self.out[...] = self.every[...].astype(self.out.dtype)

    def begin(self):
        self.start(2 if self.taken_up else 0)


class SmallSum(Peers):
    last = 4

    def __init__(self, pack, from_core, half, from_pairs, by_group, every, sems):
        super().__init__()
        self.pack, self.from_core, self.half, self.from_pairs = pack, from_core, half, from_pairs
        self.by_group, self.every, self.sems = by_group, every, sems

    @staticmethod
    def scratch(pairs, ways, tiles):
        tile = (tiles, 16, LANES)
        shapes = ((2, pairs), (pairs,), (pairs,), (pairs - 1,), (ways,), (2, pairs))
        found = [pltpu.VMEM((*lead, *tile), BF16) for lead in shapes]
        return found + [pltpu.SemaphoreType.DMA((2, 5, max(pairs, ways)))]

    def copies(self, stage):
        if stage == 0:
            pieces = [(self.pack.at[1 - self.core], self.from_core, self.sibling)]
        elif stage == 1:
            pieces = [
                (self.half.at[to], self.from_pairs.at[k], self.in_pairs[k])
                for k, to in enumerate(self.to_pairs)
            ]
        elif stage == 2:
            own = self.by_group.at[self.group]
            pieces = [(own, own, device) for device in self.in_batch]
        elif stage == 3:
            own = self.every.at[self.core, self.pair]
            pieces = [(own, own, device) for device in self.in_pairs]
        else:
            own = self.every.at[self.core]
            pieces = [(own, own, self.sibling)]
        return [
            self.remote(src, dst, self.sems, stage, k, device)
            for k, (src, dst, device) in enumerate(pieces)
        ]

    def add(self, stage):
        if stage == 0:
            self.half[...] = together(self.pack[self.core], self.from_core[...]).astype(BF16)
        elif stage == 1:
            others = (self.from_pairs[k] for k in range(self.pairs - 1))
            self.by_group[self.group] = together(self.half[self.pair], *others).astype(BF16)
        elif stage == 2:
            total = together(*(self.by_group[k] for k in range(self.ways)))
            self.every[self.core, self.pair] = total.astype(BF16)


class TinySum(Peers):
    last = 2

    def __init__(self, pack, from_core, by_pair, by_group, total, sems):
        super().__init__()
        self.pack, self.from_core, self.by_pair = pack, from_core, by_pair
        self.by_group, self.total, self.sems = by_group, total, sems

    @staticmethod
    def scratch(pairs, ways, rows):
        found = [pltpu.VMEM((rows, LANES), BF16)] * 2
        found += [pltpu.VMEM((many, rows, LANES), BF16) for many in (pairs, ways)]
        return found + [pltpu.VMEM((rows, LANES), F32), pltpu.SemaphoreType.DMA((2, 3, max(pairs, ways)))]

    def copies(self, stage):
        if stage == 0:
            pieces = [(self.pack, self.from_core, self.sibling)]
        elif stage == 1:
            own = self.by_pair.at[self.pair]
            pieces = [(own, own, device) for device in self.in_pairs]
        else:
            own = self.by_group.at[self.group]
            pieces = [(own, own, device) for device in self.in_batch]
        return [
            self.remote(src, dst, self.sems, stage, k, device)
            for k, (src, dst, device) in enumerate(pieces)
        ]

    def add(self, stage):
        if stage == 0:
            self.by_pair[self.pair] = together(self.pack[...], self.from_core[...]).astype(BF16)
        elif stage == 1:
            total = together(*(self.by_pair[k] for k in range(self.pairs)))
            self.by_group[self.group] = total.astype(BF16)
        else:
            self.total[...] = together(*(self.by_group[k] for k in range(self.ways)))


def summings(kinds, ins, outs, scratch):
    found, at = [], 0
    for (kind, many), local, out in zip(kinds, ins, outs):
        found.append(Summing(kind, local, out, scratch[at : at + many]))
        at += many
    return found


class Halving:
    def __init__(self, local, x_first, sems=None):
        assert lax.axis_size("batch") == 4
        group, self.place = lax.axis_index("batch"), lax.axis_index("expert")
        by_x = group + 1 - 2 * lax.rem(group, 2)
        by_y = group + 2 - 4 * (group // 2)
        self.local, self.sems, self.group, self.across = local, sems, group, 3 - group
        self.near, self.far = (by_x, by_y) if x_first else (by_y, by_x)
        self.rows = local.shape[0] // 4

    def chunk(self, index):
        return self.local.at[pl.ds(pl.multiple_of(index * self.rows, self.rows), self.rows)]

    def copy(self, src, dst, k, device):
        return pltpu.make_async_remote_copy(
            src_ref=src,
            dst_ref=dst,
            send_sem=self.sems.at[0, k],
            recv_sem=self.sems.at[1, k],
            device_id=(device, self.place),
            device_id_type=MESH,
        )

    def first(self, landing):
        return [
            self.copy(self.chunk(index), landing.at[k], k, self.near)
            for k, index in enumerate((self.near, self.across))
        ]

    def second(self, src, landing):
        return self.copy(src, landing, 0, self.far)


class Side:
    def __init__(self, src, dst, sems):
        self.src, self.dst, self.sems = src, dst, sems
        self.count, self.me = lax.axis_size("expert"), lax.axis_index("expert")

    @staticmethod
    def scratch(count):
        return pltpu.SemaphoreType.DMA((2, count))

    def copy(self, k):
        return self.copy_to(lax.rem(self.me + k, self.count))

    def copy_to(self, to):
        return pltpu.make_async_remote_copy(
            src_ref=self.src.at[to],
            dst_ref=self.dst.at[self.me],
            send_sem=self.sems.at[0, to],
            recv_sem=self.sems.at[1, self.me],
            device_id=(lax.axis_index("batch"), to),
            device_id_type=MESH,
        )

    def brought(self, place):
        return pltpu.make_async_remote_copy(
            src_ref=self.src.at[place],
            dst_ref=self.dst.at[place],
            send_sem=self.sems.at[0, place],
            recv_sem=self.sems.at[1, place],
            device_id=(lax.axis_index("batch"), place),
            device_id_type=MESH,
        )

    def own(self):
        return pltpu.make_async_copy(
            self.src.at[self.me], self.dst.at[self.me], self.sems.at[0, self.me]
        )

    def start(self, part=0, parts=((0, 1),)):
        if part == 0:
            self.own().start()
        least, most = (1 + round(share * (self.count - 1)) for share in parts[part])
        for k in range(least, most):
            self.copy(k).start()

    def wait(self):
        self.own().wait()
        self.wait_others()

    def wait_others(self):
        for k in range(1, self.count):
            place = lax.rem(self.me + k, self.count)
            self.copy_to(place).wait_send()
            self.brought(place).wait_recv()


def greet_others():
    barrier = pltpu.get_barrier_semaphore()
    group, place = lax.axis_index("batch"), lax.axis_index("expert")
    ways, count = lax.axis_size("batch"), lax.axis_size("expert")
    others = [(group, lax.rem(place + k, count)) for k in range(1, count)]
    others += [(lax.rem(group + k, ways), place) for k in range(1, ways)]
    for device in others:
        pl.semaphore_signal(barrier, inc=1, device_id=device, device_id_type=MESH)
    pl.semaphore_wait(barrier, len(others))


def greet_experts():
    barrier = pltpu.get_barrier_semaphore()
    count, me = lax.axis_size("expert"), lax.axis_index("expert")
    for k in range(1, count):
        device = (lax.axis_index("batch"), lax.rem(me + k, count))
        pl.semaphore_signal(barrier, inc=1, device_id=device, device_id_type=MESH)
    pl.semaphore_wait(barrier, count - 1)


def gelu_parts(v):
    size = jnp.abs(v) * 0.7071067811865476
    t = 1.0 / (1.0 + 0.3275911 * size)
    bell = jnp.exp2(v * v * (-0.5 * LOG2E))
    poly = t * (
        0.127414796
        + t * (-0.142248368 + t * (0.7107068705 + t * (-0.7265760135 + t * 0.5307027145)))
    )
    tail = poly * bell
    phi = jnp.where(v >= 0.0, 1.0 - tail, tail)
    return v * phi, phi + v * (bell * 0.3989422804014327)


FF_TILE = 512


def experts_kernel(slots, tile, *refs):
    normed_ref, row_ref, col_ref, router_ref, upstream_ref, in_hbm, out_hbm = refs[:7]
    grad_ref, result_ref, in_grad_hbm, out_grad_hbm, router_grad_ref = refs[7:12]
    w_in, w_out, sent, got, home, slot_grad, active, hid_grad, row_grad = refs[12:21]
    in_grad, out_grad, there_sems, back_sems, load_sems, store_sems, router = refs[21:28]
    gates, logit_grads, back = refs[28:]
    rows = row_grad
    count, me = lax.axis_size("expert"), lax.axis_index("expert")
    width, hidden = w_in.shape
    total = count * slots
    tiles = hidden // tile
    router[...] = padded_rows(router_ref, LANES)
    loads = [
        pltpu.make_async_copy(in_hbm.at[0], w_in, load_sems.at[0]),
        pltpu.make_async_copy(out_hbm.at[0], w_out, load_sems.at[1]),
    ]
    for load in loads:
        load.start()
    greet_experts()
    there = Side(sent, got, there_sems)
    returning = Side(back, home, back_sems)
    tokens = normed_ref.shape[0]
    slot_id = lax.broadcasted_iota(jnp.int32, (slots, tokens), 0)

    upper = me // (count // 2)
    quarter = count // 4
    groups = (
        (upper * 2 * quarter, 2 * quarter),
        ((2 - upper) * quarter, quarter),
        ((3 - 3 * upper) * quarter, quarter),
    )

    def dispatch(to, carry):
        picked = (slot_id + to * slots == row_ref[...]).astype(F32).astype(BF16)
        chunk = jnp.dot(picked, normed_ref[...], preferred_element_type=F32).astype(BF16)
        sent[to] = chunk

        @pl.when(to != me)
        def _():
            there.copy_to(to).start()

        @pl.when(to == me)
        def _():
            got[me] = chunk

        return carry

    for first, many in groups:
        lax.fori_loop(first, first + many, dispatch, 0)
    over_inner = (((1,), (1,)), ((), ()))
    for load in loads:
        load.wait()
    for first, many in groups:

        def arrive(place, carry):
            @pl.when(place != me)
            def _():
                there.brought(place).wait_recv()

            return carry

        lax.fori_loop(first, first + many, arrive, 0)
        high = many * slots
        places = pl.ds(first, many)
        at_rows = pl.ds(pl.multiple_of(first * slots, 16), high)
        x = got[places].reshape(high, width)
        logits = lax.dot_general(x, router[...], over_inner, preferred_element_type=F32)
        lane = lax.broadcasted_iota(jnp.int32, logits.shape, 1)
        logits = jnp.where(lane < count, logits, -1e30)
        scores = jnp.exp(logits - jnp.max(logits, axis=1, keepdims=True))
        probs = scores / jnp.sum(scores, axis=1, keepdims=True)
        mine = (lane == me).astype(F32)
        gate = jnp.sum(probs * mine, axis=1, keepdims=True)
        gates[at_rows, :] = jnp.broadcast_to(gate, (high, LANES))
        upstream = upstream_ref[places].reshape(high, width).astype(F32)
        slot_grad[at_rows, :] = (gate * upstream).astype(BF16)
        row_grad[at_rows, :] = jnp.zeros((high, width), F32)

        def inward(t, picked, x=x, at_rows=at_rows):
            at = pl.ds(pl.multiple_of(t * tile, tile), tile)
            pre = jnp.dot(x, w_in[:, at], preferred_element_type=F32)
            act_grad = lax.dot_general(
                slot_grad[at_rows, :], w_out[at, :], over_inner, preferred_element_type=F32
            )
            value, slope = gelu_parts(pre)
            active[at_rows, at] = value.astype(BF16)
            low = (act_grad * slope).astype(BF16)
            hid_grad[at_rows, at] = low
            row_grad[at_rows, :] += lax.dot_general(
                low, w_in[:, at], over_inner, preferred_element_type=F32
            )
            return picked + jnp.sum(value * act_grad, axis=1, keepdims=True)

        picked = lax.fori_loop(0, tiles, inward, jnp.zeros((high, 1), F32))
        logit_grad = (picked * (mine - probs)).astype(BF16)
        logit_grads[at_rows, :] = logit_grad
        whole = row_grad[at_rows, :] + jnp.dot(logit_grad, router[...], preferred_element_type=F32)
        back[places] = whole.astype(BF16).reshape(many, slots, width)

        def give_back(place, carry):
            @pl.when(place != me)
            def _():
                returning.copy_to(place).start()

            @pl.when(place == me)
            def _():
                home[me] = back[me]

            return carry

        lax.fori_loop(first, first + many, give_back, 0)

    router_grad = lax.dot_general(
        logit_grads[...],
        got[...].reshape(total, width),
        (((0,), (0,)), ((), ())),
        preferred_element_type=F32,
    )
    router_grad_ref[...] = router_grad[:count]
    rows[...] = jnp.zeros(rows.shape, F32)

    def stores(t):
        at = pl.ds(pl.multiple_of(t * tile, tile), tile)
        return (
            pltpu.make_async_copy(in_grad.at[:, at], in_grad_hbm.at[:, at], store_sems.at[0, t]),
            pltpu.make_async_copy(out_grad.at[at], out_grad_hbm.at[at], store_sems.at[1, t]),
        )

    def outward(t, carry):
        at = pl.ds(pl.multiple_of(t * tile, tile), tile)
        over_rows = (((0,), (0,)), ((), ()))
        in_grad[:, at] = lax.dot_general(
            got[...].reshape(total, width), hid_grad[:, at], over_rows, preferred_element_type=F32
        ).astype(BF16)
        out_grad[at, :] = lax.dot_general(
            active[:, at], slot_grad[...], over_rows, preferred_element_type=F32
        ).astype(BF16)
        for store in stores(t):
            store.start()
        rows[...] += jnp.dot(active[:, at], w_out[at, :], preferred_element_type=F32)
        return carry

    lax.fori_loop(0, tiles, outward, 0)
    result_ref[...] = (gates[:, :1] * rows[...]).astype(BF16).reshape(count, slots, width)
    returning.wait_others()
    for k in range(1, count):
        there.copy(k).wait_send()
    slot_id = lax.broadcasted_iota(jnp.int32, (tokens, total), 1)
    chosen = (slot_id == col_ref[...]).astype(F32).astype(BF16)
    grad_ref[...] = jnp.dot(
        chosen, home[...].reshape(total, width), preferred_element_type=F32
    )
    for t in range(tiles):
        for store in stores(t):
            store.wait()


def run_experts(
    normed, row, col, router, upstream, expert_in, expert_out, slots, collective_id
):
    tokens, width = normed.shape
    count = lax.axis_size("expert")
    hidden = expert_in.shape[2]
    tile = FF_TILE if hidden % FF_TILE == 0 else hidden
    total = count * slots
    exchanged = (count, slots, width)
    vmem = pl.BlockSpec(memory_space=pltpu.VMEM)
    hbm = pl.BlockSpec(memory_space=pl.ANY)
    grad, result, in_grad, out_grad, router_grad = pl.pallas_call(
        functools.partial(experts_kernel, slots, tile),
        out_shape=[
            jax.ShapeDtypeStruct((tokens, width), F32),
            jax.ShapeDtypeStruct(exchanged, BF16),
            jax.ShapeDtypeStruct((width, hidden), BF16),
            jax.ShapeDtypeStruct((hidden, width), BF16),
            jax.ShapeDtypeStruct(router.shape, F32),
        ],
        in_specs=[vmem] * 5 + [hbm] * 2,
        out_specs=[vmem, vmem, hbm, hbm, vmem],
        scratch_shapes=[
            pltpu.VMEM((width, hidden), BF16),
            pltpu.VMEM((hidden, width), BF16),
            pltpu.VMEM(exchanged, BF16),
            pltpu.VMEM(exchanged, BF16),
            pltpu.VMEM(exchanged, BF16),
            pltpu.VMEM((total, width), BF16),
            pltpu.VMEM((total, hidden), BF16),
            pltpu.VMEM((total, hidden), BF16),
            pltpu.VMEM((total, width), F32),
            pltpu.VMEM((width, hidden), BF16),
            pltpu.VMEM((hidden, width), BF16),
            Side.scratch(count),
            Side.scratch(count),
            pltpu.SemaphoreType.DMA((2,)),
            pltpu.SemaphoreType.DMA((2, hidden // tile)),
            pltpu.VMEM((LANES, width), BF16),
            pltpu.VMEM((total, LANES), F32),
            pltpu.VMEM((total, LANES), BF16),
            pltpu.VMEM(exchanged, BF16),
        ],
        compiler_params=params(collective_id=collective_id, has_side_effects=True),
        name="experts",
    )(normed, row, col, router, upstream, expert_in, expert_out)
    return grad, result, in_grad, out_grad, router_grad


def in_segments(value_ref, turn):
    steps = value_ref.shape[0] // SEGS
    parts = []
    for lane in range(turn.shape[0]):
        lanes = slice(lane * LANES, (lane + 1) * LANES)
        for s in range(SEGS):
            rows = value_ref[s * steps : (s + 1) * steps, lanes].astype(F32)
            turn[lane, pl.ds(s, steps, stride=SEGS), :] = rows
        parts.append(turn[lane].astype(BF16))
    return jnp.concatenate(parts, axis=1)


def over_blocks(width, size, body):
    def one(n, carry):
        body(pl.ds(pl.multiple_of(n * size, size), size))
        return carry

    lax.fori_loop(0, width // size, one, 0)


def slot_targets(route, experts, capacity, slots):
    count = route.shape[1]
    steps = count // SEGS
    high = max(experts, 16)
    onehot = lax.broadcasted_iota(jnp.int32, (high, count), 0) == route
    onehot = onehot.astype(F32)
    token_of = lambda p: (p % SEGS) * steps + p // SEGS
    first = token_of(lax.broadcasted_iota(jnp.int32, (count, count), 0))
    second = token_of(lax.broadcasted_iota(jnp.int32, (count, count), 1))
    earlier = (first <= second).astype(F32).astype(BF16)
    running = jnp.dot(onehot.astype(BF16), earlier, preferred_element_type=F32)
    place = (jnp.sum(running * onehot, axis=0, keepdims=True) - 1.0).astype(jnp.int32)
    return jnp.where(place < capacity, route * slots + place, -1)


def forward_kernel(sizes, *refs):
    states, steps, rank, capacity = sizes
    tokens_hbm, upstream_hbm, in_proj_hbm, out_proj_hbm = refs[:4]
    route_ref, gain_ref, gain_two_ref, conv_ref, bias_ref, x_proj_ref, dt_proj_ref = refs[4:11]
    dt_bias_ref, skip_ref, rate_log_ref = refs[11:14]
    ssm_ref, held_ref, gated_ref, hidden_ref, normed_two_ref, row_ref, col_ref, before_ref = refs[14:22]
    side_out = refs[22]
    kept_hbm, refs = refs[23:32], refs[32:]
    tokens_in, upstream_in, in_proj, out_proj, turn, ext_in, tail, sent = refs[:8]
    kept, refs = refs[8:17], refs[17:]
    tokens, upstream, normed, inner, gate_z, mixed, pre, delta, proj = kept
    in_s, bb, cb, run_a, run_b, side_sems, load_sems, keep_sems, halo_sems = refs[:9]
    x_proj, dt_proj, small, before, carry_refs = *refs[9:13], refs[13:]
    phase, block = pl.program_id(0), pl.program_id(1)
    blocks = carry_refs[2].shape[1]
    carries = Carries(states, blocks, True, *carry_refs)
    side = Side(sent, side_out, side_sems)
    parts = ((0, 2 / 7), (2 / 7, 3 / 7), (3 / 7, 1))
    rate2 = -jnp.exp(rate_log_ref[...]) * LOG2E
    rates = [over_sublanes(rate2[n : n + 1, :]) for n in range(states)]
    here = pl.ds(pl.multiple_of(block * LANES, LANES), LANES)
    count, width = tokens.shape
    inner_width = inner.shape[1]
    reach = conv_ref.shape[0] - 1
    rim = reach * SEGS
    experts, me = lax.axis_size("expert"), lax.axis_index("expert")
    slots = sent.shape[1]
    half = inner_width
    loads = [
        pltpu.make_async_copy(src, dst, load_sems.at[i])
        for i, (src, dst) in enumerate(
            (
                (tokens_hbm.at[0], tokens_in),
                (in_proj_hbm.at[:, :half], in_proj.at[:, :half]),
                (in_proj_hbm.at[:, half:], in_proj.at[:, half:]),
                (upstream_hbm.at[0], upstream_in),
                (out_proj_hbm, out_proj),
            )
        )
    ]
    keeps = [
        pltpu.make_async_copy(src, dst, keep_sems.at[i])
        for i, (src, dst) in enumerate(zip(kept, kept_hbm))
    ]

    def front():
        for load in loads:
            load.start()
        small[0:1, :] = as_row(skip_ref)
        small[1:2, :] = as_row(bias_ref)
        small[2:3, :] = as_row(dt_bias_ref)
        x_proj[...] = padded_rows(x_proj_ref, LANES)
        dt_proj[...] = padded_rows(dt_proj_ref, LANES)
        loads[0].wait()
        tokens[...] = in_segments(tokens_in, turn)
        normed[...] = rms(tokens[...].astype(F32), as_row(gain_ref)).astype(BF16)
        loads[1].wait()

        def to_inner(at):
            inner[:, at] = jnp.dot(
                normed[...], in_proj[:, at], preferred_element_type=F32
            ).astype(BF16)

        over_blocks(inner_width, 4 * LANES, to_inner)
        last = inner[count - rim - rim % 16 :, :].astype(F32)[rim % 16 :]
        for k in range(reach):
            tail[k : k + 1, :] = last[(k + 1) * SEGS - 1 : (k + 1) * SEGS]
        greet_experts()
        halo = pltpu.make_async_remote_copy(
            src_ref=tail,
            dst_ref=before,
            send_sem=halo_sems.at[0],
            recv_sem=halo_sems.at[1],
            device_id=(lax.axis_index("batch"), lax.rem(me + 1, experts)),
            device_id_type=MESH,
        )

        @pl.when(me < experts - 1)
        def _():
            halo.start()

        @pl.when(me == 0)
        def _():
            before[...] = jnp.zeros(before.shape, F32)

        loads[2].wait()

        def to_gate(at):
            lanes = pl.ds(pl.multiple_of(half + at.start, LANES), at.size)
            gate_z[:, at] = jnp.dot(normed[...], in_proj[:, lanes], preferred_element_type=F32)

        over_blocks(inner_width, 4 * LANES, to_gate)
        for keep in keeps[2:5]:
            keep.start()
        keeps[0].start()
        loads[3].wait()
        upstream[...] = in_segments(upstream_in, turn)
        keeps[1].start()
        target = slot_targets(route_ref[...], experts, capacity, slots)
        row_ref[...] = target
        wide = jnp.broadcast_to(target.astype(F32), (SEGS, count))
        col_ref[...] = jnp.transpose(wide)[:, :1].astype(jnp.int32)
        slot_id = lax.broadcasted_iota(jnp.int32, (slots, count), 0)

        def dispatch(e, carry):
            picked = (slot_id + e * slots == row_ref[...]).astype(F32).astype(BF16)
            sent[e] = jnp.dot(picked, upstream[...], preferred_element_type=F32).astype(BF16)
            return carry

        lax.fori_loop(0, experts, dispatch, 0)
        side.start(0, parts)

        @pl.when(me < experts - 1)
        def _():
            halo.wait_send()

        @pl.when(me > 0)
        def _():
            halo.wait_recv()

        before_ref[...] = before[...]

        def to_mixed(at):
            own = inner[:, at].astype(F32)
            for k in range(reach):
                tile = own[count - rim + k * SEGS : count - rim + (k + 1) * SEGS]
                ext_in[k * SEGS : (k + 1) * SEGS, at] = shifted_in(
                    tile, before[k : k + 1, at], True
                )
            ext_in[rim:, at] = own
            total = jnp.broadcast_to(small[1:2, at], own.shape)
            for k in range(reach + 1):
                total = total + conv_ref[k : k + 1, at] * ext_in[k * SEGS : k * SEGS + count, at]
            mixed[:, at] = silu(total).astype(BF16)

        over_blocks(inner_width, 2 * LANES, to_mixed)
        keeps[5].start()
        proj[...] = lax.dot_general(
            mixed[...], x_proj[...], (((1,), (1,)), ((), ())), preferred_element_type=F32
        )
        keeps[8].start()

        def to_delta(at):
            own = jnp.dot(
                proj[...].astype(BF16), dt_proj[:, at], preferred_element_type=F32
            )
            own = own + small[2:3, at]
            pre[:, at] = own
            delta[:, at] = softplus(own)

        over_blocks(inner_width, 2 * LANES, to_delta)
        keeps[6].start()
        keeps[7].start()

    @pl.when((phase == 0) & (block == 0))
    def _():
        front()

    for part, (at_phase, at_block) in enumerate(((0, blocks // 2), (1, 1))):

        @pl.when((phase == at_phase) & (block == at_block))
        def _():
            side.start(part + 1, parts)

    def ends(first):
        in_s[...] = delta[:, here] * mixed[:, here].astype(F32)
        sums = jnp.sum(delta[:, here].reshape(steps, SEGS, LANES), axis=0)

        def one(j, held):
            rows = tile_rows(j)
            d, u = delta[rows, here], in_s[rows, :]
            tile = proj[rows, :] if first else None
            new = []
            for n in range(states):
                if first:
                    b = over_lanes(tile[:, rank + n : rank + n + 1])
                    bb[j, n] = b
                    cb[j, n] = over_lanes(tile[:, rank + states + n : rank + states + n + 1])
                else:
                    b = bb[j, n]
                new.append(jnp.exp2(d * rates[n]) * held[n] + u * b)
            return tuple(new)

        zero = jnp.zeros((SEGS, LANES), F32)
        held = lax.fori_loop(0, steps, one, (zero,) * states, unroll=4)
        carries.put(block, held, sums, rates, run_a, run_b)

    @pl.when((phase == 0) & (block == 0))
    def _():
        ends(True)

    @pl.when((phase == 0) & (block > 0))
    def _():
        ends(False)

    @pl.when(phase == 1)
    def _():
        carries.await_group(block)
        start = carries.starts(block, rate2, run_a, run_b)
        own = mixed[:, here].astype(F32)
        in_s[...] = delta[:, here] * own
        ssm_ref[...] = small[0:1, here] * own
        for n in range(states):
            held_ref[0, 0, n] = start[n]

        def one(j, held):
            rows = tile_rows(j)
            d, u = delta[rows, here], in_s[rows, :]
            total = ssm_ref[rows, :]
            new = []
            for n in range(states):
                h = jnp.exp2(d * rates[n]) * held[n] + u * bb[j, n]
                held_ref[0, j + 1, n] = h
                total = total + cb[j, n] * h
                new.append(h)
            ssm_ref[rows, :] = total
            return tuple(new)

        lax.fori_loop(0, steps, one, tuple(start), unroll=4)
        gated_ref[:, here] = (ssm_ref[...] * silu(gate_z[:, here])).astype(BF16)

    @pl.when((phase == 1) & (block == blocks - 1))
    def _():
        loads[4].wait()
        hidden = tokens[...].astype(F32) + jnp.dot(
            gated_ref[...], out_proj[...], preferred_element_type=F32
        )
        hidden_ref[...] = hidden
        normed_two_ref[...] = rms(hidden, as_row(gain_two_ref)).astype(BF16)
        side.wait()
        for keep in keeps:
            keep.wait()


def forward(
    tokens,
    upstream,
    in_proj,
    out_proj,
    route,
    gain_one,
    gain_two,
    conv_weight,
    conv_bias,
    x_proj,
    dt_proj,
    dt_bias,
    skip,
    rate_log,
    sizes,
    collective_id,
):
    rank, capacity, slots = sizes
    count, width = tokens.shape[1:]
    inner_width = out_proj.shape[0]
    states, steps, blocks = rate_log.shape[0], count // SEGS, inner_width // LANES
    experts = lax.axis_size("expert")
    rim = (conv_weight.shape[0] - 1) * SEGS
    vmem, hbm = (pl.BlockSpec(memory_space=m) for m in (pltpu.VMEM, pl.ANY))
    spread = pltpu.VMEM((steps, states, SEGS, LANES), F32)
    run = pltpu.VMEM((blocks, states, SEGS, LANES), F32)
    whole = lambda *shape: pl.BlockSpec(shape, lambda p, c: (0,) * len(shape))
    shape_of = jax.ShapeDtypeStruct
    kept = [
        shape_of((count, width), BF16),
        shape_of((count, width), BF16),
        shape_of((count, width), BF16),
        shape_of((count, inner_width), BF16),
        shape_of((count, inner_width), F32),
        shape_of((count, inner_width), BF16),
        shape_of((count, inner_width), F32),
        shape_of((count, inner_width), F32),
        shape_of((count, LANES), F32),
    ]
    exchanged = (experts, slots, width)
    out = pl.pallas_call(
        functools.partial(forward_kernel, (states, steps, rank, capacity)),
        grid=(2, blocks),
        out_shape=[
            shape_of((count, inner_width), F32),
            shape_of((blocks, steps + 1, states, SEGS, LANES), F32),
            shape_of((count, inner_width), BF16),
            shape_of((count, width), F32),
            shape_of((count, width), BF16),
            shape_of((1, count), jnp.int32),
            shape_of((count, 1), jnp.int32),
            shape_of((SEGS, inner_width), F32),
            shape_of(exchanged, BF16),
        ]
        + kept,
        in_specs=[hbm] * 4
        + [vmem] * 9
        + [pl.BlockSpec((states, LANES), lambda p, c: (0, c))],
        out_specs=[
            pl.BlockSpec((count, LANES), lambda p, c: (0, p * c)),
            pl.BlockSpec((1, steps + 1, states, SEGS, LANES), lambda p, c: (p * c, 0, 0, 0, 0)),
            whole(count, inner_width),
            whole(count, width),
            whole(count, width),
            whole(1, count),
            whole(count, 1),
            vmem,
            hbm,
        ]
        + [hbm] * len(kept),
        scratch_shapes=[
            pltpu.VMEM((count, width), BF16),
            pltpu.VMEM((count, width), BF16),
            pltpu.VMEM(in_proj.shape, BF16),
            pltpu.VMEM(out_proj.shape, BF16),
            pltpu.VMEM((width // LANES, count, LANES), F32),
            pltpu.VMEM((count + rim, inner_width), F32),
            pltpu.VMEM((SEGS, inner_width), F32),
            pltpu.VMEM(exchanged, BF16),
        ]
        + [pltpu.VMEM(k.shape, k.dtype) for k in kept]
        + [
            pltpu.VMEM((count, LANES), F32),
            spread,
            spread,
            run,
            run,
            Side.scratch(experts),
            pltpu.SemaphoreType.DMA((5,)),
            pltpu.SemaphoreType.DMA((len(kept),)),
            pltpu.SemaphoreType.DMA((2,)),
            pltpu.VMEM((LANES, inner_width), BF16),
            pltpu.VMEM((LANES, inner_width), BF16),
            pltpu.VMEM((SEGS, inner_width), F32),
            pltpu.VMEM((SEGS, inner_width), F32),
        ]
        + Carries.scratch(states, blocks, experts),
        compiler_params=params(collective_id=collective_id, has_side_effects=True),
        name="forward",
    )(
        tokens,
        upstream,
        in_proj,
        out_proj,
        route,
        gain_one,
        gain_two,
        conv_weight,
        conv_bias,
        x_proj,
        dt_proj,
        dt_bias,
        skip,
        rate_log,
    )
    return out[:9], out[9:]


def backward_kernel(states, steps, rank, kinds, *refs):
    many = len(kinds)
    expert_hbm, sum_in, refs = refs[:2], refs[2 : 2 + many], refs[2 + many :]
    delta_hbm, g_hbm, in_hbm, pre_hbm, bc_ref, rate_ref, skip_ref, held_ref, side_in = refs[:9]
    sum_out, refs = refs[9 : 9 + many], refs[9 + many :]
    pre_grad_ref, mixed_grad_ref, rate_grad_ref, skip_grad_ref, bias_grad_ref = refs[:5]
    bc_grad_ref, side_out = refs[5:7]
    landings, refs = refs[7:9], refs[9:]
    in_s, rate_sum, in_sum, bb, cb, b_acc, c_acc, run_a, run_b, side_sems = refs[:10]
    skip_row, halving_sems, refs = refs[10], refs[11:13], refs[13:]
    delta_ref, g_ref, in_ref, pre_ref, load_sems = refs[:5]
    carry_refs, sum_refs = refs[5:10], refs[10:]
    loads = [
        pltpu.make_async_copy(src, dst, load_sems.at[i])
        for i, (src, dst) in enumerate(
            ((delta_hbm, delta_ref), (g_hbm, g_ref), (in_hbm, in_ref), (pre_hbm, pre_ref))
        )
    ]
    halvings = [Halving(expert_hbm[i], i == 0, halving_sems[i]) for i in range(2)]
    phase, block = pl.program_id(0), pl.program_id(1)
    here = pl.ds(pl.multiple_of(block * LANES, LANES), LANES)
    blocks = carry_refs[2].shape[1]
    carries = Carries(states, blocks, False, *carry_refs)
    sums = summings(kinds, sum_in, sum_out, sum_refs)
    side = Side(side_in, side_out, side_sems)
    rate2 = -jnp.exp(rate_ref[:, here]) * LOG2E
    rates = [over_sublanes(rate2[n : n + 1, :]) for n in range(states)]
    zero = jnp.zeros((SEGS, LANES), F32)

    @pl.when((phase == 0) & (block == 0))
    def _():
        for load in loads:
            load.start()
        skip_row[...] = as_row(skip_ref)
        greet_others()
        for item in sums:
            item.start(0)
        for halving, landing in zip(halvings, landings):
            for copy in halving.first(landing):
                copy.start()
        for load in loads[:2]:
            load.wait()

    @pl.when((phase == 1) & (block == 0))
    def _():
        for load in loads[2:]:
            load.wait()

    @pl.when((phase == 0) & (block == blocks - 3))
    def _():
        for item in sums:
            if not item.pairs_first:
                item.advance(0)

    @pl.when((phase == 1) & (block == 1))
    def _():
        for item in sums:
            if item.pairs_first:
                item.advance(0)

    @pl.when((phase == 1) & (block == blocks // 2 - 1))
    def _():
        side.start()

    def ends(first):
        sums = jnp.sum(delta_ref[:, here].reshape(steps, SEGS, LANES), axis=0)

        def one(i, held):
            j = steps - 1 - i
            d, g = delta_ref[tile_rows(j), here], g_ref[tile_rows(j), here]
            tile = bc_ref[tile_rows(j), :] if first else None
            new = []
            for n in range(states):
                if first:
                    c = over_lanes(tile[:, rank + states + n : rank + states + n + 1])
                    bb[j, n] = over_lanes(tile[:, rank + n : rank + n + 1])
                    cb[j, n] = c
                else:
                    c = cb[j, n]
                new.append(jnp.exp2(d * rates[n]) * (held[n] + g * c))
            return tuple(new)

        held = lax.fori_loop(0, steps, one, (zero,) * states, unroll=4)
        carries.put(block, held, sums, rates, run_a, run_b)

    @pl.when((phase == 0) & (block == 0))
    def _():
        ends(True)

    @pl.when((phase == 0) & (block > 0))
    def _():
        ends(False)

    def grads(first, last):
        start = carries.starts(block, rate2, run_a, run_b)
        delta, g = delta_ref[:, here], g_ref[:, here]
        mixed = in_ref[:, here].astype(F32)
        in_s[...] = delta * mixed
        place = lax.broadcasted_iota(jnp.int32, (SEGS, LANES), 1)

        def one(i, carry):
            edge, rate_acc = carry
            j = steps - 1 - i
            rows = tile_rows(j)
            d, u, g = delta_ref[rows, here], in_s[rows, :], g_ref[rows, here]
            by_rate = by_b = sums = zero
            new_edge, new_acc = [], []
            for n in range(states):
                b, c = bb[j, n], cb[j, n]
                q = c * g + edge[n]
                e = jnp.exp2(d * rates[n]) * q
                v = e * held_ref[0, j, n]
                by_rate = by_rate + rates[n] * v
                by_b = by_b + b * q
                to_b = q * u
                to_c = g * held_ref[0, j + 1, n]
                if not first:
                    to_b = b_acc[j, n] + to_b
                    to_c = c_acc[j, n] + to_c
                if last:
                    sums = jnp.where(place == rank + n, jnp.sum(to_b, axis=1, keepdims=True), sums)
                    to_c = jnp.sum(to_c, axis=1, keepdims=True)
                    sums = jnp.where(place == rank + states + n, to_c, sums)
                else:
                    b_acc[j, n] = to_b
                    c_acc[j, n] = to_c
                new_edge.append(e)
                new_acc.append(rate_acc[n] + d * v)
            rate_sum[rows, :] = by_rate
            in_sum[rows, :] = by_b
            if last:
                bc_grad_ref[rows, :] = sums
            return tuple(new_edge), tuple(new_acc)

        _, rate_acc = lax.fori_loop(
            0, steps, one, (tuple(start), (zero,) * states), unroll=4
        )
        for n in range(states):
            rate_grad_ref[n : n + 1, here] = (
                LN2 * rate2[n : n + 1, :] * jnp.sum(rate_acc[n], axis=0, keepdims=True)
            )
        by_b = in_sum[...]
        pre_grad = (LN2 * rate_sum[...] + mixed * by_b) * jax.nn.sigmoid(pre_ref[:, here])
        pre_grad_ref[:, here] = pre_grad.astype(BF16)
        bias_grad_ref[:, here] = jnp.sum(pre_grad, axis=0, keepdims=True)
        mixed_grad_ref[:, here] = delta * by_b + skip_row[:, here] * g
        skip_grad_ref[:, here] = jnp.sum(g * mixed, axis=0, keepdims=True)

    @pl.when(phase == 1)
    def _():
        carries.await_group(block)

    @pl.when((phase == 1) & (block == 0))
    def _():
        grads(True, False)

    @pl.when((phase == 1) & (block > 0) & (block < blocks - 1))
    def _():
        grads(False, False)

    @pl.when((phase == 1) & (block == blocks - 1))
    def _():
        grads(False, True)
        side.wait()
        for item in sums:
            item.wait(1)
            item.add(1)
        for halving, landing in zip(halvings, landings):
            for copy in halving.first(landing):
                copy.wait()


def mixer_grads(
    pre, delta, mixed, ssm_grad, bc, rate_log, skip, held, beside, experts, rank, items, collective_id
):
    count, width = delta.shape
    states, steps, blocks = rate_log.shape[0], count // SEGS, width // LANES
    spread = pltpu.VMEM((steps, states, SEGS, LANES), F32)
    run = pltpu.VMEM((blocks, states, SEGS, LANES), F32)
    flat = pltpu.VMEM((count, LANES), F32)
    sum_scratch = [item.first_scratch() for item in items]
    kinds = tuple((item.kind(), len(refs)) for item, refs in zip(items, sum_scratch))
    spread_specs = [
        pl.BlockSpec(item.spread_shape().shape, lambda p, c, rank=len(item.spread_shape().shape): (0,) * rank)
        for item in items
    ]
    outs = pl.pallas_call(
        functools.partial(backward_kernel, states, steps, rank, kinds),
        grid=(2, blocks),
        out_shape=[item.spread_shape() for item in items]
        + [
            jax.ShapeDtypeStruct((count, width), BF16),
            jax.ShapeDtypeStruct((count, width), F32),
            jax.ShapeDtypeStruct((states, width), F32),
            jax.ShapeDtypeStruct((1, width), F32),
            jax.ShapeDtypeStruct((1, width), F32),
            jax.ShapeDtypeStruct((count, LANES), F32),
            jax.ShapeDtypeStruct(beside.shape, beside.dtype),
        ]
        + [jax.ShapeDtypeStruct((2, e.shape[0] // 4, e.shape[1]), BF16) for e in experts],
        in_specs=[pl.BlockSpec(memory_space=pl.ANY)] * (2 + len(items))
        + [pl.BlockSpec(memory_space=pl.ANY)] * 4
        + [pl.BlockSpec(memory_space=pltpu.VMEM)] * 3
        + [
            pl.BlockSpec((1, steps + 1, states, SEGS, LANES), lambda p, c: (p * c, 0, 0, 0, 0)),
            pl.BlockSpec(memory_space=pl.ANY),
        ],
        out_specs=spread_specs
        + [pl.BlockSpec(memory_space=pltpu.VMEM)] * 6
        + [pl.BlockSpec(memory_space=pl.ANY)] * 3,
        scratch_shapes=[flat, flat, flat, spread, spread, spread, spread, run, run]
        + [Side.scratch(lax.axis_size("expert")), pltpu.VMEM((1, width), F32)]
        + [pltpu.SemaphoreType.DMA((2, 2))] * 2
        + [pltpu.VMEM((count, width), kind) for kind in (F32, F32, BF16, F32)]
        + [pltpu.SemaphoreType.DMA((4,))]
        + Carries.scratch(states, blocks, lax.axis_size("expert"))
        + [ref for refs in sum_scratch for ref in refs],
        compiler_params=params(collective_id=collective_id, has_side_effects=True),
        name="mixer_grads",
    )(*experts, *(item.local for item in items), delta, ssm_grad, mixed, pre, bc, rate_log, skip, held, beside)
    return outs


def shifted_in(tile, row, forward):
    if forward:
        return jnp.concatenate([row, tile[: SEGS - 1]], axis=0)
    return jnp.concatenate([tile[1:], row], axis=0)


def middle_kernel(*refs):
    hidden_ref, grad_ref, upstream_ref, gain_ref, normed_ref = refs[:5]
    gated_ref, ssm_ref, gate_ref, out_proj_ref = refs[5:9]
    hidden_grad_ref, gain_out, ssm_grad_ref, gate_grad_ref, out_local_ref, gate_local_ref = refs[9:15]
    branch = refs[15]

    @pl.when(pl.program_id(0) == 0)
    def _():
        to_hidden, to_gain = rms_back(hidden_ref[...], as_row(gain_ref), grad_ref[...])
        total = upstream_ref[...].astype(F32) + to_hidden
        hidden_grad_ref[...] = total
        branch[...] = total.astype(BF16)
        gain_out[...] = to_gain[None]

    over_rows = (((0,), (0,)), ((), ()))
    out_local_ref[...] = lax.dot_general(
        gated_ref[...], branch[...], over_rows, preferred_element_type=F32
    ).astype(BF16)
    gated_grad = lax.dot_general(
        branch[...], out_proj_ref[...], (((1,), (1,)), ((), ())), preferred_element_type=F32
    )
    gate = gate_ref[...]
    s = jax.nn.sigmoid(gate)
    ssm_grad_ref[...] = gated_grad * (gate * s)
    low = (gated_grad * ssm_ref[...] * (s * (1.0 + gate * (1.0 - s)))).astype(BF16)
    gate_grad_ref[...] = low
    gate_local_ref[...] = lax.dot_general(
        normed_ref[...], low, over_rows, preferred_element_type=F32
    ).astype(BF16)


def middle(hidden, grad, upstream, gain, normed, gated, ssm, gate_z, out_proj):
    count, width = hidden.shape
    inner_width = out_proj.shape[0]
    wide = 2 * LANES
    vmem = pl.BlockSpec(memory_space=pltpu.VMEM)
    whole = lambda *shape: pl.BlockSpec(shape, lambda c: (0,) * len(shape))
    lanes = lambda rows: pl.BlockSpec((rows, wide), lambda c: (0, c))
    rows = pl.BlockSpec((wide, width), lambda c: (c, 0))
    shape_of = jax.ShapeDtypeStruct
    return pl.pallas_call(
        middle_kernel,
        grid=(inner_width // wide,),
        out_shape=[
            shape_of((count, width), F32),
            shape_of((1, width), F32),
            shape_of((count, inner_width), F32),
            shape_of((count, inner_width), BF16),
            shape_of((inner_width, width), BF16),
            shape_of((width, inner_width), BF16),
        ],
        in_specs=[vmem] * 5 + [lanes(count)] * 3 + [rows],
        out_specs=[whole(count, width), whole(1, width), lanes(count), lanes(count), rows]
        + [lanes(width)],
        scratch_shapes=[pltpu.VMEM((count, width), BF16)],
        compiler_params=params(),
        name="middle",
    )(hidden, grad, upstream, gain, normed, gated, ssm, gate_z, out_proj)


WIDE = 2 * LANES


def put_by_token(out_ref, value, turn):
    steps = value.shape[0] // SEGS
    for lane in range(turn.shape[0]):
        lanes = slice(lane * LANES, (lane + 1) * LANES)
        turn[lane] = value[:, lanes]
        for s in range(SEGS):
            rows = turn[lane, pl.ds(s, steps, stride=SEGS), :]
            out_ref[s * steps : (s + 1) * steps, lanes] = rows.astype(out_ref.dtype)


def tile_places(pack, flat):
    _, pairs, each = pack.shape[:3]
    across = flat.shape[1] // LANES
    for t in range(2 * pairs * each):
        row, lane = t // across * 16, t % across * LANES
        inside = (slice(row, row + 16), slice(lane, lane + LANES)) if row < flat.shape[0] else None
        yield (t // (pairs * each), t // each % pairs, t % each), inside


def put_tiles(pack, flat):
    for tile, inside in tile_places(pack, flat):
        if inside is None:
            pack[tile] = jnp.zeros((16, LANES), BF16)
        else:
            pack[tile] = flat[inside].astype(BF16)


def get_tiles(flat, pack):
    for tile, inside in tile_places(pack, flat):
        if inside is not None:
            flat[inside] = pack[tile].astype(F32)


def finish_kernel(rank, states, kinds, *refs):
    loads_hbm, expert_hbm, landed_hbm, refs = refs[:11], refs[11:13], refs[13:15], refs[15:]
    bc_grad_ref, low_ref, x_proj_ref, dt_proj_ref, conv_ref, bias_ref = refs[:6]
    before_ref, gain_ref, rate_ref, dt_bias_ref, skip_ref, gain_two_ref, router_ref = refs[6:13]
    col_ref, gate_spread, out_spread = refs[13:16]
    output_ref, tokens_grad_ref, in_proj_out, out_proj_out, flat, last_flat = refs[16:22]
    second_hbm, refs = refs[22:24], refs[24:]
    halving_refs, halving_sems, refs = refs[:4], refs[4:8], refs[8:]
    halvings = [Halving(expert_hbm[i], i == 0, halving_sems[i]) for i in range(2)]
    loaded, refs = refs[:11], refs[11:]
    pre_grad, mixed_part, mixed, inner, normed, in_proj, gate_grad, tokens, hidden_grad = loaded[:9]
    hidden, home = loaded[9:]
    ext_in, ext_grad, inner_grad, proj_grad, rows, head, after = refs[:7]
    turn, load_sems, halo_sems = refs[7:10]
    small, last_small = SmallSum(*refs[10:17]), TinySum(*refs[17:23])
    x_proj, dt_proj, bias_row = refs[23:26]
    parts, refs = len(kinds) - 2, refs[26:]
    locals_, sum_refs = refs[:parts], refs[parts:]
    count, width = tokens.shape
    inner_width = inner.shape[1]
    reach = conv_ref.shape[0] - 1
    rim = reach * SEGS
    experts, me = lax.axis_size("expert"), lax.axis_index("expert")
    group = lax.axis_index("batch")
    half = inner_width

    loads = [
        pltpu.make_async_copy(src, dst, load_sems.at[i])
        for i, (src, dst) in enumerate(zip(loads_hbm, loaded))
    ]
    halving_loads = []
    for i, halving in enumerate(halvings):
        for k, src in enumerate((halving.chunk(halving.far), landed_hbm[i].at[1])):
            halving_loads.append(
                pltpu.make_async_copy(src, halving_refs[2 * i + k], halving_sems[2 + i].at[k])
            )
    for load in loads[:1] + halving_loads + loads[1:]:
        load.start()
    ends = [0]
    for ref in locals_:
        ends.append(ends[-1] + ref.shape[2])
    inner_rows = [slice(ends[i], ends[i + 1]) for i in range(parts)]
    gate_sum, out_sum, *inner_sums = summings(
        kinds,
        (gate_spread, out_spread, *locals_),
        (in_proj_out.at[:, half:], out_proj_out)
        + tuple(in_proj_out.at[at, :half] for at in inner_rows),
        sum_refs,
    )
    greet_others()
    gate_sum.begin()
    out_sum.begin()
    x_proj[...] = padded_rows(x_proj_ref, LANES)
    dt_proj[...] = padded_rows(dt_proj_ref, LANES)
    bias_row[...] = as_row(bias_ref)
    low = low_ref[...].astype(BF16)
    flat[...] = jnp.zeros(flat.shape, F32)
    last_flat[...] = jnp.zeros(last_flat.shape, F32)
    last_small.total[...] = jnp.zeros(last_small.total.shape, F32)

    seconds = []
    for i, halving in enumerate(halvings):
        own, brought = halving_refs[2 * i : 2 * i + 2]
        for load in halving_loads[2 * i : 2 * i + 2]:
            load.wait()

        def join(n, carry, own=own, brought=brought):
            at = pl.ds(pl.multiple_of(n * 16, 16), 16)
            own[at, :] = together(own[at, :], brought[at, :]).astype(BF16)
            return carry

        lax.fori_loop(0, own.shape[0] // 16, join, 0)
        seconds.append(halving.second(own, second_hbm[i]))
        seconds[i].start()

    loads[0].wait()
    over_inner = (((1,), (1,)), ((), ()))
    over_rows = (((0,), (0,)), ((), ()))
    low_grad = lax.dot_general(
        pre_grad[...], dt_proj[...], over_inner, preferred_element_type=F32
    )
    proj_grad[...] = (low_grad + bc_grad_ref[...]).astype(BF16)

    for load in loads[1:4]:
        load.wait()

    def before_silu(at):
        own = inner[:, at].astype(F32)
        for k in range(reach):
            tile = own[count - rim + k * SEGS : count - rim + (k + 1) * SEGS]
            ext_in[k * SEGS : (k + 1) * SEGS, at] = shifted_in(tile, before_ref[k : k + 1, at], True)
        ext_in[rim:, at] = own
        total = jnp.dot(proj_grad[...], x_proj[:, at], preferred_element_type=F32)
        total = total + mixed_part[:, at]
        conv_pre = jnp.broadcast_to(bias_row[:, at], total.shape)
        for k in range(reach + 1):
            conv_pre = conv_pre + conv_ref[k : k + 1, at] * ext_in[k * SEGS : k * SEGS + count, at]
        total = total * silu_slope(conv_pre)
        ext_grad[:count, at] = total
        for k in range(reach):
            head[k : k + 1, at] = total[k * SEGS : k * SEGS + 1]

    over_blocks(inner_width, WIDE, before_silu)
    halo = pltpu.make_async_remote_copy(
        src_ref=head,
        dst_ref=after,
        send_sem=halo_sems.at[0],
        recv_sem=halo_sems.at[1],
        device_id=(group, lax.rem(me + experts - 1, experts)),
        device_id_type=MESH,
    )

    @pl.when(me > 0)
    def _():
        halo.start()

    @pl.when(me == experts - 1)
    def _():
        after[...] = jnp.zeros(after.shape, F32)

    at_dt = rank + 2 * states
    x_local = lax.dot_general(proj_grad[...], mixed[...], over_rows, preferred_element_type=F32)
    flat[:at_dt, :] = x_local[:at_dt]
    dt_local = lax.dot_general(low, pre_grad[...], over_rows, preferred_element_type=F32)
    flat[at_dt : at_dt + rank, :] = dt_local[:rank]
    at = at_dt + rank + states
    flat[at_dt + rank : at, :] = rate_ref[...]
    flat[at : at + 1, :] = dt_bias_ref[...]
    flat[at + 1 : at + 2, :] = skip_ref[...]
    flat[at + 2 : at + 3, :width] = gain_two_ref[...]
    fold = router_ref.shape[0] // 2
    flat[at + 3 : at + 3 + fold, :width] = router_ref[:fold, :]
    flat[at + 3 : at + 3 + fold, width:] = router_ref[fold:, :]
    put_tiles(small.pack, flat)
    small.start(0)
    for load in loads[4:7]:
        load.wait()
    rows[...] = lax.dot_general(
        gate_grad[...], in_proj[:, half:], over_inner, preferred_element_type=F32
    )

    @pl.when(me > 0)
    def _():
        halo.wait_send()

    @pl.when(me < experts - 1)
    def _():
        halo.wait_recv()

    def before_taps(at):
        for k in range(reach):
            tile = ext_grad[k * SEGS : (k + 1) * SEGS, at]
            ext_grad[count + k * SEGS : count + (k + 1) * SEGS, at] = shifted_in(
                tile, after[k : k + 1, at], False
            )
        total = conv_ref[0:1, at] * ext_grad[rim : rim + count, at]
        for k in range(1, reach + 1):
            first = (reach - k) * SEGS
            total = total + conv_ref[k : k + 1, at] * ext_grad[first : first + count, at]
        inner_grad[:, at] = total.astype(BF16)

    over_blocks(inner_width, WIDE, before_taps)
    chunk = width // experts
    share = inner_width // lax.axis_size("batch")

    def to_in_proj(at):
        total = lax.dot_general(
            normed[...], inner_grad[:, at], over_rows, preferred_element_type=F32
        ).astype(BF16)
        for e in range(experts):
            own = total[e * chunk : (e + 1) * chunk]
            for ref, rows_at in zip(locals_, inner_rows):
                ref[e // 2, e % 2, :, at] = own[rows_at]

    over_blocks(inner_width, share, to_in_proj)
    for item in inner_sums:
        item.begin()
    small.advance(0)


    def to_taps(at):
        grad = ext_grad[:count, at]
        for k in range(reach + 1):
            last_flat[k : k + 1, at] = jnp.sum(
                grad * ext_in[k * SEGS : k * SEGS + count, at], axis=0, keepdims=True
            )
        last_flat[reach + 1 : reach + 2, at] = jnp.sum(grad, axis=0, keepdims=True)

    for item in inner_sums:
        item.advance(0)
    over_blocks(inner_width, WIDE, to_taps)
    for load in loads[7:]:
        load.wait()
    grad = rows[...] + lax.dot_general(
        inner_grad[...], in_proj[:, :half], over_inner, preferred_element_type=F32
    )
    values = tokens[...].astype(F32)
    to_values, to_gain = rms_back(values, as_row(gain_ref), grad)
    put_by_token(tokens_grad_ref, to_values + hidden_grad[...], turn)

    last_flat[reach + 2 : reach + 3, :width] = to_gain[None]
    across = inner_width // LANES
    for t in range((reach + 3) * across):
        row, lane = t // across, t % across * LANES
        last_small.total[t : t + 1, :] = last_flat[row : row + 1, lane : lane + LANES]
    last_small.pack[...] = last_small.total[...].astype(BF16)
    last_small.start(0)
    gate_sum.advance(2)
    out_sum.advance(2)
    small.advance(1)
    last_small.advance(0)
    for item in inner_sums:
        item.advance(1)
    last_small.advance(1)
    small.advance(2)

    slots = home.shape[1]
    slot_id = lax.broadcasted_iota(jnp.int32, (count, experts * slots), 1)
    chosen = (slot_id == col_ref[...]).astype(F32).astype(BF16)
    returned = jnp.dot(
        chosen, home[...].reshape(experts * slots, width), preferred_element_type=F32
    )
    put_by_token(output_ref, hidden[...] + returned, turn)

    last_small.advance(2)
    gate_sum.advance(3)
    out_sum.advance(3)
    for item in inner_sums:
        item.advance(2)
    small.advance(3)
    small.advance(4)
    get_tiles(flat, small.every)
    for item in inner_sums:
        item.advance(3)
    for t in range((reach + 3) * across):
        row, lane = t // across, t % across * LANES
        last_flat[row : row + 1, lane : lane + LANES] = last_small.total[t : t + 1, :]
    for copy in seconds:
        copy.wait()


def finish(loaded, experts, landed, small, early, rank, states, collective_id):
    pre_grad, in_proj, tokens = loaded[0], loaded[5], loaded[7]
    conv_weight, router_local = small[4], small[12]
    count, inner_width = pre_grad.shape
    width = tokens.shape[1]
    count_experts, ways = lax.axis_size("expert"), lax.axis_size("batch")
    pairs, chunk = count_experts // 2, width // count_experts
    chunks = [(e.shape[0] // 4, e.shape[1]) for e in experts]
    taps = conv_weight.shape[0]
    vmem, hbm = (pl.BlockSpec(memory_space=m) for m in (pltpu.VMEM, pl.ANY))
    split = (chunk // 3, chunk * 2 // 3) if chunk % 48 == 0 else (chunk,)
    locals_ = [jax.ShapeDtypeStruct((pairs, 2, part, inner_width), BF16) for part in split]
    items = early + [Total(local, 1, i == 1) for i, local in enumerate(locals_)]
    scratch = [item.scratch() for item in items]
    kinds = tuple((item.kind(), len(refs)) for item, refs in zip(items, scratch))
    used = 2 * rank + 3 * states + 3 + router_local.shape[0] // 2
    high, low = (-(-rows // 16) * 16 for rows in (used, taps + 2))
    tiles = [-(-(rows // 16 * inner_width // LANES) // (2 * pairs)) for rows in (high, low)]
    f32 = lambda *shape: jax.ShapeDtypeStruct(shape, F32)
    halo = pltpu.VMEM((SEGS, inner_width), F32)
    rim = (taps - 1) * SEGS
    return pl.pallas_call(
        functools.partial(finish_kernel, rank, states, kinds),
        out_shape=[
            jax.ShapeDtypeStruct((count, width), BF16),
            f32(count, width),
            jax.ShapeDtypeStruct((chunk, 2 * inner_width), BF16),
            jax.ShapeDtypeStruct(early[1].chunk, BF16),
            f32(high, inner_width),
            f32(low, inner_width),
        ]
        + [jax.ShapeDtypeStruct(shape, BF16) for shape in chunks],
        in_specs=[hbm] * (len(loaded) + 4) + [vmem] * (len(small) + len(early)),
        out_specs=[vmem] * 6 + [hbm] * 2,
        scratch_shapes=[pltpu.VMEM(shape, BF16) for shape in chunks for _ in range(2)]
        + [pltpu.SemaphoreType.DMA((2, 1))] * 2
        + [pltpu.SemaphoreType.DMA((2,))] * 2
        + [pltpu.VMEM(a.shape, a.dtype) for a in loaded]
        + [
            pltpu.VMEM((count + rim, inner_width), F32),
            pltpu.VMEM((count + rim, inner_width), F32),
            pltpu.VMEM((count, inner_width), BF16),
            pltpu.VMEM((count, LANES), BF16),
            pltpu.VMEM((count, width), F32),
            halo,
            halo,
            pltpu.VMEM((width // LANES, count, LANES), F32),
            pltpu.SemaphoreType.DMA((len(loaded),)),
            pltpu.SemaphoreType.DMA((2,)),
        ]
        + SmallSum.scratch(pairs, ways, tiles[0])
        + TinySum.scratch(pairs, ways, -(-(taps + 2) * inner_width // LANES // 16) * 16)
        + [
            pltpu.VMEM((LANES, inner_width), BF16),
            pltpu.VMEM((LANES, inner_width), BF16),
            pltpu.VMEM((1, inner_width), F32),
        ]
        + [pltpu.VMEM(local.shape, BF16) for local in locals_]
        + [ref for refs in scratch for ref in refs],
        compiler_params=params(collective_id=collective_id, has_side_effects=True),
        name="finish",
    )(*loaded, *experts, *landed, *small, *(item.local for item in early))


def deliver_kernel(*refs):
    output_in, tokens_grad_in, in_proj, out_proj, flat, last = refs[:6]
    expert_hbm, landed_hbm, second_hbm, refs = refs[6:8], refs[8:10], refs[10:12], refs[12:]
    output, tokens_grad, gain, in_proj_out, conv, bias, x_proj, dt_proj, dt_bias, rate = refs[:10]
    skip, out_proj_out, gain_two, router, expert_in_out, expert_out_out = refs[10:16]
    held, sems = refs[16:22], refs[22]
    loads = []
    for i in range(2):
        halving = Halving(expert_hbm[i], i == 0)
        parts = (halving.chunk(halving.group), landed_hbm[i].at[0], second_hbm[i])
        for k, src in enumerate(parts):
            loads.append(pltpu.make_async_copy(src, held[3 * i + k], sems.at[i, k]))
    for load in loads:
        load.start()
    output[0] = output_in[...]
    tokens_grad[0] = tokens_grad_in[...]
    at, width = 0, gain.shape[0]
    for ref in (x_proj, dt_proj, rate):
        ref[...] = flat[at : at + ref.shape[0], :]
        at += ref.shape[0]
    fold = router.shape[0] // 2
    dt_bias[...] = flat[at : at + 1, :].reshape(dt_bias.shape)
    skip[...] = flat[at + 1 : at + 2, :].reshape(skip.shape)
    gain_two[...] = flat[at + 2 : at + 3, :width].reshape(gain_two.shape)
    router[:fold, :] = flat[at + 3 : at + 3 + fold, :width]
    router[fold:, :] = flat[at + 3 : at + 3 + fold, width:]
    taps = conv.shape[0]
    conv[...] = last[:taps, :]
    bias[...] = last[taps : taps + 1, :].reshape(bias.shape)
    gain[...] = last[taps + 1 : taps + 2, :width].reshape(gain.shape)
    in_proj_out[...] = in_proj[...].astype(F32)
    out_proj_out[...] = out_proj[...].astype(F32)
    for i, out in enumerate((expert_in_out, expert_out_out)):
        for load in loads[3 * i : 3 * i + 3]:
            load.wait()
        total = together(*(ref[...] for ref in held[3 * i : 3 * i + 3]))
        out[0] = total.astype(BF16).astype(F32)


def deliver(made, experts, landed, shapes):
    vmem = pl.BlockSpec(memory_space=pltpu.VMEM)
    hbm = pl.BlockSpec(memory_space=pl.ANY)
    output, tokens_grad, in_proj, out_proj, flat, last = made[:6]
    chunks = [(e.shape[0] // 4, e.shape[1]) for e in experts]
    f32 = lambda *shape: jax.ShapeDtypeStruct(shape, F32)
    outs = [
        jax.ShapeDtypeStruct((1, *output.shape), BF16),
        f32(1, *tokens_grad.shape),
        shapes[0],
        f32(*in_proj.shape),
        *shapes[1:8],
        f32(*out_proj.shape),
        *shapes[8:],
        *(f32(1, *shape) for shape in chunks),
    ]
    return pl.pallas_call(
        deliver_kernel,
        out_shape=outs,
        in_specs=[vmem] * 6 + [hbm] * 6,
        out_specs=[vmem] * len(outs),
        scratch_shapes=[pltpu.VMEM(shape, BF16) for shape in chunks for _ in range(3)]
        + [pltpu.SemaphoreType.DMA((2, 3))],
        compiler_params=params(),
        name="deliver",
    )(*made[:6], *experts, *landed, *made[6:])


def silu(v):
    return v * jax.nn.sigmoid(v)


def silu_slope(v):
    s = jax.nn.sigmoid(v)
    return s * (1.0 + v * (1.0 - s))


def rms_back(values, gain, grad):
    r = lax.rsqrt(jnp.mean(values * values, axis=-1, keepdims=True) + 1e-05)
    u = gain * grad
    mean = jnp.mean(values * u, axis=-1, keepdims=True)
    return r * u - values * (r * r * r) * mean, jnp.sum(grad * values * r, axis=0)


def rms(values, gain):
    return values * lax.rsqrt(jnp.mean(values * values, axis=-1, keepdims=True) + 1e-05) * gain


def per_device(
    tokens,
    routes,
    gain_one,
    in_proj,
    conv_weight,
    conv_bias,
    x_proj,
    dt_proj,
    dt_bias,
    rate_log,
    skip,
    out_proj,
    gain_two,
    router,
    expert_in,
    expert_out,
    cotangent,
):
    count, width = tokens.shape[1], tokens.shape[2]
    steps = count // SEGS
    inner_width = out_proj.shape[0]
    rank = dt_proj.shape[0]
    experts = router.shape[0]
    capacity = 5 * count // (4 * experts)
    slots = -(-capacity // 16) * 16
    states = rate_log.shape[0]
    route = routes.reshape(SEGS, steps).T.reshape(1, count)
    made, kept = forward(
        tokens,
        cotangent,
        in_proj,
        out_proj,
        route,
        gain_one,
        gain_two,
        conv_weight,
        conv_bias,
        x_proj,
        dt_proj,
        dt_bias,
        skip,
        rate_log,
        (rank, capacity, slots),
        2,
    )
    ssm, held, gated, hidden, normed_two, row, col, before, slot_upstream = made
    tokens_low, upstream_low, normed_one, inner, gate_z, mixed, pre, delta, proj = kept

    normed_two_grad, results, *expert_grads, router_local = run_experts(
        normed_two, row, col, router, slot_upstream, expert_in, expert_out, slots, 4
    )

    hidden_grad, gain_two_local, ssm_grad, gate_z_grad, out_proj_local, in_proj_gate_local = middle(
        hidden, normed_two_grad, upstream_low, gain_two, normed_one, gated, ssm, gate_z, out_proj
    )
    ways, pairs = lax.axis_size("batch"), experts // 2
    early = [
        Total(
            in_proj_gate_local.reshape(pairs, 2, width // experts, inner_width),
            1,
        ),
        Total(
            out_proj_local.reshape(
                pairs, 2, ways, inner_width // (experts * ways), width
            ),
            0,
            True,
        ),
    ]
    (
        in_proj_gate_spread,
        out_proj_spread,
        pre_grad,
        mixed_grad,
        rate_log_local,
        skip_local,
        dt_bias_local,
        bc_grad,
        returned,
        *landed,
    ) = mixer_grads(
        pre, delta, mixed, ssm_grad, proj, rate_log, skip, held, results, expert_grads, rank, early, 3
    )
    early = [early[0].resumed(in_proj_gate_spread), early[1].resumed(out_proj_spread)]
    outs = finish(
        [
            pre_grad,
            mixed_grad,
            mixed,
            inner,
            normed_one,
            in_proj,
            gate_z_grad,
            tokens_low,
            hidden_grad,
            hidden,
            returned,
        ],
        expert_grads,
        landed,
        [
            bc_grad,
            proj,
            x_proj,
            dt_proj,
            conv_weight,
            conv_bias,
            before,
            gain_one,
            rate_log_local,
            dt_bias_local,
            skip_local,
            gain_two_local,
            router_local,
            col,
        ],
        early,
        rank,
        states,
        1,
    )
    outs = (*outs[:3], outs[3].reshape(-1, width), *outs[4:])
    weights = (gain_one, conv_weight, conv_bias, x_proj, dt_proj, dt_bias, rate_log, skip)
    shapes = [jax.ShapeDtypeStruct(w.shape, F32) for w in (*weights, gain_two, router)]
    return tuple(deliver(outs, expert_grads, landed, shapes))


def solution(mesh):
    split = P("batch", "expert", None)
    one = P("expert", None, None)
    both = P("expert", "batch", None)
    in_specs = (split, split) + (P(),) * 12 + (one, one, split)
    out_specs = (split, split, P(), P("expert", None)) + (P(),) * 7
    out_specs += (P("expert", None), P(), P(), both, both)
    return jax.shard_map(
        per_device, mesh=mesh, in_specs=in_specs, out_specs=out_specs, check_vma=False
    )
```

```python
import functools

import jax
import jax.numpy as jnp
from jax import lax
from jax.experimental import pallas as pl
from jax.experimental.pallas import tpu as pltpu
from jax.sharding import PartitionSpec as P

F32, BF16 = jnp.float32, jnp.bfloat16
SEGS = 8
LANES = 128
LOG2E = 1.4426950408889634
LN2 = 0.6931471805599453
VMEM_LIMIT = 60 * 1024 * 1024
MESH = pl.DeviceIdType.MESH


def params(**kw):
    return pltpu.CompilerParams(vmem_limit_bytes=VMEM_LIMIT, **kw)


def softplus(v):
    return jnp.maximum(v, 0.0) + jnp.log1p(jnp.exp(-jnp.abs(v)))


def as_row(ref):
    return ref[...].reshape(1, ref.shape[0])


def padded_rows(ref, high):
    low = jnp.zeros((high - ref.shape[0], ref.shape[1]), F32)
    return jnp.concatenate([ref[...].astype(F32), low], axis=0).astype(BF16)


def over_sublanes(row):
    return jnp.broadcast_to(row, (SEGS, LANES))


def over_lanes(column):
    return jnp.broadcast_to(column, (SEGS, LANES))


def tile_rows(j):
    return pl.ds(pl.multiple_of(j * SEGS, SEGS), SEGS)


def run_of_segments(a, b, forward):
    at = lax.broadcasted_iota(jnp.int32, (SEGS, LANES), 0)
    for step in (1, 2, 4):
        if forward:
            inside, turn = at >= step, step
        else:
            inside, turn = at < SEGS - step, SEGS - step
        before_a = jnp.where(inside, pltpu.roll(a, turn, 0), 1.0)
        before_b = jnp.where(inside, pltpu.roll(b, turn, 0), 0.0)
        a, b = a * before_a, a * before_b + b
    return a, b


class Carries:
    groups = 2

    def __init__(self, states, blocks, forward, own, lengths, got, got_lengths, sems):
        self.states, self.blocks, self.forward = states, blocks, forward
        self.own, self.lengths, self.got, self.got_lengths = own, lengths, got, got_lengths
        self.sems = sems
        self.count, self.me = lax.axis_size("expert"), lax.axis_index("expert")
        self.per = blocks // self.groups

    @staticmethod
    def scratch(states, blocks, count):
        per = blocks // Carries.groups
        assert blocks % Carries.groups == 0 and per <= SEGS
        return [
            pltpu.VMEM((blocks, states, LANES), BF16),
            pltpu.VMEM((Carries.groups, SEGS, LANES), F32),
            pltpu.VMEM((count, blocks, states, LANES), BF16),
            pltpu.VMEM((count, Carries.groups, SEGS, LANES), F32),
            pltpu.SemaphoreType.DMA((2, 2, Carries.groups, count)),
        ]

    def other(self, k):
        return (lax.axis_index("batch"), lax.rem(self.me + k, self.count))

    def copies(self, group):
        blocks = pl.ds(group * self.per, self.per)
        found = []
        for k in range(1, self.count):
            pairs = (
                (self.own.at[blocks], self.got.at[k - 1, blocks]),
                (self.lengths.at[group], self.got_lengths.at[k - 1, group]),
            )
            for i, (src, dst) in enumerate(pairs):
                found.append(
                    pltpu.make_async_remote_copy(
                        src_ref=src,
                        dst_ref=dst,
                        send_sem=self.sems.at[0, i, group, k - 1],
                        recv_sem=self.sems.at[1, i, group, k - 1],
                        device_id=self.other(k),
                        device_id_type=MESH,
                    )
                )
        return found

    def put(self, block, ends, sums, rates, run_a, run_b):
        edge = SEGS - 1 if self.forward else 0
        rows = []
        for n in range(self.states):
            a, b = run_of_segments(jnp.exp2(rates[n] * sums), ends[n], self.forward)
            run_a[block, n] = a
            run_b[block, n] = b
            rows.append(b[edge : edge + 1])
        end = jnp.concatenate(rows, axis=0).astype(BF16)
        total = jnp.sum(sums, axis=0, keepdims=True)
        last = self.count - 1
        self.own[block] = end
        self.got[last, block] = end
        for group in range(self.groups):

            @pl.when(block // self.per == group)
            def _():
                row = pl.ds(lax.rem(block, self.per), 1)
                self.lengths[group, row, :] = total
                self.got_lengths[last, group, row, :] = total

            @pl.when(block == (group + 1) * self.per - 1)
            def _():
                for copy in self.copies(group):
                    copy.start()

    def await_group(self, block):
        for group in range(self.groups):

            @pl.when(block == group * self.per)
            def _():
                for copy in self.copies(group):
                    copy.wait()

    def starts(self, block, rate, run_a, run_b):
        group, row = block // self.per, pl.ds(lax.rem(block, self.per), 1)
        entering = jnp.zeros((self.states, LANES), F32)
        order = range(self.count) if self.forward else range(self.count - 1, -1, -1)
        for place in order:
            slot = lax.rem(self.me - place - 1 + 2 * self.count, self.count)
            length = self.got_lengths[slot, group, row, :]
            joined = jnp.exp2(rate * length) * entering + self.got[slot, block].astype(F32)
            ahead = (place < self.me) if self.forward else (place > self.me)
            entering = jnp.where(ahead, joined, entering)
        found = []
        for n in range(self.states):
            first = entering[n : n + 1]
            after = run_a[block, n] * over_sublanes(first) + run_b[block, n]
            found.append(shifted_in(after, first, self.forward))
        return found


def together(*parts):
    return sum(p.astype(F32) for p in parts)


class Total:
    def __init__(self, local, axis, pairs_first=False, chunk=None):
        self.local, self.axis, self.pairs_first = local, axis, pairs_first
        self.ways = lax.axis_size("batch")
        self.taken_up = chunk is not None
        self.pairs, self.chunk = lax.axis_size("expert") // 2, chunk or local.shape[2:]
        part = list(self.chunk)
        part[axis] //= self.ways
        self.part = tuple(part)

    def kind(self):
        return self.axis, self.pairs_first, self.part, self.taken_up

    def spread_shape(self):
        shape = self.chunk if self.pairs_first else (self.pairs, *self.part)
        return jax.ShapeDtypeStruct(shape, BF16)

    def resumed(self, spread):
        return Total(spread, self.axis, self.pairs_first, self.chunk)

    def first_scratch(self):
        first = (self.pairs - 1, *self.chunk)
        if not self.pairs_first:
            first = (self.ways - 1, self.pairs, *self.part)
        return [
            pltpu.VMEM((2, self.pairs, *self.chunk), BF16),
            pltpu.VMEM((self.pairs, *self.chunk), BF16),
            pltpu.VMEM(first, BF16),
            pltpu.SemaphoreType.DMA((2, 2, max(self.ways, self.pairs))),
        ]

    def second_scratch(self):
        second = self.ways - 1 if self.pairs_first else self.pairs - 1
        return [
            pltpu.VMEM((second, *self.part), BF16),
            pltpu.VMEM(self.part, BF16),
            pltpu.VMEM(self.chunk, BF16),
            pltpu.SemaphoreType.DMA((2, 4, max(self.ways, self.pairs))),
        ]

    def scratch(self):
        if self.taken_up:
            return self.second_scratch()
        spread = self.spread_shape()
        return self.first_scratch() + [pltpu.VMEM(spread.shape, BF16)] + self.second_scratch()


def part_of(ref, lead, axis, size, index):
    start = index * size
    if axis == len(ref.shape) - lead - 1:
        start = pl.multiple_of(start, LANES)
    where = [slice(None)] * len(ref.shape)
    where[lead + axis] = pl.ds(start, size)
    return ref.at[tuple(where)]


class Peers:
    def __init__(self):
        self.ways, self.pairs = lax.axis_size("batch"), lax.axis_size("expert") // 2
        self.group, place = lax.axis_index("batch"), lax.axis_index("expert")
        self.pair, self.core = place // 2, lax.rem(place, 2)
        self.sibling = (self.group, self.pair * 2 + 1 - self.core)
        self.to_batch = [lax.rem(self.group + k, self.ways) for k in range(1, self.ways)]
        self.to_pairs = [lax.rem(self.pair + k, self.pairs) for k in range(1, self.pairs)]
        self.in_batch = [(to, place) for to in self.to_batch]
        self.in_pairs = [(self.group, to * 2 + self.core) for to in self.to_pairs]

    def remote(self, src, dst, sems, stage, k, device):
        return pltpu.make_async_remote_copy(
            src_ref=src,
            dst_ref=dst,
            send_sem=sems.at[0, stage, k],
            recv_sem=sems.at[1, stage, k],
            device_id=device,
            device_id_type=MESH,
        )

    def start(self, stage):
        for copy in self.copies(stage):
            copy.start()

    def wait(self, stage):
        for copy in self.copies(stage):
            copy.wait()

    def advance(self, stage):
        self.wait(stage)
        self.add(stage)
        if stage < self.last:
            self.start(stage + 1)


class Summing(Peers):
    last = 3

    def __init__(self, kind, local, out, scratch):
        super().__init__()
        self.axis, self.pairs_first, part, self.taken_up = kind
        self.local, self.out, self.size = local, out, part[self.axis]
        if self.taken_up:
            self.spread = local
            self.from_second, self.mine, self.every, self.late_sems = scratch
        else:
            self.both, self.by_chip, self.from_first, self.sems = scratch[:4]
            self.spread = out
            if len(scratch) > 4:
                self.spread, self.from_second, self.mine, self.every, self.late_sems = scratch[4:]

    def share(self, ref, lead, index):
        return part_of(ref, lead, self.axis, self.size, index)

    def copies(self, stage):
        if stage == 0:
            own = pltpu.make_async_copy(
                self.local.at[:, self.core], self.both.at[0], self.sems.at[0, 0, 1]
            )
            away = self.local.at[:, 1 - self.core]
            return [own, self.remote(away, self.both.at[1], self.sems, 0, 0, self.sibling)]
        if stage == 3:
            own, devices = self.share(self.every, 0, self.group), self.in_batch
            pieces = [(self.mine, own) for _ in devices]
        elif (stage == 1) == self.pairs_first:
            devices = self.in_pairs
            src, dst = (self.by_chip, self.from_first) if stage == 1 else (self.spread, self.from_second)
            pieces = [(src.at[to], dst.at[k]) for k, to in enumerate(self.to_pairs)]
        else:
            devices = self.in_batch
            src, dst = (self.by_chip, self.from_first) if stage == 1 else (self.spread, self.from_second)
            lead = 1 if stage == 1 else 0
            pieces = [
                (self.share(src, lead, to), dst.at[k]) for k, to in enumerate(self.to_batch)
            ]
        sems = self.sems if stage == 1 else self.late_sems
        return [
            self.remote(src, dst, sems, stage, k, devices[k]) for k, (src, dst) in enumerate(pieces)
        ]

    def add(self, stage):
        if stage == 0:

            def over_cores(z, carry):
                self.by_chip[z] = together(self.both[0, z], self.both[1, z]).astype(BF16)
                return carry

            lax.fori_loop(0, self.pairs, over_cores, 0)
        elif stage == 1 and self.pairs_first:
            others = (self.from_first[k] for k in range(self.pairs - 1))
            self.spread[...] = together(self.by_chip[self.pair], *others).astype(BF16)
        elif stage == 1:
            own = self.share(self.by_chip, 1, self.group)

            def over_batch(z, carry):
                others = (self.from_first[k, z] for k in range(self.ways - 1))
                self.spread[z] = together(own[z], *others).astype(BF16)
                return carry

            lax.fori_loop(0, self.pairs, over_batch, 0)
        elif stage == 2:
            if self.pairs_first:
                own, count = self.share(self.spread, 0, self.group)[...], self.ways
            else:
                own, count = self.spread[self.pair], self.pairs
            others = (self.from_second[k] for k in range(count - 1))
            total = together(own, *others).astype(BF16)
            self.mine[...] = total
            self.share(self.every, 0, self.group)[...] = total
        else:
            self.out[...] = self.every[...].astype(self.out.dtype)

    def begin(self):
        self.start(2 if self.taken_up else 0)


class SmallSum(Peers):
    last = 4

    def __init__(self, pack, from_core, half, from_pairs, by_group, every, sems):
        super().__init__()
        self.pack, self.from_core, self.half, self.from_pairs = pack, from_core, half, from_pairs
        self.by_group, self.every, self.sems = by_group, every, sems

    @staticmethod
    def scratch(pairs, ways, tiles):
        tile = (tiles, 16, LANES)
        shapes = ((2, pairs), (pairs,), (pairs,), (pairs - 1,), (ways,), (2, pairs))
        found = [pltpu.VMEM((*lead, *tile), BF16) for lead in shapes]
        return found + [pltpu.SemaphoreType.DMA((2, 5, max(pairs, ways)))]

    def copies(self, stage):
        if stage == 0:
            pieces = [(self.pack.at[1 - self.core], self.from_core, self.sibling)]
        elif stage == 1:
            pieces = [
                (self.half.at[to], self.from_pairs.at[k], self.in_pairs[k])
                for k, to in enumerate(self.to_pairs)
            ]
        elif stage == 2:
            own = self.by_group.at[self.group]
            pieces = [(own, own, device) for device in self.in_batch]
        elif stage == 3:
            own = self.every.at[self.core, self.pair]
            pieces = [(own, own, device) for device in self.in_pairs]
        else:
            own = self.every.at[self.core]
            pieces = [(own, own, self.sibling)]
        return [
            self.remote(src, dst, self.sems, stage, k, device)
            for k, (src, dst, device) in enumerate(pieces)
        ]

    def add(self, stage):
        if stage == 0:
            self.half[...] = together(self.pack[self.core], self.from_core[...]).astype(BF16)
        elif stage == 1:
            others = (self.from_pairs[k] for k in range(self.pairs - 1))
            self.by_group[self.group] = together(self.half[self.pair], *others).astype(BF16)
        elif stage == 2:
            total = together(*(self.by_group[k] for k in range(self.ways)))
            self.every[self.core, self.pair] = total.astype(BF16)


class TinySum(Peers):
    last = 2

    def __init__(self, pack, from_core, by_pair, by_group, total, sems):
        super().__init__()
        self.pack, self.from_core, self.by_pair = pack, from_core, by_pair
        self.by_group, self.total, self.sems = by_group, total, sems

    @staticmethod
    def scratch(pairs, ways, rows):
        found = [pltpu.VMEM((rows, LANES), BF16)] * 2
        found += [pltpu.VMEM((many, rows, LANES), BF16) for many in (pairs, ways)]
        return found + [pltpu.VMEM((rows, LANES), F32), pltpu.SemaphoreType.DMA((2, 3, max(pairs, ways)))]

    def copies(self, stage):
        if stage == 0:
            pieces = [(self.pack, self.from_core, self.sibling)]
        elif stage == 1:
            own = self.by_pair.at[self.pair]
            pieces = [(own, own, device) for device in self.in_pairs]
        else:
            own = self.by_group.at[self.group]
            pieces = [(own, own, device) for device in self.in_batch]
        return [
            self.remote(src, dst, self.sems, stage, k, device)
            for k, (src, dst, device) in enumerate(pieces)
        ]

    def add(self, stage):
        if stage == 0:
            self.by_pair[self.pair] = together(self.pack[...], self.from_core[...]).astype(BF16)
        elif stage == 1:
            total = together(*(self.by_pair[k] for k in range(self.pairs)))
            self.by_group[self.group] = total.astype(BF16)
        else:
            self.total[...] = together(*(self.by_group[k] for k in range(self.ways)))


def summings(kinds, ins, outs, scratch):
    found, at = [], 0
    for (kind, many), local, out in zip(kinds, ins, outs):
        found.append(Summing(kind, local, out, scratch[at : at + many]))
        at += many
    return found


class Halving:
    def __init__(self, local, x_first, sems=None):
        assert lax.axis_size("batch") == 4
        group, self.place = lax.axis_index("batch"), lax.axis_index("expert")
        by_x = group + 1 - 2 * lax.rem(group, 2)
        by_y = group + 2 - 4 * (group // 2)
        self.local, self.sems, self.group, self.across = local, sems, group, 3 - group
        self.near, self.far = (by_x, by_y) if x_first else (by_y, by_x)
        self.rows = local.shape[0] // 4

    def chunk(self, index):
        return self.local.at[pl.ds(pl.multiple_of(index * self.rows, self.rows), self.rows)]

    def copy(self, src, dst, k, device):
        return pltpu.make_async_remote_copy(
            src_ref=src,
            dst_ref=dst,
            send_sem=self.sems.at[0, k],
            recv_sem=self.sems.at[1, k],
            device_id=(device, self.place),
            device_id_type=MESH,
        )

    def first(self, landing):
        return [
            self.copy(self.chunk(index), landing.at[k], k, self.near)
            for k, index in enumerate((self.near, self.across))
        ]

    def second(self, src, landing):
        return self.copy(src, landing, 0, self.far)


class Side:
    def __init__(self, src, dst, sems):
        self.src, self.dst, self.sems = src, dst, sems
        self.count, self.me = lax.axis_size("expert"), lax.axis_index("expert")

    @staticmethod
    def scratch(count):
        return pltpu.SemaphoreType.DMA((2, count))

    def copy(self, k):
        return self.copy_to(lax.rem(self.me + k, self.count))

    def copy_to(self, to):
        return pltpu.make_async_remote_copy(
            src_ref=self.src.at[to],
            dst_ref=self.dst.at[self.me],
            send_sem=self.sems.at[0, to],
            recv_sem=self.sems.at[1, self.me],
            device_id=(lax.axis_index("batch"), to),
            device_id_type=MESH,
        )

    def brought(self, place):
        return pltpu.make_async_remote_copy(
            src_ref=self.src.at[place],
            dst_ref=self.dst.at[place],
            send_sem=self.sems.at[0, place],
            recv_sem=self.sems.at[1, place],
            device_id=(lax.axis_index("batch"), place),
            device_id_type=MESH,
        )

    def own(self):
        return pltpu.make_async_copy(
            self.src.at[self.me], self.dst.at[self.me], self.sems.at[0, self.me]
        )

    def start(self, part=0, parts=((0, 1),)):
        if part == 0:
            self.own().start()
        least, most = (1 + round(share * (self.count - 1)) for share in parts[part])
        for k in range(least, most):
            self.copy(k).start()

    def wait(self):
        self.own().wait()
        self.wait_others()

    def wait_others(self):
        for k in range(1, self.count):
            place = lax.rem(self.me + k, self.count)
            self.copy_to(place).wait_send()
            self.brought(place).wait_recv()


def greet_others():
    barrier = pltpu.get_barrier_semaphore()
    group, place = lax.axis_index("batch"), lax.axis_index("expert")
    ways, count = lax.axis_size("batch"), lax.axis_size("expert")
    others = [(group, lax.rem(place + k, count)) for k in range(1, count)]
    others += [(lax.rem(group + k, ways), place) for k in range(1, ways)]
    for device in others:
        pl.semaphore_signal(barrier, inc=1, device_id=device, device_id_type=MESH)
    pl.semaphore_wait(barrier, len(others))


def greet_experts():
    barrier = pltpu.get_barrier_semaphore()
    count, me = lax.axis_size("expert"), lax.axis_index("expert")
    for k in range(1, count):
        device = (lax.axis_index("batch"), lax.rem(me + k, count))
        pl.semaphore_signal(barrier, inc=1, device_id=device, device_id_type=MESH)
    pl.semaphore_wait(barrier, count - 1)


def gelu_parts(v):
    size = jnp.abs(v) * 0.7071067811865476
    t = 1.0 / (1.0 + 0.3275911 * size)
    bell = jnp.exp2(v * v * (-0.5 * LOG2E))
    poly = t * (
        0.127414796
        + t * (-0.142248368 + t * (0.7107068705 + t * (-0.7265760135 + t * 0.5307027145)))
    )
    tail = poly * bell
    phi = jnp.where(v >= 0.0, 1.0 - tail, tail)
    return v * phi, phi + v * (bell * 0.3989422804014327)


FF_TILE = 512


def experts_kernel(slots, tile, *refs):
    normed_ref, row_ref, col_ref, router_ref, upstream_ref, in_hbm, out_hbm = refs[:7]
    grad_ref, result_ref, in_grad_hbm, out_grad_hbm, router_grad_ref = refs[7:12]
    w_in, w_out, sent, got, home, slot_grad, active, hid_grad, row_grad = refs[12:21]
    in_grad, out_grad, there_sems, back_sems, load_sems, store_sems, router = refs[21:28]
    gates, logit_grads, back = refs[28:]
    rows = row_grad
    count, me = lax.axis_size("expert"), lax.axis_index("expert")
    width, hidden = w_in.shape
    total = count * slots
    tiles = hidden // tile
    router[...] = padded_rows(router_ref, LANES)
    loads = [
        pltpu.make_async_copy(in_hbm.at[0], w_in, load_sems.at[0]),
        pltpu.make_async_copy(out_hbm.at[0], w_out, load_sems.at[1]),
    ]
    for load in loads:
        load.start()
    greet_experts()
    there = Side(sent, got, there_sems)
    returning = Side(back, home, back_sems)
    tokens = normed_ref.shape[0]
    slot_id = lax.broadcasted_iota(jnp.int32, (slots, tokens), 0)

    upper = me // (count // 2)
    quarter = count // 4
    groups = (
        (upper * 2 * quarter, 2 * quarter),
        ((2 - upper) * quarter, quarter),
        ((3 - 3 * upper) * quarter, quarter),
    )

    def dispatch(to, carry):
        picked = (slot_id + to * slots == row_ref[...]).astype(F32).astype(BF16)
        chunk = jnp.dot(picked, normed_ref[...], preferred_element_type=F32).astype(BF16)
        sent[to] = chunk

        @pl.when(to != me)
        def _():
            there.copy_to(to).start()

        @pl.when(to == me)
        def _():
            got[me] = chunk

        return carry

    for first, many in groups:
        lax.fori_loop(first, first + many, dispatch, 0)
    over_inner = (((1,), (1,)), ((), ()))
    for load in loads:
        load.wait()
    for first, many in groups:

        def arrive(place, carry):
            @pl.when(place != me)
            def _():
                there.brought(place).wait_recv()

            return carry

        lax.fori_loop(first, first + many, arrive, 0)
        high = many * slots
        places = pl.ds(first, many)
        at_rows = pl.ds(pl.multiple_of(first * slots, 16), high)
        x = got[places].reshape(high, width)
        logits = lax.dot_general(x, router[...], over_inner, preferred_element_type=F32)
        lane = lax.broadcasted_iota(jnp.int32, logits.shape, 1)
        logits = jnp.where(lane < count, logits, -1e30)
        scores = jnp.exp(logits - jnp.max(logits, axis=1, keepdims=True))
        probs = scores / jnp.sum(scores, axis=1, keepdims=True)
        mine = (lane == me).astype(F32)
        gate = jnp.sum(probs * mine, axis=1, keepdims=True)
        gates[at_rows, :] = jnp.broadcast_to(gate, (high, LANES))
        upstream = upstream_ref[places].reshape(high, width).astype(F32)
        slot_grad[at_rows, :] = (gate * upstream).astype(BF16)
        row_grad[at_rows, :] = jnp.zeros((high, width), F32)

        def inward(t, picked, x=x, at_rows=at_rows):
            at = pl.ds(pl.multiple_of(t * tile, tile), tile)
            pre = jnp.dot(x, w_in[:, at], preferred_element_type=F32)
            act_grad = lax.dot_general(
                slot_grad[at_rows, :], w_out[at, :], over_inner, preferred_element_type=F32
            )
            value, slope = gelu_parts(pre)
            active[at_rows, at] = value.astype(BF16)
            low = (act_grad * slope).astype(BF16)
            hid_grad[at_rows, at] = low
            row_grad[at_rows, :] += lax.dot_general(
                low, w_in[:, at], over_inner, preferred_element_type=F32
            )
            return picked + jnp.sum(value * act_grad, axis=1, keepdims=True)

        picked = lax.fori_loop(0, tiles, inward, jnp.zeros((high, 1), F32))
        logit_grad = (picked * (mine - probs)).astype(BF16)
        logit_grads[at_rows, :] = logit_grad
        whole = row_grad[at_rows, :] + jnp.dot(logit_grad, router[...], preferred_element_type=F32)
        back[places] = whole.astype(BF16).reshape(many, slots, width)

        def give_back(place, carry):
            @pl.when(place != me)
            def _():
                returning.copy_to(place).start()

            @pl.when(place == me)
            def _():
                home[me] = back[me]

            return carry

        lax.fori_loop(first, first + many, give_back, 0)

    router_grad = lax.dot_general(
        logit_grads[...],
        got[...].reshape(total, width),
        (((0,), (0,)), ((), ())),
        preferred_element_type=F32,
    )
    router_grad_ref[...] = router_grad[:count]
    rows[...] = jnp.zeros(rows.shape, F32)

    def stores(t):
        at = pl.ds(pl.multiple_of(t * tile, tile), tile)
        return (
            pltpu.make_async_copy(in_grad.at[:, at], in_grad_hbm.at[:, at], store_sems.at[0, t]),
            pltpu.make_async_copy(out_grad.at[at], out_grad_hbm.at[at], store_sems.at[1, t]),
        )

    def outward(t, carry):
        at = pl.ds(pl.multiple_of(t * tile, tile), tile)
        over_rows = (((0,), (0,)), ((), ()))
        in_grad[:, at] = lax.dot_general(
            got[...].reshape(total, width), hid_grad[:, at], over_rows, preferred_element_type=F32
        ).astype(BF16)
        out_grad[at, :] = lax.dot_general(
            active[:, at], slot_grad[...], over_rows, preferred_element_type=F32
        ).astype(BF16)
        for store in stores(t):
            store.start()
        rows[...] += jnp.dot(active[:, at], w_out[at, :], preferred_element_type=F32)
        return carry

    lax.fori_loop(0, tiles, outward, 0)
    result_ref[...] = (gates[:, :1] * rows[...]).astype(BF16).reshape(count, slots, width)
    returning.wait_others()
    for k in range(1, count):
        there.copy(k).wait_send()
    slot_id = lax.broadcasted_iota(jnp.int32, (tokens, total), 1)
    chosen = (slot_id == col_ref[...]).astype(F32).astype(BF16)
    grad_ref[...] = jnp.dot(
        chosen, home[...].reshape(total, width), preferred_element_type=F32
    )
    for t in range(tiles):
        for store in stores(t):
            store.wait()


def run_experts(
    normed, row, col, router, upstream, expert_in, expert_out, slots, collective_id
):
    tokens, width = normed.shape
    count = lax.axis_size("expert")
    hidden = expert_in.shape[2]
    tile = FF_TILE if hidden % FF_TILE == 0 else hidden
    total = count * slots
    exchanged = (count, slots, width)
    vmem = pl.BlockSpec(memory_space=pltpu.VMEM)
    hbm = pl.BlockSpec(memory_space=pl.ANY)
    grad, result, in_grad, out_grad, router_grad = pl.pallas_call(
        functools.partial(experts_kernel, slots, tile),
        out_shape=[
            jax.ShapeDtypeStruct((tokens, width), F32),
            jax.ShapeDtypeStruct(exchanged, BF16),
            jax.ShapeDtypeStruct((width, hidden), BF16),
            jax.ShapeDtypeStruct((hidden, width), BF16),
            jax.ShapeDtypeStruct(router.shape, F32),
        ],
        in_specs=[vmem] * 5 + [hbm] * 2,
        out_specs=[vmem, vmem, hbm, hbm, vmem],
        scratch_shapes=[
            pltpu.VMEM((width, hidden), BF16),
            pltpu.VMEM((hidden, width), BF16),
            pltpu.VMEM(exchanged, BF16),
            pltpu.VMEM(exchanged, BF16),
            pltpu.VMEM(exchanged, BF16),
            pltpu.VMEM((total, width), BF16),
            pltpu.VMEM((total, hidden), BF16),
            pltpu.VMEM((total, hidden), BF16),
            pltpu.VMEM((total, width), F32),
            pltpu.VMEM((width, hidden), BF16),
            pltpu.VMEM((hidden, width), BF16),
            Side.scratch(count),
            Side.scratch(count),
            pltpu.SemaphoreType.DMA((2,)),
            pltpu.SemaphoreType.DMA((2, hidden // tile)),
            pltpu.VMEM((LANES, width), BF16),
            pltpu.VMEM((total, LANES), F32),
            pltpu.VMEM((total, LANES), BF16),
            pltpu.VMEM(exchanged, BF16),
        ],
        compiler_params=params(collective_id=collective_id, has_side_effects=True),
        name="experts",
    )(normed, row, col, router, upstream, expert_in, expert_out)
    return grad, result, in_grad, out_grad, router_grad


def in_segments(value_ref, turn):
    steps = value_ref.shape[0] // SEGS
    parts = []
    for lane in range(turn.shape[0]):
        lanes = slice(lane * LANES, (lane + 1) * LANES)
        for s in range(SEGS):
            rows = value_ref[s * steps : (s + 1) * steps, lanes].astype(F32)
            turn[lane, pl.ds(s, steps, stride=SEGS), :] = rows
        parts.append(turn[lane].astype(BF16))
    return jnp.concatenate(parts, axis=1)


def over_blocks(width, size, body):
    def one(n, carry):
        body(pl.ds(pl.multiple_of(n * size, size), size))
        return carry

    lax.fori_loop(0, width // size, one, 0)


def slot_targets(route, experts, capacity, slots):
    count = route.shape[1]
    steps = count // SEGS
    high = max(experts, 16)
    onehot = lax.broadcasted_iota(jnp.int32, (high, count), 0) == route
    onehot = onehot.astype(F32)
    token_of = lambda p: (p % SEGS) * steps + p // SEGS
    first = token_of(lax.broadcasted_iota(jnp.int32, (count, count), 0))
    second = token_of(lax.broadcasted_iota(jnp.int32, (count, count), 1))
    earlier = (first <= second).astype(F32).astype(BF16)
    running = jnp.dot(onehot.astype(BF16), earlier, preferred_element_type=F32)
    place = (jnp.sum(running * onehot, axis=0, keepdims=True) - 1.0).astype(jnp.int32)
    return jnp.where(place < capacity, route * slots + place, -1)


def forward_kernel(sizes, *refs):
    states, steps, rank, capacity = sizes
    tokens_hbm, upstream_hbm, in_proj_hbm, out_proj_hbm = refs[:4]
    route_ref, gain_ref, gain_two_ref, conv_ref, bias_ref, x_proj_ref, dt_proj_ref = refs[4:11]
    dt_bias_ref, skip_ref, rate_log_ref = refs[11:14]
    ssm_ref, held_ref, gated_ref, hidden_ref, normed_two_ref, row_ref, col_ref, before_ref = refs[14:22]
    side_out = refs[22]
    kept_hbm, spread_hbm, refs = refs[23:32], refs[32:34], refs[34:]
    tokens_in, upstream_in, in_proj, out_proj, turn, ext_in, tail, sent = refs[:8]
    kept, refs = refs[8:17], refs[17:]
    tokens, upstream, normed, inner, gate_z, mixed, pre, delta, proj = kept
    in_s, bb, cb, run_a, run_b, side_sems, load_sems, keep_sems, halo_sems = refs[:9]
    x_proj, dt_proj, small, before, carry_refs = *refs[9:13], refs[13:]
    phase, block = pl.program_id(0), pl.program_id(1)
    blocks = carry_refs[2].shape[1]
    carries = Carries(states, blocks, True, *carry_refs)
    side = Side(sent, side_out, side_sems)
    parts = ((0, 2 / 7), (2 / 7, 3 / 7), (3 / 7, 1))
    rate2 = -jnp.exp(rate_log_ref[...]) * LOG2E
    rates = [over_sublanes(rate2[n : n + 1, :]) for n in range(states)]
    here = pl.ds(pl.multiple_of(block * LANES, LANES), LANES)
    count, width = tokens.shape
    inner_width = inner.shape[1]
    reach = conv_ref.shape[0] - 1
    rim = reach * SEGS
    experts, me = lax.axis_size("expert"), lax.axis_index("expert")
    slots = sent.shape[1]
    half = inner_width
    loads = [
        pltpu.make_async_copy(src, dst, load_sems.at[i])
        for i, (src, dst) in enumerate(
            (
                (tokens_hbm.at[0], tokens_in),
                (in_proj_hbm.at[:, :half], in_proj.at[:, :half]),
                (in_proj_hbm.at[:, half:], in_proj.at[:, half:]),
                (upstream_hbm.at[0], upstream_in),
                (out_proj_hbm, out_proj),
            )
        )
    ]
    keeps = [
        pltpu.make_async_copy(src, dst, keep_sems.at[i])
        for i, (src, dst) in enumerate(zip((*kept, bb, cb), (*kept_hbm, *spread_hbm)))
    ]

    def front():
        for load in loads:
            load.start()
        small[0:1, :] = as_row(skip_ref)
        small[1:2, :] = as_row(bias_ref)
        small[2:3, :] = as_row(dt_bias_ref)
        x_proj[...] = padded_rows(x_proj_ref, LANES)
        dt_proj[...] = padded_rows(dt_proj_ref, LANES)
        loads[0].wait()
        tokens[...] = in_segments(tokens_in, turn)
        normed[...] = rms(tokens[...].astype(F32), as_row(gain_ref)).astype(BF16)
        loads[1].wait()

        def to_inner(at):
            inner[:, at] = jnp.dot(
                normed[...], in_proj[:, at], preferred_element_type=F32
            ).astype(BF16)

        over_blocks(inner_width, 4 * LANES, to_inner)
        last = inner[count - rim - rim % 16 :, :].astype(F32)[rim % 16 :]
        for k in range(reach):
            tail[k : k + 1, :] = last[(k + 1) * SEGS - 1 : (k + 1) * SEGS]
        greet_experts()
        halo = pltpu.make_async_remote_copy(
            src_ref=tail,
            dst_ref=before,
            send_sem=halo_sems.at[0],
            recv_sem=halo_sems.at[1],
            device_id=(lax.axis_index("batch"), lax.rem(me + 1, experts)),
            device_id_type=MESH,
        )

        @pl.when(me < experts - 1)
        def _():
            halo.start()

        @pl.when(me == 0)
        def _():
            before[...] = jnp.zeros(before.shape, F32)

        loads[2].wait()

        def to_gate(at):
            lanes = pl.ds(pl.multiple_of(half + at.start, LANES), at.size)
            gate_z[:, at] = jnp.dot(normed[...], in_proj[:, lanes], preferred_element_type=F32)

        over_blocks(inner_width, 4 * LANES, to_gate)
        for keep in keeps[2:5]:
            keep.start()
        keeps[0].start()
        loads[3].wait()
        upstream[...] = in_segments(upstream_in, turn)
        keeps[1].start()
        target = slot_targets(route_ref[...], experts, capacity, slots)
        row_ref[...] = target
        wide = jnp.broadcast_to(target.astype(F32), (SEGS, count))
        col_ref[...] = jnp.transpose(wide)[:, :1].astype(jnp.int32)
        slot_id = lax.broadcasted_iota(jnp.int32, (slots, count), 0)

        def dispatch(e, carry):
            picked = (slot_id + e * slots == row_ref[...]).astype(F32).astype(BF16)
            sent[e] = jnp.dot(picked, upstream[...], preferred_element_type=F32).astype(BF16)
            return carry

        lax.fori_loop(0, experts, dispatch, 0)
        side.start(0, parts)

        @pl.when(me < experts - 1)
        def _():
            halo.wait_send()

        @pl.when(me > 0)
        def _():
            halo.wait_recv()

        before_ref[...] = before[...]

        def to_mixed(at):
            own = inner[:, at].astype(F32)
            for k in range(reach):
                tile = own[count - rim + k * SEGS : count - rim + (k + 1) * SEGS]
                ext_in[k * SEGS : (k + 1) * SEGS, at] = shifted_in(
                    tile, before[k : k + 1, at], True
                )
            ext_in[rim:, at] = own
            total = jnp.broadcast_to(small[1:2, at], own.shape)
            for k in range(reach + 1):
                total = total + conv_ref[k : k + 1, at] * ext_in[k * SEGS : k * SEGS + count, at]
            mixed[:, at] = silu(total).astype(BF16)

        over_blocks(inner_width, 2 * LANES, to_mixed)
        keeps[5].start()
        proj[...] = lax.dot_general(
            mixed[...], x_proj[...], (((1,), (1,)), ((), ())), preferred_element_type=F32
        )
        keeps[8].start()

        def to_delta(at):
            own = jnp.dot(
                proj[...].astype(BF16), dt_proj[:, at], preferred_element_type=F32
            )
            own = own + small[2:3, at]
            pre[:, at] = own
            delta[:, at] = softplus(own)

        over_blocks(inner_width, 2 * LANES, to_delta)
        keeps[6].start()
        keeps[7].start()

    @pl.when((phase == 0) & (block == 0))
    def _():
        front()

    for part, (at_phase, at_block) in enumerate(((0, blocks // 2), (1, 1))):

        @pl.when((phase == at_phase) & (block == at_block))
        def _():
            side.start(part + 1, parts)

    @pl.when((phase == 0) & (block == 1))
    def _():
        for keep in keeps[9:]:
            keep.start()

    def ends(first):
        in_s[...] = delta[:, here] * mixed[:, here].astype(F32)
        sums = jnp.sum(delta[:, here].reshape(steps, SEGS, LANES), axis=0)

        def one(j, held):
            rows = tile_rows(j)
            d, u = delta[rows, here], in_s[rows, :]
            tile = proj[rows, :] if first else None
            new = []
            for n in range(states):
                if first:
                    b = over_lanes(tile[:, rank + n : rank + n + 1])
                    bb[j, n] = b
                    cb[j, n] = over_lanes(tile[:, rank + states + n : rank + states + n + 1])
                else:
                    b = bb[j, n]
                new.append(jnp.exp2(d * rates[n]) * held[n] + u * b)
            return tuple(new)

        zero = jnp.zeros((SEGS, LANES), F32)
        held = lax.fori_loop(0, steps, one, (zero,) * states, unroll=4)
        carries.put(block, held, sums, rates, run_a, run_b)

    @pl.when((phase == 0) & (block == 0))
    def _():
        ends(True)

    @pl.when((phase == 0) & (block > 0))
    def _():
        ends(False)

    @pl.when(phase == 1)
    def _():
        carries.await_group(block)
        start = carries.starts(block, rate2, run_a, run_b)
        own = mixed[:, here].astype(F32)
        in_s[...] = delta[:, here] * own
        ssm_ref[...] = small[0:1, here] * own
        for n in range(states):
            held_ref[0, 0, n] = start[n]

        def one(j, held):
            rows = tile_rows(j)
            d, u = delta[rows, here], in_s[rows, :]
            total = ssm_ref[rows, :]
            new = []
            for n in range(states):
                h = jnp.exp2(d * rates[n]) * held[n] + u * bb[j, n]
                held_ref[0, j + 1, n] = h
                total = total + cb[j, n] * h
                new.append(h)
            ssm_ref[rows, :] = total
            return tuple(new)

        lax.fori_loop(0, steps, one, tuple(start), unroll=4)
        gated_ref[:, here] = (ssm_ref[...] * silu(gate_z[:, here])).astype(BF16)

    @pl.when((phase == 1) & (block == blocks - 1))
    def _():
        loads[4].wait()
        hidden = tokens[...].astype(F32) + jnp.dot(
            gated_ref[...], out_proj[...], preferred_element_type=F32
        )
        hidden_ref[...] = hidden
        normed_two_ref[...] = rms(hidden, as_row(gain_two_ref)).astype(BF16)
        side.wait()
        for keep in keeps:
            keep.wait()


def forward(
    tokens,
    upstream,
    in_proj,
    out_proj,
    route,
    gain_one,
    gain_two,
    conv_weight,
    conv_bias,
    x_proj,
    dt_proj,
    dt_bias,
    skip,
    rate_log,
    sizes,
    collective_id,
):
    rank, capacity, slots = sizes
    count, width = tokens.shape[1:]
    inner_width = out_proj.shape[0]
    states, steps, blocks = rate_log.shape[0], count // SEGS, inner_width // LANES
    experts = lax.axis_size("expert")
    rim = (conv_weight.shape[0] - 1) * SEGS
    vmem, hbm = (pl.BlockSpec(memory_space=m) for m in (pltpu.VMEM, pl.ANY))
    spread = pltpu.VMEM((steps, states, SEGS, LANES), F32)
    run = pltpu.VMEM((blocks, states, SEGS, LANES), F32)
    whole = lambda *shape: pl.BlockSpec(shape, lambda p, c: (0,) * len(shape))
    shape_of = jax.ShapeDtypeStruct
    kept = [
        shape_of((count, width), BF16),
        shape_of((count, width), BF16),
        shape_of((count, width), BF16),
        shape_of((count, inner_width), BF16),
        shape_of((count, inner_width), F32),
        shape_of((count, inner_width), BF16),
        shape_of((count, inner_width), F32),
        shape_of((count, inner_width), F32),
        shape_of((count, LANES), F32),
    ]
    exchanged = (experts, slots, width)
    out = pl.pallas_call(
        functools.partial(forward_kernel, (states, steps, rank, capacity)),
        grid=(2, blocks),
        out_shape=[
            shape_of((count, inner_width), F32),
            shape_of((blocks, steps + 1, states, SEGS, LANES), F32),
            shape_of((count, inner_width), BF16),
            shape_of((count, width), F32),
            shape_of((count, width), BF16),
            shape_of((1, count), jnp.int32),
            shape_of((count, 1), jnp.int32),
            shape_of((SEGS, inner_width), F32),
            shape_of(exchanged, BF16),
        ]
        + kept
        + [shape_of((steps, states, SEGS, LANES), F32)] * 2,
        in_specs=[hbm] * 4
        + [vmem] * 9
        + [pl.BlockSpec((states, LANES), lambda p, c: (0, c))],
        out_specs=[
            pl.BlockSpec((count, LANES), lambda p, c: (0, p * c)),
            pl.BlockSpec((1, steps + 1, states, SEGS, LANES), lambda p, c: (p * c, 0, 0, 0, 0)),
            whole(count, inner_width),
            whole(count, width),
            whole(count, width),
            whole(1, count),
            whole(count, 1),
            vmem,
            hbm,
        ]
        + [hbm] * (len(kept) + 2),
        scratch_shapes=[
            pltpu.VMEM((count, width), BF16),
            pltpu.VMEM((count, width), BF16),
            pltpu.VMEM(in_proj.shape, BF16),
            pltpu.VMEM(out_proj.shape, BF16),
            pltpu.VMEM((width // LANES, count, LANES), F32),
            pltpu.VMEM((count + rim, inner_width), F32),
            pltpu.VMEM((SEGS, inner_width), F32),
            pltpu.VMEM(exchanged, BF16),
        ]
        + [pltpu.VMEM(k.shape, k.dtype) for k in kept]
        + [
            pltpu.VMEM((count, LANES), F32),
            spread,
            spread,
            run,
            run,
            Side.scratch(experts),
            pltpu.SemaphoreType.DMA((5,)),
            pltpu.SemaphoreType.DMA((len(kept) + 2,)),
            pltpu.SemaphoreType.DMA((2,)),
            pltpu.VMEM((LANES, inner_width), BF16),
            pltpu.VMEM((LANES, inner_width), BF16),
            pltpu.VMEM((SEGS, inner_width), F32),
            pltpu.VMEM((SEGS, inner_width), F32),
        ]
        + Carries.scratch(states, blocks, experts),
        compiler_params=params(collective_id=collective_id, has_side_effects=True),
        name="forward",
    )(
        tokens,
        upstream,
        in_proj,
        out_proj,
        route,
        gain_one,
        gain_two,
        conv_weight,
        conv_bias,
        x_proj,
        dt_proj,
        dt_bias,
        skip,
        rate_log,
    )
    return out[:9], out[9:18], out[18:]


def backward_kernel(states, steps, rank, kinds, *refs):
    many = len(kinds)
    expert_hbm, sum_in, refs = refs[:2], refs[2 : 2 + many], refs[2 + many :]
    delta_hbm, g_hbm, in_hbm, pre_hbm, bb_hbm, cb_hbm = refs[:6]
    rate_ref, skip_ref, held_ref, side_in = refs[6:10]
    sum_out, refs = refs[10 : 10 + many], refs[10 + many :]
    pre_grad_ref, mixed_grad_ref, rate_grad_ref, skip_grad_ref, bias_grad_ref = refs[:5]
    bc_grad_ref, side_out = refs[5:7]
    landings, refs = refs[7:9], refs[9:]
    in_s, rate_sum, in_sum, bb, cb, b_acc, c_acc, run_a, run_b, side_sems = refs[:10]
    skip_row, halving_sems, refs = refs[10], refs[11:13], refs[13:]
    delta_ref, g_ref, in_ref, pre_ref, load_sems = refs[:5]
    carry_refs, sum_refs = refs[5:10], refs[10:]
    loads = [
        pltpu.make_async_copy(src, dst, load_sems.at[i])
        for i, (src, dst) in enumerate(
            (
                (delta_hbm, delta_ref),
                (g_hbm, g_ref),
                (cb_hbm, cb),
                (in_hbm, in_ref),
                (pre_hbm, pre_ref),
                (bb_hbm, bb),
            )
        )
    ]
    halvings = [Halving(expert_hbm[i], i == 0, halving_sems[i]) for i in range(2)]
    phase, block = pl.program_id(0), pl.program_id(1)
    here = pl.ds(pl.multiple_of(block * LANES, LANES), LANES)
    blocks = carry_refs[2].shape[1]
    carries = Carries(states, blocks, False, *carry_refs)
    sums = summings(kinds, sum_in, sum_out, sum_refs)
    side = Side(side_in, side_out, side_sems)
    rate2 = -jnp.exp(rate_ref[:, here]) * LOG2E
    rates = [over_sublanes(rate2[n : n + 1, :]) for n in range(states)]
    zero = jnp.zeros((SEGS, LANES), F32)

    @pl.when((phase == 0) & (block == 0))
    def _():
        for load in loads:
            load.start()
        skip_row[...] = as_row(skip_ref)
        greet_others()
        for item in sums:
            item.start(0)
        for halving, landing in zip(halvings, landings):
            for copy in halving.first(landing):
                copy.start()
        for load in loads[:3]:
            load.wait()

    @pl.when((phase == 1) & (block == 0))
    def _():
        for load in loads[3:]:
            load.wait()

    @pl.when((phase == 0) & (block == blocks - 3))
    def _():
        for item in sums:
            if not item.pairs_first:
                item.advance(0)

    @pl.when((phase == 1) & (block == 1))
    def _():
        for item in sums:
            if item.pairs_first:
                item.advance(0)

    @pl.when((phase == 1) & (block == blocks // 2 - 1))
    def _():
        side.start()

    @pl.when(phase == 0)
    def _():
        sums = jnp.sum(delta_ref[:, here].reshape(steps, SEGS, LANES), axis=0)

        def one(i, held):
            j = steps - 1 - i
            d, g = delta_ref[tile_rows(j), here], g_ref[tile_rows(j), here]
            return tuple(
                jnp.exp2(d * rates[n]) * (held[n] + g * cb[j, n]) for n in range(states)
            )

        held = lax.fori_loop(0, steps, one, (zero,) * states, unroll=4)
        carries.put(block, held, sums, rates, run_a, run_b)

    def grads(first, last):
        start = carries.starts(block, rate2, run_a, run_b)
        delta, g = delta_ref[:, here], g_ref[:, here]
        mixed = in_ref[:, here].astype(F32)
        in_s[...] = delta * mixed
        place = lax.broadcasted_iota(jnp.int32, (SEGS, LANES), 1)

        def one(i, carry):
            edge, rate_acc = carry
            j = steps - 1 - i
            rows = tile_rows(j)
            d, u, g = delta_ref[rows, here], in_s[rows, :], g_ref[rows, here]
            by_rate = by_b = sums = zero
            new_edge, new_acc = [], []
            for n in range(states):
                b, c = bb[j, n], cb[j, n]
                q = c * g + edge[n]
                e = jnp.exp2(d * rates[n]) * q
                v = e * held_ref[0, j, n]
                by_rate = by_rate + rates[n] * v
                by_b = by_b + b * q
                to_b = q * u
                to_c = g * held_ref[0, j + 1, n]
                if not first:
                    to_b = b_acc[j, n] + to_b
                    to_c = c_acc[j, n] + to_c
                if last:
                    sums = jnp.where(place == rank + n, jnp.sum(to_b, axis=1, keepdims=True), sums)
                    to_c = jnp.sum(to_c, axis=1, keepdims=True)
                    sums = jnp.where(place == rank + states + n, to_c, sums)
                else:
                    b_acc[j, n] = to_b
                    c_acc[j, n] = to_c
                new_edge.append(e)
                new_acc.append(rate_acc[n] + d * v)
            rate_sum[rows, :] = by_rate
            in_sum[rows, :] = by_b
            if last:
                bc_grad_ref[rows, :] = sums
            return tuple(new_edge), tuple(new_acc)

        _, rate_acc = lax.fori_loop(
            0, steps, one, (tuple(start), (zero,) * states), unroll=4
        )
        for n in range(states):
            rate_grad_ref[n : n + 1, here] = (
                LN2 * rate2[n : n + 1, :] * jnp.sum(rate_acc[n], axis=0, keepdims=True)
            )
        by_b = in_sum[...]
        pre_grad = (LN2 * rate_sum[...] + mixed * by_b) * jax.nn.sigmoid(pre_ref[:, here])
        pre_grad_ref[:, here] = pre_grad.astype(BF16)
        bias_grad_ref[:, here] = jnp.sum(pre_grad, axis=0, keepdims=True)
        mixed_grad_ref[:, here] = delta * by_b + skip_row[:, here] * g
        skip_grad_ref[:, here] = jnp.sum(g * mixed, axis=0, keepdims=True)

    @pl.when(phase == 1)
    def _():
        carries.await_group(block)

    @pl.when((phase == 1) & (block == 0))
    def _():
        grads(True, False)

    @pl.when((phase == 1) & (block > 0) & (block < blocks - 1))
    def _():
        grads(False, False)

    @pl.when((phase == 1) & (block == blocks - 1))
    def _():
        grads(False, True)
        side.wait()
        for item in sums:
            item.wait(1)
            item.add(1)
        for halving, landing in zip(halvings, landings):
            for copy in halving.first(landing):
                copy.wait()


def mixer_grads(
    pre, delta, mixed, ssm_grad, spreads, rate_log, skip, held, beside, experts, rank, items, collective_id
):
    count, width = delta.shape
    states, steps, blocks = rate_log.shape[0], count // SEGS, width // LANES
    spread = pltpu.VMEM((steps, states, SEGS, LANES), F32)
    run = pltpu.VMEM((blocks, states, SEGS, LANES), F32)
    flat = pltpu.VMEM((count, LANES), F32)
    sum_scratch = [item.first_scratch() for item in items]
    kinds = tuple((item.kind(), len(refs)) for item, refs in zip(items, sum_scratch))
    spread_specs = [
        pl.BlockSpec(item.spread_shape().shape, lambda p, c, rank=len(item.spread_shape().shape): (0,) * rank)
        for item in items
    ]
    outs = pl.pallas_call(
        functools.partial(backward_kernel, states, steps, rank, kinds),
        grid=(2, blocks),
        out_shape=[item.spread_shape() for item in items]
        + [
            jax.ShapeDtypeStruct((count, width), BF16),
            jax.ShapeDtypeStruct((count, width), F32),
            jax.ShapeDtypeStruct((states, width), F32),
            jax.ShapeDtypeStruct((1, width), F32),
            jax.ShapeDtypeStruct((1, width), F32),
            jax.ShapeDtypeStruct((count, LANES), F32),
            jax.ShapeDtypeStruct(beside.shape, beside.dtype),
        ]
        + [jax.ShapeDtypeStruct((2, e.shape[0] // 4, e.shape[1]), BF16) for e in experts],
        in_specs=[pl.BlockSpec(memory_space=pl.ANY)] * (2 + len(items))
        + [pl.BlockSpec(memory_space=pl.ANY)] * 6
        + [pl.BlockSpec(memory_space=pltpu.VMEM)] * 2
        + [
            pl.BlockSpec((1, steps + 1, states, SEGS, LANES), lambda p, c: (p * c, 0, 0, 0, 0)),
            pl.BlockSpec(memory_space=pl.ANY),
        ],
        out_specs=spread_specs
        + [pl.BlockSpec(memory_space=pltpu.VMEM)] * 6
        + [pl.BlockSpec(memory_space=pl.ANY)] * 3,
        scratch_shapes=[flat, flat, flat, spread, spread, spread, spread, run, run]
        + [Side.scratch(lax.axis_size("expert")), pltpu.VMEM((1, width), F32)]
        + [pltpu.SemaphoreType.DMA((2, 2))] * 2
        + [pltpu.VMEM((count, width), kind) for kind in (F32, F32, BF16, F32)]
        + [pltpu.SemaphoreType.DMA((6,))]
        + Carries.scratch(states, blocks, lax.axis_size("expert"))
        + [ref for refs in sum_scratch for ref in refs],
        compiler_params=params(collective_id=collective_id, has_side_effects=True),
        name="mixer_grads",
    )(*experts, *(item.local for item in items), delta, ssm_grad, mixed, pre, *spreads, rate_log, skip, held, beside)
    return outs


def shifted_in(tile, row, forward):
    if forward:
        return jnp.concatenate([row, tile[: SEGS - 1]], axis=0)
    return jnp.concatenate([tile[1:], row], axis=0)


def middle_kernel(*refs):
    hidden_ref, grad_ref, upstream_ref, gain_ref, normed_ref = refs[:5]
    gated_ref, ssm_ref, gate_ref, out_proj_ref = refs[5:9]
    hidden_grad_ref, gain_out, ssm_grad_ref, gate_grad_ref, out_local_ref, gate_local_ref = refs[9:15]
    branch = refs[15]

    @pl.when(pl.program_id(0) == 0)
    def _():
        to_hidden, to_gain = rms_back(hidden_ref[...], as_row(gain_ref), grad_ref[...])
        total = upstream_ref[...].astype(F32) + to_hidden
        hidden_grad_ref[...] = total
        branch[...] = total.astype(BF16)
        gain_out[...] = to_gain[None]

    over_rows = (((0,), (0,)), ((), ()))
    out_local_ref[...] = lax.dot_general(
        gated_ref[...], branch[...], over_rows, preferred_element_type=F32
    ).astype(BF16)
    gated_grad = lax.dot_general(
        branch[...], out_proj_ref[...], (((1,), (1,)), ((), ())), preferred_element_type=F32
    )
    gate = gate_ref[...]
    s = jax.nn.sigmoid(gate)
    ssm_grad_ref[...] = gated_grad * (gate * s)
    low = (gated_grad * ssm_ref[...] * (s * (1.0 + gate * (1.0 - s)))).astype(BF16)
    gate_grad_ref[...] = low
    gate_local_ref[...] = lax.dot_general(
        normed_ref[...], low, over_rows, preferred_element_type=F32
    ).astype(BF16)


def middle(hidden, grad, upstream, gain, normed, gated, ssm, gate_z, out_proj):
    count, width = hidden.shape
    inner_width = out_proj.shape[0]
    wide = 2 * LANES
    vmem = pl.BlockSpec(memory_space=pltpu.VMEM)
    whole = lambda *shape: pl.BlockSpec(shape, lambda c: (0,) * len(shape))
    lanes = lambda rows: pl.BlockSpec((rows, wide), lambda c: (0, c))
    rows = pl.BlockSpec((wide, width), lambda c: (c, 0))
    shape_of = jax.ShapeDtypeStruct
    return pl.pallas_call(
        middle_kernel,
        grid=(inner_width // wide,),
        out_shape=[
            shape_of((count, width), F32),
            shape_of((1, width), F32),
            shape_of((count, inner_width), F32),
            shape_of((count, inner_width), BF16),
            shape_of((inner_width, width), BF16),
            shape_of((width, inner_width), BF16),
        ],
        in_specs=[vmem] * 5 + [lanes(count)] * 3 + [rows],
        out_specs=[whole(count, width), whole(1, width), lanes(count), lanes(count), rows]
        + [lanes(width)],
        scratch_shapes=[pltpu.VMEM((count, width), BF16)],
        compiler_params=params(),
        name="middle",
    )(hidden, grad, upstream, gain, normed, gated, ssm, gate_z, out_proj)


WIDE = 2 * LANES


def put_by_token(out_ref, value, turn):
    steps = value.shape[0] // SEGS
    for lane in range(turn.shape[0]):
        lanes = slice(lane * LANES, (lane + 1) * LANES)
        turn[lane] = value[:, lanes]
        for s in range(SEGS):
            rows = turn[lane, pl.ds(s, steps, stride=SEGS), :]
            out_ref[s * steps : (s + 1) * steps, lanes] = rows.astype(out_ref.dtype)


def tile_places(pack, flat):
    _, pairs, each = pack.shape[:3]
    across = flat.shape[1] // LANES
    for t in range(2 * pairs * each):
        row, lane = t // across * 16, t % across * LANES
        inside = (slice(row, row + 16), slice(lane, lane + LANES)) if row < flat.shape[0] else None
        yield (t // (pairs * each), t // each % pairs, t % each), inside


def put_tiles(pack, flat):
    for tile, inside in tile_places(pack, flat):
        if inside is None:
            pack[tile] = jnp.zeros((16, LANES), BF16)
        else:
            pack[tile] = flat[inside].astype(BF16)


def get_tiles(flat, pack):
    for tile, inside in tile_places(pack, flat):
        if inside is not None:
            flat[inside] = pack[tile].astype(F32)


def finish_kernel(rank, states, kinds, *refs):
    loads_hbm, expert_hbm, landed_hbm, refs = refs[:11], refs[11:13], refs[13:15], refs[15:]
    bc_grad_ref, low_ref, x_proj_ref, dt_proj_ref, conv_ref, bias_ref = refs[:6]
    before_ref, gain_ref, rate_ref, dt_bias_ref, skip_ref, gain_two_ref, router_ref = refs[6:13]
    col_ref, gate_spread, out_spread = refs[13:16]
    output_ref, tokens_grad_ref, in_proj_out, out_proj_out, flat, last_flat = refs[16:22]
    second_hbm, refs = refs[22:24], refs[24:]
    halving_refs, halving_sems, refs = refs[:4], refs[4:8], refs[8:]
    halvings = [Halving(expert_hbm[i], i == 0, halving_sems[i]) for i in range(2)]
    loaded, refs = refs[:11], refs[11:]
    pre_grad, mixed_part, mixed, inner, normed, in_proj, gate_grad, tokens, hidden_grad = loaded[:9]
    hidden, home = loaded[9:]
    ext_in, ext_grad, inner_grad, proj_grad, rows, head, after = refs[:7]
    turn, load_sems, halo_sems = refs[7:10]
    small, last_small = SmallSum(*refs[10:17]), TinySum(*refs[17:23])
    x_proj, dt_proj, bias_row = refs[23:26]
    parts, refs = len(kinds) - 2, refs[26:]
    locals_, sum_refs = refs[:parts], refs[parts:]
    count, width = tokens.shape
    inner_width = inner.shape[1]
    reach = conv_ref.shape[0] - 1
    rim = reach * SEGS
    experts, me = lax.axis_size("expert"), lax.axis_index("expert")
    group = lax.axis_index("batch")
    half = inner_width

    loads = [
        pltpu.make_async_copy(src, dst, load_sems.at[i])
        for i, (src, dst) in enumerate(zip(loads_hbm, loaded))
    ]
    halving_loads = []
    for i, halving in enumerate(halvings):
        for k, src in enumerate((halving.chunk(halving.far), landed_hbm[i].at[1])):
            halving_loads.append(
                pltpu.make_async_copy(src, halving_refs[2 * i + k], halving_sems[2 + i].at[k])
            )
    for load in loads[:1] + halving_loads + loads[1:]:
        load.start()
    ends = [0]
    for ref in locals_:
        ends.append(ends[-1] + ref.shape[2])
    inner_rows = [slice(ends[i], ends[i + 1]) for i in range(parts)]
    gate_sum, out_sum, *inner_sums = summings(
        kinds,
        (gate_spread, out_spread, *locals_),
        (in_proj_out.at[:, half:], out_proj_out)
        + tuple(in_proj_out.at[at, :half] for at in inner_rows),
        sum_refs,
    )
    greet_others()
    gate_sum.begin()
    out_sum.begin()
    x_proj[...] = padded_rows(x_proj_ref, LANES)
    dt_proj[...] = padded_rows(dt_proj_ref, LANES)
    bias_row[...] = as_row(bias_ref)
    low = low_ref[...].astype(BF16)
    flat[...] = jnp.zeros(flat.shape, F32)
    last_flat[...] = jnp.zeros(last_flat.shape, F32)
    last_small.total[...] = jnp.zeros(last_small.total.shape, F32)

    seconds = []
    for i, halving in enumerate(halvings):
        own, brought = halving_refs[2 * i : 2 * i + 2]
        for load in halving_loads[2 * i : 2 * i + 2]:
            load.wait()

        def join(n, carry, own=own, brought=brought):
            at = pl.ds(pl.multiple_of(n * 16, 16), 16)
            own[at, :] = together(own[at, :], brought[at, :]).astype(BF16)
            return carry

        lax.fori_loop(0, own.shape[0] // 16, join, 0)
        seconds.append(halving.second(own, second_hbm[i]))
        seconds[i].start()

    loads[0].wait()
    over_inner = (((1,), (1,)), ((), ()))
    over_rows = (((0,), (0,)), ((), ()))
    low_grad = lax.dot_general(
        pre_grad[...], dt_proj[...], over_inner, preferred_element_type=F32
    )
    proj_grad[...] = (low_grad + bc_grad_ref[...]).astype(BF16)

    for load in loads[1:4]:
        load.wait()

    def before_silu(at):
        own = inner[:, at].astype(F32)
        for k in range(reach):
            tile = own[count - rim + k * SEGS : count - rim + (k + 1) * SEGS]
            ext_in[k * SEGS : (k + 1) * SEGS, at] = shifted_in(tile, before_ref[k : k + 1, at], True)
        ext_in[rim:, at] = own
        total = jnp.dot(proj_grad[...], x_proj[:, at], preferred_element_type=F32)
        total = total + mixed_part[:, at]
        conv_pre = jnp.broadcast_to(bias_row[:, at], total.shape)
        for k in range(reach + 1):
            conv_pre = conv_pre + conv_ref[k : k + 1, at] * ext_in[k * SEGS : k * SEGS + count, at]
        total = total * silu_slope(conv_pre)
        ext_grad[:count, at] = total
        for k in range(reach):
            head[k : k + 1, at] = total[k * SEGS : k * SEGS + 1]

    over_blocks(inner_width, WIDE, before_silu)
    halo = pltpu.make_async_remote_copy(
        src_ref=head,
        dst_ref=after,
        send_sem=halo_sems.at[0],
        recv_sem=halo_sems.at[1],
        device_id=(group, lax.rem(me + experts - 1, experts)),
        device_id_type=MESH,
    )

    @pl.when(me > 0)
    def _():
        halo.start()

    @pl.when(me == experts - 1)
    def _():
        after[...] = jnp.zeros(after.shape, F32)

    at_dt = rank + 2 * states
    x_local = lax.dot_general(proj_grad[...], mixed[...], over_rows, preferred_element_type=F32)
    flat[:at_dt, :] = x_local[:at_dt]
    dt_local = lax.dot_general(low, pre_grad[...], over_rows, preferred_element_type=F32)
    flat[at_dt : at_dt + rank, :] = dt_local[:rank]
    at = at_dt + rank + states
    flat[at_dt + rank : at, :] = rate_ref[...]
    flat[at : at + 1, :] = dt_bias_ref[...]
    flat[at + 1 : at + 2, :] = skip_ref[...]
    flat[at + 2 : at + 3, :width] = gain_two_ref[...]
    fold = router_ref.shape[0] // 2
    flat[at + 3 : at + 3 + fold, :width] = router_ref[:fold, :]
    flat[at + 3 : at + 3 + fold, width:] = router_ref[fold:, :]
    put_tiles(small.pack, flat)
    small.start(0)
    for load in loads[4:7]:
        load.wait()
    rows[...] = lax.dot_general(
        gate_grad[...], in_proj[:, half:], over_inner, preferred_element_type=F32
    )

    @pl.when(me > 0)
    def _():
        halo.wait_send()

    @pl.when(me < experts - 1)
    def _():
        halo.wait_recv()

    def before_taps(at):
        for k in range(reach):
            tile = ext_grad[k * SEGS : (k + 1) * SEGS, at]
            ext_grad[count + k * SEGS : count + (k + 1) * SEGS, at] = shifted_in(
                tile, after[k : k + 1, at], False
            )
        total = conv_ref[0:1, at] * ext_grad[rim : rim + count, at]
        for k in range(1, reach + 1):
            first = (reach - k) * SEGS
            total = total + conv_ref[k : k + 1, at] * ext_grad[first : first + count, at]
        inner_grad[:, at] = total.astype(BF16)

    over_blocks(inner_width, WIDE, before_taps)
    chunk = width // experts
    share = inner_width // lax.axis_size("batch")

    def to_in_proj(at):
        total = lax.dot_general(
            normed[...], inner_grad[:, at], over_rows, preferred_element_type=F32
        ).astype(BF16)
        for e in range(experts):
            own = total[e * chunk : (e + 1) * chunk]
            for ref, rows_at in zip(locals_, inner_rows):
                ref[e // 2, e % 2, :, at] = own[rows_at]

    over_blocks(inner_width, share, to_in_proj)
    for item in inner_sums:
        item.begin()
    small.advance(0)


    def to_taps(at):
        grad = ext_grad[:count, at]
        for k in range(reach + 1):
            last_flat[k : k + 1, at] = jnp.sum(
                grad * ext_in[k * SEGS : k * SEGS + count, at], axis=0, keepdims=True
            )
        last_flat[reach + 1 : reach + 2, at] = jnp.sum(grad, axis=0, keepdims=True)

    for item in inner_sums:
        item.advance(0)
    over_blocks(inner_width, WIDE, to_taps)
    for load in loads[7:]:
        load.wait()
    grad = rows[...] + lax.dot_general(
        inner_grad[...], in_proj[:, :half], over_inner, preferred_element_type=F32
    )
    values = tokens[...].astype(F32)
    to_values, to_gain = rms_back(values, as_row(gain_ref), grad)
    put_by_token(tokens_grad_ref, to_values + hidden_grad[...], turn)

    last_flat[reach + 2 : reach + 3, :width] = to_gain[None]
    across = inner_width // LANES
    for t in range((reach + 3) * across):
        row, lane = t // across, t % across * LANES
        last_small.total[t : t + 1, :] = last_flat[row : row + 1, lane : lane + LANES]
    last_small.pack[...] = last_small.total[...].astype(BF16)
    last_small.start(0)
    gate_sum.advance(2)
    out_sum.advance(2)
    small.advance(1)
    last_small.advance(0)
    for item in inner_sums:
        item.advance(1)
    last_small.advance(1)
    small.advance(2)

    slots = home.shape[1]
    slot_id = lax.broadcasted_iota(jnp.int32, (count, experts * slots), 1)
    chosen = (slot_id == col_ref[...]).astype(F32).astype(BF16)
    returned = jnp.dot(
        chosen, home[...].reshape(experts * slots, width), preferred_element_type=F32
    )
    put_by_token(output_ref, hidden[...] + returned, turn)

    last_small.advance(2)
    gate_sum.advance(3)
    out_sum.advance(3)
    for item in inner_sums:
        item.advance(2)
    small.advance(3)
    small.advance(4)
    get_tiles(flat, small.every)
    for item in inner_sums:
        item.advance(3)
    for t in range((reach + 3) * across):
        row, lane = t // across, t % across * LANES
        last_flat[row : row + 1, lane : lane + LANES] = last_small.total[t : t + 1, :]
    for copy in seconds:
        copy.wait()


def finish(loaded, experts, landed, small, early, rank, states, collective_id):
    pre_grad, in_proj, tokens = loaded[0], loaded[5], loaded[7]
    conv_weight, router_local = small[4], small[12]
    count, inner_width = pre_grad.shape
    width = tokens.shape[1]
    count_experts, ways = lax.axis_size("expert"), lax.axis_size("batch")
    pairs, chunk = count_experts // 2, width // count_experts
    chunks = [(e.shape[0] // 4, e.shape[1]) for e in experts]
    taps = conv_weight.shape[0]
    vmem, hbm = (pl.BlockSpec(memory_space=m) for m in (pltpu.VMEM, pl.ANY))
    split = (chunk // 3, chunk * 2 // 3) if chunk % 48 == 0 else (chunk,)
    locals_ = [jax.ShapeDtypeStruct((pairs, 2, part, inner_width), BF16) for part in split]
    items = early + [Total(local, 1, i == 1) for i, local in enumerate(locals_)]
    scratch = [item.scratch() for item in items]
    kinds = tuple((item.kind(), len(refs)) for item, refs in zip(items, scratch))
    used = 2 * rank + 3 * states + 3 + router_local.shape[0] // 2
    high, low = (-(-rows // 16) * 16 for rows in (used, taps + 2))
    tiles = [-(-(rows // 16 * inner_width // LANES) // (2 * pairs)) for rows in (high, low)]
    f32 = lambda *shape: jax.ShapeDtypeStruct(shape, F32)
    halo = pltpu.VMEM((SEGS, inner_width), F32)
    rim = (taps - 1) * SEGS
    return pl.pallas_call(
        functools.partial(finish_kernel, rank, states, kinds),
        out_shape=[
            jax.ShapeDtypeStruct((count, width), BF16),
            f32(count, width),
            jax.ShapeDtypeStruct((chunk, 2 * inner_width), BF16),
            jax.ShapeDtypeStruct(early[1].chunk, BF16),
            f32(high, inner_width),
            f32(low, inner_width),
        ]
        + [jax.ShapeDtypeStruct(shape, BF16) for shape in chunks],
        in_specs=[hbm] * (len(loaded) + 4) + [vmem] * (len(small) + len(early)),
        out_specs=[vmem] * 6 + [hbm] * 2,
        scratch_shapes=[pltpu.VMEM(shape, BF16) for shape in chunks for _ in range(2)]
        + [pltpu.SemaphoreType.DMA((2, 1))] * 2
        + [pltpu.SemaphoreType.DMA((2,))] * 2
        + [pltpu.VMEM(a.shape, a.dtype) for a in loaded]
        + [
            pltpu.VMEM((count + rim, inner_width), F32),
            pltpu.VMEM((count + rim, inner_width), F32),
            pltpu.VMEM((count, inner_width), BF16),
            pltpu.VMEM((count, LANES), BF16),
            pltpu.VMEM((count, width), F32),
            halo,
            halo,
            pltpu.VMEM((width // LANES, count, LANES), F32),
            pltpu.SemaphoreType.DMA((len(loaded),)),
            pltpu.SemaphoreType.DMA((2,)),
        ]
        + SmallSum.scratch(pairs, ways, tiles[0])
        + TinySum.scratch(pairs, ways, -(-(taps + 2) * inner_width // LANES // 16) * 16)
        + [
            pltpu.VMEM((LANES, inner_width), BF16),
            pltpu.VMEM((LANES, inner_width), BF16),
            pltpu.VMEM((1, inner_width), F32),
        ]
        + [pltpu.VMEM(local.shape, BF16) for local in locals_]
        + [ref for refs in scratch for ref in refs],
        compiler_params=params(collective_id=collective_id, has_side_effects=True),
        name="finish",
    )(*loaded, *experts, *landed, *small, *(item.local for item in early))


def deliver_kernel(*refs):
    output_in, tokens_grad_in, in_proj, out_proj, flat, last = refs[:6]
    expert_hbm, landed_hbm, second_hbm, refs = refs[6:8], refs[8:10], refs[10:12], refs[12:]
    output, tokens_grad, gain, in_proj_out, conv, bias, x_proj, dt_proj, dt_bias, rate = refs[:10]
    skip, out_proj_out, gain_two, router, expert_in_out, expert_out_out = refs[10:16]
    held, sums, sems, store_sems = refs[16:22], refs[22:24], refs[24], refs[25]
    stores = [
        pltpu.make_async_copy(src, dst.at[0], store_sems.at[i])
        for i, (src, dst) in enumerate(
            (
                (output_in, output),
                (tokens_grad_in, tokens_grad),
                (sums[0], expert_in_out),
                (sums[1], expert_out_out),
            )
        )
    ]
    loads = []
    for i in range(2):
        halving = Halving(expert_hbm[i], i == 0)
        parts = (halving.chunk(halving.group), landed_hbm[i].at[0], second_hbm[i])
        for k, src in enumerate(parts):
            loads.append(pltpu.make_async_copy(src, held[3 * i + k], sems.at[i, k]))
    for load in loads:
        load.start()
    for store in stores[:2]:
        store.start()
    for i in range(2):
        for load in loads[3 * i : 3 * i + 3]:
            load.wait()
        total = together(*(ref[...] for ref in held[3 * i : 3 * i + 3]))
        sums[i][...] = total.astype(BF16).astype(F32)
        stores[2 + i].start()
    at, width = 0, gain.shape[0]
    for ref in (x_proj, dt_proj, rate):
        ref[...] = flat[at : at + ref.shape[0], :]
        at += ref.shape[0]
    fold = router.shape[0] // 2
    dt_bias[...] = flat[at : at + 1, :].reshape(dt_bias.shape)
    skip[...] = flat[at + 1 : at + 2, :].reshape(skip.shape)
    gain_two[...] = flat[at + 2 : at + 3, :width].reshape(gain_two.shape)
    router[:fold, :] = flat[at + 3 : at + 3 + fold, :width]
    router[fold:, :] = flat[at + 3 : at + 3 + fold, width:]
    taps = conv.shape[0]
    conv[...] = last[:taps, :]
    bias[...] = last[taps : taps + 1, :].reshape(bias.shape)
    gain[...] = last[taps + 1 : taps + 2, :width].reshape(gain.shape)
    in_proj_out[...] = in_proj[...].astype(F32)
    out_proj_out[...] = out_proj[...].astype(F32)
    for store in stores:
        store.wait()


def deliver(made, experts, landed, shapes):
    vmem = pl.BlockSpec(memory_space=pltpu.VMEM)
    hbm = pl.BlockSpec(memory_space=pl.ANY)
    output, tokens_grad, in_proj, out_proj, flat, last = made[:6]
    chunks = [(e.shape[0] // 4, e.shape[1]) for e in experts]
    f32 = lambda *shape: jax.ShapeDtypeStruct(shape, F32)
    outs = [
        jax.ShapeDtypeStruct((1, *output.shape), BF16),
        f32(1, *tokens_grad.shape),
        shapes[0],
        f32(*in_proj.shape),
        *shapes[1:8],
        f32(*out_proj.shape),
        *shapes[8:],
        *(f32(1, *shape) for shape in chunks),
    ]
    return pl.pallas_call(
        deliver_kernel,
        out_shape=outs,
        in_specs=[vmem] * 6 + [hbm] * 6,
        out_specs=[hbm] * 2 + [vmem] * (len(outs) - 4) + [hbm] * 2,
        scratch_shapes=[pltpu.VMEM(shape, BF16) for shape in chunks for _ in range(3)]
        + [pltpu.VMEM(shape, F32) for shape in chunks]
        + [pltpu.SemaphoreType.DMA((2, 3)), pltpu.SemaphoreType.DMA((4,))],
        compiler_params=params(),
        name="deliver",
    )(*made[:6], *experts, *landed, *made[6:])


def silu(v):
    return v * jax.nn.sigmoid(v)


def silu_slope(v):
    s = jax.nn.sigmoid(v)
    return s * (1.0 + v * (1.0 - s))


def rms_back(values, gain, grad):
    r = lax.rsqrt(jnp.mean(values * values, axis=-1, keepdims=True) + 1e-05)
    u = gain * grad
    mean = jnp.mean(values * u, axis=-1, keepdims=True)
    return r * u - values * (r * r * r) * mean, jnp.sum(grad * values * r, axis=0)


def rms(values, gain):
    return values * lax.rsqrt(jnp.mean(values * values, axis=-1, keepdims=True) + 1e-05) * gain


def per_device(
    tokens,
    routes,
    gain_one,
    in_proj,
    conv_weight,
    conv_bias,
    x_proj,
    dt_proj,
    dt_bias,
    rate_log,
    skip,
    out_proj,
    gain_two,
    router,
    expert_in,
    expert_out,
    cotangent,
):
    count, width = tokens.shape[1], tokens.shape[2]
    steps = count // SEGS
    inner_width = out_proj.shape[0]
    rank = dt_proj.shape[0]
    experts = router.shape[0]
    capacity = 5 * count // (4 * experts)
    slots = -(-capacity // 16) * 16
    states = rate_log.shape[0]
    route = routes.reshape(SEGS, steps).T.reshape(1, count)
    made, kept, spreads = forward(
        tokens,
        cotangent,
        in_proj,
        out_proj,
        route,
        gain_one,
        gain_two,
        conv_weight,
        conv_bias,
        x_proj,
        dt_proj,
        dt_bias,
        skip,
        rate_log,
        (rank, capacity, slots),
        2,
    )
    ssm, held, gated, hidden, normed_two, row, col, before, slot_upstream = made
    tokens_low, upstream_low, normed_one, inner, gate_z, mixed, pre, delta, proj = kept

    normed_two_grad, results, *expert_grads, router_local = run_experts(
        normed_two, row, col, router, slot_upstream, expert_in, expert_out, slots, 4
    )

    hidden_grad, gain_two_local, ssm_grad, gate_z_grad, out_proj_local, in_proj_gate_local = middle(
        hidden, normed_two_grad, upstream_low, gain_two, normed_one, gated, ssm, gate_z, out_proj
    )
    ways, pairs = lax.axis_size("batch"), experts // 2
    early = [
        Total(
            in_proj_gate_local.reshape(pairs, 2, width // experts, inner_width),
            1,
        ),
        Total(
            out_proj_local.reshape(
                pairs, 2, ways, inner_width // (experts * ways), width
            ),
            0,
            True,
        ),
    ]
    (
        in_proj_gate_spread,
        out_proj_spread,
        pre_grad,
        mixed_grad,
        rate_log_local,
        skip_local,
        dt_bias_local,
        bc_grad,
        returned,
        *landed,
    ) = mixer_grads(
        pre, delta, mixed, ssm_grad, spreads, rate_log, skip, held, results, expert_grads, rank, early, 3
    )
    early = [early[0].resumed(in_proj_gate_spread), early[1].resumed(out_proj_spread)]
    outs = finish(
        [
            pre_grad,
            mixed_grad,
            mixed,
            inner,
            normed_one,
            in_proj,
            gate_z_grad,
            tokens_low,
            hidden_grad,
            hidden,
            returned,
        ],
        expert_grads,
        landed,
        [
            bc_grad,
            proj,
            x_proj,
            dt_proj,
            conv_weight,
            conv_bias,
            before,
            gain_one,
            rate_log_local,
            dt_bias_local,
            skip_local,
            gain_two_local,
            router_local,
            col,
        ],
        early,
        rank,
        states,
        1,
    )
    outs = (*outs[:3], outs[3].reshape(-1, width), *outs[4:])
    weights = (gain_one, conv_weight, conv_bias, x_proj, dt_proj, dt_bias, rate_log, skip)
    shapes = [jax.ShapeDtypeStruct(w.shape, F32) for w in (*weights, gain_two, router)]
    return tuple(deliver(outs, expert_grads, landed, shapes))


def solution(mesh):
    split = P("batch", "expert", None)
    one = P("expert", None, None)
    both = P("expert", "batch", None)
    in_specs = (split, split) + (P(),) * 12 + (one, one, split)
    out_specs = (split, split, P(), P("expert", None)) + (P(),) * 7
    out_specs += (P("expert", None), P(), P(), both, both)
    return jax.shard_map(
        per_device, mesh=mesh, in_specs=in_specs, out_specs=out_specs, check_vma=False
    )
```

```python
import functools

import jax
import jax.numpy as jnp
from jax import lax
from jax.experimental import pallas as pl
from jax.experimental.pallas import tpu as pltpu
from jax.sharding import PartitionSpec as P

F32, BF16 = jnp.float32, jnp.bfloat16
SEGS = 8
LANES = 128
LOG2E = 1.4426950408889634
LN2 = 0.6931471805599453
VMEM_LIMIT = 60 * 1024 * 1024
MESH = pl.DeviceIdType.MESH


def params(**kw):
    return pltpu.CompilerParams(vmem_limit_bytes=VMEM_LIMIT, **kw)


def softplus(v):
    return jnp.maximum(v, 0.0) + jnp.log1p(jnp.exp(-jnp.abs(v)))


def as_row(ref):
    return ref[...].reshape(1, ref.shape[0])


def padded_rows(ref, high):
    low = jnp.zeros((high - ref.shape[0], ref.shape[1]), F32)
    return jnp.concatenate([ref[...].astype(F32), low], axis=0).astype(BF16)


def over_sublanes(row):
    return jnp.broadcast_to(row, (SEGS, LANES))


def over_lanes(column):
    return jnp.broadcast_to(column, (SEGS, LANES))


def tile_rows(j):
    return pl.ds(pl.multiple_of(j * SEGS, SEGS), SEGS)


def run_of_segments(a, b, forward):
    at = lax.broadcasted_iota(jnp.int32, (SEGS, LANES), 0)
    for step in (1, 2, 4):
        if forward:
            inside, turn = at >= step, step
        else:
            inside, turn = at < SEGS - step, SEGS - step
        before_a = jnp.where(inside, pltpu.roll(a, turn, 0), 1.0)
        before_b = jnp.where(inside, pltpu.roll(b, turn, 0), 0.0)
        a, b = a * before_a, a * before_b + b
    return a, b


class Carries:
    groups = 2

    def __init__(self, states, blocks, forward, own, lengths, got, got_lengths, sems):
        self.states, self.blocks, self.forward = states, blocks, forward
        self.own, self.lengths, self.got, self.got_lengths = own, lengths, got, got_lengths
        self.sems = sems
        self.count, self.me = lax.axis_size("expert"), lax.axis_index("expert")
        self.per = blocks // self.groups

    @staticmethod
    def scratch(states, blocks, count):
        per = blocks // Carries.groups
        assert blocks % Carries.groups == 0 and per <= SEGS
        return [
            pltpu.VMEM((blocks, states, LANES), BF16),
            pltpu.VMEM((Carries.groups, SEGS, LANES), F32),
            pltpu.VMEM((count, blocks, states, LANES), BF16),
            pltpu.VMEM((count, Carries.groups, SEGS, LANES), F32),
            pltpu.SemaphoreType.DMA((2, 2, Carries.groups, count)),
        ]

    def other(self, k):
        return (lax.axis_index("batch"), lax.rem(self.me + k, self.count))

    def copies(self, group):
        blocks = pl.ds(group * self.per, self.per)
        found = []
        for k in range(1, self.count):
            pairs = (
                (self.own.at[blocks], self.got.at[k - 1, blocks]),
                (self.lengths.at[group], self.got_lengths.at[k - 1, group]),
            )
            for i, (src, dst) in enumerate(pairs):
                found.append(
                    pltpu.make_async_remote_copy(
                        src_ref=src,
                        dst_ref=dst,
                        send_sem=self.sems.at[0, i, group, k - 1],
                        recv_sem=self.sems.at[1, i, group, k - 1],
                        device_id=self.other(k),
                        device_id_type=MESH,
                    )
                )
        return found

    def put(self, block, ends, sums, rates, run_a, run_b):
        edge = SEGS - 1 if self.forward else 0
        rows = []
        for n in range(self.states):
            a, b = run_of_segments(jnp.exp2(rates[n] * sums), ends[n], self.forward)
            run_a[block, n] = a
            run_b[block, n] = b
            rows.append(b[edge : edge + 1])
        end = jnp.concatenate(rows, axis=0).astype(BF16)
        total = jnp.sum(sums, axis=0, keepdims=True)
        last = self.count - 1
        self.own[block] = end
        self.got[last, block] = end
        for group in range(self.groups):

            @pl.when(block // self.per == group)
            def _():
                row = pl.ds(lax.rem(block, self.per), 1)
                self.lengths[group, row, :] = total
                self.got_lengths[last, group, row, :] = total

            @pl.when(block == (group + 1) * self.per - 1)
            def _():
                for copy in self.copies(group):
                    copy.start()

    def await_group(self, block):
        for group in range(self.groups):

            @pl.when(block == group * self.per)
            def _():
                for copy in self.copies(group):
                    copy.wait()

    def starts(self, block, rate, run_a, run_b):
        group, row = block // self.per, pl.ds(lax.rem(block, self.per), 1)
        entering = jnp.zeros((self.states, LANES), F32)
        order = range(self.count) if self.forward else range(self.count - 1, -1, -1)
        for place in order:
            slot = lax.rem(self.me - place - 1 + 2 * self.count, self.count)
            length = self.got_lengths[slot, group, row, :]
            joined = jnp.exp2(rate * length) * entering + self.got[slot, block].astype(F32)
            ahead = (place < self.me) if self.forward else (place > self.me)
            entering = jnp.where(ahead, joined, entering)
        found = []
        for n in range(self.states):
            first = entering[n : n + 1]
            after = run_a[block, n] * over_sublanes(first) + run_b[block, n]
            found.append(shifted_in(after, first, self.forward))
        return found


def together(*parts):
    return sum(p.astype(F32) for p in parts)


class Total:
    def __init__(self, local, axis, pairs_first=False, chunk=None):
        self.local, self.axis, self.pairs_first = local, axis, pairs_first
        self.ways = lax.axis_size("batch")
        self.taken_up = chunk is not None
        self.pairs, self.chunk = lax.axis_size("expert") // 2, chunk or local.shape[2:]
        part = list(self.chunk)
        part[axis] //= self.ways
        self.part = tuple(part)

    def kind(self):
        return self.axis, self.pairs_first, self.part, self.taken_up

    def spread_shape(self):
        shape = self.chunk if self.pairs_first else (self.pairs, *self.part)
        return jax.ShapeDtypeStruct(shape, BF16)

    def resumed(self, spread):
        return Total(spread, self.axis, self.pairs_first, self.chunk)

    def first_scratch(self):
        first = (self.pairs - 1, *self.chunk)
        if not self.pairs_first:
            first = (self.ways - 1, self.pairs, *self.part)
        return [
            pltpu.VMEM((2, self.pairs, *self.chunk), BF16),
            pltpu.VMEM((self.pairs, *self.chunk), BF16),
            pltpu.VMEM(first, BF16),
            pltpu.SemaphoreType.DMA((2, 2, max(self.ways, self.pairs))),
        ]

    def second_scratch(self):
        second = self.ways - 1 if self.pairs_first else self.pairs - 1
        return [
            pltpu.VMEM((second, *self.part), BF16),
            pltpu.VMEM(self.part, BF16),
            pltpu.VMEM(self.chunk, BF16),
            pltpu.SemaphoreType.DMA((2, 4, max(self.ways, self.pairs))),
        ]

    def scratch(self):
        if self.taken_up:
            return self.second_scratch()
        spread = self.spread_shape()
        return self.first_scratch() + [pltpu.VMEM(spread.shape, BF16)] + self.second_scratch()


def part_of(ref, lead, axis, size, index):
    start = index * size
    if axis == len(ref.shape) - lead - 1:
        start = pl.multiple_of(start, LANES)
    where = [slice(None)] * len(ref.shape)
    where[lead + axis] = pl.ds(start, size)
    return ref.at[tuple(where)]


class Peers:
    def __init__(self):
        self.ways, self.pairs = lax.axis_size("batch"), lax.axis_size("expert") // 2
        self.group, place = lax.axis_index("batch"), lax.axis_index("expert")
        self.pair, self.core = place // 2, lax.rem(place, 2)
        self.sibling = (self.group, self.pair * 2 + 1 - self.core)
        self.to_batch = [lax.rem(self.group + k, self.ways) for k in range(1, self.ways)]
        self.to_pairs = [lax.rem(self.pair + k, self.pairs) for k in range(1, self.pairs)]
        self.in_batch = [(to, place) for to in self.to_batch]
        self.in_pairs = [(self.group, to * 2 + self.core) for to in self.to_pairs]

    def remote(self, src, dst, sems, stage, k, device):
        return pltpu.make_async_remote_copy(
            src_ref=src,
            dst_ref=dst,
            send_sem=sems.at[0, stage, k],
            recv_sem=sems.at[1, stage, k],
            device_id=device,
            device_id_type=MESH,
        )

    def start(self, stage):
        for copy in self.copies(stage):
            copy.start()

    def wait(self, stage):
        for copy in self.copies(stage):
            copy.wait()

    def advance(self, stage):
        self.wait(stage)
        self.add(stage)
        if stage < self.last:
            self.start(stage + 1)


class Summing(Peers):
    last = 3

    def __init__(self, kind, local, out, scratch):
        super().__init__()
        self.axis, self.pairs_first, part, self.taken_up = kind
        self.local, self.out, self.size = local, out, part[self.axis]
        if self.taken_up:
            self.spread = local
            self.from_second, self.mine, self.every, self.late_sems = scratch
        else:
            self.both, self.by_chip, self.from_first, self.sems = scratch[:4]
            self.spread = out
            if len(scratch) > 4:
                self.spread, self.from_second, self.mine, self.every, self.late_sems = scratch[4:]

    def share(self, ref, lead, index):
        return part_of(ref, lead, self.axis, self.size, index)

    def copies(self, stage):
        if stage == 0:
            own = pltpu.make_async_copy(
                self.local.at[:, self.core], self.both.at[0], self.sems.at[0, 0, 1]
            )
            away = self.local.at[:, 1 - self.core]
            return [own, self.remote(away, self.both.at[1], self.sems, 0, 0, self.sibling)]
        if stage == 3:
            own, devices = self.share(self.every, 0, self.group), self.in_batch
            pieces = [(self.mine, own) for _ in devices]
        elif (stage == 1) == self.pairs_first:
            devices = self.in_pairs
            src, dst = (self.by_chip, self.from_first) if stage == 1 else (self.spread, self.from_second)
            pieces = [(src.at[to], dst.at[k]) for k, to in enumerate(self.to_pairs)]
        else:
            devices = self.in_batch
            src, dst = (self.by_chip, self.from_first) if stage == 1 else (self.spread, self.from_second)
            lead = 1 if stage == 1 else 0
            pieces = [
                (self.share(src, lead, to), dst.at[k]) for k, to in enumerate(self.to_batch)
            ]
        sems = self.sems if stage == 1 else self.late_sems
        return [
            self.remote(src, dst, sems, stage, k, devices[k]) for k, (src, dst) in enumerate(pieces)
        ]

    def add(self, stage):
        if stage == 0:

            def over_cores(z, carry):
                self.by_chip[z] = together(self.both[0, z], self.both[1, z]).astype(BF16)
                return carry

            lax.fori_loop(0, self.pairs, over_cores, 0)
        elif stage == 1 and self.pairs_first:
            others = (self.from_first[k] for k in range(self.pairs - 1))
            self.spread[...] = together(self.by_chip[self.pair], *others).astype(BF16)
        elif stage == 1:
            own = self.share(self.by_chip, 1, self.group)

            def over_batch(z, carry):
                others = (self.from_first[k, z] for k in range(self.ways - 1))
                self.spread[z] = together(own[z], *others).astype(BF16)
                return carry

            lax.fori_loop(0, self.pairs, over_batch, 0)
        elif stage == 2:
            if self.pairs_first:
                own, count = self.share(self.spread, 0, self.group)[...], self.ways
            else:
                own, count = self.spread[self.pair], self.pairs
            others = (self.from_second[k] for k in range(count - 1))
            total = together(own, *others).astype(BF16)
            self.mine[...] = total
            self.share(self.every, 0, self.group)[...] = total
        else:
            self.out[...] = self.every[...].astype(self.out.dtype)

    def begin(self):
        self.start(2 if self.taken_up else 0)


class SmallSum(Peers):
    last = 4

    def __init__(self, pack, from_core, half, from_pairs, by_group, every, sems):
        super().__init__()
        self.pack, self.from_core, self.half, self.from_pairs = pack, from_core, half, from_pairs
        self.by_group, self.every, self.sems = by_group, every, sems

    @staticmethod
    def scratch(pairs, ways, tiles):
        tile = (tiles, 16, LANES)
        shapes = ((2, pairs), (pairs,), (pairs,), (pairs - 1,), (ways,), (2, pairs))
        found = [pltpu.VMEM((*lead, *tile), BF16) for lead in shapes]
        return found + [pltpu.SemaphoreType.DMA((2, 5, max(pairs, ways)))]

    def copies(self, stage):
        if stage == 0:
            pieces = [(self.pack.at[1 - self.core], self.from_core, self.sibling)]
        elif stage == 1:
            pieces = [
                (self.half.at[to], self.from_pairs.at[k], self.in_pairs[k])
                for k, to in enumerate(self.to_pairs)
            ]
        elif stage == 2:
            own = self.by_group.at[self.group]
            pieces = [(own, own, device) for device in self.in_batch]
        elif stage == 3:
            own = self.every.at[self.core, self.pair]
            pieces = [(own, own, device) for device in self.in_pairs]
        else:
            own = self.every.at[self.core]
            pieces = [(own, own, self.sibling)]
        return [
            self.remote(src, dst, self.sems, stage, k, device)
            for k, (src, dst, device) in enumerate(pieces)
        ]

    def add(self, stage):
        if stage == 0:
            self.half[...] = together(self.pack[self.core], self.from_core[...]).astype(BF16)
        elif stage == 1:
            others = (self.from_pairs[k] for k in range(self.pairs - 1))
            self.by_group[self.group] = together(self.half[self.pair], *others).astype(BF16)
        elif stage == 2:
            total = together(*(self.by_group[k] for k in range(self.ways)))
            self.every[self.core, self.pair] = total.astype(BF16)


class TinySum(Peers):
    last = 2

    def __init__(self, pack, from_core, by_pair, by_group, total, sems):
        super().__init__()
        self.pack, self.from_core, self.by_pair = pack, from_core, by_pair
        self.by_group, self.total, self.sems = by_group, total, sems

    @staticmethod
    def scratch(pairs, ways, rows):
        found = [pltpu.VMEM((rows, LANES), BF16)] * 2
        found += [pltpu.VMEM((many, rows, LANES), BF16) for many in (pairs, ways)]
        return found + [pltpu.VMEM((rows, LANES), F32), pltpu.SemaphoreType.DMA((2, 3, max(pairs, ways)))]

    def copies(self, stage):
        if stage == 0:
            pieces = [(self.pack, self.from_core, self.sibling)]
        elif stage == 1:
            own = self.by_pair.at[self.pair]
            pieces = [(own, own, device) for device in self.in_pairs]
        else:
            own = self.by_group.at[self.group]
            pieces = [(own, own, device) for device in self.in_batch]
        return [
            self.remote(src, dst, self.sems, stage, k, device)
            for k, (src, dst, device) in enumerate(pieces)
        ]

    def add(self, stage):
        if stage == 0:
            self.by_pair[self.pair] = together(self.pack[...], self.from_core[...]).astype(BF16)
        elif stage == 1:
            total = together(*(self.by_pair[k] for k in range(self.pairs)))
            self.by_group[self.group] = total.astype(BF16)
        else:
            self.total[...] = together(*(self.by_group[k] for k in range(self.ways)))


def summings(kinds, ins, outs, scratch):
    found, at = [], 0
    for (kind, many), local, out in zip(kinds, ins, outs):
        found.append(Summing(kind, local, out, scratch[at : at + many]))
        at += many
    return found


class Halving:
    def __init__(self, local, x_first, sems=None):
        assert lax.axis_size("batch") == 4
        group, self.place = lax.axis_index("batch"), lax.axis_index("expert")
        by_x = group + 1 - 2 * lax.rem(group, 2)
        by_y = group + 2 - 4 * (group // 2)
        self.local, self.sems, self.group, self.across = local, sems, group, 3 - group
        self.near, self.far = (by_x, by_y) if x_first else (by_y, by_x)
        self.rows = local.shape[0] // 4

    def chunk(self, index):
        return self.local.at[pl.ds(pl.multiple_of(index * self.rows, self.rows), self.rows)]

    def copy(self, src, dst, k, device):
        return pltpu.make_async_remote_copy(
            src_ref=src,
            dst_ref=dst,
            send_sem=self.sems.at[0, k],
            recv_sem=self.sems.at[1, k],
            device_id=(device, self.place),
            device_id_type=MESH,
        )

    def first(self, landing):
        return [
            self.copy(self.chunk(index), landing.at[k], k, self.near)
            for k, index in enumerate((self.near, self.across))
        ]

    def second(self, src, landing):
        return self.copy(src, landing, 0, self.far)


class Side:
    def __init__(self, src, dst, sems):
        self.src, self.dst, self.sems = src, dst, sems
        self.count, self.me = lax.axis_size("expert"), lax.axis_index("expert")

    @staticmethod
    def scratch(count):
        return pltpu.SemaphoreType.DMA((2, count))

    def copy(self, k):
        return self.copy_to(lax.rem(self.me + k, self.count))

    def copy_to(self, to):
        return pltpu.make_async_remote_copy(
            src_ref=self.src.at[to],
            dst_ref=self.dst.at[self.me],
            send_sem=self.sems.at[0, to],
            recv_sem=self.sems.at[1, self.me],
            device_id=(lax.axis_index("batch"), to),
            device_id_type=MESH,
        )

    def brought(self, place):
        return pltpu.make_async_remote_copy(
            src_ref=self.src.at[place],
            dst_ref=self.dst.at[place],
            send_sem=self.sems.at[0, place],
            recv_sem=self.sems.at[1, place],
            device_id=(lax.axis_index("batch"), place),
            device_id_type=MESH,
        )

    def own(self):
        return pltpu.make_async_copy(
            self.src.at[self.me], self.dst.at[self.me], self.sems.at[0, self.me]
        )

    def start(self, part=0, parts=((0, 1),)):
        if part == 0:
            self.own().start()
        least, most = (1 + round(share * (self.count - 1)) for share in parts[part])
        for k in range(least, most):
            self.copy(k).start()

    def wait(self):
        self.own().wait()
        self.wait_others()

    def wait_others(self):
        for k in range(1, self.count):
            place = lax.rem(self.me + k, self.count)
            self.copy_to(place).wait_send()
            self.brought(place).wait_recv()


def greet_others():
    barrier = pltpu.get_barrier_semaphore()
    group, place = lax.axis_index("batch"), lax.axis_index("expert")
    ways, count = lax.axis_size("batch"), lax.axis_size("expert")
    others = [(group, lax.rem(place + k, count)) for k in range(1, count)]
    others += [(lax.rem(group + k, ways), place) for k in range(1, ways)]
    for device in others:
        pl.semaphore_signal(barrier, inc=1, device_id=device, device_id_type=MESH)
    pl.semaphore_wait(barrier, len(others))


def greet_experts():
    barrier = pltpu.get_barrier_semaphore()
    count, me = lax.axis_size("expert"), lax.axis_index("expert")
    for k in range(1, count):
        device = (lax.axis_index("batch"), lax.rem(me + k, count))
        pl.semaphore_signal(barrier, inc=1, device_id=device, device_id_type=MESH)
    pl.semaphore_wait(barrier, count - 1)


def gelu_parts(v):
    size = jnp.abs(v) * 0.7071067811865476
    t = 1.0 / (1.0 + 0.3275911 * size)
    bell = jnp.exp2(v * v * (-0.5 * LOG2E))
    poly = t * (
        0.127414796
        + t * (-0.142248368 + t * (0.7107068705 + t * (-0.7265760135 + t * 0.5307027145)))
    )
    tail = poly * bell
    phi = jnp.where(v >= 0.0, 1.0 - tail, tail)
    return v * phi, phi + v * (bell * 0.3989422804014327)


FF_TILE = 512


def experts_kernel(slots, tile, *refs):
    normed_ref, row_ref, col_ref, router_ref, upstream_ref, in_hbm, out_hbm = refs[:7]
    grad_ref, result_ref, in_grad_hbm, out_grad_hbm, router_grad_ref = refs[7:12]
    w_in, w_out, sent, got, home, slot_grad, active, hid_grad, row_grad = refs[12:21]
    in_grad, out_grad, there_sems, back_sems, load_sems, store_sems, router = refs[21:28]
    gates, logit_grads, back = refs[28:]
    rows = row_grad
    count, me = lax.axis_size("expert"), lax.axis_index("expert")
    width, hidden = w_in.shape
    total = count * slots
    tiles = hidden // tile
    router[...] = padded_rows(router_ref, LANES)
    loads = [
        pltpu.make_async_copy(in_hbm.at[0], w_in, load_sems.at[0]),
        pltpu.make_async_copy(out_hbm.at[0], w_out, load_sems.at[1]),
    ]
    for load in loads:
        load.start()
    greet_experts()
    there = Side(sent, got, there_sems)
    returning = Side(back, home, back_sems)
    tokens = normed_ref.shape[0]
    slot_id = lax.broadcasted_iota(jnp.int32, (slots, tokens), 0)

    upper = me // (count // 2)
    quarter = count // 4
    groups = (
        (upper * 2 * quarter, 2 * quarter),
        ((2 - upper) * quarter, quarter),
        ((3 - 3 * upper) * quarter, quarter),
    )

    def dispatch(to, carry):
        picked = (slot_id + to * slots == row_ref[...]).astype(F32).astype(BF16)
        chunk = jnp.dot(picked, normed_ref[...], preferred_element_type=F32).astype(BF16)
        sent[to] = chunk

        @pl.when(to != me)
        def _():
            there.copy_to(to).start()

        @pl.when(to == me)
        def _():
            got[me] = chunk

        return carry

    for first, many in groups:
        lax.fori_loop(first, first + many, dispatch, 0)
    over_inner = (((1,), (1,)), ((), ()))
    for load in loads:
        load.wait()
    for first, many in groups:

        def arrive(place, carry):
            @pl.when(place != me)
            def _():
                there.brought(place).wait_recv()

            return carry

        lax.fori_loop(first, first + many, arrive, 0)
        high = many * slots
        places = pl.ds(first, many)
        at_rows = pl.ds(pl.multiple_of(first * slots, 16), high)
        x = got[places].reshape(high, width)
        logits = lax.dot_general(x, router[...], over_inner, preferred_element_type=F32)
        lane = lax.broadcasted_iota(jnp.int32, logits.shape, 1)
        logits = jnp.where(lane < count, logits, -1e30)
        scores = jnp.exp(logits - jnp.max(logits, axis=1, keepdims=True))
        probs = scores / jnp.sum(scores, axis=1, keepdims=True)
        mine = (lane == me).astype(F32)
        gate = jnp.sum(probs * mine, axis=1, keepdims=True)
        gates[at_rows, :] = jnp.broadcast_to(gate, (high, LANES))
        upstream = upstream_ref[places].reshape(high, width).astype(F32)
        slot_grad[at_rows, :] = (gate * upstream).astype(BF16)
        row_grad[at_rows, :] = jnp.zeros((high, width), F32)

        def inward(t, picked, x=x, at_rows=at_rows):
            at = pl.ds(pl.multiple_of(t * tile, tile), tile)
            pre = jnp.dot(x, w_in[:, at], preferred_element_type=F32)
            act_grad = lax.dot_general(
                slot_grad[at_rows, :], w_out[at, :], over_inner, preferred_element_type=F32
            )
            value, slope = gelu_parts(pre)
            active[at_rows, at] = value.astype(BF16)
            low = (act_grad * slope).astype(BF16)
            hid_grad[at_rows, at] = low
            row_grad[at_rows, :] += lax.dot_general(
                low, w_in[:, at], over_inner, preferred_element_type=F32
            )
            return picked + jnp.sum(value * act_grad, axis=1, keepdims=True)

        picked = lax.fori_loop(0, tiles, inward, jnp.zeros((high, 1), F32), unroll=2)
        logit_grad = (picked * (mine - probs)).astype(BF16)
        logit_grads[at_rows, :] = logit_grad
        whole = row_grad[at_rows, :] + jnp.dot(logit_grad, router[...], preferred_element_type=F32)
        back[places] = whole.astype(BF16).reshape(many, slots, width)

        def give_back(place, carry):
            @pl.when(place != me)
            def _():
                returning.copy_to(place).start()

            @pl.when(place == me)
            def _():
                home[me] = back[me]

            return carry

        lax.fori_loop(first, first + many, give_back, 0)

    router_grad = lax.dot_general(
        logit_grads[...],
        got[...].reshape(total, width),
        (((0,), (0,)), ((), ())),
        preferred_element_type=F32,
    )
    router_grad_ref[...] = router_grad[:count]
    rows[...] = jnp.zeros(rows.shape, F32)

    def stores(t):
        at = pl.ds(pl.multiple_of(t * tile, tile), tile)
        return (
            pltpu.make_async_copy(in_grad.at[:, at], in_grad_hbm.at[:, at], store_sems.at[0, t]),
            pltpu.make_async_copy(out_grad.at[at], out_grad_hbm.at[at], store_sems.at[1, t]),
        )

    def outward(t, carry):
        at = pl.ds(pl.multiple_of(t * tile, tile), tile)
        over_rows = (((0,), (0,)), ((), ()))
        in_grad[:, at] = lax.dot_general(
            got[...].reshape(total, width), hid_grad[:, at], over_rows, preferred_element_type=F32
        ).astype(BF16)
        out_grad[at, :] = lax.dot_general(
            active[:, at], slot_grad[...], over_rows, preferred_element_type=F32
        ).astype(BF16)
        for store in stores(t):
            store.start()
        rows[...] += jnp.dot(active[:, at], w_out[at, :], preferred_element_type=F32)
        return carry

    lax.fori_loop(0, tiles, outward, 0)
    result_ref[...] = (gates[:, :1] * rows[...]).astype(BF16).reshape(count, slots, width)
    returning.wait_others()
    for k in range(1, count):
        there.copy(k).wait_send()
    slot_id = lax.broadcasted_iota(jnp.int32, (tokens, total), 1)
    chosen = (slot_id == col_ref[...]).astype(F32).astype(BF16)
    grad_ref[...] = jnp.dot(
        chosen, home[...].reshape(total, width), preferred_element_type=F32
    )
    for t in range(tiles):
        for store in stores(t):
            store.wait()


def run_experts(
    normed, row, col, router, upstream, expert_in, expert_out, slots, collective_id
):
    tokens, width = normed.shape
    count = lax.axis_size("expert")
    hidden = expert_in.shape[2]
    tile = FF_TILE if hidden % FF_TILE == 0 else hidden
    total = count * slots
    exchanged = (count, slots, width)
    vmem = pl.BlockSpec(memory_space=pltpu.VMEM)
    hbm = pl.BlockSpec(memory_space=pl.ANY)
    grad, result, in_grad, out_grad, router_grad = pl.pallas_call(
        functools.partial(experts_kernel, slots, tile),
        out_shape=[
            jax.ShapeDtypeStruct((tokens, width), F32),
            jax.ShapeDtypeStruct(exchanged, BF16),
            jax.ShapeDtypeStruct((width, hidden), BF16),
            jax.ShapeDtypeStruct((hidden, width), BF16),
            jax.ShapeDtypeStruct(router.shape, F32),
        ],
        in_specs=[vmem] * 5 + [hbm] * 2,
        out_specs=[vmem, vmem, hbm, hbm, vmem],
        scratch_shapes=[
            pltpu.VMEM((width, hidden), BF16),
            pltpu.VMEM((hidden, width), BF16),
            pltpu.VMEM(exchanged, BF16),
            pltpu.VMEM(exchanged, BF16),
            pltpu.VMEM(exchanged, BF16),
            pltpu.VMEM((total, width), BF16),
            pltpu.VMEM((total, hidden), BF16),
            pltpu.VMEM((total, hidden), BF16),
            pltpu.VMEM((total, width), F32),
            pltpu.VMEM((width, hidden), BF16),
            pltpu.VMEM((hidden, width), BF16),
            Side.scratch(count),
            Side.scratch(count),
            pltpu.SemaphoreType.DMA((2,)),
            pltpu.SemaphoreType.DMA((2, hidden // tile)),
            pltpu.VMEM((LANES, width), BF16),
            pltpu.VMEM((total, LANES), F32),
            pltpu.VMEM((total, LANES), BF16),
            pltpu.VMEM(exchanged, BF16),
        ],
        compiler_params=params(collective_id=collective_id, has_side_effects=True),
        name="experts",
    )(normed, row, col, router, upstream, expert_in, expert_out)
    return grad, result, in_grad, out_grad, router_grad


def in_segments(value_ref, turn):
    steps = value_ref.shape[0] // SEGS
    parts = []
    for lane in range(turn.shape[0]):
        lanes = slice(lane * LANES, (lane + 1) * LANES)
        for s in range(SEGS):
            rows = value_ref[s * steps : (s + 1) * steps, lanes].astype(F32)
            turn[lane, pl.ds(s, steps, stride=SEGS), :] = rows
        parts.append(turn[lane].astype(BF16))
    return jnp.concatenate(parts, axis=1)


def over_blocks(width, size, body):
    def one(n, carry):
        body(pl.ds(pl.multiple_of(n * size, size), size))
        return carry

    lax.fori_loop(0, width // size, one, 0)


def slot_targets(route, experts, capacity, slots):
    count = route.shape[1]
    steps = count // SEGS
    high = max(experts, 16)
    onehot = lax.broadcasted_iota(jnp.int32, (high, count), 0) == route
    onehot = onehot.astype(F32)
    token_of = lambda p: (p % SEGS) * steps + p // SEGS
    first = token_of(lax.broadcasted_iota(jnp.int32, (count, count), 0))
    second = token_of(lax.broadcasted_iota(jnp.int32, (count, count), 1))
    earlier = (first <= second).astype(F32).astype(BF16)
    running = jnp.dot(onehot.astype(BF16), earlier, preferred_element_type=F32)
    place = (jnp.sum(running * onehot, axis=0, keepdims=True) - 1.0).astype(jnp.int32)
    return jnp.where(place < capacity, route * slots + place, -1)


def forward_kernel(sizes, *refs):
    states, steps, rank, capacity = sizes
    tokens_hbm, upstream_hbm, in_proj_hbm, out_proj_hbm = refs[:4]
    route_ref, gain_ref, gain_two_ref, conv_ref, bias_ref, x_proj_ref, dt_proj_ref = refs[4:11]
    dt_bias_ref, skip_ref, rate_log_ref = refs[11:14]
    ssm_ref, held_ref, gated_ref, hidden_ref, normed_two_ref, row_ref, col_ref, before_ref = refs[14:22]
    side_out = refs[22]
    kept_hbm, spread_hbm, refs = refs[23:32], refs[32:34], refs[34:]
    tokens_in, upstream_in, in_proj, out_proj, turn, ext_in, tail, sent = refs[:8]
    kept, refs = refs[8:17], refs[17:]
    tokens, upstream, normed, inner, gate_z, mixed, pre, delta, proj = kept
    in_s, bb, cb, run_a, run_b, side_sems, load_sems, keep_sems, halo_sems = refs[:9]
    x_proj, dt_proj, small, before, carry_refs = *refs[9:13], refs[13:]
    phase, block = pl.program_id(0), pl.program_id(1)
    blocks = carry_refs[2].shape[1]
    carries = Carries(states, blocks, True, *carry_refs)
    side = Side(sent, side_out, side_sems)
    parts = ((0, 2 / 7), (2 / 7, 3 / 7), (3 / 7, 1))
    rate2 = -jnp.exp(rate_log_ref[...]) * LOG2E
    rates = [over_sublanes(rate2[n : n + 1, :]) for n in range(states)]
    here = pl.ds(pl.multiple_of(block * LANES, LANES), LANES)
    count, width = tokens.shape
    inner_width = inner.shape[1]
    reach = conv_ref.shape[0] - 1
    rim = reach * SEGS
    experts, me = lax.axis_size("expert"), lax.axis_index("expert")
    slots = sent.shape[1]
    half = inner_width
    loads = [
        pltpu.make_async_copy(src, dst, load_sems.at[i])
        for i, (src, dst) in enumerate(
            (
                (tokens_hbm.at[0], tokens_in),
                (in_proj_hbm.at[:, :half], in_proj.at[:, :half]),
                (in_proj_hbm.at[:, half:], in_proj.at[:, half:]),
                (upstream_hbm.at[0], upstream_in),
                (out_proj_hbm, out_proj),
            )
        )
    ]
    keeps = [
        pltpu.make_async_copy(src, dst, keep_sems.at[i])
        for i, (src, dst) in enumerate(zip((*kept, bb, cb), (*kept_hbm, *spread_hbm)))
    ]

    def front():
        for load in loads:
            load.start()
        small[0:1, :] = as_row(skip_ref)
        small[1:2, :] = as_row(bias_ref)
        small[2:3, :] = as_row(dt_bias_ref)
        x_proj[...] = padded_rows(x_proj_ref, LANES)
        dt_proj[...] = padded_rows(dt_proj_ref, LANES)
        loads[0].wait()
        tokens[...] = in_segments(tokens_in, turn)
        normed[...] = rms(tokens[...].astype(F32), as_row(gain_ref)).astype(BF16)
        loads[1].wait()

        def to_inner(at):
            inner[:, at] = jnp.dot(
                normed[...], in_proj[:, at], preferred_element_type=F32
            ).astype(BF16)

        over_blocks(inner_width, 4 * LANES, to_inner)
        last = inner[count - rim - rim % 16 :, :].astype(F32)[rim % 16 :]
        for k in range(reach):
            tail[k : k + 1, :] = last[(k + 1) * SEGS - 1 : (k + 1) * SEGS]
        greet_experts()
        halo = pltpu.make_async_remote_copy(
            src_ref=tail,
            dst_ref=before,
            send_sem=halo_sems.at[0],
            recv_sem=halo_sems.at[1],
            device_id=(lax.axis_index("batch"), lax.rem(me + 1, experts)),
            device_id_type=MESH,
        )

        @pl.when(me < experts - 1)
        def _():
            halo.start()

        @pl.when(me == 0)
        def _():
            before[...] = jnp.zeros(before.shape, F32)

        loads[2].wait()

        def to_gate(at):
            lanes = pl.ds(pl.multiple_of(half + at.start, LANES), at.size)
            gate_z[:, at] = jnp.dot(normed[...], in_proj[:, lanes], preferred_element_type=F32)

        over_blocks(inner_width, 4 * LANES, to_gate)
        for keep in keeps[2:5]:
            keep.start()
        keeps[0].start()
        loads[3].wait()
        upstream[...] = in_segments(upstream_in, turn)
        keeps[1].start()
        target = slot_targets(route_ref[...], experts, capacity, slots)
        row_ref[...] = target
        wide = jnp.broadcast_to(target.astype(F32), (SEGS, count))
        col_ref[...] = jnp.transpose(wide)[:, :1].astype(jnp.int32)
        slot_id = lax.broadcasted_iota(jnp.int32, (slots, count), 0)

        def dispatch(e, carry):
            picked = (slot_id + e * slots == row_ref[...]).astype(F32).astype(BF16)
            sent[e] = jnp.dot(picked, upstream[...], preferred_element_type=F32).astype(BF16)
            return carry

        lax.fori_loop(0, experts, dispatch, 0)
        side.start(0, parts)

        @pl.when(me < experts - 1)
        def _():
            halo.wait_send()

        @pl.when(me > 0)
        def _():
            halo.wait_recv()

        before_ref[...] = before[...]

        def to_mixed(at):
            own = inner[:, at].astype(F32)
            for k in range(reach):
                tile = own[count - rim + k * SEGS : count - rim + (k + 1) * SEGS]
                ext_in[k * SEGS : (k + 1) * SEGS, at] = shifted_in(
                    tile, before[k : k + 1, at], True
                )
            ext_in[rim:, at] = own
            total = jnp.broadcast_to(small[1:2, at], own.shape)
            for k in range(reach + 1):
                total = total + conv_ref[k : k + 1, at] * ext_in[k * SEGS : k * SEGS + count, at]
            mixed[:, at] = silu(total).astype(BF16)

        over_blocks(inner_width, 2 * LANES, to_mixed)
        keeps[5].start()
        proj[...] = lax.dot_general(
            mixed[...], x_proj[...], (((1,), (1,)), ((), ())), preferred_element_type=F32
        )
        keeps[8].start()

        def to_delta(at):
            own = jnp.dot(
                proj[...].astype(BF16), dt_proj[:, at], preferred_element_type=F32
            )
            own = own + small[2:3, at]
            pre[:, at] = own
            delta[:, at] = softplus(own)

        over_blocks(inner_width, 2 * LANES, to_delta)
        keeps[6].start()
        keeps[7].start()

    @pl.when((phase == 0) & (block == 0))
    def _():
        front()

    for part, (at_phase, at_block) in enumerate(((0, blocks // 2), (1, 1))):

        @pl.when((phase == at_phase) & (block == at_block))
        def _():
            side.start(part + 1, parts)

    @pl.when((phase == 0) & (block == 1))
    def _():
        for keep in keeps[9:]:
            keep.start()

    def ends(first):
        in_s[...] = delta[:, here] * mixed[:, here].astype(F32)
        sums = jnp.sum(delta[:, here].reshape(steps, SEGS, LANES), axis=0)

        def one(j, held):
            rows = tile_rows(j)
            d, u = delta[rows, here], in_s[rows, :]
            tile = proj[rows, :] if first else None
            new = []
            for n in range(states):
                if first:
                    b = over_lanes(tile[:, rank + n : rank + n + 1])
                    bb[j, n] = b
                    cb[j, n] = over_lanes(tile[:, rank + states + n : rank + states + n + 1])
                else:
                    b = bb[j, n]
                new.append(jnp.exp2(d * rates[n]) * held[n] + u * b)
            return tuple(new)

        zero = jnp.zeros((SEGS, LANES), F32)
        held = lax.fori_loop(0, steps, one, (zero,) * states, unroll=4)
        carries.put(block, held, sums, rates, run_a, run_b)

    @pl.when((phase == 0) & (block == 0))
    def _():
        ends(True)

    @pl.when((phase == 0) & (block > 0))
    def _():
        ends(False)

    @pl.when(phase == 1)
    def _():
        carries.await_group(block)
        start = carries.starts(block, rate2, run_a, run_b)
        own = mixed[:, here].astype(F32)
        in_s[...] = delta[:, here] * own
        ssm_ref[...] = small[0:1, here] * own
        for n in range(states):
            held_ref[0, 0, n] = start[n]

        def one(j, held):
            rows = tile_rows(j)
            d, u = delta[rows, here], in_s[rows, :]
            total = ssm_ref[rows, :]
            new = []
            for n in range(states):
                h = jnp.exp2(d * rates[n]) * held[n] + u * bb[j, n]
                held_ref[0, j + 1, n] = h
                total = total + cb[j, n] * h
                new.append(h)
            ssm_ref[rows, :] = total
            return tuple(new)

        lax.fori_loop(0, steps, one, tuple(start), unroll=4)
        gated_ref[:, here] = (ssm_ref[...] * silu(gate_z[:, here])).astype(BF16)

    @pl.when((phase == 1) & (block == blocks - 1))
    def _():
        loads[4].wait()
        hidden = tokens[...].astype(F32) + jnp.dot(
            gated_ref[...], out_proj[...], preferred_element_type=F32
        )
        hidden_ref[...] = hidden
        normed_two_ref[...] = rms(hidden, as_row(gain_two_ref)).astype(BF16)
        side.wait()
        for keep in keeps:
            keep.wait()


def forward(
    tokens,
    upstream,
    in_proj,
    out_proj,
    route,
    gain_one,
    gain_two,
    conv_weight,
    conv_bias,
    x_proj,
    dt_proj,
    dt_bias,
    skip,
    rate_log,
    sizes,
    collective_id,
):
    rank, capacity, slots = sizes
    count, width = tokens.shape[1:]
    inner_width = out_proj.shape[0]
    states, steps, blocks = rate_log.shape[0], count // SEGS, inner_width // LANES
    experts = lax.axis_size("expert")
    rim = (conv_weight.shape[0] - 1) * SEGS
    vmem, hbm = (pl.BlockSpec(memory_space=m) for m in (pltpu.VMEM, pl.ANY))
    spread = pltpu.VMEM((steps, states, SEGS, LANES), F32)
    run = pltpu.VMEM((blocks, states, SEGS, LANES), F32)
    whole = lambda *shape: pl.BlockSpec(shape, lambda p, c: (0,) * len(shape))
    shape_of = jax.ShapeDtypeStruct
    kept = [
        shape_of((count, width), BF16),
        shape_of((count, width), BF16),
        shape_of((count, width), BF16),
        shape_of((count, inner_width), BF16),
        shape_of((count, inner_width), F32),
        shape_of((count, inner_width), BF16),
        shape_of((count, inner_width), F32),
        shape_of((count, inner_width), F32),
        shape_of((count, LANES), F32),
    ]
    exchanged = (experts, slots, width)
    out = pl.pallas_call(
        functools.partial(forward_kernel, (states, steps, rank, capacity)),
        grid=(2, blocks),
        out_shape=[
            shape_of((count, inner_width), F32),
            shape_of((blocks, steps + 1, states, SEGS, LANES), F32),
            shape_of((count, inner_width), BF16),
            shape_of((count, width), F32),
            shape_of((count, width), BF16),
            shape_of((1, count), jnp.int32),
            shape_of((count, 1), jnp.int32),
            shape_of((SEGS, inner_width), F32),
            shape_of(exchanged, BF16),
        ]
        + kept
        + [shape_of((steps, states, SEGS, LANES), F32)] * 2,
        in_specs=[hbm] * 4
        + [vmem] * 9
        + [pl.BlockSpec((states, LANES), lambda p, c: (0, c))],
        out_specs=[
            pl.BlockSpec((count, LANES), lambda p, c: (0, p * c)),
            pl.BlockSpec((1, steps + 1, states, SEGS, LANES), lambda p, c: (p * c, 0, 0, 0, 0)),
            whole(count, inner_width),
            whole(count, width),
            whole(count, width),
            whole(1, count),
            whole(count, 1),
            vmem,
            hbm,
        ]
        + [hbm] * (len(kept) + 2),
        scratch_shapes=[
            pltpu.VMEM((count, width), BF16),
            pltpu.VMEM((count, width), BF16),
            pltpu.VMEM(in_proj.shape, BF16),
            pltpu.VMEM(out_proj.shape, BF16),
            pltpu.VMEM((width // LANES, count, LANES), F32),
            pltpu.VMEM((count + rim, inner_width), F32),
            pltpu.VMEM((SEGS, inner_width), F32),
            pltpu.VMEM(exchanged, BF16),
        ]
        + [pltpu.VMEM(k.shape, k.dtype) for k in kept]
        + [
            pltpu.VMEM((count, LANES), F32),
            spread,
            spread,
            run,
            run,
            Side.scratch(experts),
            pltpu.SemaphoreType.DMA((5,)),
            pltpu.SemaphoreType.DMA((len(kept) + 2,)),
            pltpu.SemaphoreType.DMA((2,)),
            pltpu.VMEM((LANES, inner_width), BF16),
            pltpu.VMEM((LANES, inner_width), BF16),
            pltpu.VMEM((SEGS, inner_width), F32),
            pltpu.VMEM((SEGS, inner_width), F32),
        ]
        + Carries.scratch(states, blocks, experts),
        compiler_params=params(collective_id=collective_id, has_side_effects=True),
        name="forward",
    )(
        tokens,
        upstream,
        in_proj,
        out_proj,
        route,
        gain_one,
        gain_two,
        conv_weight,
        conv_bias,
        x_proj,
        dt_proj,
        dt_bias,
        skip,
        rate_log,
    )
    return out[:9], out[9:18], out[18:]


def backward_kernel(states, steps, rank, kinds, *refs):
    many = len(kinds)
    expert_hbm, sum_in, refs = refs[:2], refs[2 : 2 + many], refs[2 + many :]
    delta_hbm, g_hbm, in_hbm, pre_hbm, bb_hbm, cb_hbm = refs[:6]
    rate_ref, skip_ref, held_ref, side_in = refs[6:10]
    sum_out, refs = refs[10 : 10 + many], refs[10 + many :]
    pre_grad_ref, mixed_grad_ref, rate_grad_ref, skip_grad_ref, bias_grad_ref = refs[:5]
    bc_grad_ref, side_out = refs[5:7]
    landings, refs = refs[7:9], refs[9:]
    in_s, rate_sum, in_sum, bb, cb, b_acc, c_acc, run_a, run_b, side_sems = refs[:10]
    skip_row, halving_sems, refs = refs[10], refs[11:13], refs[13:]
    delta_ref, g_ref, in_ref, pre_ref, load_sems = refs[:5]
    carry_refs, sum_refs = refs[5:10], refs[10:]
    loads = [
        pltpu.make_async_copy(src, dst, load_sems.at[i])
        for i, (src, dst) in enumerate(
            (
                (delta_hbm, delta_ref),
                (g_hbm, g_ref),
                (cb_hbm, cb),
                (in_hbm, in_ref),
                (pre_hbm, pre_ref),
                (bb_hbm, bb),
            )
        )
    ]
    halvings = [Halving(expert_hbm[i], i == 0, halving_sems[i]) for i in range(2)]
    phase, block = pl.program_id(0), pl.program_id(1)
    here = pl.ds(pl.multiple_of(block * LANES, LANES), LANES)
    blocks = carry_refs[2].shape[1]
    carries = Carries(states, blocks, False, *carry_refs)
    sums = summings(kinds, sum_in, sum_out, sum_refs)
    side = Side(side_in, side_out, side_sems)
    rate2 = -jnp.exp(rate_ref[:, here]) * LOG2E
    rates = [over_sublanes(rate2[n : n + 1, :]) for n in range(states)]
    zero = jnp.zeros((SEGS, LANES), F32)

    @pl.when((phase == 0) & (block == 0))
    def _():
        for load in loads:
            load.start()
        skip_row[...] = as_row(skip_ref)
        greet_others()
        for item in sums:
            item.start(0)
        for halving, landing in zip(halvings, landings):
            for copy in halving.first(landing):
                copy.start()
        for load in loads[:3]:
            load.wait()

    @pl.when((phase == 1) & (block == 0))
    def _():
        for load in loads[3:]:
            load.wait()

    @pl.when((phase == 0) & (block == blocks - 3))
    def _():
        for item in sums:
            if not item.pairs_first:
                item.advance(0)

    @pl.when((phase == 1) & (block == 1))
    def _():
        for item in sums:
            if item.pairs_first:
                item.advance(0)

    @pl.when((phase == 1) & (block == blocks // 2 - 1))
    def _():
        side.start()

    @pl.when(phase == 0)
    def _():
        sums = jnp.sum(delta_ref[:, here].reshape(steps, SEGS, LANES), axis=0)

        def one(i, held):
            j = steps - 1 - i
            d, g = delta_ref[tile_rows(j), here], g_ref[tile_rows(j), here]
            return tuple(
                jnp.exp2(d * rates[n]) * (held[n] + g * cb[j, n]) for n in range(states)
            )

        held = lax.fori_loop(0, steps, one, (zero,) * states, unroll=4)
        carries.put(block, held, sums, rates, run_a, run_b)

    def grads(first, last):
        start = carries.starts(block, rate2, run_a, run_b)
        delta, g = delta_ref[:, here], g_ref[:, here]
        mixed = in_ref[:, here].astype(F32)
        in_s[...] = delta * mixed
        place = lax.broadcasted_iota(jnp.int32, (SEGS, LANES), 1)

        def one(i, carry):
            edge, rate_acc = carry
            j = steps - 1 - i
            rows = tile_rows(j)
            d, u, g = delta_ref[rows, here], in_s[rows, :], g_ref[rows, here]
            by_rate = by_b = sums = zero
            new_edge, new_acc = [], []
            for n in range(states):
                b, c = bb[j, n], cb[j, n]
                q = c * g + edge[n]
                e = jnp.exp2(d * rates[n]) * q
                v = e * held_ref[0, j, n]
                by_rate = by_rate + rates[n] * v
                by_b = by_b + b * q
                to_b = q * u
                to_c = g * held_ref[0, j + 1, n]
                if not first:
                    to_b = b_acc[j, n] + to_b
                    to_c = c_acc[j, n] + to_c
                if last:
                    sums = jnp.where(place == rank + n, jnp.sum(to_b, axis=1, keepdims=True), sums)
                    to_c = jnp.sum(to_c, axis=1, keepdims=True)
                    sums = jnp.where(place == rank + states + n, to_c, sums)
                else:
                    b_acc[j, n] = to_b
                    c_acc[j, n] = to_c
                new_edge.append(e)
                new_acc.append(rate_acc[n] + d * v)
            rate_sum[rows, :] = by_rate
            in_sum[rows, :] = by_b
            if last:
                bc_grad_ref[rows, :] = sums
            return tuple(new_edge), tuple(new_acc)

        _, rate_acc = lax.fori_loop(
            0, steps, one, (tuple(start), (zero,) * states), unroll=4
        )
        for n in range(states):
            rate_grad_ref[n : n + 1, here] = (
                LN2 * rate2[n : n + 1, :] * jnp.sum(rate_acc[n], axis=0, keepdims=True)
            )
        by_b = in_sum[...]
        pre_grad = (LN2 * rate_sum[...] + mixed * by_b) * jax.nn.sigmoid(pre_ref[:, here])
        pre_grad_ref[:, here] = pre_grad.astype(BF16)
        bias_grad_ref[:, here] = jnp.sum(pre_grad, axis=0, keepdims=True)
        mixed_grad_ref[:, here] = delta * by_b + skip_row[:, here] * g
        skip_grad_ref[:, here] = jnp.sum(g * mixed, axis=0, keepdims=True)

    @pl.when(phase == 1)
    def _():
        carries.await_group(block)

    @pl.when((phase == 1) & (block == 0))
    def _():
        grads(True, False)

    @pl.when((phase == 1) & (block > 0) & (block < blocks - 1))
    def _():
        grads(False, False)

    @pl.when((phase == 1) & (block == blocks - 1))
    def _():
        grads(False, True)
        side.wait()
        for item in sums:
            item.wait(1)
            item.add(1)
        for halving, landing in zip(halvings, landings):
            for copy in halving.first(landing):
                copy.wait()


def mixer_grads(
    pre, delta, mixed, ssm_grad, spreads, rate_log, skip, held, beside, experts, rank, items, collective_id
):
    count, width = delta.shape
    states, steps, blocks = rate_log.shape[0], count // SEGS, width // LANES
    spread = pltpu.VMEM((steps, states, SEGS, LANES), F32)
    run = pltpu.VMEM((blocks, states, SEGS, LANES), F32)
    flat = pltpu.VMEM((count, LANES), F32)
    sum_scratch = [item.first_scratch() for item in items]
    kinds = tuple((item.kind(), len(refs)) for item, refs in zip(items, sum_scratch))
    spread_specs = [
        pl.BlockSpec(item.spread_shape().shape, lambda p, c, rank=len(item.spread_shape().shape): (0,) * rank)
        for item in items
    ]
    outs = pl.pallas_call(
        functools.partial(backward_kernel, states, steps, rank, kinds),
        grid=(2, blocks),
        out_shape=[item.spread_shape() for item in items]
        + [
            jax.ShapeDtypeStruct((count, width), BF16),
            jax.ShapeDtypeStruct((count, width), F32),
            jax.ShapeDtypeStruct((states, width), F32),
            jax.ShapeDtypeStruct((1, width), F32),
            jax.ShapeDtypeStruct((1, width), F32),
            jax.ShapeDtypeStruct((count, LANES), F32),
            jax.ShapeDtypeStruct(beside.shape, beside.dtype),
        ]
        + [jax.ShapeDtypeStruct((2, e.shape[0] // 4, e.shape[1]), BF16) for e in experts],
        in_specs=[pl.BlockSpec(memory_space=pl.ANY)] * (2 + len(items))
        + [pl.BlockSpec(memory_space=pl.ANY)] * 6
        + [pl.BlockSpec(memory_space=pltpu.VMEM)] * 2
        + [
            pl.BlockSpec((1, steps + 1, states, SEGS, LANES), lambda p, c: (p * c, 0, 0, 0, 0)),
            pl.BlockSpec(memory_space=pl.ANY),
        ],
        out_specs=spread_specs
        + [pl.BlockSpec(memory_space=pltpu.VMEM)] * 6
        + [pl.BlockSpec(memory_space=pl.ANY)] * 3,
        scratch_shapes=[flat, flat, flat, spread, spread, spread, spread, run, run]
        + [Side.scratch(lax.axis_size("expert")), pltpu.VMEM((1, width), F32)]
        + [pltpu.SemaphoreType.DMA((2, 2))] * 2
        + [pltpu.VMEM((count, width), kind) for kind in (F32, F32, BF16, F32)]
        + [pltpu.SemaphoreType.DMA((6,))]
        + Carries.scratch(states, blocks, lax.axis_size("expert"))
        + [ref for refs in sum_scratch for ref in refs],
        compiler_params=params(collective_id=collective_id, has_side_effects=True),
        name="mixer_grads",
    )(*experts, *(item.local for item in items), delta, ssm_grad, mixed, pre, *spreads, rate_log, skip, held, beside)
    return outs


def shifted_in(tile, row, forward):
    if forward:
        return jnp.concatenate([row, tile[: SEGS - 1]], axis=0)
    return jnp.concatenate([tile[1:], row], axis=0)


def middle_kernel(*refs):
    hidden_ref, grad_ref, upstream_ref, gain_ref, normed_ref = refs[:5]
    gated_ref, ssm_ref, gate_ref, out_proj_ref = refs[5:9]
    hidden_grad_ref, gain_out, ssm_grad_ref, gate_grad_ref, out_local_ref, gate_local_ref = refs[9:15]
    branch = refs[15]

    @pl.when(pl.program_id(0) == 0)
    def _():
        to_hidden, to_gain = rms_back(hidden_ref[...], as_row(gain_ref), grad_ref[...])
        total = upstream_ref[...].astype(F32) + to_hidden
        hidden_grad_ref[...] = total
        branch[...] = total.astype(BF16)
        gain_out[...] = to_gain[None]

    over_rows = (((0,), (0,)), ((), ()))
    out_local_ref[...] = lax.dot_general(
        gated_ref[...], branch[...], over_rows, preferred_element_type=F32
    ).astype(BF16)
    gated_grad = lax.dot_general(
        branch[...], out_proj_ref[...], (((1,), (1,)), ((), ())), preferred_element_type=F32
    )
    gate = gate_ref[...]
    s = jax.nn.sigmoid(gate)
    ssm_grad_ref[...] = gated_grad * (gate * s)
    low = (gated_grad * ssm_ref[...] * (s * (1.0 + gate * (1.0 - s)))).astype(BF16)
    gate_grad_ref[...] = low
    gate_local_ref[...] = lax.dot_general(
        normed_ref[...], low, over_rows, preferred_element_type=F32
    ).astype(BF16)


def middle(hidden, grad, upstream, gain, normed, gated, ssm, gate_z, out_proj):
    count, width = hidden.shape
    inner_width = out_proj.shape[0]
    wide = 2 * LANES
    vmem = pl.BlockSpec(memory_space=pltpu.VMEM)
    whole = lambda *shape: pl.BlockSpec(shape, lambda c: (0,) * len(shape))
    lanes = lambda rows: pl.BlockSpec((rows, wide), lambda c: (0, c))
    rows = pl.BlockSpec((wide, width), lambda c: (c, 0))
    shape_of = jax.ShapeDtypeStruct
    return pl.pallas_call(
        middle_kernel,
        grid=(inner_width // wide,),
        out_shape=[
            shape_of((count, width), F32),
            shape_of((1, width), F32),
            shape_of((count, inner_width), F32),
            shape_of((count, inner_width), BF16),
            shape_of((inner_width, width), BF16),
            shape_of((width, inner_width), BF16),
        ],
        in_specs=[vmem] * 5 + [lanes(count)] * 3 + [rows],
        out_specs=[whole(count, width), whole(1, width), lanes(count), lanes(count), rows]
        + [lanes(width)],
        scratch_shapes=[pltpu.VMEM((count, width), BF16)],
        compiler_params=params(),
        name="middle",
    )(hidden, grad, upstream, gain, normed, gated, ssm, gate_z, out_proj)


WIDE = 2 * LANES


def put_by_token(out_ref, value, turn):
    steps = value.shape[0] // SEGS
    for lane in range(turn.shape[0]):
        lanes = slice(lane * LANES, (lane + 1) * LANES)
        turn[lane] = value[:, lanes]
        for s in range(SEGS):
            rows = turn[lane, pl.ds(s, steps, stride=SEGS), :]
            out_ref[s * steps : (s + 1) * steps, lanes] = rows.astype(out_ref.dtype)


def tile_places(pack, flat):
    _, pairs, each = pack.shape[:3]
    across = flat.shape[1] // LANES
    for t in range(2 * pairs * each):
        row, lane = t // across * 16, t % across * LANES
        inside = (slice(row, row + 16), slice(lane, lane + LANES)) if row < flat.shape[0] else None
        yield (t // (pairs * each), t // each % pairs, t % each), inside


def put_tiles(pack, flat):
    for tile, inside in tile_places(pack, flat):
        if inside is None:
            pack[tile] = jnp.zeros((16, LANES), BF16)
        else:
            pack[tile] = flat[inside].astype(BF16)


def get_tiles(flat, pack):
    for tile, inside in tile_places(pack, flat):
        if inside is not None:
            flat[inside] = pack[tile].astype(F32)


def finish_kernel(rank, states, kinds, *refs):
    loads_hbm, expert_hbm, landed_hbm, refs = refs[:11], refs[11:13], refs[13:15], refs[15:]
    bc_grad_ref, low_ref, x_proj_ref, dt_proj_ref, conv_ref, bias_ref = refs[:6]
    before_ref, gain_ref, rate_ref, dt_bias_ref, skip_ref, gain_two_ref, router_ref = refs[6:13]
    col_ref, gate_spread, out_spread = refs[13:16]
    output_ref, tokens_grad_ref, in_proj_out, out_proj_out, flat, last_flat = refs[16:22]
    second_hbm, refs = refs[22:24], refs[24:]
    halving_refs, halving_sems, refs = refs[:4], refs[4:8], refs[8:]
    halvings = [Halving(expert_hbm[i], i == 0, halving_sems[i]) for i in range(2)]
    loaded, refs = refs[:11], refs[11:]
    pre_grad, mixed_part, mixed, inner, normed, in_proj, gate_grad, tokens, hidden_grad = loaded[:9]
    hidden, home = loaded[9:]
    ext_in, ext_grad, inner_grad, proj_grad, rows, head, after = refs[:7]
    turn, load_sems, halo_sems = refs[7:10]
    small, last_small = SmallSum(*refs[10:17]), TinySum(*refs[17:23])
    x_proj, dt_proj, bias_row = refs[23:26]
    parts, refs = len(kinds) - 2, refs[26:]
    locals_, sum_refs = refs[:parts], refs[parts:]
    count, width = tokens.shape
    inner_width = inner.shape[1]
    reach = conv_ref.shape[0] - 1
    rim = reach * SEGS
    experts, me = lax.axis_size("expert"), lax.axis_index("expert")
    group = lax.axis_index("batch")
    half = inner_width

    loads = [
        pltpu.make_async_copy(src, dst, load_sems.at[i])
        for i, (src, dst) in enumerate(zip(loads_hbm, loaded))
    ]
    halving_loads = []
    for i, halving in enumerate(halvings):
        for k, src in enumerate((halving.chunk(halving.far), landed_hbm[i].at[1])):
            halving_loads.append(
                pltpu.make_async_copy(src, halving_refs[2 * i + k], halving_sems[2 + i].at[k])
            )
    for load in loads[:1] + halving_loads + loads[1:]:
        load.start()
    ends = [0]
    for ref in locals_:
        ends.append(ends[-1] + ref.shape[2])
    inner_rows = [slice(ends[i], ends[i + 1]) for i in range(parts)]
    gate_sum, out_sum, *inner_sums = summings(
        kinds,
        (gate_spread, out_spread, *locals_),
        (in_proj_out.at[:, half:], out_proj_out)
        + tuple(in_proj_out.at[at, :half] for at in inner_rows),
        sum_refs,
    )
    greet_others()
    gate_sum.begin()
    out_sum.begin()
    x_proj[...] = padded_rows(x_proj_ref, LANES)
    dt_proj[...] = padded_rows(dt_proj_ref, LANES)
    bias_row[...] = as_row(bias_ref)
    low = low_ref[...].astype(BF16)
    flat[...] = jnp.zeros(flat.shape, F32)
    last_flat[...] = jnp.zeros(last_flat.shape, F32)
    last_small.total[...] = jnp.zeros(last_small.total.shape, F32)

    seconds = []
    for i, halving in enumerate(halvings):
        own, brought = halving_refs[2 * i : 2 * i + 2]
        for load in halving_loads[2 * i : 2 * i + 2]:
            load.wait()

        def join(n, carry, own=own, brought=brought):
            at = pl.ds(pl.multiple_of(n * 16, 16), 16)
            own[at, :] = together(own[at, :], brought[at, :]).astype(BF16)
            return carry

        lax.fori_loop(0, own.shape[0] // 16, join, 0)
        seconds.append(halving.second(own, second_hbm[i]))
        seconds[i].start()

    loads[0].wait()
    over_inner = (((1,), (1,)), ((), ()))
    over_rows = (((0,), (0,)), ((), ()))
    low_grad = lax.dot_general(
        pre_grad[...], dt_proj[...], over_inner, preferred_element_type=F32
    )
    proj_grad[...] = (low_grad + bc_grad_ref[...]).astype(BF16)

    for load in loads[1:4]:
        load.wait()

    def before_silu(at):
        own = inner[:, at].astype(F32)
        for k in range(reach):
            tile = own[count - rim + k * SEGS : count - rim + (k + 1) * SEGS]
            ext_in[k * SEGS : (k + 1) * SEGS, at] = shifted_in(tile, before_ref[k : k + 1, at], True)
        ext_in[rim:, at] = own
        total = jnp.dot(proj_grad[...], x_proj[:, at], preferred_element_type=F32)
        total = total + mixed_part[:, at]
        conv_pre = jnp.broadcast_to(bias_row[:, at], total.shape)
        for k in range(reach + 1):
            conv_pre = conv_pre + conv_ref[k : k + 1, at] * ext_in[k * SEGS : k * SEGS + count, at]
        total = total * silu_slope(conv_pre)
        ext_grad[:count, at] = total
        for k in range(reach):
            head[k : k + 1, at] = total[k * SEGS : k * SEGS + 1]

    over_blocks(inner_width, WIDE, before_silu)
    halo = pltpu.make_async_remote_copy(
        src_ref=head,
        dst_ref=after,
        send_sem=halo_sems.at[0],
        recv_sem=halo_sems.at[1],
        device_id=(group, lax.rem(me + experts - 1, experts)),
        device_id_type=MESH,
    )

    @pl.when(me > 0)
    def _():
        halo.start()

    @pl.when(me == experts - 1)
    def _():
        after[...] = jnp.zeros(after.shape, F32)

    at_dt = rank + 2 * states
    x_local = lax.dot_general(proj_grad[...], mixed[...], over_rows, preferred_element_type=F32)
    flat[:at_dt, :] = x_local[:at_dt]
    dt_local = lax.dot_general(low, pre_grad[...], over_rows, preferred_element_type=F32)
    flat[at_dt : at_dt + rank, :] = dt_local[:rank]
    at = at_dt + rank + states
    flat[at_dt + rank : at, :] = rate_ref[...]
    flat[at : at + 1, :] = dt_bias_ref[...]
    flat[at + 1 : at + 2, :] = skip_ref[...]
    flat[at + 2 : at + 3, :width] = gain_two_ref[...]
    fold = router_ref.shape[0] // 2
    flat[at + 3 : at + 3 + fold, :width] = router_ref[:fold, :]
    flat[at + 3 : at + 3 + fold, width:] = router_ref[fold:, :]
    put_tiles(small.pack, flat)
    small.start(0)
    for load in loads[4:7]:
        load.wait()
    rows[...] = lax.dot_general(
        gate_grad[...], in_proj[:, half:], over_inner, preferred_element_type=F32
    )

    @pl.when(me > 0)
    def _():
        halo.wait_send()

    @pl.when(me < experts - 1)
    def _():
        halo.wait_recv()

    def before_taps(at):
        for k in range(reach):
            tile = ext_grad[k * SEGS : (k + 1) * SEGS, at]
            ext_grad[count + k * SEGS : count + (k + 1) * SEGS, at] = shifted_in(
                tile, after[k : k + 1, at], False
            )
        total = conv_ref[0:1, at] * ext_grad[rim : rim + count, at]
        for k in range(1, reach + 1):
            first = (reach - k) * SEGS
            total = total + conv_ref[k : k + 1, at] * ext_grad[first : first + count, at]
        inner_grad[:, at] = total.astype(BF16)

    over_blocks(inner_width, WIDE, before_taps)
    chunk = width // experts
    share = inner_width // lax.axis_size("batch")

    def to_in_proj(at):
        total = lax.dot_general(
            normed[...], inner_grad[:, at], over_rows, preferred_element_type=F32
        ).astype(BF16)
        for e in range(experts):
            own = total[e * chunk : (e + 1) * chunk]
            for ref, rows_at in zip(locals_, inner_rows):
                ref[e // 2, e % 2, :, at] = own[rows_at]

    over_blocks(inner_width, share, to_in_proj)
    for item in inner_sums:
        item.begin()
    small.advance(0)


    def to_taps(at):
        grad = ext_grad[:count, at]
        for k in range(reach + 1):
            last_flat[k : k + 1, at] = jnp.sum(
                grad * ext_in[k * SEGS : k * SEGS + count, at], axis=0, keepdims=True
            )
        last_flat[reach + 1 : reach + 2, at] = jnp.sum(grad, axis=0, keepdims=True)

    for item in inner_sums:
        item.advance(0)
    over_blocks(inner_width, WIDE, to_taps)
    for load in loads[7:]:
        load.wait()
    grad = rows[...] + lax.dot_general(
        inner_grad[...], in_proj[:, :half], over_inner, preferred_element_type=F32
    )
    values = tokens[...].astype(F32)
    to_values, to_gain = rms_back(values, as_row(gain_ref), grad)
    put_by_token(tokens_grad_ref, to_values + hidden_grad[...], turn)

    last_flat[reach + 2 : reach + 3, :width] = to_gain[None]
    across = inner_width // LANES
    for t in range((reach + 3) * across):
        row, lane = t // across, t % across * LANES
        last_small.total[t : t + 1, :] = last_flat[row : row + 1, lane : lane + LANES]
    last_small.pack[...] = last_small.total[...].astype(BF16)
    last_small.start(0)
    gate_sum.advance(2)
    out_sum.advance(2)
    small.advance(1)
    last_small.advance(0)
    for item in inner_sums:
        item.advance(1)
    last_small.advance(1)
    small.advance(2)

    slots = home.shape[1]
    slot_id = lax.broadcasted_iota(jnp.int32, (count, experts * slots), 1)
    chosen = (slot_id == col_ref[...]).astype(F32).astype(BF16)
    returned = jnp.dot(
        chosen, home[...].reshape(experts * slots, width), preferred_element_type=F32
    )
    put_by_token(output_ref, hidden[...] + returned, turn)

    last_small.advance(2)
    gate_sum.advance(3)
    out_sum.advance(3)
    for item in inner_sums:
        item.advance(2)
    small.advance(3)
    small.advance(4)
    get_tiles(flat, small.every)
    for item in inner_sums:
        item.advance(3)
    for t in range((reach + 3) * across):
        row, lane = t // across, t % across * LANES
        last_flat[row : row + 1, lane : lane + LANES] = last_small.total[t : t + 1, :]
    for copy in seconds:
        copy.wait()


def finish(loaded, experts, landed, small, early, rank, states, collective_id):
    pre_grad, in_proj, tokens = loaded[0], loaded[5], loaded[7]
    conv_weight, router_local = small[4], small[12]
    count, inner_width = pre_grad.shape
    width = tokens.shape[1]
    count_experts, ways = lax.axis_size("expert"), lax.axis_size("batch")
    pairs, chunk = count_experts // 2, width // count_experts
    chunks = [(e.shape[0] // 4, e.shape[1]) for e in experts]
    taps = conv_weight.shape[0]
    vmem, hbm = (pl.BlockSpec(memory_space=m) for m in (pltpu.VMEM, pl.ANY))
    split = (chunk // 3, chunk * 2 // 3) if chunk % 48 == 0 else (chunk,)
    locals_ = [jax.ShapeDtypeStruct((pairs, 2, part, inner_width), BF16) for part in split]
    items = early + [Total(local, 1, i == 1) for i, local in enumerate(locals_)]
    scratch = [item.scratch() for item in items]
    kinds = tuple((item.kind(), len(refs)) for item, refs in zip(items, scratch))
    used = 2 * rank + 3 * states + 3 + router_local.shape[0] // 2
    high, low = (-(-rows // 16) * 16 for rows in (used, taps + 2))
    tiles = [-(-(rows // 16 * inner_width // LANES) // (2 * pairs)) for rows in (high, low)]
    f32 = lambda *shape: jax.ShapeDtypeStruct(shape, F32)
    halo = pltpu.VMEM((SEGS, inner_width), F32)
    rim = (taps - 1) * SEGS
    return pl.pallas_call(
        functools.partial(finish_kernel, rank, states, kinds),
        out_shape=[
            jax.ShapeDtypeStruct((count, width), BF16),
            f32(count, width),
            jax.ShapeDtypeStruct((chunk, 2 * inner_width), BF16),
            jax.ShapeDtypeStruct(early[1].chunk, BF16),
            f32(high, inner_width),
            f32(low, inner_width),
        ]
        + [jax.ShapeDtypeStruct(shape, BF16) for shape in chunks],
        in_specs=[hbm] * (len(loaded) + 4) + [vmem] * (len(small) + len(early)),
        out_specs=[vmem] * 6 + [hbm] * 2,
        scratch_shapes=[pltpu.VMEM(shape, BF16) for shape in chunks for _ in range(2)]
        + [pltpu.SemaphoreType.DMA((2, 1))] * 2
        + [pltpu.SemaphoreType.DMA((2,))] * 2
        + [pltpu.VMEM(a.shape, a.dtype) for a in loaded]
        + [
            pltpu.VMEM((count + rim, inner_width), F32),
            pltpu.VMEM((count + rim, inner_width), F32),
            pltpu.VMEM((count, inner_width), BF16),
            pltpu.VMEM((count, LANES), BF16),
            pltpu.VMEM((count, width), F32),
            halo,
            halo,
            pltpu.VMEM((width // LANES, count, LANES), F32),
            pltpu.SemaphoreType.DMA((len(loaded),)),
            pltpu.SemaphoreType.DMA((2,)),
        ]
        + SmallSum.scratch(pairs, ways, tiles[0])
        + TinySum.scratch(pairs, ways, -(-(taps + 2) * inner_width // LANES // 16) * 16)
        + [
            pltpu.VMEM((LANES, inner_width), BF16),
            pltpu.VMEM((LANES, inner_width), BF16),
            pltpu.VMEM((1, inner_width), F32),
        ]
        + [pltpu.VMEM(local.shape, BF16) for local in locals_]
        + [ref for refs in scratch for ref in refs],
        compiler_params=params(collective_id=collective_id, has_side_effects=True),
        name="finish",
    )(*loaded, *experts, *landed, *small, *(item.local for item in early))


def deliver_kernel(*refs):
    output_in, tokens_grad_in, in_proj, out_proj, flat, last = refs[:6]
    expert_hbm, landed_hbm, second_hbm, refs = refs[6:8], refs[8:10], refs[10:12], refs[12:]
    output, tokens_grad, gain, in_proj_out, conv, bias, x_proj, dt_proj, dt_bias, rate = refs[:10]
    skip, out_proj_out, gain_two, router, expert_in_out, expert_out_out = refs[10:16]
    held, sums, sems, store_sems = refs[16:22], refs[22:24], refs[24], refs[25]
    stores = [
        pltpu.make_async_copy(src, dst.at[0], store_sems.at[i])
        for i, (src, dst) in enumerate(
            (
                (output_in, output),
                (tokens_grad_in, tokens_grad),
                (sums[0], expert_in_out),
                (sums[1], expert_out_out),
            )
        )
    ]
    loads = []
    for i in range(2):
        halving = Halving(expert_hbm[i], i == 0)
        parts = (halving.chunk(halving.group), landed_hbm[i].at[0], second_hbm[i])
        for k, src in enumerate(parts):
            loads.append(pltpu.make_async_copy(src, held[3 * i + k], sems.at[i, k]))
    for load in loads:
        load.start()
    for store in stores[:2]:
        store.start()
    for i in range(2):
        for load in loads[3 * i : 3 * i + 3]:
            load.wait()
        total = together(*(ref[...] for ref in held[3 * i : 3 * i + 3]))
        sums[i][...] = total.astype(BF16).astype(F32)
        stores[2 + i].start()
    at, width = 0, gain.shape[0]
    for ref in (x_proj, dt_proj, rate):
        ref[...] = flat[at : at + ref.shape[0], :]
        at += ref.shape[0]
    fold = router.shape[0] // 2
    dt_bias[...] = flat[at : at + 1, :].reshape(dt_bias.shape)
    skip[...] = flat[at + 1 : at + 2, :].reshape(skip.shape)
    gain_two[...] = flat[at + 2 : at + 3, :width].reshape(gain_two.shape)
    router[:fold, :] = flat[at + 3 : at + 3 + fold, :width]
    router[fold:, :] = flat[at + 3 : at + 3 + fold, width:]
    taps = conv.shape[0]
    conv[...] = last[:taps, :]
    bias[...] = last[taps : taps + 1, :].reshape(bias.shape)
    gain[...] = last[taps + 1 : taps + 2, :width].reshape(gain.shape)
    in_proj_out[...] = in_proj[...].astype(F32)
    out_proj_out[...] = out_proj[...].astype(F32)
    for store in stores:
        store.wait()


def deliver(made, experts, landed, shapes):
    vmem = pl.BlockSpec(memory_space=pltpu.VMEM)
    hbm = pl.BlockSpec(memory_space=pl.ANY)
    output, tokens_grad, in_proj, out_proj, flat, last = made[:6]
    chunks = [(e.shape[0] // 4, e.shape[1]) for e in experts]
    f32 = lambda *shape: jax.ShapeDtypeStruct(shape, F32)
    outs = [
        jax.ShapeDtypeStruct((1, *output.shape), BF16),
        f32(1, *tokens_grad.shape),
        shapes[0],
        f32(*in_proj.shape),
        *shapes[1:8],
        f32(*out_proj.shape),
        *shapes[8:],
        *(f32(1, *shape) for shape in chunks),
    ]
    return pl.pallas_call(
        deliver_kernel,
        out_shape=outs,
        in_specs=[vmem] * 6 + [hbm] * 6,
        out_specs=[hbm] * 2 + [vmem] * (len(outs) - 4) + [hbm] * 2,
        scratch_shapes=[pltpu.VMEM(shape, BF16) for shape in chunks for _ in range(3)]
        + [pltpu.VMEM(shape, F32) for shape in chunks]
        + [pltpu.SemaphoreType.DMA((2, 3)), pltpu.SemaphoreType.DMA((4,))],
        compiler_params=params(),
        name="deliver",
    )(*made[:6], *experts, *landed, *made[6:])


def silu(v):
    return v * jax.nn.sigmoid(v)


def silu_slope(v):
    s = jax.nn.sigmoid(v)
    return s * (1.0 + v * (1.0 - s))


def rms_back(values, gain, grad):
    r = lax.rsqrt(jnp.mean(values * values, axis=-1, keepdims=True) + 1e-05)
    u = gain * grad
    mean = jnp.mean(values * u, axis=-1, keepdims=True)
    return r * u - values * (r * r * r) * mean, jnp.sum(grad * values * r, axis=0)


def rms(values, gain):
    return values * lax.rsqrt(jnp.mean(values * values, axis=-1, keepdims=True) + 1e-05) * gain


def per_device(
    tokens,
    routes,
    gain_one,
    in_proj,
    conv_weight,
    conv_bias,
    x_proj,
    dt_proj,
    dt_bias,
    rate_log,
    skip,
    out_proj,
    gain_two,
    router,
    expert_in,
    expert_out,
    cotangent,
):
    count, width = tokens.shape[1], tokens.shape[2]
    steps = count // SEGS
    inner_width = out_proj.shape[0]
    rank = dt_proj.shape[0]
    experts = router.shape[0]
    capacity = 5 * count // (4 * experts)
    slots = -(-capacity // 16) * 16
    states = rate_log.shape[0]
    route = routes.reshape(SEGS, steps).T.reshape(1, count)
    made, kept, spreads = forward(
        tokens,
        cotangent,
        in_proj,
        out_proj,
        route,
        gain_one,
        gain_two,
        conv_weight,
        conv_bias,
        x_proj,
        dt_proj,
        dt_bias,
        skip,
        rate_log,
        (rank, capacity, slots),
        2,
    )
    ssm, held, gated, hidden, normed_two, row, col, before, slot_upstream = made
    tokens_low, upstream_low, normed_one, inner, gate_z, mixed, pre, delta, proj = kept

    normed_two_grad, results, *expert_grads, router_local = run_experts(
        normed_two, row, col, router, slot_upstream, expert_in, expert_out, slots, 4
    )

    hidden_grad, gain_two_local, ssm_grad, gate_z_grad, out_proj_local, in_proj_gate_local = middle(
        hidden, normed_two_grad, upstream_low, gain_two, normed_one, gated, ssm, gate_z, out_proj
    )
    ways, pairs = lax.axis_size("batch"), experts // 2
    early = [
        Total(
            in_proj_gate_local.reshape(pairs, 2, width // experts, inner_width),
            1,
        ),
        Total(
            out_proj_local.reshape(
                pairs, 2, ways, inner_width // (experts * ways), width
            ),
            0,
            True,
        ),
    ]
    (
        in_proj_gate_spread,
        out_proj_spread,
        pre_grad,
        mixed_grad,
        rate_log_local,
        skip_local,
        dt_bias_local,
        bc_grad,
        returned,
        *landed,
    ) = mixer_grads(
        pre, delta, mixed, ssm_grad, spreads, rate_log, skip, held, results, expert_grads, rank, early, 3
    )
    early = [early[0].resumed(in_proj_gate_spread), early[1].resumed(out_proj_spread)]
    outs = finish(
        [
            pre_grad,
            mixed_grad,
            mixed,
            inner,
            normed_one,
            in_proj,
            gate_z_grad,
            tokens_low,
            hidden_grad,
            hidden,
            returned,
        ],
        expert_grads,
        landed,
        [
            bc_grad,
            proj,
            x_proj,
            dt_proj,
            conv_weight,
            conv_bias,
            before,
            gain_one,
            rate_log_local,
            dt_bias_local,
            skip_local,
            gain_two_local,
            router_local,
            col,
        ],
        early,
        rank,
        states,
        1,
    )
    outs = (*outs[:3], outs[3].reshape(-1, width), *outs[4:])
    weights = (gain_one, conv_weight, conv_bias, x_proj, dt_proj, dt_bias, rate_log, skip)
    shapes = [jax.ShapeDtypeStruct(w.shape, F32) for w in (*weights, gain_two, router)]
    return tuple(deliver(outs, expert_grads, landed, shapes))


def solution(mesh):
    split = P("batch", "expert", None)
    one = P("expert", None, None)
    both = P("expert", "batch", None)
    in_specs = (split, split) + (P(),) * 12 + (one, one, split)
    out_specs = (split, split, P(), P("expert", None)) + (P(),) * 7
    out_specs += (P("expert", None), P(), P(), both, both)
    return jax.shard_map(
        per_device, mesh=mesh, in_specs=in_specs, out_specs=out_specs, check_vma=False
    )
```
